32 devices in a mesh: dp: 8 (over z, core), block: 4 (over y, x).
Axes of the slice: x: 2, y: 2, z: 4, core: 2. Of those that a mesh axis runs over, the one named last changes fastest.
Arguments:
- tokens: bfloat16 [2, 512, 16384], P(None, 'block', 'dp'), may hold values from -6 to 6
- cotangent: float32 [2, 512, 16384], P(None, 'block', 'dp'), may hold values from -6 to 6
- item_lengths: int32 [2, 16], P(None, 'dp'), may hold values from 0 to 2048, as said below
- item_offsets: int32 [2, 16], P(None, 'dp'), may hold values from 0 to 2048
- norm_gain: float32 [2, 512], P(None, 'block'), may hold values from 0.5 to 1.5
- lambda_log: float32 [2, 384], P(None, 'block'), may hold values from -3 to 1
- lambda_imag: float32 [2, 384], P(None, 'block'), may hold values from -50 to 50
- log_step: float32 [2, 384], P(None, 'block'), may hold values from -6.9 to -2.3
- input_map: bfloat16 [2, 2, 384, 512], P(None, None, 'block'), may hold values from -0.25 to 0.25
- output_map: bfloat16 [2, 4, 384, 512], P(None, None, 'block'), may hold values from -0.75 to 0.75
- skip_weight: float32 [2, 512], P(None, 'block'), may hold values from -4 to 4
Outputs:
- output: float32 [2, 512, 16384], P(None, 'block', 'dp')
- input_grad: float32 [2, 512, 16384], P(None, 'block', 'dp')
- grad_norm_gain: float32 [2, 512], P(None, 'block')
- grad_lambda_log: float32 [2, 384], P(None, 'block')
- grad_lambda_imag: float32 [2, 384], P(None, 'block')
- grad_log_step: float32 [2, 384], P(None, 'block')
- grad_input_map: float32 [2, 2, 384, 512], P(None, None, 'block')
- grad_output_map: float32 [2, 4, 384, 512], P(None, None, 'block')
- grad_skip_weight: float32 [2, 512], P(None, 'block')
The draws below stay inside these ranges and needn't reach their ends.
Inputs may be any that keep to these rules, and one draw needn't show every extreme that they name: `item_lengths`: each run of 2048 slots holds its 2 items in order, without correlation, between them and around them padding slots. An item of length 0 has offset 2048. In every micro-batch one run holds a single item that fills all its slots.
All inputs are finite; a program needn't handle non-finite values.
Results may differ from the reference program's by a relative error of at most 0.039.
Values may be sent and summed in bfloat16 or wider, within the bound.
No kernel may reach another device: no remote copies, remote signals or barrier semaphores. Data moves between devices by JAX's collectives and lax.ppermute only.
A program may use at most 384 MiB of HBM per device.

```python
import jax
import jax.numpy as jnp
from jax import lax

H = 512
P_SIZE = 384
TOK_DEV = 2048
ITEMS = 2
MICRO = 2
LAYERS = 2
TOKENS = 16384
ITEMS_ALL = 16
N_DP = 8


def item_layout(key):
    devices = ITEMS_ALL // ITEMS
    key_list = jax.random.split(key, 5)
    padding = jax.random.randint(key_list[0], (MICRO, devices), 0, TOK_DEV // 2)
    chosen = jax.random.randint(key_list[1], (MICRO, 1), 0, devices)
    single = jnp.arange(devices, dtype=jnp.int32)[None, :] == chosen
    padding = jnp.where(single, 0, padding)
    filled = TOK_DEV - padding
    margin = TOK_DEV // 8
    first_len = jax.random.randint(key_list[2], (MICRO, devices), margin, filled - margin + 1)
    lead_gap = jax.random.randint(key_list[3], (MICRO, devices), 0, padding + 1)
    mid_gap = jax.random.randint(key_list[4], (MICRO, devices), 0, padding - lead_gap + 1)
    second_len = filled - first_len
    lengths = jnp.stack([jnp.where(single, TOK_DEV, first_len), jnp.where(single, 0, second_len)], axis=-1)
    offsets = jnp.stack([jnp.where(single, 0, lead_gap), jnp.where(single, TOK_DEV, lead_gap + first_len + mid_gap)], axis=-1)
    return (lengths.reshape(MICRO, devices * ITEMS).astype(jnp.int32), offsets.reshape(MICRO, devices * ITEMS).astype(jnp.int32))


def draw_item_lengths(key, part):
    shared = item_layout(key)
    return shared[0]


def draw_item_offsets(key, part):
    shared = item_layout(key)
    return shared[1]


def steps_of(own_key, shape, cuts, low, top_value):
    factor_of, own = 1.0, jax.random.fold_in(own_key, 6)
    for dim, blocks in cuts:
        heights = jnp.exp(jax.random.uniform(jax.random.fold_in(own, dim), (blocks,), jnp.float32, low / len(cuts), top_value / len(cuts)))
        factor_of = factor_of * jnp.repeat(heights, shape[dim] // blocks).reshape([-1 if axis == dim else 1 for axis in range(len(shape))])
    return factor_of


def bell_draw(rng, dims, scale, limit, shards=(), held_as=jnp.bfloat16):
    gain = steps_of(rng, dims, shards, -0.22, 0.18) if shards else 1.0
    values = jax.random.normal(rng, dims, jnp.float32) * scale * gain
    return jnp.minimum(jnp.maximum(values, -limit), limit).astype(held_as)


def setup_inputs(seed: int = 0) -> dict:
    key_of = jax.random.split(jax.random.key(seed), 12)
    tokens = bell_draw(key_of[0], (MICRO, H, TOKENS), 1.0, 6.0, ((1, 4), (2, 8)))
    cotangent = bell_draw(key_of[1], (MICRO, H, TOKENS), 1.0, 6.0, ((1, 4), (2, 8)), jnp.float32)
    item_lengths = draw_item_lengths(jax.random.fold_in(key_of[11], 71), 0)
    item_offsets = draw_item_offsets(jax.random.fold_in(key_of[11], 71), 0)
    norm_gain = jnp.clip(1.0 + 0.1 * jax.random.normal(key_of[4], (LAYERS, H), jnp.float32), 0.5, 1.5)
    lambda_log = jnp.clip(-3.0 + 4.0 * jax.random.uniform(key_of[5], (LAYERS, P_SIZE), jnp.float32) ** steps_of(key_of[5], (LAYERS, P_SIZE), ((1, 4),), -0.2, 0.2), -3.0, 1.0)
    lambda_imag = jnp.clip(jax.random.uniform(key_of[6], (LAYERS, P_SIZE), jnp.float32, -50.0, 50.0) * steps_of(key_of[6], (LAYERS, P_SIZE), ((1, 4),), -0.4, 0.0), -50.0, 50.0)
    log_step = jnp.clip(-6.9 + 4.6000001430511475 * jax.random.uniform(key_of[7], (LAYERS, P_SIZE), jnp.float32) ** steps_of(key_of[7], (LAYERS, P_SIZE), ((1, 4),), -0.2, 0.2), -6.9, -2.3)
    input_map = bell_draw(key_of[8], (LAYERS, 2, P_SIZE, H), H ** -0.5, 0.25, ((2, 4),))
    output_map = bell_draw(key_of[9], (LAYERS, 4, P_SIZE, H), (P_SIZE // 6) ** -0.5, 0.75, ((2, 4),))
    skip_weight = bell_draw(key_of[10], (LAYERS, H), 1.0, 4.0, ((1, 4),), jnp.float32)
    return {"tokens": tokens, "cotangent": cotangent, "item_lengths": item_lengths, "item_offsets": item_offsets, "norm_gain": norm_gain, "lambda_log": lambda_log, "lambda_imag": lambda_imag, "log_step": log_step, "input_map": input_map, "output_map": output_map, "skip_weight": skip_weight}


EPSILON = 1e-05
HIGHEST = lax.Precision.HIGHEST

@jax.custom_vjp
def low(v):
    return lax.optimization_barrier(v.astype(jnp.bfloat16)).astype(jnp.float32)

@jax.custom_vjp
def low_back(v):
    return v

def low_keep(v):
    return (low(v), None)

def low_pass(kept, grad):
    return (grad,)

def back_keep(v):
    return (v, None)

def back_low(kept, grad):
    return (low(grad),)
low.defvjp(low_keep, low_pass)
low_back.defvjp(back_keep, back_low)

def item_masks(lengths, offsets, count):
    position = jnp.arange(count, dtype=jnp.int32)[:, None]
    begin = offsets[..., None, :]
    finish = begin + lengths[..., None, :]
    inside = jnp.logical_and(position >= begin, position < finish)
    starting = jnp.logical_and(position == begin, lengths[..., None, :] > 0)
    return (jnp.any(inside, axis=-1).astype(jnp.float32), jnp.any(starting, axis=-1).astype(jnp.float32))

def complex_mul(left_real, left_imag, right_real, right_imag):
    return (left_real * right_real - left_imag * right_imag, left_real * right_imag + left_imag * right_real)

def combine(earlier, latter):
    factor_real, factor_imag = complex_mul(latter[0], latter[1], earlier[0], earlier[1])
    carry_real, carry_imag = complex_mul(latter[0], latter[1], earlier[2], earlier[3])
    return (factor_real, factor_imag, carry_real + latter[2], carry_imag + latter[3])

def discretize(lambda_log, lambda_imag, log_step, input_map):
    input_map = jnp.swapaxes(input_map, 1, 2)
    step_size = jnp.exp(log_step)
    lambda_real = -jnp.exp(lambda_log)
    modulus = jnp.exp(lambda_real * step_size)
    decay_real = modulus * jnp.cos(lambda_imag * step_size)
    decay_imag = modulus * jnp.sin(lambda_imag * step_size)
    denominator = lambda_real * lambda_real + lambda_imag * lambda_imag
    scale_real = ((decay_real - 1.0) * lambda_real + decay_imag * lambda_imag) / denominator
    scale_imag = (decay_imag * lambda_real - (decay_real - 1.0) * lambda_imag) / denominator
    drive_real = scale_real * input_map[0] - scale_imag * input_map[1]
    drive_imag = scale_real * input_map[1] + scale_imag * input_map[0]
    return (decay_real, decay_imag, jnp.concatenate([drive_real, drive_imag], axis=-1))

def both_ways(live_mask, opening, decay_real, decay_imag, driven):
    states_half = decay_real.shape[0]
    token_axis = driven.ndim - 2
    onward = live_mask * (1.0 - opening)
    onward_next = jnp.concatenate([onward[..., 1:], jnp.zeros_like(onward[..., :1])], axis=-1)
    inputs = driven * live_mask[..., None]
    forward_states = lax.associative_scan(combine, (onward[..., None] * decay_real, onward[..., None] * decay_imag, inputs[..., :states_half], inputs[..., states_half:]), axis=token_axis)
    backward_states = lax.associative_scan(combine, (onward_next[..., None] * decay_real, onward_next[..., None] * decay_imag, inputs[..., :states_half], inputs[..., states_half:]), reverse=True, axis=token_axis)
    return jnp.concatenate([forward_states[2], forward_states[3], backward_states[2], backward_states[3]], axis=-1)

def output_rows(output_map):
    sign_rows = jnp.array([2.0, -2.0, 2.0, -2.0], dtype=output_map.dtype)[:, None, None]
    return (output_map * sign_rows).reshape(-1, output_map.shape[-1])

def s5_layer(inputs, gain_row, lambda_log, lambda_imag, log_step, input_map, output_map, skip_row, live_mask, opening):
    mean_square = lax.optimization_barrier(jnp.mean(inputs * inputs, axis=-1, keepdims=True))
    normed = low(inputs * lax.rsqrt(mean_square + EPSILON) * gain_row)
    decay_real, decay_imag, drive_map = discretize(lambda_log, lambda_imag, log_step, input_map)
    driven = low_back(jnp.einsum('mdth,hq->mdtq', normed, low(drive_map), precision=HIGHEST))
    states = low(both_ways(live_mask, opening, decay_real, decay_imag, driven))
    mixed_rows = low_back(jnp.einsum('mdtq,qh->mdth', states, output_rows(output_map), precision=HIGHEST))
    return inputs + live_mask[..., None] * jax.nn.gelu(mixed_rows + skip_row * normed)

def reference(tokens, cotangent, item_lengths, item_offsets, norm_gain, lambda_log, lambda_imag, log_step, input_map, output_map, skip_weight):
    batches = tokens.shape[0]
    blocked_shape = (batches, N_DP, TOK_DEV, H)
    token_rows = jnp.swapaxes(tokens.astype(jnp.float32), 1, 2).reshape(blocked_shape)
    cot_rows = jnp.swapaxes(cotangent, 1, 2).reshape(blocked_shape)
    live_mask, opening = item_masks(item_lengths.reshape(batches, N_DP, ITEMS), item_offsets.reshape(batches, N_DP, ITEMS), TOK_DEV)

    def forward(token_rows, norm_gain, lambda_log, lambda_imag, log_step, input_map, output_map, skip_weight):
        hidden = token_rows
        for layer_index in range(LAYERS):
            hidden = s5_layer(hidden, norm_gain[layer_index], lambda_log[layer_index], lambda_imag[layer_index], log_step[layer_index], input_map[layer_index], output_map[layer_index], skip_weight[layer_index], live_mask, opening)
        return hidden
    result, pullback = jax.vjp(forward, token_rows, norm_gain, lambda_log, lambda_imag, log_step, input_map.astype(jnp.float32), output_map.astype(jnp.float32), skip_weight)
    gradients = pullback(cot_rows)
    row_shape = (batches, N_DP * TOK_DEV, H)
    out_rows = jnp.swapaxes(result.reshape(row_shape), 1, 2)
    grad_rows = jnp.swapaxes(gradients[0].reshape(row_shape), 1, 2)
    return (out_rows, grad_rows, gradients[1], gradients[2], gradients[3], gradients[4], gradients[5], gradients[6], gradients[7])
```

```python
from functools import partial
from typing import NamedTuple

import jax
import jax.numpy as jnp
from jax import lax
from jax.experimental import pallas as pl
from jax.experimental.pallas import tpu as pltpu
from jax.sharding import PartitionSpec as P

EPSILON = 1e-05
SEGS = 16
LANES = 128
BF = jnp.bfloat16
F32 = jnp.float32
GELU_C = 0.7978845608028654
GELU_A = 0.044715


class Sizes(NamedTuple):
    blocks: int
    chunks: int
    toks: int
    run: int
    steps: int
    width: int
    states: int
    items: int


def nt(a, b):
    return lax.dot_general(a, b, (((1,), (1,)), ((), ())), preferred_element_type=F32)


def nn(a, b):
    return lax.dot_general(a, b, (((1,), (0,)), ((), ())), preferred_element_type=F32)


def tn(a, b):
    return lax.dot_general(a, b, (((0,), (0,)), ((), ())), preferred_element_type=F32)


def cmul(ar, ai, br, bi):
    return ar * br - ai * bi, ar * bi + ai * br


def rows_of(step):
    return pl.ds(pl.multiple_of(step * SEGS, SEGS), SEGS)


def widen(mask, count):
    return jnp.concatenate([mask] * count, axis=1)


def item_of(sz, meta, index):
    begin = meta[2 + sz.items + index]
    return begin, begin + meta[2 + index]


def fill_masks(sz, meta, live, ahead, behind):
    base = meta[1] * sz.toks
    seg = lax.broadcasted_iota(jnp.int32, (SEGS, LANES), 0)

    def body(step, carry):
        pos = base + seg * sz.steps + step
        inside = jnp.zeros((SEGS, LANES), F32)
        onward = jnp.zeros((SEGS, LANES), F32)
        onward_next = jnp.zeros((SEGS, LANES), F32)
        for index in range(sz.items):
            begin, end = item_of(sz, meta, index)
            inside = jnp.where((pos >= begin) & (pos < end), 1.0, inside)
            onward = jnp.where((pos > begin) & (pos < end), 1.0, onward)
            onward_next = jnp.where((pos >= begin) & (pos + 1 < end), 1.0, onward_next)
        onward_next = jnp.where(pos + 1 < sz.run, onward_next, 0.0)
        if live is not None:
            live[rows_of(step), :] = inside
        ahead[rows_of(step), :] = onward
        behind[rows_of(step), :] = onward_next
        return carry

    lax.fori_loop(0, sz.steps, body, 0, unroll=4)


def through(sz, meta, first, length):
    ahead = behind = False
    for index in range(sz.items):
        begin, end = item_of(sz, meta, index)
        ahead = ahead | ((begin < first) & (end >= first + length))
        behind = behind | ((begin <= first) & (end > first + length))
    behind = behind & (first + length < sz.run)
    return ahead, behind


def power(pair, count):
    while count > 1:
        pair = cmul(*pair, *pair)
        count //= 2
    return pair


def column_blocks(sz, decay):
    out = []
    for q in range(sz.states // LANES):
        cols = slice(q * LANES, (q + 1) * LANES)
        out.append((decay[0:1, cols], decay[1:2, cols]))
    return out


def spread(pairs):
    return [tuple(jnp.broadcast_to(v, (SEGS, LANES)) for v in pair) for pair in pairs]


def chain_ends(sz, decay, ahead, behind, source, ahead_col, behind_col, ends):
    nq = sz.states // LANES
    d = spread(column_blocks(sz, decay))
    zero = jnp.zeros((SEGS, LANES), F32)

    def body(step, held):
        up, down = rows_of(step), rows_of(sz.steps - 1 - step)
        on_up, on_down = ahead[up, :], behind[down, :]
        new = []
        for q in range(nq):
            for side, (rows, on, col) in enumerate(((up, on_up, ahead_col), (down, on_down, behind_col))):
                re, im = held[2 * q + side]
                re, im = cmul(*d[q], re * on, im * on)
                re += source[rows, col + q * LANES : col + (q + 1) * LANES]
                im += source[rows, col + sz.states + q * LANES : col + sz.states + (q + 1) * LANES]
                new.append((re, im))
        return tuple(new)

    held = lax.fori_loop(0, sz.steps, body, tuple((zero, zero) for _ in range(2 * nq)), unroll=4)
    for q in range(nq):
        cols = slice(q * LANES, (q + 1) * LANES)
        for side in range(2):
            ends[2 * side, :, cols] = held[2 * q + side][0]
            ends[2 * side + 1, :, cols] = held[2 * q + side][1]


def enter_states(sz, meta, decay, ends, start, enter):
    pair = (decay[0:1, :], decay[1:2, :])
    jump = power(pair, sz.steps)
    base = meta[1] * sz.toks
    state = list(start)
    for count in range(SEGS):
        for side, seg in ((0, count), (1, SEGS - 1 - count)):
            re, im = state[side]
            enter[2 * side, seg : seg + 1, :] = re
            enter[2 * side + 1, seg : seg + 1, :] = im
            passes = through(sz, meta, base + seg * sz.steps, sz.steps)[side]
            gain = jnp.where(passes, 1.0, 0.0).astype(F32)
            re, im = cmul(jump[0] * gain, jump[1] * gain, re, im)
            state[side] = (
                re + ends[2 * side, seg : seg + 1, :],
                im + ends[2 * side + 1, seg : seg + 1, :],
            )
    return state


def send_ends(sz, meta, decay, ends, enter, send):
    zero = jnp.zeros((1, sz.states), F32)
    ahead, behind = enter_states(sz, meta, decay, ends, ((zero, zero), (zero, zero)), enter)
    me = meta[1]
    for dist in range(1, sz.chunks):
        up = (me ^ dist) > me
        for part in range(2):
            send[dist - 1, part : part + 1, :] = jnp.where(up, ahead[part], behind[part])


def received(sz, meta, decay, recv):
    me = meta[1]
    zero = jnp.zeros((1, sz.states), F32)
    pair = (decay[0:1, :], decay[1:2, :])
    jump = power(pair, sz.toks) if sz.chunks > 2 else None
    sides = []
    for side in range(2):
        re, im = zero, zero
        order = range(sz.chunks) if side == 0 else range(sz.chunks - 1, -1, -1)
        for other in order:
            use = (other < me) if side == 0 else (other > me)
            slot = jnp.maximum((me ^ other) - 1, 0)
            got = recv[slot]
            new_re, new_im = got[0:1, :], got[1:2, :]
            if sz.chunks > 2:
                passes = through(sz, meta, other * sz.toks, sz.toks)[side]
                gain = jnp.where(passes, 1.0, 0.0).astype(F32)
                moved = cmul(jump[0] * gain, jump[1] * gain, re, im)
                new_re, new_im = new_re + moved[0], new_im + moved[1]
            re, im = jnp.where(use, new_re, re), jnp.where(use, new_im, im)
        sides.append((re, im))
    return sides


def load_enter(sz, enter):
    held = []
    for q in range(sz.states // LANES):
        cols = slice(q * LANES, (q + 1) * LANES)
        for side in range(2):
            held.append((enter[2 * side, :, cols], enter[2 * side + 1, :, cols]))
    return tuple(held)


def chain_states(sz, decay, ahead, behind, source, enter, states):
    nq = sz.states // LANES
    n = sz.states
    d = spread(column_blocks(sz, decay))

    def body(step, held):
        up, down = rows_of(step), rows_of(sz.steps - 1 - step)
        on_up, on_down = ahead[up, :], behind[down, :]
        new = []
        for q in range(nq):
            for side, (rows, on) in enumerate(((up, on_up), (down, on_down))):
                re, im = held[2 * q + side]
                re, im = cmul(*d[q], re * on, im * on)
                lo = q * LANES
                re += source[rows, lo : lo + LANES]
                im += source[rows, n + lo : n + lo + LANES]
                at = 2 * side * n + lo
                states[rows, at : at + LANES] = re.astype(BF)
                states[rows, at + n : at + n + LANES] = (-im).astype(BF)
                new.append((re, im))
        return tuple(new)

    lax.fori_loop(0, sz.steps, body, load_enter(sz, enter), unroll=4)


def adjoint_chains(sz, decay, ahead, behind, source, enter, states, half, grad_driven, grad_decay):
    nq = sz.states // LANES
    n = sz.states
    d = spread(column_blocks(sz, decay))
    zero = jnp.zeros((SEGS, LANES), F32)

    def make(second):
        def body(step, carry):
            held, sums = carry
            up, down = rows_of(step), rows_of(sz.steps - 1 - step)
            on_up, on_down = ahead[up, :], behind[down, :]
            new, total = [], []
            for q in range(nq):
                lo = q * LANES
                acc_re, acc_im = sums[q]
                for side, (rows, on, src, st) in enumerate(((up, on_up, 2 * n, 2 * n), (down, on_down, 0, 0))):
                    re, im = held[2 * q + side]
                    re, im = re * on, im * on
                    s_re = states[rows, st + lo : st + lo + LANES].astype(F32)
                    s_im = states[rows, st + n + lo : st + n + lo + LANES].astype(F32)
                    acc_re += re * s_re + im * s_im
                    acc_im += re * s_im - im * s_re
                    re, im = cmul(*d[q], re, im)
                    re += source[rows, src + lo : src + lo + LANES]
                    im += source[rows, src + n + lo : src + n + lo + LANES]
                    new.append((re, im))
                    if second:
                        out_re = re + half[rows, lo : lo + LANES]
                        out_im = im + half[rows, n + lo : n + lo + LANES]
                        grad_driven[rows, lo : lo + LANES] = out_re.astype(BF)
                        grad_driven[rows, n + lo : n + lo + LANES] = (-out_im).astype(BF)
                    else:
                        half[rows, lo : lo + LANES] = re
                        half[rows, n + lo : n + lo + LANES] = im
                total.append((acc_re, acc_im))
            return tuple(new), tuple(total)

        return body

    carry = (load_enter(sz, enter), tuple((zero, zero) for _ in range(nq)))
    carry = lax.fori_loop(0, sz.steps // 2, make(False), carry, unroll=2)
    carry = lax.fori_loop(sz.steps // 2, sz.steps, make(True), carry, unroll=2)
    for q in range(nq):
        cols = slice(q * LANES, (q + 1) * LANES)
        grad_decay[0:1, cols] = jnp.sum(carry[1][q][0], axis=0, keepdims=True)
        grad_decay[1:2, cols] = jnp.sum(carry[1][q][1], axis=0, keepdims=True)


ROWS = 64


def over_rows(sz, body, init=0):
    def step(index, carry):
        return body(pl.ds(pl.multiple_of(index * ROWS, ROWS), ROWS), carry)

    return lax.fori_loop(0, sz.toks // ROWS, step, init)


def norm_rows(sz, hidden, gain, live, normed):
    def body(rows, carry):
        u = hidden[rows, :].astype(F32)
        scale = lax.rsqrt(jnp.mean(u * u, axis=1, keepdims=True) + EPSILON)
        v = u * scale * gain[...]
        normed[rows, :] = (v * widen(live[rows, :], sz.width // LANES)).astype(BF)
        return carry

    over_rows(sz, body)


def matmul_nt(a, b, out, tile=256):
    for lo in range(0, b.shape[0], tile):
        out[:, lo : lo + tile] = nt(a[...], b[lo : lo + tile, :]).astype(out.dtype)


def matmul_nn(a, b, out, tile=256):
    for lo in range(0, b.shape[1], tile):
        out[:, lo : lo + tile] = nn(a[...], b[:, lo : lo + tile]).astype(out.dtype)


def matmul_tn(a, b, out, tile=256):
    for lo in range(0, a.shape[1], tile):
        out[lo : lo + tile, :] = tn(a[:, lo : lo + tile], b[...]).astype(out.dtype)


def finish_rows(sz, mixed, skip, normed, live, hidden, slope, result):
    def body(rows, carry):
        pre = 2.0 * mixed[rows, :] + skip[...] * normed[rows, :].astype(F32)
        square = pre * pre
        th = jnp.tanh(pre * (GELU_C + (GELU_C * GELU_A) * square))
        on = widen(live[rows, :], sz.width // LANES)
        part = 0.5 * (1.0 + th)
        deriv = part + 0.5 * pre * (1.0 - th * th) * (GELU_C + (3.0 * GELU_C * GELU_A) * square)
        slope[rows, :] = (on * deriv).astype(slope.dtype)
        result[rows, :] = (hidden[rows, :].astype(F32) + on * (pre * part)).astype(result.dtype)
        return carry

    over_rows(sz, body)


def layer_open(sz, meta, hidden, gain, w_in, decay, live, ahead, behind, normed, driven, ends, enter, send):
    norm_rows(sz, hidden, gain, live, normed)
    matmul_nt(normed, w_in, driven)
    chain_ends(sz, decay, ahead, behind, driven, 0, 0, ends)
    send_ends(sz, meta, decay, ends, enter, send)


def layer_close(sz, meta, recv, decay, ends, driven, normed, hidden, w_out, skip, live, ahead, behind, enter, mixed, states, slope, result):
    enter_states(sz, meta, decay, ends, received(sz, meta, decay, recv), enter)
    chain_states(sz, decay, ahead, behind, driven, enter, states)
    matmul_nn(states, w_out, mixed)
    finish_rows(sz, mixed, skip, normed, live, hidden, slope, result)


def back_open(sz, meta, upstream, slope, normed, w_out, decay, ahead, behind, twice, grad_states, grad_skip, ends, enter, send):
    def body(rows, total):
        e = upstream[rows, :] * slope[rows, :].astype(F32)
        low = e.astype(BF)
        twice[rows, :] = low + low
        part = e * normed[rows, :].astype(F32)
        return total + jnp.sum(part.reshape(ROWS // 8, 8, sz.width), axis=0)

    total = over_rows(sz, body, jnp.zeros((8, sz.width), F32))
    grad_skip[...] = jnp.sum(total, axis=0, keepdims=True)
    matmul_nt(twice, w_out, grad_states)
    chain_ends(sz, decay, ahead, behind, grad_states, 2 * sz.states, 0, ends)
    send_ends(sz, meta, decay, ends, enter, send)


def back_close(sz, meta, recv, decay, ends, grad_states, states, upstream, slope, skip, hidden, gain, w_in, ahead, behind,
               enter, half, grad_normed, grad_driven, grad_decay, grad_gain, result):
    enter_states(sz, meta, decay, ends, received(sz, meta, decay, recv), enter)
    adjoint_chains(sz, decay, ahead, behind, grad_states, enter, states, half, grad_driven, grad_decay)
    matmul_nn(grad_driven, w_in, grad_normed)

    def body(rows, total):
        u = hidden[rows, :].astype(F32)
        r = upstream[rows, :]
        gn = grad_normed[rows, :] + r * slope[rows, :].astype(F32) * skip[...]
        scale = lax.rsqrt(jnp.mean(u * u, axis=1, keepdims=True) + EPSILON)
        part = gn * u * scale
        dn = gn * gain[...]
        inner = jnp.sum(dn * u, axis=1, keepdims=True) * (1.0 / sz.width)
        result[rows, :] = (r + scale * dn - u * (scale * scale * scale * inner)).astype(result.dtype)
        return total + jnp.sum(part.reshape(ROWS // 8, 8, sz.width), axis=0)

    total = over_rows(sz, body, jnp.zeros((8, sz.width), F32))
    grad_gain[...] = jnp.sum(total, axis=0, keepdims=True)


def place_pieces(sz, meta, pieces, stacked):
    part = sz.width // sz.blocks
    for dist, piece in enumerate(pieces):
        owner = meta[0] ^ dist
        stacked[pl.ds(pl.multiple_of(owner * part, part), part), :] = piece[...]


def cut_pieces(sz, meta, rows, perm, stacked, pieces):
    part = sz.width // sz.blocks
    matmul_tn(rows, perm, stacked)
    for dist, piece in enumerate(pieces):
        owner = meta[0] ^ dist
        piece[...] = stacked[pl.ds(pl.multiple_of(owner * part, part), part), :]


def enter_kernel(sz, meta, gain, w_in, decay, perm, *refs):
    pieces, refs = refs[: sz.blocks], refs[sz.blocks :]
    hidden, normed, driven, ends, send, stacked, live, ahead, behind, enter = refs
    place_pieces(sz, meta, pieces, stacked)
    matmul_nt(perm, stacked, hidden)
    fill_masks(sz, meta, live, ahead, behind)
    layer_open(sz, meta, hidden, gain, w_in, decay, live, ahead, behind, normed, driven, ends, enter, send)


def middle_kernel(sz, meta, recv, decay, ends, driven, normed, hidden, w_out, skip, gain_b, w_in_b, decay_b,
                  states, slope, hidden_b, normed_b, driven_b, ends_b, send_b, live, ahead, behind, enter, mixed):
    fill_masks(sz, meta, live, ahead, behind)
    layer_close(sz, meta, recv, decay, ends, driven, normed, hidden, w_out, skip, live, ahead, behind, enter, mixed, states, slope, hidden_b)
    layer_open(sz, meta, hidden_b, gain_b, w_in_b, decay_b, live, ahead, behind, normed_b, driven_b, ends_b, enter, send_b)


def leave_kernel(sz, meta, recv, decay, ends, driven, normed, hidden, w_out, skip, perm, states, slope, *refs):
    pieces, refs = refs[: sz.blocks], refs[sz.blocks :]
    live, ahead, behind, enter, mixed, last, stacked = refs
    fill_masks(sz, meta, live, ahead, behind)
    layer_close(sz, meta, recv, decay, ends, driven, normed, hidden, w_out, skip, live, ahead, behind, enter, mixed, states, slope, last)
    cut_pieces(sz, meta, last, perm, stacked, pieces)


def turn_kernel(sz, meta, slope, normed, w_out, decay, perm, *refs):
    pieces, refs = refs[: sz.blocks], refs[sz.blocks :]
    upstream, twice, grad_states, grad_skip, ends, send, stacked, ahead, behind, enter = refs
    place_pieces(sz, meta, pieces, stacked)
    matmul_nt(perm, stacked, upstream)
    fill_masks(sz, meta, None, ahead, behind)
    back_open(sz, meta, upstream, slope, normed, w_out, decay, ahead, behind, twice, grad_states, grad_skip, ends, enter, send)


def back_middle_kernel(sz, meta, recv, decay, ends, grad_states, states, upstream, slope, skip, hidden, gain, w_in,
                       slope_b, normed_b, w_out_b, decay_b,
                       grad_driven, grad_decay, grad_gain, upstream_b, twice_b, grad_states_b, grad_skip_b, ends_b, send_b,
                       ahead, behind, enter, half, grad_normed):
    fill_masks(sz, meta, None, ahead, behind)
    back_close(sz, meta, recv, decay, ends, grad_states, states, upstream, slope, skip, hidden, gain, w_in, ahead, behind,
               enter, half, grad_normed, grad_driven, grad_decay, grad_gain, upstream_b)
    back_open(sz, meta, upstream_b, slope_b, normed_b, w_out_b, decay_b, ahead, behind, twice_b, grad_states_b, grad_skip_b, ends_b, enter, send_b)


def back_leave_kernel(sz, meta, recv, decay, ends, grad_states, states, upstream, slope, skip, hidden, gain, w_in, perm,
                      grad_driven, grad_decay, grad_gain, *refs):
    pieces, refs = refs[: sz.blocks], refs[sz.blocks :]
    ahead, behind, enter, half, grad_normed, last, stacked = refs
    fill_masks(sz, meta, None, ahead, behind)
    back_close(sz, meta, recv, decay, ends, grad_states, states, upstream, slope, skip, hidden, gain, w_in, ahead, behind,
               enter, half, grad_normed, grad_driven, grad_decay, grad_gain, last)
    cut_pieces(sz, meta, last, perm, stacked, pieces)


def weight_kernel(left, right, out):
    matmul_tn(left, right, out)


VMEM = pl.BlockSpec(memory_space=pltpu.VMEM)
SMEM = pl.BlockSpec(memory_space=pltpu.SMEM)


def call(name, body, meta, args, outs, scratch, flops, limit=20):
    has_meta = meta is not None
    out_shape = [jax.ShapeDtypeStruct(shape, dtype) for shape, dtype in outs]
    moved = sum(a.size * a.dtype.itemsize for a in args) + sum(o.size * o.dtype.itemsize for o in out_shape)
    return pl.pallas_call(
        body,
        out_shape=out_shape,
        in_specs=[SMEM] * has_meta + [VMEM] * len(args),
        out_specs=[VMEM] * len(outs),
        scratch_shapes=[pltpu.VMEM(shape, dtype) for shape, dtype in scratch],
        compiler_params=pltpu.CompilerParams(vmem_limit_bytes=limit << 20),
        cost_estimate=pl.CostEstimate(flops=flops, bytes_accessed=moved, transcendentals=0),
        name=name,
    )(*([meta] if has_meta else []), *args)


def discretize(lambda_log, lambda_imag, log_step, input_map):
    step_size = jnp.exp(log_step)
    lambda_real = -jnp.exp(lambda_log)
    modulus = jnp.exp(lambda_real * step_size)
    decay_real = modulus * jnp.cos(lambda_imag * step_size)
    decay_imag = modulus * jnp.sin(lambda_imag * step_size)
    denominator = lambda_real * lambda_real + lambda_imag * lambda_imag
    scale_real = ((decay_real - 1.0) * lambda_real + decay_imag * lambda_imag) / denominator
    scale_imag = (decay_imag * lambda_real - (decay_real - 1.0) * lambda_imag) / denominator
    scale_real, scale_imag = scale_real[:, None], scale_imag[:, None]
    drive_real = scale_real * input_map[0] - scale_imag * input_map[1]
    drive_imag = scale_real * input_map[1] + scale_imag * input_map[0]
    return decay_real, decay_imag, jnp.stack([drive_real, drive_imag])


def on_device(tokens, cotangent, item_lengths, item_offsets, norm_gain, lambda_log, lambda_imag, log_step, input_map, output_map, skip_weight):
    micro, part, run = tokens.shape
    layers = norm_gain.shape[0]
    blocks = lax.axis_size("block")
    chunks = blocks // micro
    toks = run // chunks
    own = lambda_log.shape[1]
    width, states = part * blocks, own * blocks
    sz = Sizes(blocks, chunks, toks, run, toks // SEGS, width, states, item_lengths.shape[1])
    me = lax.axis_index("block")
    mine, chunk = me // chunks, me % chunks

    def swap(x, dist):
        return lax.ppermute(x, "block", [(i, i ^ dist) for i in range(blocks)])

    def to_chunks(x):
        out = []
        for dist in range(blocks):
            to = me ^ dist
            piece = lax.dynamic_slice(x, (to // chunks, 0, (to % chunks) * toks), (1, part, toks))[0].astype(BF)
            out.append(swap(piece, dist) if dist else piece)
        return out

    def from_chunks(pieces):
        out = jnp.zeros((micro, part, run), F32)
        for dist, piece in enumerate(pieces):
            got = swap(piece, dist) if dist else piece
            owner = me ^ dist
            out = lax.dynamic_update_slice(out, got.astype(F32)[None], (owner // chunks, 0, (owner % chunks) * toks))
        return out

    def exchange(send):
        return jnp.stack([swap(send[dist - 1], dist) for dist in range(1, chunks)])

    meta = jnp.concatenate([
        jnp.stack([me, chunk]).astype(jnp.int32),
        lax.dynamic_index_in_dim(item_lengths, mine, 0, keepdims=False),
        lax.dynamic_index_in_dim(item_offsets, mine, 0, keepdims=False),
    ])
    row = jnp.arange(toks, dtype=jnp.int32)[:, None]
    col = jnp.arange(toks, dtype=jnp.int32)[None, :]
    perm = ((row % SEGS) * sz.steps + row // SEGS == col).astype(BF)

    token_pieces = to_chunks(tokens)
    discrete, pulls = [], []
    for layer in range(layers):
        values, pull = jax.vjp(discretize, lambda_log[layer], lambda_imag[layer], log_step[layer], input_map[layer].astype(F32))
        discrete.append(values)
        pulls.append(pull)
    small = jnp.concatenate(
        [norm_gain, skip_weight, jnp.stack([v[0] for v in discrete]), jnp.stack([v[1] for v in discrete])], axis=1
    )
    small = lax.all_gather(small, "block", axis=0)
    joined = lambda lo, n: jnp.swapaxes(small[:, :, lo : lo + n], 0, 1).reshape(layers, blocks * n)
    gains = joined(0, part)
    skips = joined(part, part)
    decays = jnp.stack([joined(2 * part, own), joined(2 * part + own, own)], axis=1)
    w_in = [lax.all_gather(v[2].astype(BF), "block", axis=1, tiled=True).reshape(2 * states, width) for v in discrete]
    w_out = [lax.all_gather(output_map[l], "block", axis=1, tiled=True).reshape(4 * states, width) for l in range(layers)]
    gain = [gains[l : l + 1] for l in range(layers)]
    skip = [skips[l : l + 1] for l in range(layers)]
    decay = [decays[l] for l in range(layers)]

    mask = ((toks, LANES), F32)
    enter = ((4, SEGS, states), F32)
    stacked = ((width, toks), BF)
    rows_f, rows_b = ((toks, width), F32), ((toks, width), BF)
    drv = ((toks, 2 * states), F32)
    sts = ((toks, 4 * states), BF)
    gst = ((toks, 4 * states), F32)
    snd = ((chunks - 1, 2, states), F32)
    line, gdec = ((1, width), F32), ((2, states), F32)
    piece_out = [((part, toks), BF)] * blocks
    unit = 2 * toks * width * states

    hidden_a, normed_a, driven_a, ends_a, send_a = call(
        "enter", partial(enter_kernel, sz), meta, [gain[0], w_in[0], decay[0], perm, *token_pieces],
        [rows_b, rows_b, drv, enter, snd], [stacked, mask, mask, mask, enter], 4 * unit)
    cot_pieces = to_chunks(cotangent)
    recv = exchange(send_a)
    states_a, slope_a, hidden_b, normed_b, driven_b, ends_b, send_b = call(
        "middle", partial(middle_kernel, sz), meta,
        [recv, decay[0], ends_a, driven_a, normed_a, hidden_a, w_out[0], skip[0], gain[1], w_in[1], decay[1]],
        [sts, rows_b, rows_f, rows_b, drv, enter, snd], [mask, mask, mask, enter, rows_f], 8 * unit)
    recv = exchange(send_b)
    states_b, slope_b, *out_pieces = call(
        "leave", partial(leave_kernel, sz), meta, [recv, decay[1], ends_b, driven_b, normed_b, hidden_b, w_out[1], skip[1], perm],
        [sts, rows_b, *piece_out], [mask, mask, mask, enter, rows_f, rows_b, stacked], 7 * unit)
    output = from_chunks(out_pieces)

    up_b, twice_b, gstates_b, gskip_b, ends, send = call(
        "turn", partial(turn_kernel, sz), meta, [slope_b, normed_b, w_out[1], decay[1], perm, *cot_pieces],
        [rows_f, rows_b, gst, line, enter, snd], [stacked, mask, mask, enter], 7 * unit)
    recv = exchange(send)
    (gout_b,) = call("grad_out_b", weight_kernel, None, [states_b, twice_b], [((4 * states, width), BF)], [], 4 * unit)
    gdriven_b, gdecay_b, ggain_b, up_a, twice_a, gstates_a, gskip_a, ends, send = call(
        "back_middle", partial(back_middle_kernel, sz), meta,
        [recv, decay[1], ends, gstates_b, states_b, up_b, slope_b, skip[1], hidden_b, gain[1], w_in[1], slope_a, normed_a, w_out[0], decay[0]],
        [((toks, 2 * states), BF), gdec, line, rows_f, rows_b, gst, line, enter, snd], [mask, mask, enter, drv, rows_f], 10 * unit)
    recv = exchange(send)
    (gin_b,) = call("grad_in_b", weight_kernel, None, [gdriven_b, normed_b], [((2 * states, width), BF)], [], 2 * unit)
    (gout_a,) = call("grad_out_a", weight_kernel, None, [states_a, twice_a], [((4 * states, width), BF)], [], 4 * unit)
    gdriven_a, gdecay_a, ggain_a, *grad_pieces = call(
        "back_leave", partial(back_leave_kernel, sz), meta,
        [recv, decay[0], ends, gstates_a, states_a, up_a, slope_a, skip[0], hidden_a, gain[0], w_in[0], perm],
        [((toks, 2 * states), BF), gdec, line, *piece_out], [mask, mask, enter, drv, rows_f, rows_b, stacked], 6 * unit)
    input_grad = from_chunks(grad_pieces)
    (gin_a,) = call("grad_in_a", weight_kernel, None, [gdriven_a, normed_a], [((2 * states, width), BF)], [], 2 * unit)

    def reduce_weights(gin, gout):
        whole = jnp.concatenate([gin.reshape(2, states, width), gout.reshape(4, states, width)])
        shard = lax.psum_scatter(whole, "block", scatter_dimension=1, tiled=True)
        return lax.psum(shard, "dp").astype(F32)

    big = jnp.stack([reduce_weights(gin_a, gout_a), reduce_weights(gin_b, gout_b)])
    tiny = jnp.concatenate([
        jnp.concatenate([ggain_a, ggain_b]), jnp.concatenate([gskip_a, gskip_b]),
        jnp.stack([gdecay_a, gdecay_b]).reshape(layers, 2 * states)], axis=1)
    tiny = lax.psum(tiny, ("dp", "block"))
    cut = lambda lo, n: lax.dynamic_slice_in_dim(tiny, lo + me * n, n, 1)
    grad_gain, grad_skip = cut(0, part), cut(width, part)
    gdr, gdi = cut(2 * width, own), cut(2 * width + states, own)
    pulled = [pulls[l]((gdr[l], gdi[l], big[l, :2])) for l in range(layers)]
    grad_log, grad_imag, grad_step, grad_in = (jnp.stack([p[i] for p in pulled]) for i in range(4))
    return output, input_grad, grad_gain, grad_log, grad_imag, grad_step, grad_in, big[:, 2:], grad_skip


def solution(mesh):
    half = P(None, "block")
    maps = P(None, None, "block", None)
    acts = P(None, "block", "dp")
    items = P(None, "dp")
    return jax.shard_map(
        on_device,
        mesh=mesh,
        in_specs=(acts, acts, items, items, half, half, half, half, maps, maps, half),
        out_specs=(acts, acts, half, half, half, half, maps, maps, half),
        check_vma=False,
    )
```

```python
from functools import partial
from typing import NamedTuple

import jax
import jax.numpy as jnp
from jax import lax
from jax.experimental import pallas as pl
from jax.experimental.pallas import tpu as pltpu
from jax.sharding import Mesh, PartitionSpec as P

EPSILON = 1e-05
SEGS = 16
LANES = 128
BF = jnp.bfloat16
F32 = jnp.float32
GELU_C = 0.7978845608028654
GELU_A = 0.044715
COST = 400_000_000


class Sizes(NamedTuple):
    blocks: int
    chunks: int
    toks: int
    run: int
    steps: int
    width: int
    states: int
    items: int


def place_of(sz, table):
    me, core = lax.axis_index("block"), lax.axis_index("core")
    q = lax.div(me, 2) * 2 + core
    mine, chunk = lax.div(q, sz.chunks), lax.rem(q, sz.chunks)
    out = [me, chunk, core, lax.axis_index("plane"), q]
    if table is not None:
        side = lax.rem(me, 2) ^ core
        for which in range(2):
            out += [table[side, which, mine, index] for index in range(sz.items)]
    return out


def nt(a, b):
    return lax.dot_general(a, b, (((1,), (1,)), ((), ())), preferred_element_type=F32)


def nn(a, b):
    return lax.dot_general(a, b, (((1,), (0,)), ((), ())), preferred_element_type=F32)


def tn(a, b):
    return lax.dot_general(a, b, (((0,), (0,)), ((), ())), preferred_element_type=F32)


def after(*values):
    return lax.optimization_barrier(values)


def cmul(ar, ai, br, bi):
    return ar * br - ai * bi, ar * bi + ai * br


def rows_of(step):
    return pl.ds(pl.multiple_of(step * SEGS, SEGS), SEGS)


def widen(mask, count):
    return jnp.concatenate([mask] * count, axis=1)


def item_of(sz, meta, index):
    begin = meta[5 + sz.items + index]
    return begin, begin + meta[5 + index]


def fill_masks(sz, meta, live, ahead, behind):
    base = meta[1] * sz.toks
    seg = lax.broadcasted_iota(jnp.int32, (SEGS, LANES), 0)

    def body(step, carry):
        pos = base + seg * sz.steps + step
        inside = jnp.zeros((SEGS, LANES), F32)
        onward = jnp.zeros((SEGS, LANES), F32)
        onward_next = jnp.zeros((SEGS, LANES), F32)
        for index in range(sz.items):
            begin, end = item_of(sz, meta, index)
            inside = jnp.where((pos >= begin) & (pos < end), 1.0, inside)
            onward = jnp.where((pos > begin) & (pos < end), 1.0, onward)
            onward_next = jnp.where((pos >= begin) & (pos + 1 < end), 1.0, onward_next)
        onward_next = jnp.where(pos + 1 < sz.run, onward_next, 0.0)
        if live is not None:
            live[rows_of(step), :] = inside
        ahead[rows_of(step), :] = onward
        behind[rows_of(step), :] = onward_next
        return carry

    lax.fori_loop(0, sz.steps, body, 0, unroll=4)


def through(sz, meta, first, length):
    ahead = behind = False
    for index in range(sz.items):
        begin, end = item_of(sz, meta, index)
        ahead = ahead | ((begin < first) & (end >= first + length))
        behind = behind | ((begin <= first) & (end > first + length))
    behind = behind & (first + length < sz.run)
    return ahead, behind


def power(pair, count):
    while count > 1:
        pair = cmul(*pair, *pair)
        count //= 2
    return pair


def column_blocks(sz, decay):
    out = []
    for q in range(sz.states // LANES):
        cols = slice(q * LANES, (q + 1) * LANES)
        out.append((decay[0:1, cols], decay[1:2, cols]))
    return out


def spread(pairs):
    return [tuple(jnp.broadcast_to(v, (SEGS, LANES)) for v in pair) for pair in pairs]


def chain_ends(sz, decay, ahead, behind, source, ahead_col, behind_col, ends):
    nq = sz.states // LANES
    d = spread(column_blocks(sz, decay))
    zero = jnp.zeros((SEGS, LANES), F32)

    def body(step, held):
        up, down = rows_of(step), rows_of(sz.steps - 1 - step)
        on_up, on_down = ahead[up, :], behind[down, :]
        new = []
        for q in range(nq):
            for side, (rows, on, col) in enumerate(((up, on_up, ahead_col), (down, on_down, behind_col))):
                re, im = held[2 * q + side]
                re, im = cmul(*d[q], re * on, im * on)
                re += source[rows, col + q * LANES : col + (q + 1) * LANES]
                im += source[rows, col + sz.states + q * LANES : col + sz.states + (q + 1) * LANES]
                new.append((re, im))
        return tuple(new)

    held = lax.fori_loop(0, sz.steps, body, tuple((zero, zero) for _ in range(2 * nq)), unroll=4)
    for q in range(nq):
        cols = slice(q * LANES, (q + 1) * LANES)
        for side in range(2):
            ends[2 * side, :, cols] = held[2 * q + side][0]
            ends[2 * side + 1, :, cols] = held[2 * q + side][1]


def enter_states(sz, meta, decay, ends, start, enter):
    pair = (decay[0:1, :], decay[1:2, :])
    jump = power(pair, sz.steps)
    base = meta[1] * sz.toks
    state = list(start)
    for count in range(SEGS):
        for side, seg in ((0, count), (1, SEGS - 1 - count)):
            re, im = state[side]
            enter[2 * side, seg : seg + 1, :] = re
            enter[2 * side + 1, seg : seg + 1, :] = im
            passes = through(sz, meta, base + seg * sz.steps, sz.steps)[side]
            gain = jnp.where(passes, 1.0, 0.0).astype(F32)
            re, im = cmul(jump[0] * gain, jump[1] * gain, re, im)
            state[side] = (
                re + ends[2 * side, seg : seg + 1, :],
                im + ends[2 * side + 1, seg : seg + 1, :],
            )
    return state


def send_ends(sz, meta, decay, ends, enter, send):
    zero = jnp.zeros((1, sz.states), F32)
    ahead, behind = enter_states(sz, meta, decay, ends, ((zero, zero), (zero, zero)), enter)
    me = meta[1]
    for dist in range(1, sz.chunks):
        up = (me ^ dist) > me
        for part in range(2):
            send[dist - 1, part : part + 1, :] = jnp.where(up, ahead[part], behind[part])


def received(sz, meta, decay, recv):
    me = meta[1]
    zero = jnp.zeros((1, sz.states), F32)
    pair = (decay[0:1, :], decay[1:2, :])
    jump = power(pair, sz.toks) if sz.chunks > 2 else None
    sides = []
    for side in range(2):
        re, im = zero, zero
        order = range(sz.chunks) if side == 0 else range(sz.chunks - 1, -1, -1)
        for other in order:
            use = (other < me) if side == 0 else (other > me)
            slot = jnp.maximum((me ^ other) - 1, 0)
            got = recv[slot]
            new_re, new_im = got[0:1, :], got[1:2, :]
            if sz.chunks > 2:
                passes = through(sz, meta, other * sz.toks, sz.toks)[side]
                gain = jnp.where(passes, 1.0, 0.0).astype(F32)
                moved = cmul(jump[0] * gain, jump[1] * gain, re, im)
                new_re, new_im = new_re + moved[0], new_im + moved[1]
            re, im = jnp.where(use, new_re, re), jnp.where(use, new_im, im)
        sides.append((re, im))
    return sides


def load_enter(sz, enter):
    held = []
    for q in range(sz.states // LANES):
        cols = slice(q * LANES, (q + 1) * LANES)
        for side in range(2):
            held.append((enter[2 * side, :, cols], enter[2 * side + 1, :, cols]))
    return tuple(held)


def chain_states(sz, decay, ahead, behind, source, enter, states):
    nq = sz.states // LANES
    n = sz.states
    d = spread(column_blocks(sz, decay))

    def body(step, held):
        up, down = rows_of(step), rows_of(sz.steps - 1 - step)
        on_up, on_down = ahead[up, :], behind[down, :]
        new = []
        for q in range(nq):
            for side, (rows, on) in enumerate(((up, on_up), (down, on_down))):
                re, im = held[2 * q + side]
                re, im = cmul(*d[q], re * on, im * on)
                lo = q * LANES
                re += source[rows, lo : lo + LANES]
                im += source[rows, n + lo : n + lo + LANES]
                at = 2 * side * n + lo
                states[rows, at : at + LANES] = re.astype(BF)
                states[rows, at + n : at + n + LANES] = (-im).astype(BF)
                new.append((re, im))
        return tuple(new)

    lax.fori_loop(0, sz.steps, body, load_enter(sz, enter), unroll=4)


def adjoint_chains(sz, decay, ahead, behind, source, enter, states, half, grad_driven, grad_decay):
    nq = sz.states // LANES
    n = sz.states
    d = spread(column_blocks(sz, decay))
    zero = jnp.zeros((SEGS, LANES), F32)

    def make(second):
        def body(step, carry):
            held, sums = carry
            up, down = rows_of(step), rows_of(sz.steps - 1 - step)
            on_up, on_down = ahead[up, :], behind[down, :]
            new, total = [], []
            for q in range(nq):
                lo = q * LANES
                acc_re, acc_im = sums[q]
                for side, (rows, on, src, st) in enumerate(((up, on_up, 2 * n, 2 * n), (down, on_down, 0, 0))):
                    re, im = held[2 * q + side]
                    re, im = re * on, im * on
                    s_re = states[rows, st + lo : st + lo + LANES].astype(F32)
                    s_im = states[rows, st + n + lo : st + n + lo + LANES].astype(F32)
                    acc_re += re * s_re + im * s_im
                    acc_im += re * s_im - im * s_re
                    re, im = cmul(*d[q], re, im)
                    re += source[rows, src + lo : src + lo + LANES]
                    im += source[rows, src + n + lo : src + n + lo + LANES]
                    new.append((re, im))
                    if second:
                        out_re = re + half[rows, lo : lo + LANES]
                        out_im = im + half[rows, n + lo : n + lo + LANES]
                        grad_driven[rows, lo : lo + LANES] = out_re.astype(BF)
                        grad_driven[rows, n + lo : n + lo + LANES] = (-out_im).astype(BF)
                    else:
                        half[rows, lo : lo + LANES] = re
                        half[rows, n + lo : n + lo + LANES] = im
                total.append((acc_re, acc_im))
            return tuple(new), tuple(total)

        return body

    carry = (load_enter(sz, enter), tuple((zero, zero) for _ in range(nq)))
    carry = lax.fori_loop(0, sz.steps // 2, make(False), carry, unroll=2)
    carry = lax.fori_loop(sz.steps // 2, sz.steps, make(True), carry, unroll=2)
    for q in range(nq):
        cols = slice(q * LANES, (q + 1) * LANES)
        grad_decay[0:1, cols] = jnp.sum(carry[1][q][0], axis=0, keepdims=True)
        grad_decay[1:2, cols] = jnp.sum(carry[1][q][1], axis=0, keepdims=True)


ROWS = 64


def over_rows(sz, body, init=0):
    def step(index, carry):
        return body(pl.ds(pl.multiple_of(index * ROWS, ROWS), ROWS), carry)

    return lax.fori_loop(0, sz.toks // ROWS, step, init)


def norm_rows(sz, hidden, gain, live, normed):
    def body(rows, carry):
        u = hidden[rows, :].astype(F32)
        scale = lax.rsqrt(jnp.mean(u * u, axis=1, keepdims=True) + EPSILON)
        v = u * scale * gain[...]
        normed[rows, :] = (v * widen(live[rows, :], sz.width // LANES)).astype(BF)
        return carry

    over_rows(sz, body)


def matmul_nt(a, b, out, tile=256):
    for lo in range(0, b.shape[0], tile):
        out[:, lo : lo + tile] = nt(a[...], b[lo : lo + tile, :]).astype(out.dtype)


def matmul_nn(a, b, out, tile=256):
    for lo in range(0, b.shape[1], tile):
        out[:, lo : lo + tile] = nn(a[...], b[:, lo : lo + tile]).astype(out.dtype)


def matmul_tn(a, b, out, tile=256):
    for lo in range(0, a.shape[1], tile):
        out[lo : lo + tile, :] = tn(a[:, lo : lo + tile], b[...]).astype(out.dtype)


def finish_rows(sz, mixed, skip, normed, live, hidden, slope, result):
    def body(rows, carry):
        pre = 2.0 * mixed[rows, :] + skip[...] * normed[rows, :].astype(F32)
        square = pre * pre
        th = jnp.tanh(pre * (GELU_C + (GELU_C * GELU_A) * square))
        on = widen(live[rows, :], sz.width // LANES)
        part = 0.5 * (1.0 + th)
        deriv = part + 0.5 * pre * (1.0 - th * th) * (GELU_C + (3.0 * GELU_C * GELU_A) * square)
        slope[rows, :] = (on * deriv).astype(slope.dtype)
        result[rows, :] = (hidden[rows, :].astype(F32) + on * (pre * part)).astype(result.dtype)
        return carry

    over_rows(sz, body)


def layer_open(sz, meta, hidden, gain, w_in, decay, live, ahead, behind, normed, driven, ends, enter, send):
    norm_rows(sz, hidden, gain, live, normed)
    matmul_nt(normed, w_in, driven)
    chain_ends(sz, decay, ahead, behind, driven, 0, 0, ends)
    send_ends(sz, meta, decay, ends, enter, send)


def layer_close(sz, meta, recv, decay, ends, driven, normed, hidden, w_out, skip, live, ahead, behind, enter, mixed, states, slope, result):
    enter_states(sz, meta, decay, ends, received(sz, meta, decay, recv), enter)
    chain_states(sz, decay, ahead, behind, driven, enter, states)
    matmul_nn(states, w_out, mixed)
    finish_rows(sz, mixed, skip, normed, live, hidden, slope, result)


def back_open(sz, meta, upstream, slope, normed, w_out, decay, ahead, behind, twice, grad_states, grad_skip, ends, enter, send):
    def body(rows, total):
        e = upstream[rows, :] * slope[rows, :].astype(F32)
        low = e.astype(BF)
        twice[rows, :] = low + low
        part = e * normed[rows, :].astype(F32)
        return total + jnp.sum(part.reshape(ROWS // 8, 8, sz.width), axis=0)

    total = over_rows(sz, body, jnp.zeros((8, sz.width), F32))
    grad_skip[...] = jnp.sum(total, axis=0, keepdims=True)
    matmul_nt(twice, w_out, grad_states)
    chain_ends(sz, decay, ahead, behind, grad_states, 2 * sz.states, 0, ends)
    send_ends(sz, meta, decay, ends, enter, send)


def back_close(sz, meta, recv, decay, ends, grad_states, states, upstream, slope, skip, hidden, gain, w_in, ahead, behind,
               enter, half, grad_normed, grad_driven, grad_decay, grad_gain, result):
    enter_states(sz, meta, decay, ends, received(sz, meta, decay, recv), enter)
    adjoint_chains(sz, decay, ahead, behind, grad_states, enter, states, half, grad_driven, grad_decay)
    matmul_nn(grad_driven, w_in, grad_normed)

    def body(rows, total):
        u = hidden[rows, :].astype(F32)
        r = upstream[rows, :]
        gn = grad_normed[rows, :] + r * slope[rows, :].astype(F32) * skip[...]
        scale = lax.rsqrt(jnp.mean(u * u, axis=1, keepdims=True) + EPSILON)
        part = gn * u * scale
        dn = gn * gain[...]
        inner = jnp.sum(dn * u, axis=1, keepdims=True) * (1.0 / sz.width)
        result[rows, :] = (r + scale * dn - u * (scale * scale * scale * inner)).astype(result.dtype)
        return total + jnp.sum(part.reshape(ROWS // 8, 8, sz.width), axis=0)

    total = over_rows(sz, body, jnp.zeros((8, sz.width), F32))
    grad_gain[...] = jnp.sum(total, axis=0, keepdims=True)


def gain_of(params, layer):
    return params[layer : layer + 1, :]


def skip_of(params, layer):
    return params[2 + layer : 3 + layer, :]


def decay_of(sz, params, layer):
    return params[4 + 2 * layer : 6 + 2 * layer, 0 : sz.states]


def place_pieces(sz, meta, pieces, stacked):
    part = sz.width // sz.blocks
    for dist, piece in enumerate(pieces):
        owner = meta[4] ^ dist
        stacked[pl.ds(pl.multiple_of(owner * part, part), part), :] = piece[0:part, :]


def cut_pieces(sz, meta, rows, perm, stacked, pieces):
    part = sz.width // sz.blocks
    matmul_tn(rows, perm, stacked)
    for dist, piece in enumerate(pieces):
        owner = meta[4] ^ dist
        piece[...] = stacked[pl.ds(pl.multiple_of(owner * part, part), part), :]


def cut_kernel(sz, meta, whole, *refs):
    outs, wide, sems = refs[: sz.blocks], refs[-2], refs[-1]
    straight = whole.dtype == BF
    copies = []
    for dist in range(sz.blocks):
        to = meta[0] ^ dist
        cols = pl.ds(pl.multiple_of(lax.rem(to, sz.chunks) * sz.toks, LANES), sz.toks)
        source = whole.at[lax.div(to, sz.chunks), :, cols]
        copy = pltpu.make_async_copy(source, outs[dist] if straight else wide.at[dist], sems.at[dist])
        copy.start()
        copies.append(copy)
    for dist, copy in enumerate(copies):
        copy.wait()
        if not straight:
            outs[dist][...] = wide[dist].astype(BF)


def discretize(lambda_log, lambda_imag, log_step):
    step_size = jnp.exp(log_step)
    lambda_real = -jnp.exp(lambda_log)
    modulus = jnp.exp(lambda_real * step_size)
    decay_real = modulus * jnp.cos(lambda_imag * step_size)
    decay_imag = modulus * jnp.sin(lambda_imag * step_size)
    denominator = lambda_real * lambda_real + lambda_imag * lambda_imag
    scale_real = ((decay_real - 1.0) * lambda_real + decay_imag * lambda_imag) / denominator
    scale_imag = (decay_imag * lambda_real - (decay_real - 1.0) * lambda_imag) / denominator
    return decay_real, decay_imag, scale_real, scale_imag


def first_rows(sz):
    part, own = sz.width // sz.blocks, sz.states // sz.blocks
    return part, part + own * sz.width // sz.toks


def half_map_parts(sz):
    top, end = first_rows(sz)
    rows = end - top
    for index in range(sz.toks // sz.width):
        yield slice(index * rows, (index + 1) * rows), slice(top, end), slice(index * sz.width, (index + 1) * sz.width)


def split3(x):
    hi = x.astype(BF).astype(F32)
    mid = (x - hi).astype(BF).astype(F32)
    return hi, mid, x - hi - mid


def prepare_kernel(sz, meta, tokens, *refs):
    inputs, refs = refs[:7], refs[7:]
    outs, refs = refs[: sz.blocks], refs[sz.blocks :]
    drive_b, half_b, half_c = refs[:3]
    held, small, lines, drive_a, sems = refs[3:10], refs[10], refs[11], refs[12], refs[13]
    top, end = first_rows(sz)
    own, part = sz.states // sz.blocks, sz.width // sz.blocks
    loads, copies = [], []
    for index, (source, target) in enumerate(zip(inputs, held)):
        loads.append(pltpu.make_async_copy(source, target, sems.at[index]))
    for dist in range(sz.blocks):
        to = meta[0] ^ dist
        cols = pl.ds(pl.multiple_of(lax.rem(to, sz.chunks) * sz.toks, LANES), sz.toks)
        source = tokens.at[lax.div(to, sz.chunks), :, cols]
        copies.append(pltpu.make_async_copy(source, outs[dist].at[0:top, :], sems.at[len(inputs) + dist]))
    for copy in copies + loads:
        copy.start()
    for copy in loads[:6]:
        copy.wait()
    gain, skip, lambda_log, lambda_imag, log_step, input_map, output_map = held
    dr, di, sr, si = discretize(lambda_log[...], lambda_imag[...], log_step[...])
    small[...] = jnp.zeros_like(small)
    lines[...] = jnp.zeros_like(lines)
    small[0:2, 0:part] = gain[...]
    small[2:4, 0:part] = skip[...]
    for layer in range(2):
        small[4 + 2 * layer : 5 + 2 * layer, 0:own] = dr[layer : layer + 1]
        small[5 + 2 * layer : 6 + 2 * layer, 0:own] = di[layer : layer + 1]
    lines[0:2, 0:own] = sr
    lines[2:4, 0:own] = si
    cols = lines[...].T
    for layer in range(2):
        qr, qi = cols[0:own, layer : layer + 1], cols[0:own, 2 + layer : 3 + layer]
        br, bi = input_map[layer, 0].astype(F32), input_map[layer, 1].astype(F32)
        for index, value in enumerate((qr * br - qi * bi, qr * bi + qi * br)):
            (drive_a, drive_b)[layer][index] = value.astype(BF)
    rows = jnp.concatenate([*split3(small[...]), jnp.zeros((8, sz.toks - 3 * LANES), F32)], axis=1)
    rows = jnp.concatenate([rows, jnp.zeros((8, sz.toks), F32)], axis=0).astype(BF)
    for dist, out in enumerate(outs):
        half = lax.rem(meta[0] ^ dist, 2)
        for from_rows, to_rows, lanes in half_map_parts(sz):
            out[to_rows, lanes] = drive_a[half, from_rows, :]
        out[end:, :] = rows
    loads[6].wait()
    core = meta[2]
    for index in range(2):
        half_b[index] = output_map[0, 2 * core + index]
        half_c[index] = output_map[1, 2 * core + index]
    half_b[2] = drive_b[core]
    for copy in copies:
        copy.wait()


def params_of(sz, piece):
    rows = piece[piece.shape[0] - 16 :, 0 : 3 * LANES].astype(F32)[0:8]
    return rows[:, 0:LANES] + rows[:, LANES : 2 * LANES] + rows[:, 2 * LANES :]


def join_kernel(sz, meta, *refs):
    pieces, maps, params = refs[: sz.blocks], refs[-2], refs[-1]
    own = sz.states // sz.blocks
    collect_params(sz, meta, [params_of(sz, piece) for piece in pieces], params)
    for dist, piece in enumerate(pieces):
        base = (meta[4] ^ dist) * own
        for to_rows, from_rows, lanes in half_map_parts(sz):
            rows = pl.ds(pl.multiple_of(base + to_rows.start, 16), to_rows.stop - to_rows.start)
            maps[rows, :] = piece[from_rows, lanes]


def collect_params(sz, meta, smalls, params):
    own = sz.states // sz.blocks
    part = sz.width // sz.blocks
    lane = lax.broadcasted_iota(jnp.int32, (8, LANES), 1)
    row = lax.broadcasted_iota(jnp.int32, (8, LANES), 0)
    pad = jnp.zeros((8, sz.width - LANES), F32)
    total = jnp.zeros((8, sz.width), F32)
    for block in range(sz.blocks):
        piece = smalls[0]
        for dist in range(1, sz.blocks):
            piece = jnp.where((meta[4] ^ dist) == block, smalls[dist], piece)
        for first, count, size in ((0, 4, part), (4, 4, own)):
            mine = jnp.where((row >= first) & (row < first + count) & (lane < size), piece, 0.0)
            wide = jnp.concatenate([mine, pad], axis=1)
            total += pltpu.roll(wide, block * size, 1) if block else wide
    params[...] = total


def place_maps(sz, meta, own_maps, mine, other, skip, out):
    own = sz.states // sz.blocks
    count = own_maps.shape[0] // 2

    def put(index, owner, value):
        out[pl.ds(pl.multiple_of(index * sz.states + owner * own, own), own), :] = value

    for index in range(2 * count):
        put(index, meta[0], own_maps[index])
    for side, pieces in ((meta[2], mine), (1 - meta[2], other)):
        for dist, piece in enumerate(pieces):
            for index in range(count):
                put(side * count + index, meta[0] ^ (dist + 1), piece[skip + index])


def enter_kernel(sz, meta, perm, params, maps, other, *refs):
    pieces, refs = refs[: sz.blocks], refs[sz.blocks :]
    w_in, hidden, normed, driven, ends, send, stacked, live, ahead, behind, enter = refs
    gain, decay = gain_of(params, 0), decay_of(sz, params, 0)
    place_pieces(sz, meta, pieces, stacked)
    matmul_nt(perm, stacked, hidden)
    for side, half in ((meta[2], maps), (1 - meta[2], other)):
        w_in[pl.ds(pl.multiple_of(side * sz.states, sz.states), sz.states), :] = half[...]
    fill_masks(sz, meta, live, ahead, behind)
    layer_open(sz, meta, hidden, gain, w_in, decay, live, ahead, behind, normed, driven, ends, enter, send)


def middle_kernel(sz, meta, recv, params, ends, driven, normed, hidden, own_out, own_in, *refs):
    decay, skip, gain_b, decay_b = decay_of(sz, params, 0), skip_of(params, 0), gain_of(params, 1), decay_of(sz, params, 1)
    far = sz.blocks - 1
    mine, other, refs = refs[:far], refs[far : 2 * far], refs[2 * far :]
    w_out, w_in_b, states, slope, hidden_b, normed_b, driven_b, ends_b, send_b, live, ahead, behind, enter, mixed = refs
    place_maps(sz, meta, own_out, mine, other, 0, w_out)
    place_maps(sz, meta, own_in, mine, other, 2, w_in_b)
    fill_masks(sz, meta, live, ahead, behind)
    layer_close(sz, meta, recv, decay, ends, driven, normed, hidden, w_out, skip, live, ahead, behind, enter, mixed, states, slope, hidden_b)
    layer_open(sz, meta, hidden_b, gain_b, w_in_b, decay_b, live, ahead, behind, normed_b, driven_b, ends_b, enter, send_b)


def leave_kernel(sz, meta, recv, params, ends, driven, normed, hidden, perm, own_out, *refs):
    decay, skip = decay_of(sz, params, 1), skip_of(params, 1)
    far = sz.blocks - 1
    mine, other, refs = refs[:far], refs[far : 2 * far], refs[2 * far :]
    w_out, states, slope, refs = *refs[:3], refs[3:]
    place_maps(sz, meta, own_out, mine, other, 0, w_out)
    pieces, refs = refs[: sz.blocks], refs[sz.blocks :]
    live, ahead, behind, enter, mixed, last, stacked = refs
    fill_masks(sz, meta, live, ahead, behind)
    layer_close(sz, meta, recv, decay, ends, driven, normed, hidden, w_out, skip, live, ahead, behind, enter, mixed, states, slope, last)
    cut_pieces(sz, meta, last, perm, stacked, pieces)


def turn_kernel(sz, meta, slope, normed, w_out, params, perm, *refs):
    decay = decay_of(sz, params, 1)
    pieces, refs = refs[: sz.blocks], refs[sz.blocks :]
    upstream, twice, grad_states, grad_skip, ends, send, stacked, ahead, behind, enter = refs
    place_pieces(sz, meta, pieces, stacked)
    matmul_nt(perm, stacked, upstream)
    fill_masks(sz, meta, None, ahead, behind)
    back_open(sz, meta, upstream, slope, normed, w_out, decay, ahead, behind, twice, grad_states, grad_skip, ends, enter, send)


def back_middle_kernel(sz, meta, recv, params, ends, grad_states, states, upstream, slope, hidden, w_in,
                       slope_b, normed_b, w_out_b,
                       grad_driven, grad_decay, grad_gain, upstream_b, twice_b, grad_states_b, grad_skip_b, ends_b, send_b,
                       ahead, behind, enter, half, grad_normed):
    decay, skip, gain, decay_b = decay_of(sz, params, 1), skip_of(params, 1), gain_of(params, 1), decay_of(sz, params, 0)
    fill_masks(sz, meta, None, ahead, behind)
    back_close(sz, meta, recv, decay, ends, grad_states, states, upstream, slope, skip, hidden, gain, w_in, ahead, behind,
               enter, half, grad_normed, grad_driven, grad_decay, grad_gain, upstream_b)
    back_open(sz, meta, upstream_b, slope_b, normed_b, w_out_b, decay_b, ahead, behind, twice_b, grad_states_b, grad_skip_b, ends_b, enter, send_b)


def back_leave_kernel(sz, meta, recv, params, ends, grad_states, states, upstream, slope, hidden, w_in, perm,
                      gain_b, skip_a, skip_b, decay_b, *refs):
    done, refs = refs[: sz.blocks], refs[sz.blocks :]
    grad_driven, tiny, refs = refs[0], refs[1], refs[2:]
    decay, skip, gain = decay_of(sz, params, 0), skip_of(params, 0), gain_of(params, 0)
    pieces, refs = refs[: sz.blocks], refs[sz.blocks :]
    ahead, behind, enter, half, grad_normed, last, stacked, grad_decay, grad_gain = refs
    fill_masks(sz, meta, None, ahead, behind)
    back_close(sz, meta, recv, decay, ends, grad_states, states, upstream, slope, skip, hidden, gain, w_in, ahead, behind,
               enter, half, grad_normed, grad_driven, grad_decay, grad_gain, last)
    tiny[...] = jnp.zeros_like(tiny)
    for row, line in enumerate((grad_gain, gain_b, skip_a, skip_b)):
        tiny[row : row + 1, :] = line[...]
    tiny[4:6, 0 : sz.states] = grad_decay[...]
    tiny[6:8, 0 : sz.states] = decay_b[...]
    part = sz.width // sz.blocks
    for piece, first in zip(pieces, done):
        piece[0:part, :] = first[...]
    cut_pieces(sz, meta, last, perm, stacked, [piece.at[part : 2 * part, :] for piece in pieces])


def weight_kernel(counts, sz, meta, *refs):
    for half, out in ((1 - meta[2], refs[-2]), (meta[2], refs[-1])):
        at = 0
        for index, count in enumerate(counts):
            left, right = refs[2 * index], refs[2 * index + 1]
            for group in range(count):
                cols = pl.ds(pl.multiple_of((half * count + group) * sz.states, LANES), sz.states)
                out[at : at + sz.states, :] = tn(left[:, cols], right[...]).astype(out.dtype)
                at += sz.states


def fold_core_kernel(count, sz, meta, keep, got, *pieces):
    own = sz.states // sz.blocks
    part = sz.width // sz.blocks
    tiny = None
    if len(pieces) > sz.blocks:
        tiny, pieces = pieces[0][...] + pieces[1][...], pieces[2:]
        row = lax.broadcasted_iota(jnp.int32, (8, LANES), 0)
        lane = lax.broadcasted_iota(jnp.int32, (8, LANES), 1)
    for dist, piece in enumerate(pieces):
        owner = meta[0] ^ dist
        for group in range(count):
            rows = pl.ds(pl.multiple_of(group * sz.states + owner * own, own), own)
            piece[group * own : (group + 1) * own, :] = (keep[rows, :].astype(F32) + got[rows, :].astype(F32)).astype(BF)
        if tiny is not None:
            value = jnp.zeros((8, LANES), F32)
            for block in range(sz.blocks):
                wide = pltpu.roll(tiny, sz.width - block * part, 1) if block else tiny
                deep = pltpu.roll(tiny, sz.width - block * own, 1) if block else tiny
                mine = jnp.where(row < 4, jnp.where(lane < part, wide[:, :LANES], 0.0), jnp.where(lane < own, deep[:, :LANES], 0.0))
                value = jnp.where(owner == block, mine, value)
            hi, lo = split2(value)
            rest = jnp.zeros((8, sz.width - 2 * LANES), F32)
            wide = jnp.concatenate([jnp.concatenate([hi, lo, rest], axis=1), jnp.zeros((8, sz.width), F32)], axis=0)
            piece[count * own : count * own + 16, :] = wide.astype(BF)


def split2(x):
    hi = x.astype(BF).astype(F32)
    return hi, x - hi


def fold_block_kernel(planes, counts, with_tiny, sz, meta, *refs):
    lanes = sz.width // LANES
    groups = len(counts)
    got, refs = refs[: groups * sz.blocks], refs[groups * sz.blocks :]
    outs, talls = refs[:planes], refs[planes:]
    at = 0
    for index, rows in enumerate(counts):
        pieces = got[index * sz.blocks : (index + 1) * sz.blocks]
        total = pieces[0][...].astype(F32)
        for piece in pieces[1:]:
            total += piece[...].astype(F32)
        tall = talls[index]
        padded = tall.shape[0] // lanes
        for block in range(lanes):
            tall[block * padded : block * padded + rows, :] = total[0:rows, block * LANES : (block + 1) * LANES].astype(BF)
            if padded > rows:
                tall[block * padded + rows : (block + 1) * padded, :] = jnp.zeros((padded - rows, LANES), BF)
        part = tall.shape[0] // planes
        for dist, out in enumerate(outs):
            out[at : at + part, :] = tall[pl.ds(pl.multiple_of((meta[3] ^ dist) * part, part), part), :]
        at += part
    if with_tiny:
        value = total[counts[-1] : counts[-1] + 8, 0:LANES] + total[counts[-1] : counts[-1] + 8, LANES : 2 * LANES]
        rows = jnp.concatenate(split2(value), axis=0).astype(BF)
        for out in outs:
            out[at : at + 16, :] = rows


def fold_plane_kernel(sz, meta, *refs):
    total = refs[0][...].astype(F32)
    for piece in refs[1:-1]:
        total += piece[...].astype(F32)
    refs[-1][...] = total.astype(BF)


def join_plane_kernel(sz, meta, first, *refs):
    parts, out, tiny = refs[:-2], refs[-2], refs[-1]
    total = parts[0][...].astype(F32)
    for piece in parts[1:]:
        total += piece[...].astype(F32)
    rows = total.shape[0] - 16
    out[0 : first.shape[0], :] = first[...]
    out[first.shape[0] :, :] = total[0:rows].astype(BF)
    tiny[...] = total[rows : rows + 8] + total[rows + 8 :]


def finish_kernel(planes, groups, sz, meta, *refs):
    count = 2 * planes
    pieces, refs = refs[:count], refs[count:]
    tiny, lambda_log, lambda_imag, log_step, input_map = refs[:5]
    grad_gain, grad_skip, grad_log, grad_imag, grad_step, grad_maps, grad_out = refs[5:12]
    talls, grad_in, lines = refs[12:-2], refs[-2], refs[-1]
    own = sz.states // sz.blocks
    lanes = sz.width // LANES
    start = 0
    for tall, group in zip(talls, groups):
        padded = tall.shape[0] // lanes
        part = tall.shape[0] // planes
        for side in range(2):
            half = meta[2] ^ side
            for dist in range(planes):
                rows = pl.ds(pl.multiple_of((meta[3] ^ dist) * part, part), part)
                tall[rows, :] = pieces[side * planes + dist][start : start + part, :]
            at = 0
            for which, layer, maps in group:
                out = grad_in if which == 0 else grad_out
                for one in range(maps):
                    for block in range(lanes):
                        rows = slice(block * padded + at, block * padded + at + own)
                        out[layer, half * maps + one, :, block * LANES : (block + 1) * LANES] = tall[rows, :].astype(F32)
                    at += own
        start += part
    width = sz.width // sz.blocks
    grad_gain[...] = tiny[0:2, 0:width]
    grad_skip[...] = tiny[2:4, 0:width]
    dr, di, sr, si = discretize(lambda_log[...], lambda_imag[...], log_step[...])
    lines[...] = jnp.zeros_like(lines)
    lines[0:2, 0:own] = sr
    lines[2:4, 0:own] = si
    cols = lines[...].T
    back = []
    for layer in range(2):
        qr, qi = cols[0:own, layer : layer + 1], cols[0:own, 2 + layer : 3 + layer]
        wr, wi = grad_in[layer, 0], grad_in[layer, 1]
        br, bi = input_map[layer, 0].astype(F32), input_map[layer, 1].astype(F32)
        grad_maps[layer, 0] = qr * wr + qi * wi
        grad_maps[layer, 1] = qr * wi - qi * wr
        back.append(jnp.sum(wr * br + wi * bi, axis=1, keepdims=True))
        back.append(jnp.sum(wi * br - wr * bi, axis=1, keepdims=True))
    lines[...] = jnp.zeros_like(lines)
    for index, col in enumerate(back):
        lines[0:own, index : index + 1] = col
    rows = lines[...].T
    step = jnp.exp(log_step[...])
    lr, li = -jnp.exp(lambda_log[...]), lambda_imag[...]
    norm = 1.0 / (lr * lr + li * li)
    for layer in range(2):
        at = slice(layer, layer + 1)
        a, b, h = (lr[at], li[at]), (dr[at], di[at]), step[at]
        gq = rows[2 * layer : 2 * layer + 1, 0:own], rows[2 * layer + 1 : 2 * layer + 2, 0:own]
        gd = tiny[4 + 2 * layer : 5 + 2 * layer, 0:own], tiny[5 + 2 * layer : 6 + 2 * layer, 0:own]
        inverse = a[0] * norm[at], -a[1] * norm[at]
        through = cmul(inverse[0], -inverse[1], *gq)
        gd = gd[0] + through[0], gd[1] + through[1]
        ratio = cmul(*inverse, sr[at], si[at])
        direct = cmul(ratio[0], -ratio[1], *gq)
        moved = cmul(b[0] * h, -b[1] * h, *gd)
        turn = cmul(*a, *b)
        grad_log[at, :] = (moved[0] - direct[0]) * a[0]
        grad_imag[at, :] = moved[1] - direct[1]
        grad_step[at, :] = (turn[0] * gd[0] + turn[1] * gd[1]) * h


def spread_kernel(sz, meta, *refs):
    pieces, outs, wide, sems = refs[: sz.blocks], refs[sz.blocks : -2], refs[-2], refs[-1]
    part = sz.width // sz.blocks
    copies = []
    for dist, piece in enumerate(pieces):
        owner = meta[0] ^ dist
        for index, out in enumerate(outs):
            slot = dist * len(outs) + index
            wide[slot] = piece[index * part : (index + 1) * part, :].astype(F32)
            cols = pl.ds(pl.multiple_of(lax.rem(owner, sz.chunks) * sz.toks, LANES), sz.toks)
            copy = pltpu.make_async_copy(wide.at[slot], out.at[lax.div(owner, sz.chunks), :, cols], sems.at[slot])
            copy.start()
            copies.append(copy)
    for copy in copies:
        copy.wait()


VMEM = pl.BlockSpec(memory_space=pltpu.VMEM)
SMEM = pl.BlockSpec(memory_space=pltpu.SMEM)
HBM = pl.BlockSpec(memory_space=pltpu.HBM)


def call(name, sz, body, items, args, outs, scratch, limit=10, in_spec=VMEM, out_spec=VMEM, time=0.0):
    out_shape = [jax.ShapeDtypeStruct(shape, dtype) for shape, dtype in outs]

    def kernel(*refs):
        body(sz, place_of(sz, refs[0] if items else None), *refs[len(items) :])

    return pl.pallas_call(
        kernel,
        out_shape=out_shape,
        in_specs=[SMEM] * len(items) + [in_spec] * len(args),
        out_specs=[out_spec] * len(outs),
        scratch_shapes=[pltpu.VMEM(*item) if isinstance(item, tuple) else item for item in scratch],
        compiler_params=pltpu.CompilerParams(vmem_limit_bytes=limit << 20),
        cost_estimate=pl.CostEstimate(flops=int(COST * time), bytes_accessed=1000, transcendentals=0),
        name=name,
    )(*items, *args)


def on_device(tokens, cotangent, item_lengths, item_offsets, norm_gain, lambda_log, lambda_imag, log_step, input_map, output_map, skip_weight):
    micro, part, run = tokens.shape
    layers = norm_gain.shape[0]
    blocks = lax.axis_size("block")
    planes = lax.axis_size("plane")
    chunks = blocks // micro
    toks = run // chunks
    own = lambda_log.shape[1]
    width, states = part * blocks, own * blocks
    sz = Sizes(blocks, chunks, toks, run, toks // SEGS, width, states, item_lengths.shape[1])

    def swap(x, dist, axis="block"):
        return lax.ppermute(x, axis, [(i, i ^ dist) for i in range(lax.axis_size(axis))])

    def across(x, dist, back):
        pairs = []
        for c in range(2):
            for b in range(blocks):
                q = b ^ dist
                pairs.append((c * blocks + b, (q % 2) * blocks + (q // 2) * 2 + c))
        return lax.ppermute(x, ("core", "block"), [pair[::-1] for pair in pairs] if back else pairs)

    def across_all(pieces, back=False):
        return [across(piece, dist, back) for dist, piece in enumerate(pieces)]

    table = jnp.stack([item_lengths, item_offsets])
    items = [jnp.stack([table, swap(table, 1, "core")])]

    def neighbour(x, dist):
        pairs = []
        for c in range(2):
            for b in range(blocks):
                q = ((b // 2) * 2 + c) ^ dist
                pairs.append((c * blocks + b, (q % 2) * blocks + (q // 2) * 2 + b % 2))
        return lax.ppermute(x, ("core", "block"), pairs)

    def swap_all(pieces, axis="block"):
        return [swap(piece, dist, axis) if dist else piece for dist, piece in enumerate(pieces)]

    def exchange(send):
        return jnp.stack([neighbour(send[dist - 1], dist) for dist in range(1, chunks)])

    row = jnp.arange(toks, dtype=jnp.int32)[:, None]
    col = jnp.arange(toks, dtype=jnp.int32)[None, :]
    perm = ((row % SEGS) * sz.steps + row // SEGS == col).astype(BF)

    maps_own = ((2, own, width), BF)
    half_own = ((3, own, width), BF)
    given = [norm_gain, skip_weight, lambda_log, lambda_imag, log_step, input_map, output_map]
    *first_pieces, drive_b, half_b, half_c = call(
        "prepare", sz, prepare_kernel, [], [pltpu.with_memory_space_constraint(x, pltpu.HBM) for x in [tokens, *given]],
        [((first_rows(sz)[1] + 16, toks), BF)] * blocks + [maps_own, half_own, maps_own],
        [(x.shape, x.dtype) for x in given] + [((8, LANES), F32), ((8, LANES), F32), maps_own, pltpu.SemaphoreType.DMA((len(given) + blocks,))],
        limit=6, in_spec=HBM)
    first_pieces = across_all(first_pieces)
    maps_a, params = call("join", sz, join_kernel, [], first_pieces, [((states, width), BF), ((8, width), F32)], [])
    half_b, params = after(half_b, params)
    cot_cut = call("cut_cotangent", sz, cut_kernel, [], [pltpu.with_memory_space_constraint(cotangent, pltpu.HBM)],
                   [((part, toks), BF)] * blocks, [((blocks, part, toks), F32), pltpu.SemaphoreType.DMA((blocks,))], limit=4, in_spec=HBM)
    params, cot_cut = after(params, cot_cut)
    second_mine = [swap(half_b, dist) for dist in range(1, blocks)]

    mask = ((toks, LANES), F32)
    enter = ((4, SEGS, states), F32)
    stacked = ((width, toks), BF)
    rows_f, rows_b = ((toks, width), F32), ((toks, width), BF)
    drv = ((toks, 2 * states), F32)
    sts = ((toks, 4 * states), BF)
    gst = ((toks, 4 * states), F32)
    snd = ((chunks - 1, 2, states), F32)
    w_in, w_out = ((2 * states, width), BF), ((4 * states, width), BF)
    line, gdec = ((1, width), F32), ((2, states), F32)
    piece_out = [((part, toks), BF)] * blocks

    w_in_a, hidden_a, normed_a, driven_a, ends_a, send_a = call(
        "enter", sz, enter_kernel, items, [perm, params, maps_a, swap(maps_a, 1, "core"), *first_pieces],
        [w_in, rows_b, rows_b, drv, enter, snd], [stacked, mask, mask, mask, enter], time=7)
    recv = exchange(send_a)
    second_mine, half_c, _ = after(second_mine, half_c, send_a)
    second_maps = second_mine, [swap(piece, 1, "core") for piece in second_mine]
    third_mine = [swap(half_c, dist) for dist in range(1, blocks)]
    w_out_a, w_in_b, states_a, slope_a, hidden_b, normed_b, driven_b, ends_b, send_b = call(
        "middle", sz, middle_kernel, items,
        [recv, params, ends_a, driven_a, normed_a, hidden_a, output_map[0], drive_b, *second_maps[0], *second_maps[1]],
        [w_out, w_in, sts, rows_b, rows_f, rows_b, drv, enter, snd], [mask, mask, mask, enter, rows_f], time=11)
    recv = exchange(send_b)
    third_mine, cot_cut, _ = after(third_mine, cot_cut, send_b)
    cot_pieces = across_all(cot_cut)
    third_maps = third_mine, [swap(piece, 1, "core") for piece in third_mine]
    w_out_b, states_b, slope_b, *out_pieces = call(
        "leave", sz, leave_kernel, items,
        [recv, params, ends_b, driven_b, normed_b, hidden_b, perm, output_map[1], *third_maps[0], *third_maps[1]],
        [w_out, sts, rows_b, *piece_out], [mask, mask, mask, enter, rows_f, rows_b, stacked], time=8)

    def half_grads(name, pairs, counts, first=()):
        args = [x for pair in pairs for x in pair]
        send, keep = call(name, sz, partial(weight_kernel, counts), [], args, [((sum(counts) * states, width), BF)] * 2, [])
        send, keep, first = after(send, keep, first)
        return (keep, swap(send, 1, "core")), first

    def fold_core(name, group):
        total = group[0].shape[0] // states
        rows = total * own + (16 if len(group) > 2 else 0)
        return swap_all(call(name, sz, partial(fold_core_kernel, total), [], group, [((rows, width), BF)] * blocks, []))

    def spread(pieces):
        return call("spread", sz, spread_kernel, [], pieces, [((micro, part, run), F32)] * 2,
                    [((2 * blocks, part, toks), F32), pltpu.SemaphoreType.DMA((2 * blocks,))], limit=6, out_spec=HBM)

    lanes = width // LANES

    def tall_of(rows):
        step = max(SEGS * planes // lanes, SEGS)
        return ((lanes * (-(-rows // step) * step), LANES), BF)

    def over_planes(name, groups, rows, with_tiny):
        talls = [tall_of(n) for n in rows]
        cut = sum(t[0][0] for t in talls) // planes + (16 if with_tiny else 0)
        parts = call(name, sz, partial(fold_block_kernel, planes, rows, with_tiny), [], [x for g in groups for x in g],
                     [((cut, LANES), BF)] * planes, talls)
        return swap_all(parts, "plane")

    up_b, twice_b, gstates_b, gskip_b, ends, send = call(
        "turn", sz, turn_kernel, items, [slope_b, normed_b, w_out_b, params, perm, *cot_pieces],
        [rows_f, rows_b, gst, line, enter, snd], [stacked, mask, mask, enter], time=6)
    recv = exchange(send)
    group_a, _ = half_grads("grads_a", [(states_b, twice_b)], (2,))
    sums_a = fold_core("fold_a", group_a)
    recv, sums_a[0] = after(recv, sums_a[0])
    gdriven_b, gdecay_b, ggain_b, up_a, twice_a, gstates_a, gskip_a, ends, send = call(
        "back_middle", sz, back_middle_kernel, items,
        [recv, params, ends, gstates_b, states_b, up_b, slope_b, hidden_b, w_in_b, slope_a, normed_a, w_out_a],
        [((toks, 2 * states), BF), gdec, line, rows_f, rows_b, gst, line, enter, snd], [mask, mask, enter, drv, rows_f], limit=12, time=11)
    recv = exchange(send)
    gdriven_b, sums_a = after(gdriven_b, sums_a)
    group_b, _ = half_grads("grads_b", [(gdriven_b, normed_b), (states_a, twice_a)], (1, 2))
    sums_b = fold_core("fold_b", group_b)
    recv, sums_b[0] = after(recv, sums_b[0])
    gdriven_a, tiny, *last_pieces = call(
        "back_leave", sz, back_leave_kernel, items,
        [recv, params, ends, gstates_a, states_a, up_a, slope_a, hidden_a, w_in_a, perm, ggain_b, gskip_a, gskip_b, gdecay_b, *out_pieces],
        [((toks, 2 * states), BF), ((8, width), F32)] + [((2 * part, toks), BF)] * blocks,
        [mask, mask, enter, drv, rows_f, rows_b, stacked, gdec, line], limit=12, time=9)
    group_c, sums_b = half_grads("grads_c", [(gdriven_a, normed_a)], (1,), sums_b)
    sums_c = fold_core("fold_c", [*group_c, tiny, swap(tiny, 1, "core")])
    parts_ab = over_planes("planes_ab", [sums_a, sums_b], (2 * own, 3 * own), False)
    (sum_ab,) = call("sum_ab", sz, fold_plane_kernel, [], parts_ab, [(parts_ab[0].shape, BF)], [])
    parts_c = over_planes("planes_c", [sums_c], (own,), True)
    last_pieces, parts_c[0] = after(last_pieces, parts_c[0])
    last_pieces = across_all(last_pieces, back=True)
    rows = parts_ab[0].shape[0] + parts_c[0].shape[0] - 16
    sum_all, tiny = call("sum_c", sz, join_plane_kernel, [], [sum_ab, *parts_c], [((rows, LANES), BF), ((8, LANES), F32)], [])
    whole = swap_all([sum_all] * planes, "plane")
    whole, last_pieces = after(whole, last_pieces)
    whole += [swap(x, 1, "core") for x in whole]
    output, input_grad = spread(last_pieces)
    small_out = ((layers, own), F32)
    grad_gain, grad_skip, grad_log, grad_imag, grad_step, grad_in, grad_out = call(
        "finish", sz, partial(finish_kernel, planes, ([(1, 1, 2)], [(0, 1, 1), (1, 0, 2)], [(0, 0, 1)])), [],
        [*whole, tiny, lambda_log, lambda_imag, log_step, input_map],
        [((layers, part), F32)] * 2 + [small_out] * 3 + [((layers, 2, own, width), F32), ((layers, 4, own, width), F32)],
        [tall_of(n * own) for n in (2, 3, 1)] + [((layers, 2, own, width), F32), ((LANES, LANES), F32)])
    return output, input_grad, grad_gain, grad_log, grad_imag, grad_step, grad_in, grad_out, grad_skip


def solution(mesh):
    rows, blocks = mesh.devices.shape
    inner = Mesh(mesh.devices.reshape(rows // 2, 2, blocks), ("plane", "core", "block"))
    dp = ("plane", "core")
    half = P(None, "block")
    maps = P(None, None, "block", None)
    acts = P(None, "block", dp)
    items = P(None, dp)
    return jax.shard_map(
        on_device,
        mesh=inner,
        in_specs=(acts, acts, items, items, half, half, half, half, maps, maps, half),
        out_specs=(acts, acts, half, half, half, half, maps, maps, half),
        check_vma=False,
    )
```

```python
from functools import partial
from typing import NamedTuple

import jax
import jax.numpy as jnp
from jax import lax
from jax.experimental import pallas as pl
from jax.experimental.pallas import tpu as pltpu
from jax.sharding import Mesh, PartitionSpec as P

EPSILON = 1e-05
SEGS = 16
LANES = 128
BF = jnp.bfloat16
F32 = jnp.float32
GELU_C = 0.7978845608028654
GELU_A = 0.044715
COST = 400_000_000


class Sizes(NamedTuple):
    blocks: int
    chunks: int
    toks: int
    run: int
    steps: int
    width: int
    states: int
    items: int


def place_of(sz, table):
    me, core = lax.axis_index("block"), lax.axis_index("core")
    q = lax.div(me, 2) * 2 + core
    mine, chunk = lax.div(q, sz.chunks), lax.rem(q, sz.chunks)
    out = [me, chunk, core, lax.axis_index("plane"), q]
    if table is not None:
        side = lax.rem(me, 2) ^ core
        for which in range(2):
            out += [table[side, which, mine, index] for index in range(sz.items)]
    return out


def nt(a, b):
    return lax.dot_general(a, b, (((1,), (1,)), ((), ())), preferred_element_type=F32)


def nn(a, b):
    return lax.dot_general(a, b, (((1,), (0,)), ((), ())), preferred_element_type=F32)


def tn(a, b):
    return lax.dot_general(a, b, (((0,), (0,)), ((), ())), preferred_element_type=F32)


def after(*values):
    return lax.optimization_barrier(values)


def cmul(ar, ai, br, bi):
    return ar * br - ai * bi, ar * bi + ai * br


def rows_of(step):
    return pl.ds(pl.multiple_of(step * SEGS, SEGS), SEGS)


def widen(mask, count):
    return jnp.concatenate([mask] * count, axis=1)


def item_of(sz, meta, index):
    begin = meta[5 + sz.items + index]
    return begin, begin + meta[5 + index]


def fill_masks(sz, meta, live, ahead, behind):
    base = meta[1] * sz.toks
    seg = lax.broadcasted_iota(jnp.int32, (SEGS, LANES), 0)

    def body(step, carry):
        pos = base + seg * sz.steps + step
        inside = jnp.zeros((SEGS, LANES), F32)
        onward = jnp.zeros((SEGS, LANES), F32)
        onward_next = jnp.zeros((SEGS, LANES), F32)
        for index in range(sz.items):
            begin, end = item_of(sz, meta, index)
            inside = jnp.where((pos >= begin) & (pos < end), 1.0, inside)
            onward = jnp.where((pos > begin) & (pos < end), 1.0, onward)
            onward_next = jnp.where((pos >= begin) & (pos + 1 < end), 1.0, onward_next)
        onward_next = jnp.where(pos + 1 < sz.run, onward_next, 0.0)
        if live is not None:
            live[rows_of(step), :] = inside
        if ahead is not None:
            ahead[rows_of(step), :] = onward
            behind[rows_of(step), :] = onward_next
        return carry

    lax.fori_loop(0, sz.steps, body, 0, unroll=4)


def through(sz, meta, first, length):
    ahead = behind = False
    for index in range(sz.items):
        begin, end = item_of(sz, meta, index)
        ahead = ahead | ((begin < first) & (end >= first + length))
        behind = behind | ((begin <= first) & (end > first + length))
    behind = behind & (first + length < sz.run)
    return ahead, behind


def power(pair, count):
    while count > 1:
        pair = cmul(*pair, *pair)
        count //= 2
    return pair


def column_blocks(sz, decay):
    out = []
    for q in range(sz.states // LANES):
        cols = slice(q * LANES, (q + 1) * LANES)
        out.append((decay[0:1, cols], decay[1:2, cols]))
    return out


def spread(pairs):
    return [tuple(jnp.broadcast_to(v, (SEGS, LANES)) for v in pair) for pair in pairs]


def chain_ends(sz, decay, ahead, behind, source, ahead_col, behind_col, ends):
    nq = sz.states // LANES
    d = spread(column_blocks(sz, decay))
    zero = jnp.zeros((SEGS, LANES), F32)

    def body(step, held):
        up, down = rows_of(step), rows_of(sz.steps - 1 - step)
        on_up, on_down = ahead[up, :], behind[down, :]
        new = []
        for q in range(nq):
            for side, (rows, on, col) in enumerate(((up, on_up, ahead_col), (down, on_down, behind_col))):
                re, im = held[2 * q + side]
                re, im = cmul(*d[q], re * on, im * on)
                re += source[rows, col + q * LANES : col + (q + 1) * LANES]
                im += source[rows, col + sz.states + q * LANES : col + sz.states + (q + 1) * LANES]
                new.append((re, im))
        return tuple(new)

    held = lax.fori_loop(0, sz.steps, body, tuple((zero, zero) for _ in range(2 * nq)), unroll=4)
    for q in range(nq):
        cols = slice(q * LANES, (q + 1) * LANES)
        for side in range(2):
            ends[2 * side, :, cols] = held[2 * q + side][0]
            ends[2 * side + 1, :, cols] = held[2 * q + side][1]


def enter_states(sz, meta, decay, ends, start, enter):
    pair = (decay[0:1, :], decay[1:2, :])
    jump = power(pair, sz.steps)
    base = meta[1] * sz.toks
    state = list(start)
    for count in range(SEGS):
        for side, seg in ((0, count), (1, SEGS - 1 - count)):
            re, im = state[side]
            enter[2 * side, seg : seg + 1, :] = re
            enter[2 * side + 1, seg : seg + 1, :] = im
            passes = through(sz, meta, base + seg * sz.steps, sz.steps)[side]
            gain = jnp.where(passes, 1.0, 0.0).astype(F32)
            re, im = cmul(jump[0] * gain, jump[1] * gain, re, im)
            state[side] = (
                re + ends[2 * side, seg : seg + 1, :],
                im + ends[2 * side + 1, seg : seg + 1, :],
            )
    return state


def send_ends(sz, meta, decay, ends, enter, send):
    zero = jnp.zeros((1, sz.states), F32)
    ahead, behind = enter_states(sz, meta, decay, ends, ((zero, zero), (zero, zero)), enter)
    me = meta[1]
    for dist in range(1, sz.chunks):
        up = (me ^ dist) > me
        for part in range(2):
            send[dist - 1, part : part + 1, :] = jnp.where(up, ahead[part], behind[part])


def received(sz, meta, decay, recv):
    me = meta[1]
    zero = jnp.zeros((1, sz.states), F32)
    pair = (decay[0:1, :], decay[1:2, :])
    jump = power(pair, sz.toks) if sz.chunks > 2 else None
    sides = []
    for side in range(2):
        re, im = zero, zero
        order = range(sz.chunks) if side == 0 else range(sz.chunks - 1, -1, -1)
        for other in order:
            use = (other < me) if side == 0 else (other > me)
            slot = jnp.maximum((me ^ other) - 1, 0)
            got = recv[slot]
            new_re, new_im = got[0:1, :], got[1:2, :]
            if sz.chunks > 2:
                passes = through(sz, meta, other * sz.toks, sz.toks)[side]
                gain = jnp.where(passes, 1.0, 0.0).astype(F32)
                moved = cmul(jump[0] * gain, jump[1] * gain, re, im)
                new_re, new_im = new_re + moved[0], new_im + moved[1]
            re, im = jnp.where(use, new_re, re), jnp.where(use, new_im, im)
        sides.append((re, im))
    return sides


def load_enter(sz, enter):
    held = []
    for q in range(sz.states // LANES):
        cols = slice(q * LANES, (q + 1) * LANES)
        for side in range(2):
            held.append((enter[2 * side, :, cols], enter[2 * side + 1, :, cols]))
    return tuple(held)


def chain_states(sz, decay, ahead, behind, source, enter, states):
    nq = sz.states // LANES
    n = sz.states
    d = spread(column_blocks(sz, decay))

    def body(step, held):
        up, down = rows_of(step), rows_of(sz.steps - 1 - step)
        on_up, on_down = ahead[up, :], behind[down, :]
        new = []
        for q in range(nq):
            for side, (rows, on) in enumerate(((up, on_up), (down, on_down))):
                re, im = held[2 * q + side]
                re, im = cmul(*d[q], re * on, im * on)
                lo = q * LANES
                re += source[rows, lo : lo + LANES]
                im += source[rows, n + lo : n + lo + LANES]
                at = 2 * side * n + lo
                states[rows, at : at + LANES] = re.astype(BF)
                states[rows, at + n : at + n + LANES] = (-im).astype(BF)
                new.append((re, im))
        return tuple(new)

    lax.fori_loop(0, sz.steps, body, load_enter(sz, enter), unroll=4)


def adjoint_chains(sz, decay, ahead, behind, source, enter, states, half, grad_driven, grad_decay):
    nq = sz.states // LANES
    n = sz.states
    d = spread(column_blocks(sz, decay))
    zero = jnp.zeros((SEGS, LANES), F32)

    def make(second):
        def body(step, carry):
            held, sums = carry
            up, down = rows_of(step), rows_of(sz.steps - 1 - step)
            on_up, on_down = ahead[up, :], behind[down, :]
            new, total = [], []
            for q in range(nq):
                lo = q * LANES
                acc_re, acc_im = sums[q]
                for side, (rows, on, src, st) in enumerate(((up, on_up, 2 * n, 2 * n), (down, on_down, 0, 0))):
                    re, im = held[2 * q + side]
                    re, im = re * on, im * on
                    s_re = states[rows, st + lo : st + lo + LANES].astype(F32)
                    s_im = states[rows, st + n + lo : st + n + lo + LANES].astype(F32)
                    acc_re += re * s_re + im * s_im
                    acc_im += re * s_im - im * s_re
                    re, im = cmul(*d[q], re, im)
                    re += source[rows, src + lo : src + lo + LANES]
                    im += source[rows, src + n + lo : src + n + lo + LANES]
                    new.append((re, im))
                    if second:
                        out_re = re + half[rows, lo : lo + LANES]
                        out_im = im + half[rows, n + lo : n + lo + LANES]
                        grad_driven[rows, lo : lo + LANES] = out_re.astype(BF)
                        grad_driven[rows, n + lo : n + lo + LANES] = (-out_im).astype(BF)
                    else:
                        half[rows, lo : lo + LANES] = re
                        half[rows, n + lo : n + lo + LANES] = im
                total.append((acc_re, acc_im))
            return tuple(new), tuple(total)

        return body

    carry = (load_enter(sz, enter), tuple((zero, zero) for _ in range(nq)))
    carry = lax.fori_loop(0, sz.steps // 2, make(False), carry, unroll=2)
    carry = lax.fori_loop(sz.steps // 2, sz.steps, make(True), carry, unroll=2)
    for q in range(nq):
        cols = slice(q * LANES, (q + 1) * LANES)
        grad_decay[0:1, cols] = jnp.sum(carry[1][q][0], axis=0, keepdims=True)
        grad_decay[1:2, cols] = jnp.sum(carry[1][q][1], axis=0, keepdims=True)


ROWS = 256


def over_rows(sz, body, init=0):
    def step(index, carry):
        return body(pl.ds(pl.multiple_of(index * ROWS, ROWS), ROWS), carry)

    return lax.fori_loop(0, sz.toks // ROWS, step, init)


def norm_rows(sz, hidden, gain, live, normed):
    def body(rows, carry):
        u = hidden[rows, :].astype(F32)
        scale = lax.rsqrt(jnp.mean(u * u, axis=1, keepdims=True) + EPSILON)
        v = u * scale * gain[...]
        normed[rows, :] = (v * widen(live[rows, :], sz.width // LANES)).astype(BF)
        return carry

    over_rows(sz, body)


def matmul_nt(a, b, out, tile=256):
    for lo in range(0, b.shape[0], tile):
        out[:, lo : lo + tile] = nt(a[...], b[lo : lo + tile, :]).astype(out.dtype)


def matmul_nn(a, b, out, tile=256):
    for lo in range(0, b.shape[1], tile):
        out[:, lo : lo + tile] = nn(a[...], b[:, lo : lo + tile]).astype(out.dtype)


def matmul_tn(a, b, out, tile=256):
    for lo in range(0, a.shape[1], tile):
        out[lo : lo + tile, :] = tn(a[:, lo : lo + tile], b[...]).astype(out.dtype)


def finish_rows(sz, mixed, skip, normed, live, hidden, slope, result):
    def body(rows, carry):
        pre = 2.0 * mixed[rows, :] + skip[...] * normed[rows, :].astype(F32)
        square = pre * pre
        th = jnp.tanh(pre * (GELU_C + (GELU_C * GELU_A) * square))
        on = widen(live[rows, :], sz.width // LANES)
        part = 0.5 * (1.0 + th)
        deriv = part + 0.5 * pre * (1.0 - th * th) * (GELU_C + (3.0 * GELU_C * GELU_A) * square)
        slope[rows, :] = (on * deriv).astype(slope.dtype)
        result[rows, :] = (hidden[rows, :].astype(F32) + on * (pre * part)).astype(result.dtype)
        return carry

    over_rows(sz, body)


def layer_open(sz, meta, hidden, gain, w_in, decay, live, ahead, behind, normed, driven, ends, enter, send):
    norm_rows(sz, hidden, gain, live, normed)
    matmul_nt(normed, w_in, driven)
    chain_ends(sz, decay, ahead, behind, driven, 0, 0, ends)
    send_ends(sz, meta, decay, ends, enter, send)


def layer_close(sz, meta, recv, decay, ends, driven, normed, hidden, w_out, skip, live, ahead, behind, enter, mixed, states, slope, result):
    enter_states(sz, meta, decay, ends, received(sz, meta, decay, recv), enter)
    chain_states(sz, decay, ahead, behind, driven, enter, states)
    matmul_nn(states, w_out, mixed)
    finish_rows(sz, mixed, skip, normed, live, hidden, slope, result)


def back_open(sz, meta, upstream, slope, normed, w_out, decay, ahead, behind, twice, grad_states, grad_skip, ends, enter, send):
    def body(rows, total):
        e = upstream[rows, :] * slope[rows, :].astype(F32)
        low = e.astype(BF)
        twice[rows, :] = low + low
        part = e * normed[rows, :].astype(F32)
        return total + jnp.sum(part.reshape(ROWS // 8, 8, sz.width), axis=0)

    total = over_rows(sz, body, jnp.zeros((8, sz.width), F32))
    grad_skip[...] = jnp.sum(total, axis=0, keepdims=True)
    matmul_nt(twice, w_out, grad_states)
    chain_ends(sz, decay, ahead, behind, grad_states, 2 * sz.states, 0, ends)
    send_ends(sz, meta, decay, ends, enter, send)


def back_close(sz, meta, recv, decay, ends, grad_states, states, upstream, slope, skip, hidden, gain, w_in, ahead, behind,
               enter, half, grad_normed, grad_driven, grad_decay, grad_gain, result):
    enter_states(sz, meta, decay, ends, received(sz, meta, decay, recv), enter)
    adjoint_chains(sz, decay, ahead, behind, grad_states, enter, states, half, grad_driven, grad_decay)
    matmul_nn(grad_driven, w_in, grad_normed)

    def body(rows, total):
        u = hidden[rows, :].astype(F32)
        r = upstream[rows, :]
        gn = grad_normed[rows, :] + r * slope[rows, :].astype(F32) * skip[...]
        scale = lax.rsqrt(jnp.mean(u * u, axis=1, keepdims=True) + EPSILON)
        part = gn * u * scale
        dn = gn * gain[...]
        inner = jnp.sum(dn * u, axis=1, keepdims=True) * (1.0 / sz.width)
        result[rows, :] = (r + scale * dn - u * (scale * scale * scale * inner)).astype(result.dtype)
        return total + jnp.sum(part.reshape(ROWS // 8, 8, sz.width), axis=0)

    total = over_rows(sz, body, jnp.zeros((8, sz.width), F32))
    grad_gain[...] = jnp.sum(total, axis=0, keepdims=True)


def gain_of(params, layer):
    return params[layer : layer + 1, :]


def skip_of(params, layer):
    return params[2 + layer : 3 + layer, :]


def decay_of(sz, params, layer):
    return params[4 + 2 * layer : 6 + 2 * layer, 0 : sz.states]


def place_pieces(sz, meta, pieces, stacked):
    part = sz.width // sz.blocks
    for dist, piece in enumerate(pieces):
        owner = meta[4] ^ dist
        stacked[pl.ds(pl.multiple_of(owner * part, part), part), :] = piece[0:part, :]


def cut_pieces(sz, meta, rows, perm, stacked, pieces):
    part = sz.width // sz.blocks
    matmul_tn(rows, perm, stacked)
    for dist, piece in enumerate(pieces):
        owner = meta[4] ^ dist
        piece[...] = stacked[pl.ds(pl.multiple_of(owner * part, part), part), :]


def cut_kernel(sz, meta, whole, *refs):
    outs, wide, sems = refs[: sz.blocks], refs[-2], refs[-1]
    straight = whole.dtype == BF
    copies = []
    for dist in range(sz.blocks):
        to = meta[0] ^ dist
        cols = pl.ds(pl.multiple_of(lax.rem(to, sz.chunks) * sz.toks, LANES), sz.toks)
        source = whole.at[lax.div(to, sz.chunks), :, cols]
        copy = pltpu.make_async_copy(source, outs[dist] if straight else wide.at[dist], sems.at[dist])
        copy.start()
        copies.append(copy)
    for dist, copy in enumerate(copies):
        copy.wait()
        if not straight:
            outs[dist][...] = wide[dist].astype(BF)


def discretize(lambda_log, lambda_imag, log_step):
    step_size = jnp.exp(log_step)
    lambda_real = -jnp.exp(lambda_log)
    modulus = jnp.exp(lambda_real * step_size)
    decay_real = modulus * jnp.cos(lambda_imag * step_size)
    decay_imag = modulus * jnp.sin(lambda_imag * step_size)
    denominator = lambda_real * lambda_real + lambda_imag * lambda_imag
    scale_real = ((decay_real - 1.0) * lambda_real + decay_imag * lambda_imag) / denominator
    scale_imag = (decay_imag * lambda_real - (decay_real - 1.0) * lambda_imag) / denominator
    return decay_real, decay_imag, scale_real, scale_imag


def first_rows(sz):
    part, own = sz.width // sz.blocks, sz.states // sz.blocks
    return part, part + own * sz.width // sz.toks


def half_map_parts(sz):
    top, end = first_rows(sz)
    rows = end - top
    for index in range(sz.toks // sz.width):
        yield slice(index * rows, (index + 1) * rows), slice(top, end), slice(index * sz.width, (index + 1) * sz.width)


def split3(x):
    hi = x.astype(BF).astype(F32)
    mid = (x - hi).astype(BF).astype(F32)
    return hi, mid, x - hi - mid


def prepare_kernel(sz, meta, tokens, *refs):
    inputs, refs = refs[:7], refs[7:]
    outs, refs = refs[: sz.blocks], refs[sz.blocks :]
    drive_b, half_b = refs[:2]
    held, small, lines, drive_a, sems = refs[2:9], refs[9], refs[10], refs[11], refs[12]
    top, end = first_rows(sz)
    own, part = sz.states // sz.blocks, sz.width // sz.blocks
    loads, copies = [], []
    for index, (source, target) in enumerate(zip(inputs, held)):
        loads.append(pltpu.make_async_copy(source, target, sems.at[index]))
    for dist in range(sz.blocks):
        to = meta[0] ^ dist
        cols = pl.ds(pl.multiple_of(lax.rem(to, sz.chunks) * sz.toks, LANES), sz.toks)
        source = tokens.at[lax.div(to, sz.chunks), :, cols]
        copies.append(pltpu.make_async_copy(source, outs[dist].at[0:top, :], sems.at[len(inputs) + dist]))
    for copy in copies + loads:
        copy.start()
    for copy in loads[:6]:
        copy.wait()
    gain, skip, lambda_log, lambda_imag, log_step, input_map, output_map = held
    dr, di, sr, si = discretize(lambda_log[...], lambda_imag[...], log_step[...])
    small[...] = jnp.zeros_like(small)
    lines[...] = jnp.zeros_like(lines)
    small[0:2, 0:part] = gain[...]
    small[2:4, 0:part] = skip[...]
    for layer in range(2):
        small[4 + 2 * layer : 5 + 2 * layer, 0:own] = dr[layer : layer + 1]
        small[5 + 2 * layer : 6 + 2 * layer, 0:own] = di[layer : layer + 1]
    lines[0:2, 0:own] = sr
    lines[2:4, 0:own] = si
    cols = lines[...].T
    for layer in range(2):
        qr, qi = cols[0:own, layer : layer + 1], cols[0:own, 2 + layer : 3 + layer]
        br, bi = input_map[layer, 0].astype(F32), input_map[layer, 1].astype(F32)
        for index, value in enumerate((qr * br - qi * bi, qr * bi + qi * br)):
            (drive_a, drive_b)[layer][index] = value.astype(BF)
    rows = jnp.concatenate([*split3(small[...]), jnp.zeros((8, sz.toks - 3 * LANES), F32)], axis=1)
    rows = jnp.concatenate([rows, jnp.zeros((8, sz.toks), F32)], axis=0).astype(BF)
    for dist, out in enumerate(outs):
        half = lax.rem(meta[0] ^ dist, 2)
        for from_rows, to_rows, lanes in half_map_parts(sz):
            out[to_rows, lanes] = drive_a[half, from_rows, :]
        out[end:, :] = rows
    loads[6].wait()
    core = meta[2]
    for index in range(2):
        half_b[index] = output_map[0, 2 * core + index]
        half_b[3 + index] = output_map[1, 2 * core + index]
    half_b[2] = drive_b[core]
    for copy in copies:
        copy.wait()


def params_of(sz, piece):
    rows = piece[piece.shape[0] - 16 :, 0 : 3 * LANES].astype(F32)[0:8]
    return rows[:, 0:LANES] + rows[:, LANES : 2 * LANES] + rows[:, 2 * LANES :]


def join_kernel(sz, meta, *refs):
    pieces, maps, params = refs[: sz.blocks], refs[-2], refs[-1]
    own = sz.states // sz.blocks
    collect_params(sz, meta, [params_of(sz, piece) for piece in pieces], params)
    for dist, piece in enumerate(pieces):
        base = (meta[4] ^ dist) * own
        for to_rows, from_rows, lanes in half_map_parts(sz):
            rows = pl.ds(pl.multiple_of(base + to_rows.start, 16), to_rows.stop - to_rows.start)
            maps[rows, :] = piece[from_rows, lanes]


def collect_params(sz, meta, smalls, params):
    own = sz.states // sz.blocks
    part = sz.width // sz.blocks
    lane = lax.broadcasted_iota(jnp.int32, (8, LANES), 1)
    row = lax.broadcasted_iota(jnp.int32, (8, LANES), 0)
    pad = jnp.zeros((8, sz.width - LANES), F32)
    total = jnp.zeros((8, sz.width), F32)
    for block in range(sz.blocks):
        piece = smalls[0]
        for dist in range(1, sz.blocks):
            piece = jnp.where((meta[4] ^ dist) == block, smalls[dist], piece)
        for first, count, size in ((0, 4, part), (4, 4, own)):
            mine = jnp.where((row >= first) & (row < first + count) & (lane < size), piece, 0.0)
            wide = jnp.concatenate([mine, pad], axis=1)
            total += pltpu.roll(wide, block * size, 1) if block else wide
    params[...] = total


def place_maps(sz, meta, own_maps, mine, other, skip, out):
    own = sz.states // sz.blocks
    count = own_maps.shape[0] // 2

    def put(index, owner, value):
        out[pl.ds(pl.multiple_of(index * sz.states + owner * own, own), own), :] = value

    for index in range(2 * count):
        put(index, meta[0], own_maps[index])
    for side, pieces in ((meta[2], mine), (1 - meta[2], other)):
        for dist, piece in enumerate(pieces):
            for index in range(count):
                put(side * count + index, meta[0] ^ (dist + 1), piece[skip + index])


def open_kernel(sz, meta, perm, params, *refs):
    pieces, (hidden, normed, stacked, live) = refs[: sz.blocks], refs[sz.blocks :]
    place_pieces(sz, meta, pieces, stacked)
    matmul_nt(perm, stacked, hidden)
    fill_masks(sz, meta, live, None, None)
    norm_rows(sz, hidden, gain_of(params, 0), live, normed)


def enter_kernel(sz, meta, params, normed, maps, other, w_in, driven, ends, send, ahead, behind, enter):
    decay = decay_of(sz, params, 0)
    for side, half in ((meta[2], maps), (1 - meta[2], other)):
        w_in[pl.ds(pl.multiple_of(side * sz.states, sz.states), sz.states), :] = half[...]
    fill_masks(sz, meta, None, ahead, behind)
    matmul_nt(normed, w_in, driven)
    chain_ends(sz, decay, ahead, behind, driven, 0, 0, ends)
    send_ends(sz, meta, decay, ends, enter, send)


def middle_kernel(sz, meta, recv, params, ends, driven, normed, hidden, own_out, own_in, *refs):
    decay, skip, gain_b, decay_b = decay_of(sz, params, 0), skip_of(params, 0), gain_of(params, 1), decay_of(sz, params, 1)
    far = sz.blocks - 1
    mine, other, refs = refs[:far], refs[far : 2 * far], refs[2 * far :]
    w_out, w_in_b, states, slope, hidden_b, normed_b, driven_b, ends_b, send_b, live, ahead, behind, enter, mixed = refs
    place_maps(sz, meta, own_out, mine, other, 0, w_out)
    place_maps(sz, meta, own_in, mine, other, 2, w_in_b)
    fill_masks(sz, meta, live, ahead, behind)
    layer_close(sz, meta, recv, decay, ends, driven, normed, hidden, w_out, skip, live, ahead, behind, enter, mixed, states, slope, hidden_b)
    layer_open(sz, meta, hidden_b, gain_b, w_in_b, decay_b, live, ahead, behind, normed_b, driven_b, ends_b, enter, send_b)


def leave_kernel(sz, meta, recv, params, ends, driven, normed, hidden, perm, own_out, *refs):
    decay, skip = decay_of(sz, params, 1), skip_of(params, 1)
    far = sz.blocks - 1
    mine, other, refs = refs[:far], refs[far : 2 * far], refs[2 * far :]
    w_out, states, slope, refs = *refs[:3], refs[3:]
    place_maps(sz, meta, own_out, mine, other, 3, w_out)
    pieces, refs = refs[: sz.blocks], refs[sz.blocks :]
    live, ahead, behind, enter, mixed, last, stacked = refs
    fill_masks(sz, meta, live, ahead, behind)
    layer_close(sz, meta, recv, decay, ends, driven, normed, hidden, w_out, skip, live, ahead, behind, enter, mixed, states, slope, last)
    cut_pieces(sz, meta, last, perm, stacked, pieces)


def turn_kernel(sz, meta, slope, normed, w_out, params, perm, *refs):
    decay = decay_of(sz, params, 1)
    pieces, refs = refs[: sz.blocks], refs[sz.blocks :]
    upstream, twice, grad_states, grad_skip, ends, send, stacked, ahead, behind, enter = refs
    place_pieces(sz, meta, pieces, stacked)
    matmul_nt(perm, stacked, upstream)
    fill_masks(sz, meta, None, ahead, behind)
    back_open(sz, meta, upstream, slope, normed, w_out, decay, ahead, behind, twice, grad_states, grad_skip, ends, enter, send)


def back_middle_kernel(sz, meta, recv, params, ends, grad_states, states, upstream, slope, hidden, w_in,
                       slope_b, normed_b, w_out_b,
                       grad_driven, grad_decay, grad_gain, upstream_b, twice_b, grad_states_b, grad_skip_b, ends_b, send_b,
                       ahead, behind, enter, half, grad_normed):
    decay, skip, gain, decay_b = decay_of(sz, params, 1), skip_of(params, 1), gain_of(params, 1), decay_of(sz, params, 0)
    fill_masks(sz, meta, None, ahead, behind)
    back_close(sz, meta, recv, decay, ends, grad_states, states, upstream, slope, skip, hidden, gain, w_in, ahead, behind,
               enter, half, grad_normed, grad_driven, grad_decay, grad_gain, upstream_b)
    back_open(sz, meta, upstream_b, slope_b, normed_b, w_out_b, decay_b, ahead, behind, twice_b, grad_states_b, grad_skip_b, ends_b, enter, send_b)


def back_leave_kernel(sz, meta, recv, params, ends, grad_states, states, upstream, slope, hidden, w_in, perm,
                      gain_b, skip_a, skip_b, decay_b, *refs):
    done, refs = refs[: sz.blocks], refs[sz.blocks :]
    grad_driven, tiny, refs = refs[0], refs[1], refs[2:]
    decay, skip, gain = decay_of(sz, params, 0), skip_of(params, 0), gain_of(params, 0)
    pieces, refs = refs[: sz.blocks], refs[sz.blocks :]
    ahead, behind, enter, half, grad_normed, last, stacked, grad_decay, grad_gain = refs
    fill_masks(sz, meta, None, ahead, behind)
    back_close(sz, meta, recv, decay, ends, grad_states, states, upstream, slope, skip, hidden, gain, w_in, ahead, behind,
               enter, half, grad_normed, grad_driven, grad_decay, grad_gain, last)
    tiny[...] = jnp.zeros_like(tiny)
    for row, line in enumerate((grad_gain, gain_b, skip_a, skip_b)):
        tiny[row : row + 1, :] = line[...]
    tiny[4:6, 0 : sz.states] = grad_decay[...]
    tiny[6:8, 0 : sz.states] = decay_b[...]
    part = sz.width // sz.blocks
    for piece, first in zip(pieces, done):
        piece[0:part, :] = first[...]
    cut_pieces(sz, meta, last, perm, stacked, [piece.at[part : 2 * part, :] for piece in pieces])


def weight_kernel(counts, other, sz, meta, *refs):
    half, out = (1 - meta[2] if other else meta[2]), refs[-1]
    at = 0
    for index, count in enumerate(counts):
        left, right = refs[2 * index], refs[2 * index + 1]
        for group in range(count):
            cols = pl.ds(pl.multiple_of((half * count + group) * sz.states, LANES), sz.states)
            out[at : at + sz.states, :] = tn(left[:, cols], right[...]).astype(out.dtype)
            at += sz.states


def fold_core_kernel(count, sz, meta, keep, got, *pieces):
    own = sz.states // sz.blocks
    part = sz.width // sz.blocks
    tiny = None
    if len(pieces) > sz.blocks:
        tiny, pieces = pieces[0][...] + pieces[1][...], pieces[2:]
        row = lax.broadcasted_iota(jnp.int32, (8, LANES), 0)
        lane = lax.broadcasted_iota(jnp.int32, (8, LANES), 1)
    for dist, piece in enumerate(pieces):
        owner = meta[0] ^ dist
        for group in range(count):
            rows = pl.ds(pl.multiple_of(group * sz.states + owner * own, own), own)
            piece[group * own : (group + 1) * own, :] = (keep[rows, :].astype(F32) + got[rows, :].astype(F32)).astype(BF)
        if tiny is not None:
            value = jnp.zeros((8, LANES), F32)
            for block in range(sz.blocks):
                wide = pltpu.roll(tiny, sz.width - block * part, 1) if block else tiny
                deep = pltpu.roll(tiny, sz.width - block * own, 1) if block else tiny
                mine = jnp.where(row < 4, jnp.where(lane < part, wide[:, :LANES], 0.0), jnp.where(lane < own, deep[:, :LANES], 0.0))
                value = jnp.where(owner == block, mine, value)
            hi, lo = split2(value)
            rest = jnp.zeros((8, sz.width - 2 * LANES), F32)
            wide = jnp.concatenate([jnp.concatenate([hi, lo, rest], axis=1), jnp.zeros((8, sz.width), F32)], axis=0)
            piece[count * own : count * own + 16, :] = wide.astype(BF)


def split2(x):
    hi = x.astype(BF).astype(F32)
    return hi, x - hi


def fold_block_kernel(planes, counts, sz, meta, *refs):
    lanes = sz.width // LANES
    groups = len(counts)
    got, refs = refs[: groups * sz.blocks], refs[groups * sz.blocks :]
    outs, talls = refs[:planes], refs[planes:]
    at = 0
    for index, rows in enumerate(counts):
        pieces = got[index * sz.blocks : (index + 1) * sz.blocks]
        total = pieces[0][...].astype(F32)
        for piece in pieces[1:]:
            total += piece[...].astype(F32)
        tall = talls[index]
        padded = tall.shape[0] // lanes
        for block in range(lanes):
            tall[block * padded : block * padded + rows, :] = total[0:rows, block * LANES : (block + 1) * LANES].astype(BF)
            if padded > rows:
                tall[block * padded + rows : (block + 1) * padded, :] = jnp.zeros((padded - rows, LANES), BF)
        part = tall.shape[0] // planes
        for dist, out in enumerate(outs):
            out[at : at + part, :] = tall[pl.ds(pl.multiple_of((meta[3] ^ dist) * part, part), part), :]
        at += part
    value = total[counts[-1] : counts[-1] + 8, 0:LANES] + total[counts[-1] : counts[-1] + 8, LANES : 2 * LANES]
    rows = jnp.concatenate(split2(value), axis=0).astype(BF)
    for out in outs:
        out[at : at + 16, :] = rows


def fold_plane_kernel(sz, meta, *refs):
    parts, out, tiny = refs[:-2], refs[-2], refs[-1]
    total = parts[0][...].astype(F32)
    for piece in parts[1:]:
        total += piece[...].astype(F32)
    rows = total.shape[0] - 16
    out[...] = total[0:rows].astype(BF)
    tiny[...] = total[rows : rows + 8] + total[rows + 8 :]


def finish_kernel(planes, groups, sz, meta, *refs):
    count = 2 * planes
    pieces, refs = refs[:count], refs[count:]
    tiny, lambda_log, lambda_imag, log_step, input_map = refs[:5]
    grad_gain, grad_skip, grad_log, grad_imag, grad_step, grad_maps, grad_out = refs[5:12]
    talls, grad_in, lines = refs[12:-2], refs[-2], refs[-1]
    own = sz.states // sz.blocks
    lanes = sz.width // LANES
    start = 0
    for tall, group in zip(talls, groups):
        padded = tall.shape[0] // lanes
        part = tall.shape[0] // planes
        for side in range(2):
            half = meta[2] ^ side
            for dist in range(planes):
                rows = pl.ds(pl.multiple_of((meta[3] ^ dist) * part, part), part)
                tall[rows, :] = pieces[side * planes + dist][start : start + part, :]
            at = 0
            for which, layer, maps in group:
                out = grad_in if which == 0 else grad_out
                for one in range(maps):
                    for block in range(lanes):
                        rows = slice(block * padded + at, block * padded + at + own)
                        out[layer, half * maps + one, :, block * LANES : (block + 1) * LANES] = tall[rows, :].astype(F32)
                    at += own
        start += part
    width = sz.width // sz.blocks
    grad_gain[...] = tiny[0:2, 0:width]
    grad_skip[...] = tiny[2:4, 0:width]
    dr, di, sr, si = discretize(lambda_log[...], lambda_imag[...], log_step[...])
    lines[...] = jnp.zeros_like(lines)
    lines[0:2, 0:own] = sr
    lines[2:4, 0:own] = si
    cols = lines[...].T
    back = []
    for layer in range(2):
        qr, qi = cols[0:own, layer : layer + 1], cols[0:own, 2 + layer : 3 + layer]
        wr, wi = grad_in[layer, 0], grad_in[layer, 1]
        br, bi = input_map[layer, 0].astype(F32), input_map[layer, 1].astype(F32)
        grad_maps[layer, 0] = qr * wr + qi * wi
        grad_maps[layer, 1] = qr * wi - qi * wr
        back.append(jnp.sum(wr * br + wi * bi, axis=1, keepdims=True))
        back.append(jnp.sum(wi * br - wr * bi, axis=1, keepdims=True))
    lines[...] = jnp.zeros_like(lines)
    for index, col in enumerate(back):
        lines[0:own, index : index + 1] = col
    rows = lines[...].T
    step = jnp.exp(log_step[...])
    lr, li = -jnp.exp(lambda_log[...]), lambda_imag[...]
    norm = 1.0 / (lr * lr + li * li)
    for layer in range(2):
        at = slice(layer, layer + 1)
        a, b, h = (lr[at], li[at]), (dr[at], di[at]), step[at]
        gq = rows[2 * layer : 2 * layer + 1, 0:own], rows[2 * layer + 1 : 2 * layer + 2, 0:own]
        gd = tiny[4 + 2 * layer : 5 + 2 * layer, 0:own], tiny[5 + 2 * layer : 6 + 2 * layer, 0:own]
        inverse = a[0] * norm[at], -a[1] * norm[at]
        through = cmul(inverse[0], -inverse[1], *gq)
        gd = gd[0] + through[0], gd[1] + through[1]
        ratio = cmul(*inverse, sr[at], si[at])
        direct = cmul(ratio[0], -ratio[1], *gq)
        moved = cmul(b[0] * h, -b[1] * h, *gd)
        turn = cmul(*a, *b)
        grad_log[at, :] = (moved[0] - direct[0]) * a[0]
        grad_imag[at, :] = moved[1] - direct[1]
        grad_step[at, :] = (turn[0] * gd[0] + turn[1] * gd[1]) * h


def spread_kernel(sz, meta, *refs):
    pieces, outs, wide, sems = refs[: sz.blocks], refs[sz.blocks : -2], refs[-2], refs[-1]
    part = sz.width // sz.blocks
    copies = []
    for dist, piece in enumerate(pieces):
        owner = meta[0] ^ dist
        for index, out in enumerate(outs):
            slot = dist * len(outs) + index
            wide[slot] = piece[index * part : (index + 1) * part, :].astype(F32)
            cols = pl.ds(pl.multiple_of(lax.rem(owner, sz.chunks) * sz.toks, LANES), sz.toks)
            copy = pltpu.make_async_copy(wide.at[slot], out.at[lax.div(owner, sz.chunks), :, cols], sems.at[slot])
            copy.start()
            copies.append(copy)
    for copy in copies:
        copy.wait()


VMEM = pl.BlockSpec(memory_space=pltpu.VMEM)
SMEM = pl.BlockSpec(memory_space=pltpu.SMEM)
HBM = pl.BlockSpec(memory_space=pltpu.HBM)


def call(name, sz, body, items, args, outs, scratch, limit=10, in_spec=VMEM, out_spec=VMEM, time=0.0):
    out_shape = [jax.ShapeDtypeStruct(shape, dtype) for shape, dtype in outs]

    def kernel(*refs):
        body(sz, place_of(sz, refs[0] if items else None), *refs[len(items) :])

    return pl.pallas_call(
        kernel,
        out_shape=out_shape,
        in_specs=[SMEM] * len(items) + [in_spec] * len(args),
        out_specs=[out_spec] * len(outs),
        scratch_shapes=[pltpu.VMEM(*item) if isinstance(item, tuple) else item for item in scratch],
        compiler_params=pltpu.CompilerParams(vmem_limit_bytes=limit << 20),
        cost_estimate=pl.CostEstimate(flops=int(COST * time), bytes_accessed=1000, transcendentals=0),
        name=name,
    )(*items, *args)


def on_device(tokens, cotangent, item_lengths, item_offsets, norm_gain, lambda_log, lambda_imag, log_step, input_map, output_map, skip_weight):
    micro, part, run = tokens.shape
    layers = norm_gain.shape[0]
    blocks = lax.axis_size("block")
    planes = lax.axis_size("plane")
    chunks = blocks // micro
    toks = run // chunks
    own = lambda_log.shape[1]
    width, states = part * blocks, own * blocks
    sz = Sizes(blocks, chunks, toks, run, toks // SEGS, width, states, item_lengths.shape[1])

    def swap(x, dist, axis="block"):
        return lax.ppermute(x, axis, [(i, i ^ dist) for i in range(lax.axis_size(axis))])

    def across(x, dist, back):
        pairs = []
        for c in range(2):
            for b in range(blocks):
                q = b ^ dist
                pairs.append((c * blocks + b, (q % 2) * blocks + (q // 2) * 2 + c))
        return lax.ppermute(x, ("core", "block"), [pair[::-1] for pair in pairs] if back else pairs)

    def across_all(pieces, back=False):
        return [across(piece, dist, back) for dist, piece in enumerate(pieces)]

    table = jnp.stack([item_lengths, item_offsets])
    items = [jnp.stack([table, swap(table, 1, "core")])]

    def neighbour(x, dist):
        pairs = []
        for c in range(2):
            for b in range(blocks):
                q = ((b // 2) * 2 + c) ^ dist
                pairs.append((c * blocks + b, (q % 2) * blocks + (q // 2) * 2 + b % 2))
        return lax.ppermute(x, ("core", "block"), pairs)

    def swap_all(pieces, axis="block"):
        return [swap(piece, dist, axis) if dist else piece for dist, piece in enumerate(pieces)]

    def exchange(send):
        return jnp.stack([neighbour(send[dist - 1], dist) for dist in range(1, chunks)])

    row = jnp.arange(toks, dtype=jnp.int32)[:, None]
    col = jnp.arange(toks, dtype=jnp.int32)[None, :]
    perm = ((row % SEGS) * sz.steps + row // SEGS == col).astype(BF)

    maps_own = ((2, own, width), BF)
    half_own = ((5, own, width), BF)
    given = [norm_gain, skip_weight, lambda_log, lambda_imag, log_step, input_map, output_map]
    *first_pieces, drive_b, half_b = call(
        "prepare", sz, prepare_kernel, [], [pltpu.with_memory_space_constraint(x, pltpu.HBM) for x in [tokens, *given]],
        [((first_rows(sz)[1] + 16, toks), BF)] * blocks + [maps_own, half_own],
        [(x.shape, x.dtype) for x in given] + [((8, LANES), F32), ((8, LANES), F32), maps_own, pltpu.SemaphoreType.DMA((len(given) + blocks,))],
        limit=6, in_spec=HBM)
    first_pieces = across_all(first_pieces)
    cot_cut = call("cut_cotangent", sz, cut_kernel, [], [pltpu.with_memory_space_constraint(cotangent, pltpu.HBM)],
                   [((part, toks), BF)] * blocks, [((blocks, part, toks), F32), pltpu.SemaphoreType.DMA((blocks,))], limit=4, in_spec=HBM)
    half_b, first_pieces[1], perm, cot_cut = after(half_b, first_pieces[1], perm, cot_cut)
    maps_a, params = call("join", sz, join_kernel, [], first_pieces, [((states, width), BF), ((8, width), F32)], [])
    second_mine = [swap(half_b, dist) for dist in range(1, blocks)]

    mask = ((toks, LANES), F32)
    enter = ((4, SEGS, states), F32)
    stacked = ((width, toks), BF)
    rows_f, rows_b = ((toks, width), F32), ((toks, width), BF)
    drv = ((toks, 2 * states), F32)
    sts = ((toks, 4 * states), BF)
    gst = ((toks, 4 * states), F32)
    snd = ((chunks - 1, 2, states), F32)
    w_in, w_out = ((2 * states, width), BF), ((4 * states, width), BF)
    line, gdec = ((1, width), F32), ((2, states), F32)
    piece_out = [((part, toks), BF)] * blocks

    other_a = swap(maps_a, 1, "core")
    hidden_a, normed_a = call("open", sz, open_kernel, items, [perm, params, *first_pieces], [rows_b, rows_b], [stacked, mask], time=3)
    w_in_a, driven_a, ends_a, send_a = call(
        "enter", sz, enter_kernel, items, [params, normed_a, maps_a, other_a], [w_in, drv, enter, snd], [mask, mask, enter])
    recv = exchange(send_a)
    second_mine, _ = after(second_mine, send_a)
    second_maps = second_mine, [swap(piece, 1, "core") for piece in second_mine]
    w_out_a, w_in_b, states_a, slope_a, hidden_b, normed_b, driven_b, ends_b, send_b = call(
        "middle", sz, middle_kernel, items,
        [recv, params, ends_a, driven_a, normed_a, hidden_a, output_map[0], drive_b, *second_maps[0], *second_maps[1]],
        [w_out, w_in, sts, rows_b, rows_f, rows_b, drv, enter, snd], [mask, mask, mask, enter, rows_f], time=11)
    recv = exchange(send_b)
    cot_cut, _ = after(cot_cut, send_a)
    cot_pieces = across_all(cot_cut)
    recv, cot_pieces = after(recv, cot_pieces)
    w_out_b, states_b, slope_b, *out_pieces = call(
        "leave", sz, leave_kernel, items,
        [recv, params, ends_b, driven_b, normed_b, hidden_b, perm, output_map[1], *second_maps[0], *second_maps[1]],
        [w_out, sts, rows_b, *piece_out], [mask, mask, mask, enter, rows_f, rows_b, stacked], time=8)

    def half_grads(name, pairs, counts, first=()):
        args = [x for pair in pairs for x in pair]
        shape = [((sum(counts) * states, width), BF)]
        (send,) = call(name + "_send", sz, partial(weight_kernel, counts, True), [], args, shape, [])
        send, first = after(send, first)
        got = swap(send, 1, "core")
        (keep,) = call(name + "_keep", sz, partial(weight_kernel, counts, False), [], args, shape, [], time=sum(counts))
        return (keep, got), first

    def fold_core(name, group):
        total = group[0].shape[0] // states
        rows = total * own + (16 if len(group) > 2 else 0)
        return swap_all(call(name, sz, partial(fold_core_kernel, total), [], group, [((rows, width), BF)] * blocks, []))

    def spread(pieces):
        return call("spread", sz, spread_kernel, [], pieces, [((micro, part, run), F32)] * 2,
                    [((2 * blocks, part, toks), F32), pltpu.SemaphoreType.DMA((2 * blocks,))], limit=6, out_spec=HBM)

    lanes = width // LANES

    def tall_of(rows):
        step = max(SEGS * planes // lanes, SEGS)
        return ((lanes * (-(-rows // step) * step), LANES), BF)

    def over_planes(name, groups, rows):
        talls = [tall_of(n) for n in rows]
        cut = sum(t[0][0] for t in talls) // planes + 16
        parts = call(name, sz, partial(fold_block_kernel, planes, rows), [], [x for g in groups for x in g],
                     [((cut, LANES), BF)] * planes, talls)
        return swap_all(parts, "plane")

    up_b, twice_b, gstates_b, gskip_b, ends, send = call(
        "turn", sz, turn_kernel, items, [slope_b, normed_b, w_out_b, params, perm, *cot_pieces],
        [rows_f, rows_b, gst, line, enter, snd], [stacked, mask, mask, enter], time=6)
    recv = exchange(send)
    group_a, _ = half_grads("grads_a", [(states_b, twice_b)], (2,))
    sums_a = fold_core("fold_a", group_a)
    recv, sums_a[0] = after(recv, sums_a[0])
    gdriven_b, gdecay_b, ggain_b, up_a, twice_a, gstates_a, gskip_a, ends, send = call(
        "back_middle", sz, back_middle_kernel, items,
        [recv, params, ends, gstates_b, states_b, up_b, slope_b, hidden_b, w_in_b, slope_a, normed_a, w_out_a],
        [((toks, 2 * states), BF), gdec, line, rows_f, rows_b, gst, line, enter, snd], [mask, mask, enter, drv, rows_f], limit=12, time=11)
    recv = exchange(send)
    gdriven_b, sums_a = after(gdriven_b, sums_a)
    group_b, _ = half_grads("grads_b", [(gdriven_b, normed_b), (states_a, twice_a)], (1, 2))
    sums_b = fold_core("fold_b", group_b)
    recv, sums_b[0] = after(recv, sums_b[0])
    gdriven_a, tiny, *last_pieces = call(
        "back_leave", sz, back_leave_kernel, items,
        [recv, params, ends, gstates_a, states_a, up_a, slope_a, hidden_a, w_in_a, perm, ggain_b, gskip_a, gskip_b, gdecay_b, *out_pieces],
        [((toks, 2 * states), BF), ((8, width), F32)] + [((2 * part, toks), BF)] * blocks,
        [mask, mask, enter, drv, rows_f, rows_b, stacked, gdec, line], limit=12, time=9)
    group_c, sums_b = half_grads("grads_c", [(gdriven_a, normed_a)], (1,), sums_b)
    sums_c = fold_core("fold_c", [*group_c, tiny, swap(tiny, 1, "core")])
    parts = over_planes("planes", [sums_a, sums_b, sums_c], (2 * own, 3 * own, own))
    last_pieces, parts[0] = after(last_pieces, parts[0])
    early = [across(piece, 2 * dist, True) for dist, piece in enumerate(last_pieces[0::2])]
    sum_all, tiny = call("sum", sz, fold_plane_kernel, [], parts, [((parts[0].shape[0] - 16, LANES), BF), ((8, LANES), F32)], [])
    whole = swap_all([sum_all] * planes, "plane")
    late, _ = after(last_pieces[1::2], sum_all)
    late = [across(piece, 2 * dist + 1, True) for dist, piece in enumerate(late)]
    output, input_grad = spread([piece for pair in zip(early, late) for piece in pair])
    whole, output = after(whole, output)
    whole += [swap(x, 1, "core") for x in whole]
    small_out = ((layers, own), F32)
    grad_gain, grad_skip, grad_log, grad_imag, grad_step, grad_in, grad_out = call(
        "finish", sz, partial(finish_kernel, planes, ([(1, 1, 2)], [(0, 1, 1), (1, 0, 2)], [(0, 0, 1)])), [],
        [*whole, tiny, lambda_log, lambda_imag, log_step, input_map],
        [((layers, part), F32)] * 2 + [small_out] * 3 + [((layers, 2, own, width), F32), ((layers, 4, own, width), F32)],
        [tall_of(n * own) for n in (2, 3, 1)] + [((layers, 2, own, width), F32), ((LANES, LANES), F32)])
    return output, input_grad, grad_gain, grad_log, grad_imag, grad_step, grad_in, grad_out, grad_skip


def solution(mesh):
    rows, blocks = mesh.devices.shape
    inner = Mesh(mesh.devices.reshape(rows // 2, 2, blocks), ("plane", "core", "block"))
    dp = ("plane", "core")
    half = P(None, "block")
    maps = P(None, None, "block", None)
    acts = P(None, "block", dp)
    items = P(None, dp)
    return jax.shard_map(
        on_device,
        mesh=inner,
        in_specs=(acts, acts, items, items, half, half, half, half, maps, maps, half),
        out_specs=(acts, acts, half, half, half, half, maps, maps, half),
        check_vma=False,
    )
```

```python
from functools import partial
from typing import NamedTuple

import jax
import jax.numpy as jnp
from jax import lax
from jax.experimental import pallas as pl
from jax.experimental.pallas import tpu as pltpu
from jax.sharding import Mesh, PartitionSpec as P

EPSILON = 1e-05
SEGS = 16
LANES = 128
BF = jnp.bfloat16
F32 = jnp.float32
GELU_C = 0.7978845608028654
GELU_A = 0.044715
COST = 400_000_000


class Sizes(NamedTuple):
    blocks: int
    chunks: int
    toks: int
    run: int
    steps: int
    width: int
    states: int
    items: int


def turned(sz, index):
    return sz.blocks - 1 - index


def farthest(index, count):
    return count - index if index else 0


def place_of(sz, table):
    me, core = lax.axis_index("block"), lax.axis_index("core")
    q = lax.div(me, 2) * 2 + core
    mine, chunk = lax.div(q, sz.chunks), lax.rem(q, sz.chunks)
    out = [me, chunk, core, lax.axis_index("plane"), q]
    if table is not None:
        side = lax.rem(me, 2) ^ core
        for which in range(2):
            out += [table[side, which, mine, index] for index in range(sz.items)]
    return out


def nt(a, b):
    return lax.dot_general(a, b, (((1,), (1,)), ((), ())), preferred_element_type=F32)


def nn(a, b):
    return lax.dot_general(a, b, (((1,), (0,)), ((), ())), preferred_element_type=F32)


def tn(a, b):
    return lax.dot_general(a, b, (((0,), (0,)), ((), ())), preferred_element_type=F32)


def after(*values):
    return lax.optimization_barrier(values)


def cmul(ar, ai, br, bi):
    return ar * br - ai * bi, ar * bi + ai * br


def rows_of(step):
    return pl.ds(pl.multiple_of(step * SEGS, SEGS), SEGS)


def widen(mask, count):
    return jnp.concatenate([mask] * count, axis=1)


def item_of(sz, meta, index):
    begin = meta[5 + sz.items + index]
    return begin, begin + meta[5 + index]


def fill_masks(sz, meta, live, ahead, behind):
    base = meta[1] * sz.toks
    seg = lax.broadcasted_iota(jnp.int32, (SEGS, LANES), 0)

    def body(step, carry):
        pos = base + seg * sz.steps + step
        inside = jnp.zeros((SEGS, LANES), F32)
        onward = jnp.zeros((SEGS, LANES), F32)
        onward_next = jnp.zeros((SEGS, LANES), F32)
        for index in range(sz.items):
            begin, end = item_of(sz, meta, index)
            inside = jnp.where((pos >= begin) & (pos < end), 1.0, inside)
            onward = jnp.where((pos > begin) & (pos < end), 1.0, onward)
            onward_next = jnp.where((pos >= begin) & (pos + 1 < end), 1.0, onward_next)
        onward_next = jnp.where(pos + 1 < sz.run, onward_next, 0.0)
        live[rows_of(step), :] = inside
        ahead[rows_of(step), :] = onward
        behind[rows_of(step), :] = onward_next
        return carry

    lax.fori_loop(0, sz.steps, body, 0, unroll=4)


def through(sz, meta, first, length):
    ahead = behind = False
    for index in range(sz.items):
        begin, end = item_of(sz, meta, index)
        ahead = ahead | ((begin < first) & (end >= first + length))
        behind = behind | ((begin <= first) & (end > first + length))
    behind = behind & (first + length < sz.run)
    return ahead, behind


def power(pair, count):
    while count > 1:
        pair = cmul(*pair, *pair)
        count //= 2
    return pair


def column_blocks(sz, decay):
    out = []
    for q in range(sz.states // LANES):
        cols = slice(q * LANES, (q + 1) * LANES)
        out.append((decay[0:1, cols], decay[1:2, cols]))
    return out


def spread(pairs):
    return [tuple(jnp.broadcast_to(v, (SEGS, LANES)) for v in pair) for pair in pairs]


def chain_ends(sz, decay, ahead, behind, source, ahead_col, behind_col, ends):
    nq = sz.states // LANES
    d = spread(column_blocks(sz, decay))
    zero = jnp.zeros((SEGS, LANES), F32)

    def body(step, held):
        up, down = rows_of(step), rows_of(sz.steps - 1 - step)
        on_up, on_down = ahead[up, :], behind[down, :]
        new = []
        for q in range(nq):
            for side, (rows, on, col) in enumerate(((up, on_up, ahead_col), (down, on_down, behind_col))):
                re, im = held[2 * q + side]
                re, im = cmul(*d[q], re * on, im * on)
                re += source[rows, col + q * LANES : col + (q + 1) * LANES]
                im += source[rows, col + sz.states + q * LANES : col + sz.states + (q + 1) * LANES]
                new.append((re, im))
        return tuple(new)

    held = lax.fori_loop(0, sz.steps, body, tuple((zero, zero) for _ in range(2 * nq)), unroll=4)
    for q in range(nq):
        cols = slice(q * LANES, (q + 1) * LANES)
        for side in range(2):
            ends[2 * side, :, cols] = held[2 * q + side][0]
            ends[2 * side + 1, :, cols] = held[2 * q + side][1]


def enter_states(sz, meta, decay, ends, start, enter):
    pair = (decay[0:1, :], decay[1:2, :])
    jump = power(pair, sz.steps)
    base = meta[1] * sz.toks
    state = list(start)
    for count in range(SEGS):
        for side, seg in ((0, count), (1, SEGS - 1 - count)):
            re, im = state[side]
            enter[2 * side, seg : seg + 1, :] = re
            enter[2 * side + 1, seg : seg + 1, :] = im
            passes = through(sz, meta, base + seg * sz.steps, sz.steps)[side]
            gain = jnp.where(passes, 1.0, 0.0).astype(F32)
            re, im = cmul(jump[0] * gain, jump[1] * gain, re, im)
            state[side] = (
                re + ends[2 * side, seg : seg + 1, :],
                im + ends[2 * side + 1, seg : seg + 1, :],
            )
    return state


def send_ends(sz, meta, decay, ends, enter, send):
    zero = jnp.zeros((1, sz.states), F32)
    ahead, behind = enter_states(sz, meta, decay, ends, ((zero, zero), (zero, zero)), enter)
    me = meta[1]
    for dist in range(1, sz.chunks):
        up = (me ^ dist) > me
        for part in range(2):
            send[dist - 1, part : part + 1, :] = jnp.where(up, ahead[part], behind[part])


def received(sz, meta, decay, recv):
    me = meta[1]
    zero = jnp.zeros((1, sz.states), F32)
    pair = (decay[0:1, :], decay[1:2, :])
    jump = power(pair, sz.toks) if sz.chunks > 2 else None
    sides = []
    for side in range(2):
        re, im = zero, zero
        order = range(sz.chunks) if side == 0 else range(sz.chunks - 1, -1, -1)
        for other in order:
            use = (other < me) if side == 0 else (other > me)
            slot = jnp.maximum((me ^ other) - 1, 0)
            got = recv[slot]
            new_re, new_im = got[0:1, :], got[1:2, :]
            if sz.chunks > 2:
                passes = through(sz, meta, other * sz.toks, sz.toks)[side]
                gain = jnp.where(passes, 1.0, 0.0).astype(F32)
                moved = cmul(jump[0] * gain, jump[1] * gain, re, im)
                new_re, new_im = new_re + moved[0], new_im + moved[1]
            re, im = jnp.where(use, new_re, re), jnp.where(use, new_im, im)
        sides.append((re, im))
    return sides


def load_enter(sz, enter):
    held = []
    for q in range(sz.states // LANES):
        cols = slice(q * LANES, (q + 1) * LANES)
        for side in range(2):
            held.append((enter[2 * side, :, cols], enter[2 * side + 1, :, cols]))
    return tuple(held)


def chain_states(sz, decay, ahead, behind, source, enter, states):
    nq = sz.states // LANES
    n = sz.states
    d = spread(column_blocks(sz, decay))

    def body(step, held):
        up, down = rows_of(step), rows_of(sz.steps - 1 - step)
        on_up, on_down = ahead[up, :], behind[down, :]
        new = []
        for q in range(nq):
            for side, (rows, on) in enumerate(((up, on_up), (down, on_down))):
                re, im = held[2 * q + side]
                re, im = cmul(*d[q], re * on, im * on)
                lo = q * LANES
                re += source[rows, lo : lo + LANES]
                im += source[rows, n + lo : n + lo + LANES]
                at = 2 * side * n + lo
                states[rows, at : at + LANES] = re.astype(BF)
                states[rows, at + n : at + n + LANES] = (-im).astype(BF)
                new.append((re, im))
        return tuple(new)

    lax.fori_loop(0, sz.steps, body, load_enter(sz, enter), unroll=4)


def adjoint_chains(sz, decay, ahead, behind, source, enter, states, half, grad_driven, grad_decay):
    nq = sz.states // LANES
    n = sz.states
    d = spread(column_blocks(sz, decay))
    zero = jnp.zeros((SEGS, LANES), F32)

    def make(second):
        def body(step, carry):
            held, sums = carry
            up, down = rows_of(step), rows_of(sz.steps - 1 - step)
            on_up, on_down = ahead[up, :], behind[down, :]
            new, total = [], []
            for q in range(nq):
                lo = q * LANES
                acc_re, acc_im = sums[q]
                for side, (rows, on, src, st) in enumerate(((up, on_up, 2 * n, 2 * n), (down, on_down, 0, 0))):
                    re, im = held[2 * q + side]
                    re, im = re * on, im * on
                    s_re = states[rows, st + lo : st + lo + LANES].astype(F32)
                    s_im = states[rows, st + n + lo : st + n + lo + LANES].astype(F32)
                    acc_re += re * s_re + im * s_im
                    acc_im += re * s_im - im * s_re
                    re, im = cmul(*d[q], re, im)
                    re += source[rows, src + lo : src + lo + LANES]
                    im += source[rows, src + n + lo : src + n + lo + LANES]
                    new.append((re, im))
                    if second:
                        out_re = re + half[rows, lo : lo + LANES]
                        out_im = im + half[rows, n + lo : n + lo + LANES]
                        grad_driven[rows, lo : lo + LANES] = out_re.astype(BF)
                        grad_driven[rows, n + lo : n + lo + LANES] = (-out_im).astype(BF)
                    else:
                        half[rows, lo : lo + LANES] = re
                        half[rows, n + lo : n + lo + LANES] = im
                total.append((acc_re, acc_im))
            return tuple(new), tuple(total)

        return body

    carry = (load_enter(sz, enter), tuple((zero, zero) for _ in range(nq)))
    carry = lax.fori_loop(0, sz.steps // 2, make(False), carry, unroll=2)
    carry = lax.fori_loop(sz.steps // 2, sz.steps, make(True), carry, unroll=2)
    for q in range(nq):
        cols = slice(q * LANES, (q + 1) * LANES)
        grad_decay[0:1, cols] = jnp.sum(carry[1][q][0], axis=0, keepdims=True)
        grad_decay[1:2, cols] = jnp.sum(carry[1][q][1], axis=0, keepdims=True)


ROWS = 512


def row_parts(sz):
    size = min(ROWS, sz.toks)
    return [slice(lo, lo + size) for lo in range(0, sz.toks, size)]


def matmul_nt(a, b, out, tile=256):
    for lo in range(0, b.shape[0], tile):
        out[:, lo : lo + tile] = nt(a[...], b[lo : lo + tile, :]).astype(out.dtype)


def matmul_tn(a, b, out, tile=256):
    for lo in range(0, a.shape[1], tile):
        out[lo : lo + tile, :] = tn(a[:, lo : lo + tile], b[...]).astype(out.dtype)


def column_sum(x):
    return jnp.sum(x.reshape(x.shape[0] // 8, 8, x.shape[1]), axis=0)


def scale_of(u):
    return lax.rsqrt(jnp.mean(u * u, axis=1, keepdims=True) + EPSILON)


def normed_rows(sz, u, gain, on):
    return (u * scale_of(u) * gain * on).astype(BF)


def finish_rows(sz, rows, states, w_out, skip, normed, on, slope):
    pre = 2.0 * nn(states[rows, :], w_out[...]) + skip * normed[rows, :].astype(F32)
    square = pre * pre
    th = jnp.tanh(pre * (GELU_C + (GELU_C * GELU_A) * square))
    part = 0.5 + 0.5 * th
    deriv = part + pre * (1.0 - th * th) * (0.5 * GELU_C + (1.5 * GELU_C * GELU_A) * square)
    slope[rows, :] = (on * deriv).astype(slope.dtype)
    return on * (pre * part)


def enter_chunk(sz, meta, recv, decay, ends, enter):
    enter_states(sz, meta, decay, ends, received(sz, meta, decay, recv), enter)


def back_rows(sz, rows, grad_driven, w_in, upstream, slope, skip, hidden, gain):
    u = hidden[rows, :].astype(F32)
    r = upstream[rows, :]
    gn = nn(grad_driven[rows, :], w_in[...]) + r * slope[rows, :].astype(F32) * skip
    scale = scale_of(u)
    moved = u * scale
    dn = gn * gain
    inner = jnp.sum(dn * moved, axis=1, keepdims=True) * (1.0 / sz.width)
    return r + scale * (dn - moved * inner), column_sum(gn * moved)


def open_rows(sz, rows, r, slope, normed, w_out, twice, grad_states):
    e = r * slope[rows, :].astype(F32)
    low = e.astype(BF)
    double = low + low
    twice[rows, :] = double
    grad_states[rows, :] = nt(double, w_out[...])
    return column_sum(e * normed[rows, :].astype(F32))


def gain_of(params, layer):
    return params[layer : layer + 1, :]


def skip_of(params, layer):
    return params[2 + layer : 3 + layer, :]


def decay_of(sz, params, layer):
    return params[4 + 2 * layer : 6 + 2 * layer, 0 : sz.states]


def place_pieces(sz, meta, pieces, stacked):
    part = sz.width // sz.blocks
    for dist, piece in enumerate(pieces):
        owner = meta[4] ^ turned(sz, dist)
        stacked[pl.ds(pl.multiple_of(owner * part, part), part), :] = piece[0:part, :]


def cut_pieces(sz, meta, rows, perm, stacked, pieces):
    part = sz.width // sz.blocks
    matmul_tn(rows, perm, stacked)
    for dist, piece in enumerate(pieces):
        owner = meta[4] ^ turned(sz, dist)
        piece[...] = stacked[pl.ds(pl.multiple_of(owner * part, part), part), :]


def cut_kernel(sz, meta, whole, *refs):
    outs, wide, sems = refs[: sz.blocks], refs[-2], refs[-1]
    straight = whole.dtype == BF
    copies = []
    for dist in range(sz.blocks):
        to = meta[0] ^ turned(sz, dist)
        cols = pl.ds(pl.multiple_of(lax.rem(to, sz.chunks) * sz.toks, LANES), sz.toks)
        source = whole.at[lax.div(to, sz.chunks), :, cols]
        copy = pltpu.make_async_copy(source, outs[dist] if straight else wide.at[dist], sems.at[dist])
        copy.start()
        copies.append(copy)
    for dist, copy in enumerate(copies):
        copy.wait()
        if not straight:
            outs[dist][...] = wide[dist].astype(BF)


def discretize(lambda_log, lambda_imag, log_step):
    step_size = jnp.exp(log_step)
    lambda_real = -jnp.exp(lambda_log)
    modulus = jnp.exp(lambda_real * step_size)
    decay_real = modulus * jnp.cos(lambda_imag * step_size)
    decay_imag = modulus * jnp.sin(lambda_imag * step_size)
    denominator = lambda_real * lambda_real + lambda_imag * lambda_imag
    scale_real = ((decay_real - 1.0) * lambda_real + decay_imag * lambda_imag) / denominator
    scale_imag = (decay_imag * lambda_real - (decay_real - 1.0) * lambda_imag) / denominator
    return decay_real, decay_imag, scale_real, scale_imag


def first_rows(sz):
    part, own = sz.width // sz.blocks, sz.states // sz.blocks
    return part, part + own * sz.width // sz.toks


def half_map_parts(sz):
    top, end = first_rows(sz)
    rows = end - top
    for index in range(sz.toks // sz.width):
        yield slice(index * rows, (index + 1) * rows), slice(top, end), slice(index * sz.width, (index + 1) * sz.width)


def split3(x):
    hi = x.astype(BF).astype(F32)
    mid = (x - hi).astype(BF).astype(F32)
    return hi, mid, x - hi - mid


def prepare_kernel(sz, meta, tokens, *refs):
    inputs, refs = refs[:7], refs[7:]
    outs, refs = refs[: sz.blocks], refs[sz.blocks :]
    drive_b, half_b = refs[:2]
    held, small, lines, drive_a, sems = refs[2:9], refs[9], refs[10], refs[11], refs[12]
    top, end = first_rows(sz)
    own, part = sz.states // sz.blocks, sz.width // sz.blocks
    loads, copies = [], []
    for index, (source, target) in enumerate(zip(inputs, held)):
        loads.append(pltpu.make_async_copy(source, target, sems.at[index]))
    for dist in range(sz.blocks):
        to = meta[0] ^ turned(sz, dist)
        cols = pl.ds(pl.multiple_of(lax.rem(to, sz.chunks) * sz.toks, LANES), sz.toks)
        source = tokens.at[lax.div(to, sz.chunks), :, cols]
        copies.append(pltpu.make_async_copy(source, outs[dist].at[0:top, :], sems.at[len(inputs) + dist]))
    for copy in copies + loads:
        copy.start()
    for copy in loads[:6]:
        copy.wait()
    gain, skip, lambda_log, lambda_imag, log_step, input_map, output_map = held
    dr, di, sr, si = discretize(lambda_log[...], lambda_imag[...], log_step[...])
    small[...] = jnp.zeros_like(small)
    lines[...] = jnp.zeros_like(lines)
    small[0:2, 0:part] = gain[...]
    small[2:4, 0:part] = skip[...]
    for layer in range(2):
        small[4 + 2 * layer : 5 + 2 * layer, 0:own] = dr[layer : layer + 1]
        small[5 + 2 * layer : 6 + 2 * layer, 0:own] = di[layer : layer + 1]
    lines[0:2, 0:own] = sr
    lines[2:4, 0:own] = si
    cols = lines[...].T
    for layer in range(2):
        qr, qi = cols[0:own, layer : layer + 1], cols[0:own, 2 + layer : 3 + layer]
        br, bi = input_map[layer, 0].astype(F32), input_map[layer, 1].astype(F32)
        for index, value in enumerate((qr * br - qi * bi, qr * bi + qi * br)):
            (drive_a, drive_b)[layer][index] = value.astype(BF)
    rows = jnp.concatenate([*split3(small[...]), jnp.zeros((8, sz.toks - 3 * LANES), F32)], axis=1)
    rows = jnp.concatenate([rows, jnp.zeros((8, sz.toks), F32)], axis=0).astype(BF)
    for dist, out in enumerate(outs):
        half = lax.rem(meta[0] ^ turned(sz, dist), 2)
        for from_rows, to_rows, lanes in half_map_parts(sz):
            out[to_rows, lanes] = drive_a[half, from_rows, :]
        out[end:, :] = rows
    loads[6].wait()
    core = meta[2]
    for index in range(2):
        half_b[index] = output_map[0, 2 * core + index]
        half_b[3 + index] = output_map[1, 2 * core + index]
    half_b[2] = drive_b[core]
    for copy in copies:
        copy.wait()


def params_of(sz, piece):
    rows = piece[piece.shape[0] - 16 :, 0 : 3 * LANES].astype(F32)[0:8]
    return rows[:, 0:LANES] + rows[:, LANES : 2 * LANES] + rows[:, 2 * LANES :]


def join_kernel(sz, meta, *refs):
    pieces, maps, params = refs[: sz.blocks], refs[-2], refs[-1]
    own = sz.states // sz.blocks
    collect_params(sz, meta, [params_of(sz, piece) for piece in pieces], params)
    for dist, piece in enumerate(pieces):
        base = (meta[4] ^ turned(sz, dist)) * own
        for to_rows, from_rows, lanes in half_map_parts(sz):
            rows = pl.ds(pl.multiple_of(base + to_rows.start, 16), to_rows.stop - to_rows.start)
            maps[rows, :] = piece[from_rows, lanes]


def collect_params(sz, meta, smalls, params):
    own = sz.states // sz.blocks
    part = sz.width // sz.blocks
    lane = lax.broadcasted_iota(jnp.int32, (8, LANES), 1)
    row = lax.broadcasted_iota(jnp.int32, (8, LANES), 0)
    pad = jnp.zeros((8, sz.width - LANES), F32)
    total = jnp.zeros((8, sz.width), F32)
    for block in range(sz.blocks):
        piece = smalls[0]
        for dist in range(1, sz.blocks):
            piece = jnp.where((meta[4] ^ turned(sz, dist)) == block, smalls[dist], piece)
        for first, count, size in ((0, 4, part), (4, 4, own)):
            mine = jnp.where((row >= first) & (row < first + count) & (lane < size), piece, 0.0)
            wide = jnp.concatenate([mine, pad], axis=1)
            total += pltpu.roll(wide, block * size, 1) if block else wide
    params[...] = total


def place_maps(sz, meta, own_maps, mine, other, skip, out):
    own = sz.states // sz.blocks
    count = own_maps.shape[0] // 2

    def put(index, owner, value):
        out[pl.ds(pl.multiple_of(index * sz.states + owner * own, own), own), :] = value

    for index in range(2 * count):
        put(index, meta[0], own_maps[index])
    for side, pieces in ((meta[2], mine), (1 - meta[2], other)):
        for dist, piece in enumerate(pieces):
            for index in range(count):
                put(side * count + index, meta[0] ^ (dist + 1), piece[skip + index])


def open_kernel(sz, meta, perm, params, *refs):
    pieces, (hidden, normed, live, ahead, behind, stacked) = refs[: sz.blocks], refs[sz.blocks :]
    fill_masks(sz, meta, live, ahead, behind)
    place_pieces(sz, meta, pieces, stacked)
    gain = gain_of(params, 0)
    for rows in row_parts(sz):
        u = nt(perm[rows, :], stacked[...])
        hidden[rows, :] = u.astype(BF)
        normed[rows, :] = normed_rows(sz, u, gain, widen(live[rows, :], sz.width // LANES))


def enter_kernel(sz, meta, ahead, behind, params, normed, maps, other, w_in, driven, ends, send, enter):
    decay = decay_of(sz, params, 0)
    for side, half in ((meta[2], maps), (1 - meta[2], other)):
        w_in[pl.ds(pl.multiple_of(side * sz.states, sz.states), sz.states), :] = half[...]
    matmul_nt(normed, w_in, driven)
    chain_ends(sz, decay, ahead, behind, driven, 0, 0, ends)
    send_ends(sz, meta, decay, ends, enter, send)


def middle_kernel(sz, meta, live, ahead, behind, recv, params, ends, driven, normed, hidden, own_out, own_in, *refs):
    decay, skip, gain_b, decay_b = decay_of(sz, params, 0), skip_of(params, 0), gain_of(params, 1), decay_of(sz, params, 1)
    far = sz.blocks - 1
    mine, other, refs = refs[:far], refs[far : 2 * far], refs[2 * far :]
    w_out, w_in_b, states, slope, hidden_b, normed_b, driven_b, ends_b, send_b, enter = refs
    place_maps(sz, meta, own_out, mine, other, 0, w_out)
    place_maps(sz, meta, own_in, mine, other, 2, w_in_b)
    enter_chunk(sz, meta, recv, decay, ends, enter)
    chain_states(sz, decay, ahead, behind, driven, enter, states)
    for rows in row_parts(sz):
        on = widen(live[rows, :], sz.width // LANES)
        u = hidden[rows, :].astype(F32) + finish_rows(sz, rows, states, w_out, skip, normed, on, slope)
        hidden_b[rows, :] = u
        v = normed_rows(sz, u, gain_b, on)
        normed_b[rows, :] = v
        driven_b[rows, :] = nt(v, w_in_b[...])
    chain_ends(sz, decay_b, ahead, behind, driven_b, 0, 0, ends_b)
    send_ends(sz, meta, decay_b, ends_b, enter, send_b)


def leave_kernel(sz, meta, live, ahead, behind, recv, params, ends, driven, normed, hidden, perm, own_out, *refs):
    decay, skip = decay_of(sz, params, 1), skip_of(params, 1)
    far = sz.blocks - 1
    mine, other, refs = refs[:far], refs[far : 2 * far], refs[2 * far :]
    w_out, states, slope, refs = *refs[:3], refs[3:]
    place_maps(sz, meta, own_out, mine, other, 3, w_out)
    pieces, (enter, last, stacked) = refs[: sz.blocks], refs[sz.blocks :]
    enter_chunk(sz, meta, recv, decay, ends, enter)
    chain_states(sz, decay, ahead, behind, driven, enter, states)
    for rows in row_parts(sz):
        on = widen(live[rows, :], sz.width // LANES)
        last[rows, :] = (hidden[rows, :] + finish_rows(sz, rows, states, w_out, skip, normed, on, slope)).astype(BF)
    cut_pieces(sz, meta, last, perm, stacked, pieces)


def turn_kernel(sz, meta, ahead, behind, slope, normed, w_out, params, perm, *refs):
    decay = decay_of(sz, params, 1)
    pieces, refs = refs[: sz.blocks], refs[sz.blocks :]
    upstream, twice, grad_states, grad_skip, ends, send, stacked, enter = refs
    place_pieces(sz, meta, pieces, stacked)
    skips = []
    for rows in row_parts(sz):
        r = nt(perm[rows, :], stacked[...])
        upstream[rows, :] = r
        skips.append(open_rows(sz, rows, r, slope, normed, w_out, twice, grad_states))
    grad_skip[...] = jnp.sum(sum(skips), axis=0, keepdims=True)
    chain_ends(sz, decay, ahead, behind, grad_states, 2 * sz.states, 0, ends)
    send_ends(sz, meta, decay, ends, enter, send)


def back_middle_kernel(sz, meta, ahead, behind, recv, params, ends, grad_states, states, upstream, slope, hidden, w_in,
                       slope_b, normed_b, w_out_b,
                       grad_driven, grad_decay, grad_gain, upstream_b, twice_b, grad_states_b, grad_skip_b, ends_b, send_b,
                       enter, half):
    decay, skip, gain, decay_b = decay_of(sz, params, 1), skip_of(params, 1), gain_of(params, 1), decay_of(sz, params, 0)
    enter_chunk(sz, meta, recv, decay, ends, enter)
    adjoint_chains(sz, decay, ahead, behind, grad_states, enter, states, half, grad_driven, grad_decay)
    gains, skips = [], []
    for rows in row_parts(sz):
        r, terms = back_rows(sz, rows, grad_driven, w_in, upstream, slope, skip, hidden, gain)
        gains.append(terms)
        upstream_b[rows, :] = r
        skips.append(open_rows(sz, rows, r, slope_b, normed_b, w_out_b, twice_b, grad_states_b))
    grad_gain[...] = jnp.sum(sum(gains), axis=0, keepdims=True)
    grad_skip_b[...] = jnp.sum(sum(skips), axis=0, keepdims=True)
    chain_ends(sz, decay_b, ahead, behind, grad_states_b, 2 * sz.states, 0, ends_b)
    send_ends(sz, meta, decay_b, ends_b, enter, send_b)


def back_chain_kernel(sz, meta, ahead, behind, recv, params, ends, grad_states, states, grad_driven, grad_decay, enter, half):
    decay = decay_of(sz, params, 0)
    enter_chunk(sz, meta, recv, decay, ends, enter)
    adjoint_chains(sz, decay, ahead, behind, grad_states, enter, states, half, grad_driven, grad_decay)


def back_leave_kernel(sz, meta, params, grad_driven, upstream, slope, hidden, w_in, perm, *refs):
    done, refs = refs[: sz.blocks], refs[sz.blocks :]
    skip, gain = skip_of(params, 0), gain_of(params, 0)
    pieces, (last, stacked) = refs[: sz.blocks], refs[sz.blocks :]
    for rows in row_parts(sz):
        r, _ = back_rows(sz, rows, grad_driven, w_in, upstream, slope, skip, hidden, gain)
        last[rows, :] = r.astype(BF)
    part = sz.width // sz.blocks
    for piece, first in zip(pieces, done):
        piece[0:part, :] = first[...]
    cut_pieces(sz, meta, last, perm, stacked, [piece.at[part : 2 * part, :] for piece in pieces])


def weight_kernel(counts, other, sz, meta, *refs):
    half = 1 - meta[2] if other else meta[2]
    pairs = 2 * len(counts)
    out, at = refs[pairs], 0
    if len(refs) > pairs + 1:
        whole, out, terms = refs[pairs:]
        value = tn(refs[0][:, pl.ds(pl.multiple_of(half * sz.states, LANES), sz.states)], refs[1][...])
        out[...] = value.astype(out.dtype)
        rows = whole[pl.ds(pl.multiple_of(half * sz.states, sz.states), sz.states), :].astype(F32)
        terms[...] = jnp.sum(column_sum(rows * value), axis=0, keepdims=True)
        return
    for index, count in enumerate(counts):
        left, right = refs[2 * index], refs[2 * index + 1]
        for group in range(count):
            cols = pl.ds(pl.multiple_of((half * count + group) * sz.states, LANES), sz.states)
            out[at : at + sz.states, :] = tn(left[:, cols], right[...]).astype(out.dtype)
            at += sz.states


def split2(x):
    hi = x.astype(BF).astype(F32)
    return hi, x - hi


class Group(NamedTuple):
    first: int
    counts: tuple
    tiny: bool

    def rows(self, sz):
        return sum(self.counts) * (sz.states // sz.blocks) + (16 if self.tiny else 0)


def bits_of(sz):
    return sz.blocks.bit_length() - 1


def step_bit(sz, step, core):
    return 1 << ((step + core) % bits_of(sz))


def far_block(sz, group, slot, core):
    return sum(step_bit(sz, group.first + j, core) for j in range(bits_of(sz)) if (slot >> j) & 1)


def own_tiny(sz, params, terms, more, gain_b, skip_a, skip_b, decay_a, decay_b, tiny):
    gain_a = (terms[...] + more[...] + skip_of(params, 0) * skip_a[...]) / gain_of(params, 0)
    tiny[...] = jnp.zeros_like(tiny)
    for index, line in enumerate((gain_a, gain_b[...], skip_a[...], skip_b[...])):
        tiny[index : index + 1, :] = line
    tiny[4:6, 0 : sz.states] = decay_a[...]
    tiny[6:8, 0 : sz.states] = decay_b[...]
    return tiny[...]


def tiny_of(sz, tiny, owner):
    own, part = sz.states // sz.blocks, sz.width // sz.blocks
    row = lax.broadcasted_iota(jnp.int32, (8, LANES), 0)
    lane = lax.broadcasted_iota(jnp.int32, (8, LANES), 1)
    value = jnp.zeros((8, LANES), F32)
    for block in range(sz.blocks):
        wide = pltpu.roll(tiny, sz.width - block * part, 1) if block else tiny
        deep = pltpu.roll(tiny, sz.width - block * own, 1) if block else tiny
        mine = jnp.where(row < 4, jnp.where(lane < part, wide[:, :LANES], 0.0), jnp.where(lane < own, deep[:, :LANES], 0.0))
        value = jnp.where(owner == block, mine, value)
    return value


def put_sums(sz, group, value, tiny, slot, kept, message, at):
    rows = value.shape[0]
    if slot % 2 == 0:
        kept[slot // 2, 0:rows, :] = value
        if group.tiny:
            kept[slot // 2, rows : rows + 8, 0:LANES] = tiny
        return at
    message[at : at + rows, :] = value.astype(BF)
    if group.tiny:
        rest = jnp.zeros((8, sz.width - 2 * LANES), F32)
        wide = jnp.concatenate([*split2(tiny), rest], axis=1)
        message[at + rows : at + rows + 16, :] = jnp.concatenate([wide, jnp.zeros_like(wide)], axis=0).astype(BF)
    return at + group.rows(sz)


def add_message(sz, group, kept, slot, message, at):
    rows = group.rows(sz) - (16 if group.tiny else 0)
    value = kept[slot, 0:rows, :] + message[at : at + rows, :].astype(F32)
    if not group.tiny:
        return value, None
    got = message[at + rows : at + rows + 16, 0 : 2 * LANES].astype(F32)[0:8]
    return value, kept[slot, rows : rows + 8, 0:LANES] + got[:, 0:LANES] + got[:, LANES:]


def step_kernel(old, new, sz, meta, *refs):
    came, refs = (refs[0], refs[1:]) if old else (None, refs)
    held, refs = refs[: len(old)], refs[len(old) :]
    if new:
        halves, refs = refs[: 2 * len(new.counts)], refs[2 * len(new.counts) :]
        if new.tiny:
            lines, refs, room = refs[:8], refs[8:-1], refs[-1]
    keeps, message = refs[:-1], refs[-1]
    at = 0
    for (group, slots, row), kept, keep in zip(old, held, keeps):
        for slot in range(slots):
            value, tiny = add_message(sz, group, kept, slot, came, row + slot * group.rows(sz))
            at = put_sums(sz, group, value, tiny, slot, keep, message, at)
    if new:
        own = sz.states // sz.blocks
        whole = own_tiny(sz, *lines, room) if new.tiny else None
        for slot in range(sz.blocks):
            owner = meta[0] ^ jnp.where(meta[2] == 0, far_block(sz, new, slot, 0), far_block(sz, new, slot, 1))
            parts = []
            for index, count in enumerate(new.counts):
                keep, got = halves[2 * index], halves[2 * index + 1]
                for one in range(count):
                    rows = pl.ds(pl.multiple_of(one * sz.states + owner * own, own), own)
                    parts.append(keep[rows, :].astype(F32) + got[rows, :].astype(F32))
            tiny = tiny_of(sz, whole, owner) if new.tiny else None
            at = put_sums(sz, new, jnp.concatenate(parts, axis=0), tiny, slot, keeps[-1], message, at)


def fold_block_kernel(planes, groups, sz, meta, *refs):
    lanes = sz.width // LANES
    held, refs = refs[: 2 * len(groups)], refs[2 * len(groups) :]
    outs, talls = refs[:planes], refs[planes:]
    at = 0
    for index, (group, row) in enumerate(groups):
        total, tiny = add_message(sz, group, held[2 * index], 0, held[2 * index + 1], row)
        rows = total.shape[0]
        tall = talls[index]
        padded = tall.shape[0] // lanes
        for block in range(lanes):
            tall[block * padded : block * padded + rows, :] = total[:, block * LANES : (block + 1) * LANES].astype(BF)
            if padded > rows:
                tall[block * padded + rows : (block + 1) * padded, :] = jnp.zeros((padded - rows, LANES), BF)
        part = tall.shape[0] // planes
        for dist, out in enumerate(outs):
            out[at : at + part, :] = tall[pl.ds(pl.multiple_of((meta[3] ^ farthest(dist, planes)) * part, part), part), :]
        at += part
    if tiny is not None:
        rows = jnp.concatenate(split2(tiny), axis=0).astype(BF)
        for out in outs:
            out[at : at + 16, :] = rows


def fold_plane_kernel(early, sz, meta, *refs):
    parts, out, tiny = refs[early:-2], refs[-2], refs[-1]
    total = refs[0][...].astype(F32)
    for piece in refs[1:early]:
        total += piece[...].astype(F32)
    top = total.shape[0]
    out[0:top, :] = total.astype(BF)
    total = parts[0][...].astype(F32)
    for piece in parts[1:]:
        total += piece[...].astype(F32)
    rows = total.shape[0] - 16
    out[top:, :] = total[0:rows].astype(BF)
    tiny[...] = total[rows : rows + 8] + total[rows + 8 :]


def finish_kernel(planes, groups, sz, meta, *refs):
    count = 2 * planes
    pieces, refs = refs[:count], refs[count:]
    tiny, lambda_log, lambda_imag, log_step, input_map = refs[0][...] + refs[1][...], *refs[2:6]
    grad_gain, grad_skip, grad_log, grad_imag, grad_step, grad_maps, grad_out = refs[6:13]
    talls, grad_in, lines = refs[13:-2], refs[-2], refs[-1]
    own = sz.states // sz.blocks
    lanes = sz.width // LANES
    start = 0
    for tall, group in zip(talls, groups):
        padded = tall.shape[0] // lanes
        part = tall.shape[0] // planes
        for side in range(2):
            half = meta[2] ^ side
            for dist in range(planes):
                rows = pl.ds(pl.multiple_of((meta[3] ^ farthest(dist, planes)) * part, part), part)
                tall[rows, :] = pieces[side * planes + dist][start : start + part, :]
            at = 0
            for which, layer, maps in group:
                out = grad_in if which == 0 else grad_out
                for one in range(maps):
                    for block in range(lanes):
                        rows = slice(block * padded + at, block * padded + at + own)
                        out[layer, half * maps + one, :, block * LANES : (block + 1) * LANES] = tall[rows, :].astype(F32)
                    at += own
        start += part
    width = sz.width // sz.blocks
    grad_gain[...] = tiny[0:2, 0:width]
    grad_skip[...] = tiny[2:4, 0:width]
    dr, di, sr, si = discretize(lambda_log[...], lambda_imag[...], log_step[...])
    lines[...] = jnp.zeros_like(lines)
    lines[0:2, 0:own] = sr
    lines[2:4, 0:own] = si
    cols = lines[...].T
    back = []
    for layer in range(2):
        qr, qi = cols[0:own, layer : layer + 1], cols[0:own, 2 + layer : 3 + layer]
        wr, wi = grad_in[layer, 0], grad_in[layer, 1]
        br, bi = input_map[layer, 0].astype(F32), input_map[layer, 1].astype(F32)
        grad_maps[layer, 0] = qr * wr + qi * wi
        grad_maps[layer, 1] = qr * wi - qi * wr
        back.append(jnp.sum(wr * br + wi * bi, axis=1, keepdims=True))
        back.append(jnp.sum(wi * br - wr * bi, axis=1, keepdims=True))
    lines[...] = jnp.zeros_like(lines)
    for index, col in enumerate(back):
        lines[0:own, index : index + 1] = col
    rows = lines[...].T
    step = jnp.exp(log_step[...])
    lr, li = -jnp.exp(lambda_log[...]), lambda_imag[...]
    norm = 1.0 / (lr * lr + li * li)
    for layer in range(2):
        at = slice(layer, layer + 1)
        a, b, h = (lr[at], li[at]), (dr[at], di[at]), step[at]
        gq = rows[2 * layer : 2 * layer + 1, 0:own], rows[2 * layer + 1 : 2 * layer + 2, 0:own]
        gd = tiny[4 + 2 * layer : 5 + 2 * layer, 0:own], tiny[5 + 2 * layer : 6 + 2 * layer, 0:own]
        inverse = a[0] * norm[at], -a[1] * norm[at]
        through = cmul(inverse[0], -inverse[1], *gq)
        gd = gd[0] + through[0], gd[1] + through[1]
        ratio = cmul(*inverse, sr[at], si[at])
        direct = cmul(ratio[0], -ratio[1], *gq)
        moved = cmul(b[0] * h, -b[1] * h, *gd)
        turn = cmul(*a, *b)
        grad_log[at, :] = (moved[0] - direct[0]) * a[0]
        grad_imag[at, :] = moved[1] - direct[1]
        grad_step[at, :] = (turn[0] * gd[0] + turn[1] * gd[1]) * h


def spread_kernel(sz, meta, *refs):
    pieces, outs, wide, sems = refs[: sz.blocks], refs[sz.blocks : -2], refs[-2], refs[-1]
    part = sz.width // sz.blocks
    copies = []
    for dist, piece in enumerate(pieces):
        owner = meta[0] ^ turned(sz, dist)
        for index, out in enumerate(outs):
            slot = dist * len(outs) + index
            wide[slot] = piece[index * part : (index + 1) * part, :].astype(F32)
            cols = pl.ds(pl.multiple_of(lax.rem(owner, sz.chunks) * sz.toks, LANES), sz.toks)
            copy = pltpu.make_async_copy(wide.at[slot], out.at[lax.div(owner, sz.chunks), :, cols], sems.at[slot])
            copy.start()
            copies.append(copy)
    for copy in copies:
        copy.wait()


VMEM = pl.BlockSpec(memory_space=pltpu.VMEM)
SMEM = pl.BlockSpec(memory_space=pltpu.SMEM)
HBM = pl.BlockSpec(memory_space=pltpu.HBM)


def call(name, sz, body, items, args, outs, scratch, limit=10, in_spec=VMEM, out_spec=VMEM, time=0.0):
    out_shape = [jax.ShapeDtypeStruct(shape, dtype) for shape, dtype in outs]

    def kernel(*refs):
        body(sz, place_of(sz, refs[0] if items else None), *refs[len(items) :])

    return pl.pallas_call(
        kernel,
        out_shape=out_shape,
        in_specs=[SMEM] * len(items) + [in_spec] * len(args),
        out_specs=[out_spec] * len(outs),
        scratch_shapes=[pltpu.VMEM(*item) if isinstance(item, tuple) else item for item in scratch],
        compiler_params=pltpu.CompilerParams(vmem_limit_bytes=limit << 20),
        cost_estimate=pl.CostEstimate(flops=int(COST * time), bytes_accessed=1000, transcendentals=0),
        name=name,
    )(*items, *args)


def on_device(tokens, cotangent, item_lengths, item_offsets, norm_gain, lambda_log, lambda_imag, log_step, input_map, output_map, skip_weight):
    micro, part, run = tokens.shape
    layers = norm_gain.shape[0]
    blocks = lax.axis_size("block")
    planes = lax.axis_size("plane")
    chunks = blocks // micro
    toks = run // chunks
    own = lambda_log.shape[1]
    width, states = part * blocks, own * blocks
    sz = Sizes(blocks, chunks, toks, run, toks // SEGS, width, states, item_lengths.shape[1])

    def swap(x, dist, axis="block"):
        return lax.ppermute(x, axis, [(i, i ^ dist) for i in range(lax.axis_size(axis))])

    def across(x, dist, back):
        pairs = []
        for c in range(2):
            for b in range(blocks):
                q = b ^ turned(sz, dist)
                pairs.append((c * blocks + b, (q % 2) * blocks + (q // 2) * 2 + c))
        return lax.ppermute(x, ("core", "block"), [pair[::-1] for pair in pairs] if back else pairs)

    def across_all(pieces, back=False):
        return [across(piece, dist, back) for dist, piece in enumerate(pieces)]

    table = jnp.stack([item_lengths, item_offsets])
    items = [jnp.stack([table, swap(table, 1, "core")])]

    def neighbour(x, dist):
        pairs = []
        for c in range(2):
            for b in range(blocks):
                q = ((b // 2) * 2 + c) ^ dist
                pairs.append((c * blocks + b, (q % 2) * blocks + (q // 2) * 2 + b % 2))
        return lax.ppermute(x, ("core", "block"), pairs)

    def swap_all(pieces, axis="block"):
        count = len(pieces)
        return [swap(piece, farthest(index, count), axis) if index else piece for index, piece in enumerate(pieces)]

    def exchange(send):
        return jnp.stack([neighbour(send[dist - 1], dist) for dist in range(1, chunks)])

    row = jnp.arange(toks, dtype=jnp.int32)[:, None]
    col = jnp.arange(toks, dtype=jnp.int32)[None, :]
    perm = ((row % SEGS) * sz.steps + row // SEGS == col).astype(BF)

    maps_own = ((2, own, width), BF)
    half_own = ((5, own, width), BF)
    given = [norm_gain, skip_weight, lambda_log, lambda_imag, log_step, input_map, output_map]
    *first_pieces, drive_b, half_b = call(
        "prepare", sz, prepare_kernel, [], [pltpu.with_memory_space_constraint(x, pltpu.HBM) for x in [tokens, *given]],
        [((first_rows(sz)[1] + 16, toks), BF)] * blocks + [maps_own, half_own],
        [(x.shape, x.dtype) for x in given] + [((8, LANES), F32), ((8, LANES), F32), maps_own, pltpu.SemaphoreType.DMA((len(given) + blocks,))],
        limit=6, in_spec=HBM)
    first_pieces = across_all(first_pieces)
    cot_cut = call("cut_cotangent", sz, cut_kernel, [], [pltpu.with_memory_space_constraint(cotangent, pltpu.HBM)],
                   [((part, toks), BF)] * blocks, [((blocks, part, toks), F32), pltpu.SemaphoreType.DMA((blocks,))], limit=4, in_spec=HBM)
    half_b, first_pieces[1], perm, cot_cut = after(half_b, first_pieces[1], perm, cot_cut)
    maps_a, params = call("join", sz, join_kernel, [], first_pieces, [((states, width), BF), ((8, width), F32)], [])
    second_mine = [swap(half_b, dist) for dist in range(1, blocks)]

    mask = ((toks, LANES), F32)
    enter = ((4, SEGS, states), F32)
    stacked = ((width, toks), BF)
    rows_f, rows_b = ((toks, width), F32), ((toks, width), BF)
    drv = ((toks, 2 * states), F32)
    sts = ((toks, 4 * states), BF)
    gst = ((toks, 4 * states), F32)
    snd = ((chunks - 1, 2, states), F32)
    w_in, w_out = ((2 * states, width), BF), ((4 * states, width), BF)
    line, gdec = ((1, width), F32), ((2, states), F32)
    piece_out = [((part, toks), BF)] * blocks

    other_a = swap(maps_a, 1, "core")
    hidden_a, normed_a, live, ahead, behind = call(
        "open", sz, open_kernel, items, [perm, params, *first_pieces], [rows_b, rows_b, mask, mask, mask], [stacked], time=3)
    w_in_a, driven_a, ends_a, send_a = call(
        "enter", sz, enter_kernel, items, [ahead, behind, params, normed_a, maps_a, other_a], [w_in, drv, enter, snd], [enter])
    recv = exchange(send_a)
    second_mine, recv = after(second_mine, recv)
    second_maps = second_mine, [swap(piece, 1, "core") for piece in second_mine]
    w_out_a, w_in_b, states_a, slope_a, hidden_b, normed_b, driven_b, ends_b, send_b = call(
        "middle", sz, middle_kernel, items,
        [live, ahead, behind, recv, params, ends_a, driven_a, normed_a, hidden_a, output_map[0], drive_b, *second_maps[0], *second_maps[1]],
        [w_out, w_in, sts, rows_b, rows_f, rows_b, drv, enter, snd], [enter], time=11)
    recv = exchange(send_b)
    cot_cut, _ = after(cot_cut, send_a)
    cot_pieces = across_all(cot_cut)
    recv, cot_pieces = after(recv, cot_pieces)
    w_out_b, states_b, slope_b, *out_pieces = call(
        "leave", sz, leave_kernel, items,
        [live, ahead, behind, recv, params, ends_b, driven_b, normed_b, hidden_b, perm, output_map[1], *second_maps[0], *second_maps[1]],
        [w_out, sts, rows_b, *piece_out], [enter, rows_b, stacked], time=8)

    def half_grads(name, other, pairs, counts, more=(), time=0.0):
        args = [x for pair in pairs for x in pair]
        outs = [((sum(counts) * states, width), BF)] + [line] * len(more)
        return call(name, sz, partial(weight_kernel, counts, other), [], [*args, *more], outs, [], time=time)

    groups = [Group(0, (2,), False), Group(1, (3,), False), Group(2, (1,), True)]
    steps = bits_of(sz)
    kept, came, place = {}, {}, {}

    def halve(step, halves=(), tiny=()):
        old, args = [], []
        for index, group in enumerate(groups):
            if 0 < step - group.first < steps:
                slots = 1 << (steps - (step - group.first))
                old.append((group, slots, place[step - 1, index]))
                args.append(kept[index])
        if old:
            args.insert(0, came[step - 1])
        new = groups[step] if step < len(groups) else None
        outs, at = [], 0
        for index, group in enumerate(groups):
            if 0 <= step - group.first < steps:
                slots = 1 << (steps - 1 - (step - group.first))
                outs.append((index, ((slots, group.rows(sz), width), F32)))
                place[step, index] = at
                at += slots * group.rows(sz)
        results = call("halve_%d" % step, sz, partial(step_kernel, old, new), [], [*args, *halves, *tiny],
                       [shape for _, shape in outs] + [((at, width), BF)], [((8, width), F32)] if tiny else [])
        for (index, _), value in zip(outs, results):
            kept[index] = value
        return results[-1]

    def send_step(step, message):
        pairs = [(c * blocks + b, c * blocks + (b ^ step_bit(sz, step, c))) for c in range(2) for b in range(blocks)]
        came[step] = lax.ppermute(message, ("core", "block"), pairs)

    def spread(pieces):
        return call("spread", sz, spread_kernel, [], pieces, [((micro, part, run), F32)] * 2,
                    [((2 * blocks, part, toks), F32), pltpu.SemaphoreType.DMA((2 * blocks,))], limit=6, out_spec=HBM)

    lanes = width // LANES

    def tall_of(rows):
        step = max(SEGS * planes // lanes, SEGS)
        return ((lanes * (-(-rows // step) * step), LANES), BF)

    def over_planes(name, which):
        ends = [(groups[index], place[groups[index].first + steps - 1, index]) for index in which]
        talls = [tall_of(sum(group.counts) * own) for group, _ in ends]
        cut = sum(t[0][0] for t in talls) // planes + (16 if ends[-1][0].tiny else 0)
        args = [x for index in which for x in (kept[index], came[groups[index].first + steps - 1])]
        return swap_all(call(name, sz, partial(fold_block_kernel, planes, ends), [], args, [((cut, LANES), BF)] * planes, talls), "plane")

    up_b, twice_b, gstates_b, gskip_b, ends, send = call(
        "turn", sz, turn_kernel, items, [ahead, behind, slope_b, normed_b, w_out_b, params, perm, *cot_pieces],
        [rows_f, rows_b, gst, line, enter, snd], [stacked, enter], time=6)
    recv = exchange(send)
    pairs = [(states_b, twice_b)]
    (send_maps,) = half_grads("grads_a_send", True, pairs, (2,))
    got = swap(send_maps, 1, "core")
    (keep,) = half_grads("grads_a_keep", False, pairs, (2,), time=2)
    message = halve(0, (keep, got))
    recv, message = after(recv, message)
    send_step(0, message)
    gdriven_b, gdecay_b, ggain_b, up_a, twice_a, gstates_a, gskip_a, ends, send = call(
        "back_middle", sz, back_middle_kernel, items,
        [ahead, behind, recv, params, ends, gstates_b, states_b, up_b, slope_b, hidden_b, w_in_b, slope_a, normed_a, w_out_a],
        [((toks, 2 * states), BF), gdec, line, rows_f, rows_b, gst, line, enter, snd], [enter, drv], limit=12, time=11)
    recv = exchange(send)
    gdriven_b, came[0] = after(gdriven_b, came[0])
    pairs = [(gdriven_b, normed_b), (states_a, twice_a)]
    (send_maps,) = half_grads("grads_b_send", True, pairs, (1, 2))
    got = swap(send_maps, 1, "core")
    (keep,) = half_grads("grads_b_keep", False, pairs, (1, 2), time=9)
    message = halve(1, (keep, got))
    recv, message = after(recv, message)
    send_step(1, message)
    gdriven_a, gdecay_a = call(
        "back_chain", sz, back_chain_kernel, items, [ahead, behind, recv, params, ends, gstates_a, states_a],
        [((toks, 2 * states), BF), gdec], [enter, drv], limit=12, time=9)
    send_maps, terms = half_grads("grads_c_send", True, [(gdriven_a, normed_a)], (1,), [w_in_a])
    gdriven_a, send_maps, came[1] = after(gdriven_a, send_maps, came[1])
    got = swap(send_maps, 1, "core")
    keep, more = half_grads("grads_c_keep", False, [(gdriven_a, normed_a)], (1,), [w_in_a], time=5)
    message = halve(2, (keep, got), (params, terms, more, ggain_b, gskip_a, gskip_b, gdecay_a, gdecay_b))
    early_sums = steps <= 2
    first_parts = over_planes("planes_a", [0]) if early_sums else []
    gdriven_a, message = after(gdriven_a, message)
    send_step(2, message)
    last_pieces = call(
        "back_leave", sz, back_leave_kernel, [], [params, gdriven_a, up_a, slope_a, hidden_a, w_in_a, perm, *out_pieces],
        [((2 * part, toks), BF)] * blocks, [rows_b, stacked], limit=12, time=9)
    last_pieces, came[2], first_parts = after(last_pieces, came[2], first_parts)
    if not early_sums:
        first_parts = over_planes("planes_a", [0])
    for step in range(3, steps + 2):
        send_step(step, halve(step))
    parts = over_planes("planes", [1, 2])
    last_pieces, parts[0] = after(last_pieces, parts[0])
    early = [across(piece, 2 * dist, True) for dist, piece in enumerate(last_pieces[0::2])]
    parts[0], early = after(parts[0], early)
    sum_all, tiny = call(
        "sum", sz, partial(fold_plane_kernel, planes), [], [*first_parts, *parts],
        [((first_parts[0].shape[0] + parts[0].shape[0] - 16, LANES), BF), ((8, LANES), F32)], [])
    whole = swap_all([sum_all] * planes, "plane")
    late, _ = after(last_pieces[1::2], sum_all)
    late = [across(piece, 2 * dist + 1, True) for dist, piece in enumerate(late)]
    output, input_grad = spread([piece for pair in zip(early, late) for piece in pair])
    whole, output = after(whole, output)
    whole += [swap(x, 1, "core") for x in whole]
    tiny_other = swap(tiny, 1, "core")
    small_out = ((layers, own), F32)
    grad_gain, grad_skip, grad_log, grad_imag, grad_step, grad_in, grad_out = call(
        "finish", sz, partial(finish_kernel, planes, ([(1, 1, 2)], [(0, 1, 1), (1, 0, 2)], [(0, 0, 1)])), [],
        [*whole, tiny, tiny_other, lambda_log, lambda_imag, log_step, input_map],
        [((layers, part), F32)] * 2 + [small_out] * 3 + [((layers, 2, own, width), F32), ((layers, 4, own, width), F32)],
        [tall_of(n * own) for n in (2, 3, 1)] + [((layers, 2, own, width), F32), ((LANES, LANES), F32)])
    return output, input_grad, grad_gain, grad_log, grad_imag, grad_step, grad_in, grad_out, grad_skip


def solution(mesh):
    rows, blocks = mesh.devices.shape
    inner = Mesh(mesh.devices.reshape(rows // 2, 2, blocks), ("plane", "core", "block"))
    dp = ("plane", "core")
    half = P(None, "block")
    maps = P(None, None, "block", None)
    acts = P(None, "block", dp)
    items = P(None, dp)
    return jax.shard_map(
        on_device,
        mesh=inner,
        in_specs=(acts, acts, items, items, half, half, half, half, maps, maps, half),
        out_specs=(acts, acts, half, half, half, half, maps, maps, half),
        check_vma=False,
    )
```

```python
from functools import partial
from typing import NamedTuple

import jax
import jax.numpy as jnp
from jax import lax
from jax.experimental import pallas as pl
from jax.experimental.pallas import tpu as pltpu
from jax.sharding import Mesh, PartitionSpec as P

EPSILON = 1e-05
SEGS = 16
LANES = 128
BF = jnp.bfloat16
F32 = jnp.float32
GELU_C = 0.7978845608028654
GELU_A = 0.044715
COST = 400_000_000


class Sizes(NamedTuple):
    blocks: int
    chunks: int
    toks: int
    run: int
    steps: int
    width: int
    states: int
    items: int


def turned(sz, index):
    return sz.blocks - 1 - index


def farthest(index, count):
    return count - index if index else 0


def place_of(sz, table):
    me, core = lax.axis_index("block"), lax.axis_index("core")
    q = lax.div(me, 2) * 2 + core
    mine, chunk = lax.div(q, sz.chunks), lax.rem(q, sz.chunks)
    out = [me, chunk, core, lax.axis_index("plane"), q]
    if table is not None:
        side = lax.rem(me, 2) ^ core
        for which in range(2):
            out += [table[side, which, mine, index] for index in range(sz.items)]
    return out


def nt(a, b):
    return lax.dot_general(a, b, (((1,), (1,)), ((), ())), preferred_element_type=F32)


def nn(a, b):
    return lax.dot_general(a, b, (((1,), (0,)), ((), ())), preferred_element_type=F32)


def tn(a, b):
    return lax.dot_general(a, b, (((0,), (0,)), ((), ())), preferred_element_type=F32)


def after(*values):
    return lax.optimization_barrier(values)


def cmul(ar, ai, br, bi):
    return ar * br - ai * bi, ar * bi + ai * br


def rows_of(step):
    return pl.ds(pl.multiple_of(step * SEGS, SEGS), SEGS)


def widen(mask, count):
    return jnp.concatenate([mask] * count, axis=1)


def item_of(sz, meta, index):
    begin = meta[5 + sz.items + index]
    return begin, begin + meta[5 + index]


def fill_masks(sz, meta, live, ahead, behind):
    base = meta[1] * sz.toks
    seg = lax.broadcasted_iota(jnp.int32, (SEGS, LANES), 0)

    def body(step, carry):
        pos = base + seg * sz.steps + step
        inside = jnp.zeros((SEGS, LANES), F32)
        onward = jnp.zeros((SEGS, LANES), F32)
        onward_next = jnp.zeros((SEGS, LANES), F32)
        for index in range(sz.items):
            begin, end = item_of(sz, meta, index)
            inside = jnp.where((pos >= begin) & (pos < end), 1.0, inside)
            onward = jnp.where((pos > begin) & (pos < end), 1.0, onward)
            onward_next = jnp.where((pos >= begin) & (pos + 1 < end), 1.0, onward_next)
        onward_next = jnp.where(pos + 1 < sz.run, onward_next, 0.0)
        live[rows_of(step), :] = inside
        ahead[rows_of(step), :] = onward
        behind[rows_of(step), :] = onward_next
        return carry

    lax.fori_loop(0, sz.steps, body, 0, unroll=4)


def through(sz, meta, first, length):
    ahead = behind = False
    for index in range(sz.items):
        begin, end = item_of(sz, meta, index)
        ahead = ahead | ((begin < first) & (end >= first + length))
        behind = behind | ((begin <= first) & (end > first + length))
    behind = behind & (first + length < sz.run)
    return ahead, behind


def power(pair, count):
    while count > 1:
        pair = cmul(*pair, *pair)
        count //= 2
    return pair


def column_blocks(sz, decay):
    out = []
    for q in range(sz.states // LANES):
        cols = slice(q * LANES, (q + 1) * LANES)
        out.append((decay[0:1, cols], decay[1:2, cols]))
    return out


def spread(pairs):
    return [tuple(jnp.broadcast_to(v, (SEGS, LANES)) for v in pair) for pair in pairs]


def chain_ends(sz, decay, ahead, behind, source, ahead_col, behind_col, ends):
    nq = sz.states // LANES
    d = spread(column_blocks(sz, decay))
    zero = jnp.zeros((SEGS, LANES), F32)

    def body(step, held):
        up, down = rows_of(step), rows_of(sz.steps - 1 - step)
        on_up, on_down = ahead[up, :], behind[down, :]
        new = []
        for q in range(nq):
            for side, (rows, on, col) in enumerate(((up, on_up, ahead_col), (down, on_down, behind_col))):
                re, im = held[2 * q + side]
                re, im = cmul(*d[q], re * on, im * on)
                re += source[rows, col + q * LANES : col + (q + 1) * LANES]
                im += source[rows, col + sz.states + q * LANES : col + sz.states + (q + 1) * LANES]
                new.append((re, im))
        return tuple(new)

    held = lax.fori_loop(0, sz.steps, body, tuple((zero, zero) for _ in range(2 * nq)), unroll=4)
    for q in range(nq):
        cols = slice(q * LANES, (q + 1) * LANES)
        for side in range(2):
            ends[2 * side, :, cols] = held[2 * q + side][0]
            ends[2 * side + 1, :, cols] = held[2 * q + side][1]


def enter_states(sz, meta, decay, ends, start, enter):
    pair = (decay[0:1, :], decay[1:2, :])
    jump = power(pair, sz.steps)
    base = meta[1] * sz.toks
    state = list(start)
    for count in range(SEGS):
        for side, seg in ((0, count), (1, SEGS - 1 - count)):
            re, im = state[side]
            enter[2 * side, seg : seg + 1, :] = re
            enter[2 * side + 1, seg : seg + 1, :] = im
            passes = through(sz, meta, base + seg * sz.steps, sz.steps)[side]
            gain = jnp.where(passes, 1.0, 0.0).astype(F32)
            re, im = cmul(jump[0] * gain, jump[1] * gain, re, im)
            state[side] = (
                re + ends[2 * side, seg : seg + 1, :],
                im + ends[2 * side + 1, seg : seg + 1, :],
            )
    return state


def send_ends(sz, meta, decay, ends, enter, send):
    zero = jnp.zeros((1, sz.states), F32)
    ahead, behind = enter_states(sz, meta, decay, ends, ((zero, zero), (zero, zero)), enter)
    me = meta[1]
    for dist in range(1, sz.chunks):
        up = (me ^ dist) > me
        for part in range(2):
            send[dist - 1, part : part + 1, :] = jnp.where(up, ahead[part], behind[part])


def received(sz, meta, decay, recv):
    me = meta[1]
    zero = jnp.zeros((1, sz.states), F32)
    pair = (decay[0:1, :], decay[1:2, :])
    jump = power(pair, sz.toks) if sz.chunks > 2 else None
    sides = []
    for side in range(2):
        re, im = zero, zero
        order = range(sz.chunks) if side == 0 else range(sz.chunks - 1, -1, -1)
        for other in order:
            use = (other < me) if side == 0 else (other > me)
            slot = jnp.maximum((me ^ other) - 1, 0)
            got = recv[slot]
            new_re, new_im = got[0:1, :], got[1:2, :]
            if sz.chunks > 2:
                passes = through(sz, meta, other * sz.toks, sz.toks)[side]
                gain = jnp.where(passes, 1.0, 0.0).astype(F32)
                moved = cmul(jump[0] * gain, jump[1] * gain, re, im)
                new_re, new_im = new_re + moved[0], new_im + moved[1]
            re, im = jnp.where(use, new_re, re), jnp.where(use, new_im, im)
        sides.append((re, im))
    return sides


def load_enter(sz, enter):
    held = []
    for q in range(sz.states // LANES):
        cols = slice(q * LANES, (q + 1) * LANES)
        for side in range(2):
            held.append((enter[2 * side, :, cols], enter[2 * side + 1, :, cols]))
    return tuple(held)


def chain_states(sz, decay, ahead, behind, source, enter, states):
    nq = sz.states // LANES
    n = sz.states
    d = spread(column_blocks(sz, decay))

    def body(step, held):
        up, down = rows_of(step), rows_of(sz.steps - 1 - step)
        on_up, on_down = ahead[up, :], behind[down, :]
        new = []
        for q in range(nq):
            for side, (rows, on) in enumerate(((up, on_up), (down, on_down))):
                re, im = held[2 * q + side]
                re, im = cmul(*d[q], re * on, im * on)
                lo = q * LANES
                re += source[rows, lo : lo + LANES]
                im += source[rows, n + lo : n + lo + LANES]
                at = 2 * side * n + lo
                states[rows, at : at + LANES] = re.astype(BF)
                states[rows, at + n : at + n + LANES] = (-im).astype(BF)
                new.append((re, im))
        return tuple(new)

    lax.fori_loop(0, sz.steps, body, load_enter(sz, enter), unroll=4)


def adjoint_chains(sz, decay, ahead, behind, source, enter, states, half, grad_driven, grad_decay):
    nq = sz.states // LANES
    n = sz.states
    d = spread(column_blocks(sz, decay))
    zero = jnp.zeros((SEGS, LANES), F32)

    def make(second):
        def body(step, carry):
            held, sums = carry
            up, down = rows_of(step), rows_of(sz.steps - 1 - step)
            on_up, on_down = ahead[up, :], behind[down, :]
            new, total = [], []
            for q in range(nq):
                lo = q * LANES
                acc_re, acc_im = sums[q]
                for side, (rows, on, src, st) in enumerate(((up, on_up, 2 * n, 2 * n), (down, on_down, 0, 0))):
                    re, im = held[2 * q + side]
                    re, im = re * on, im * on
                    s_re = states[rows, st + lo : st + lo + LANES].astype(F32)
                    s_im = states[rows, st + n + lo : st + n + lo + LANES].astype(F32)
                    acc_re += re * s_re + im * s_im
                    acc_im += re * s_im - im * s_re
                    re, im = cmul(*d[q], re, im)
                    re += source[rows, src + lo : src + lo + LANES]
                    im += source[rows, src + n + lo : src + n + lo + LANES]
                    new.append((re, im))
                    if second:
                        out_re = re + half[rows, lo : lo + LANES]
                        out_im = im + half[rows, n + lo : n + lo + LANES]
                        grad_driven[rows, lo : lo + LANES] = out_re.astype(BF)
                        grad_driven[rows, n + lo : n + lo + LANES] = (-out_im).astype(BF)
                    else:
                        half[rows, lo : lo + LANES] = re
                        half[rows, n + lo : n + lo + LANES] = im
                total.append((acc_re, acc_im))
            return tuple(new), tuple(total)

        return body

    carry = (load_enter(sz, enter), tuple((zero, zero) for _ in range(nq)))
    carry = lax.fori_loop(0, sz.steps // 2, make(False), carry, unroll=2)
    carry = lax.fori_loop(sz.steps // 2, sz.steps, make(True), carry, unroll=2)
    for q in range(nq):
        cols = slice(q * LANES, (q + 1) * LANES)
        grad_decay[0:1, cols] = jnp.sum(carry[1][q][0], axis=0, keepdims=True)
        grad_decay[1:2, cols] = jnp.sum(carry[1][q][1], axis=0, keepdims=True)


ROWS = 512


def row_parts(sz):
    size = min(ROWS, sz.toks)
    return [slice(lo, lo + size) for lo in range(0, sz.toks, size)]


def matmul_nt(a, b, out, tile=256):
    for lo in range(0, b.shape[0], tile):
        out[:, lo : lo + tile] = nt(a[...], b[lo : lo + tile, :]).astype(out.dtype)


def matmul_tn(a, b, out, tile=256):
    for lo in range(0, a.shape[1], tile):
        out[lo : lo + tile, :] = tn(a[:, lo : lo + tile], b[...]).astype(out.dtype)


def column_sum(x):
    return jnp.sum(x.reshape(x.shape[0] // 8, 8, x.shape[1]), axis=0)


def scale_of(u):
    return lax.rsqrt(jnp.mean(u * u, axis=1, keepdims=True) + EPSILON)


def normed_rows(sz, u, gain, on):
    return (u * scale_of(u) * gain * on).astype(BF)


def finish_rows(sz, rows, states, w_out, skip, normed, on, slope):
    pre = 2.0 * nn(states[rows, :], w_out[...]) + skip * normed[rows, :].astype(F32)
    square = pre * pre
    th = jnp.tanh(pre * (GELU_C + (GELU_C * GELU_A) * square))
    part = 0.5 + 0.5 * th
    deriv = part + pre * (1.0 - th * th) * (0.5 * GELU_C + (1.5 * GELU_C * GELU_A) * square)
    slope[rows, :] = (on * deriv).astype(slope.dtype)
    return on * (pre * part)


def enter_chunk(sz, meta, recv, decay, ends, enter):
    enter_states(sz, meta, decay, ends, received(sz, meta, decay, recv), enter)


def back_rows(sz, rows, grad_driven, w_in, upstream, slope, skip, hidden, gain):
    u = hidden[rows, :].astype(F32)
    r = upstream[rows, :]
    gn = nn(grad_driven[rows, :], w_in[...]) + r * slope[rows, :].astype(F32) * skip
    scale = scale_of(u)
    moved = u * scale
    dn = gn * gain
    inner = jnp.sum(dn * moved, axis=1, keepdims=True) * (1.0 / sz.width)
    return r + scale * (dn - moved * inner), column_sum(gn * moved)


def open_rows(sz, rows, r, slope, normed, w_out, twice, grad_states):
    e = r * slope[rows, :].astype(F32)
    low = e.astype(BF)
    double = low + low
    twice[rows, :] = double
    grad_states[rows, :] = nt(double, w_out[...])
    return column_sum(e * normed[rows, :].astype(F32))


def gain_of(params, layer):
    return params[layer : layer + 1, :]


def skip_of(params, layer):
    return params[2 + layer : 3 + layer, :]


def decay_of(sz, params, layer):
    return params[4 + 2 * layer : 6 + 2 * layer, 0 : sz.states]


def place_pieces(sz, meta, pieces, stacked):
    part = sz.width // sz.blocks
    for dist, piece in enumerate(pieces):
        owner = meta[4] ^ turned(sz, dist)
        stacked[pl.ds(pl.multiple_of(owner * part, part), part), :] = piece[0:part, :]


def cut_pieces(sz, meta, rows, perm, stacked, pieces):
    part = sz.width // sz.blocks
    matmul_tn(rows, perm, stacked)
    for dist, piece in enumerate(pieces):
        owner = meta[4] ^ turned(sz, dist)
        piece[...] = stacked[pl.ds(pl.multiple_of(owner * part, part), part), :]


def cut_kernel(sz, meta, whole, *refs):
    outs, wide, sems = refs[: sz.blocks], refs[-2], refs[-1]
    straight = whole.dtype == BF
    copies = []
    for dist in range(sz.blocks):
        to = meta[0] ^ turned(sz, dist)
        cols = pl.ds(pl.multiple_of(lax.rem(to, sz.chunks) * sz.toks, LANES), sz.toks)
        source = whole.at[lax.div(to, sz.chunks), :, cols]
        copy = pltpu.make_async_copy(source, outs[dist] if straight else wide.at[dist], sems.at[dist])
        copy.start()
        copies.append(copy)
    for dist, copy in enumerate(copies):
        copy.wait()
        if not straight:
            outs[dist][...] = wide[dist].astype(BF)


def discretize(lambda_log, lambda_imag, log_step):
    step_size = jnp.exp(log_step)
    lambda_real = -jnp.exp(lambda_log)
    modulus = jnp.exp(lambda_real * step_size)
    decay_real = modulus * jnp.cos(lambda_imag * step_size)
    decay_imag = modulus * jnp.sin(lambda_imag * step_size)
    denominator = lambda_real * lambda_real + lambda_imag * lambda_imag
    scale_real = ((decay_real - 1.0) * lambda_real + decay_imag * lambda_imag) / denominator
    scale_imag = (decay_imag * lambda_real - (decay_real - 1.0) * lambda_imag) / denominator
    return decay_real, decay_imag, scale_real, scale_imag


def first_rows(sz):
    part, own = sz.width // sz.blocks, sz.states // sz.blocks
    return part, part + own * sz.width // sz.toks


def half_map_parts(sz):
    top, end = first_rows(sz)
    rows = end - top
    for index in range(sz.toks // sz.width):
        yield slice(index * rows, (index + 1) * rows), slice(top, end), slice(index * sz.width, (index + 1) * sz.width)


def split3(x):
    hi = x.astype(BF).astype(F32)
    mid = (x - hi).astype(BF).astype(F32)
    return hi, mid, x - hi - mid


def prepare_kernel(sz, meta, tokens, *refs):
    inputs, refs = refs[:7], refs[7:]
    outs, refs = refs[: sz.blocks], refs[sz.blocks :]
    drive_b, half_b = refs[:2]
    held, small, lines, drive_a, sems = refs[2:9], refs[9], refs[10], refs[11], refs[12]
    top, end = first_rows(sz)
    own, part = sz.states // sz.blocks, sz.width // sz.blocks
    loads, copies = [], []
    for index, (source, target) in enumerate(zip(inputs, held)):
        loads.append(pltpu.make_async_copy(source, target, sems.at[index]))
    for dist in range(sz.blocks):
        to = meta[0] ^ turned(sz, dist)
        cols = pl.ds(pl.multiple_of(lax.rem(to, sz.chunks) * sz.toks, LANES), sz.toks)
        source = tokens.at[lax.div(to, sz.chunks), :, cols]
        copies.append(pltpu.make_async_copy(source, outs[dist].at[0:top, :], sems.at[len(inputs) + dist]))
    for copy in copies + loads:
        copy.start()
    for copy in loads[:6]:
        copy.wait()
    gain, skip, lambda_log, lambda_imag, log_step, input_map, output_map = held
    dr, di, sr, si = discretize(lambda_log[...], lambda_imag[...], log_step[...])
    small[...] = jnp.zeros_like(small)
    lines[...] = jnp.zeros_like(lines)
    small[0:2, 0:part] = gain[...]
    small[2:4, 0:part] = skip[...]
    for layer in range(2):
        small[4 + 2 * layer : 5 + 2 * layer, 0:own] = dr[layer : layer + 1]
        small[5 + 2 * layer : 6 + 2 * layer, 0:own] = di[layer : layer + 1]
    lines[0:2, 0:own] = sr
    lines[2:4, 0:own] = si
    cols = lines[...].T
    for layer in range(2):
        qr, qi = cols[0:own, layer : layer + 1], cols[0:own, 2 + layer : 3 + layer]
        br, bi = input_map[layer, 0].astype(F32), input_map[layer, 1].astype(F32)
        for index, value in enumerate((qr * br - qi * bi, qr * bi + qi * br)):
            (drive_a, drive_b)[layer][index] = value.astype(BF)
    rows = jnp.concatenate([*split3(small[...]), jnp.zeros((8, sz.toks - 3 * LANES), F32)], axis=1)
    rows = jnp.concatenate([rows, jnp.zeros((8, sz.toks), F32)], axis=0).astype(BF)
    for dist, out in enumerate(outs):
        half = lax.rem(meta[0] ^ turned(sz, dist), 2)
        for from_rows, to_rows, lanes in half_map_parts(sz):
            out[to_rows, lanes] = drive_a[half, from_rows, :]
        out[end:, :] = rows
    loads[6].wait()
    core = meta[2]
    for index in range(2):
        half_b[index] = output_map[0, 2 * core + index]
        half_b[3 + index] = output_map[1, 2 * core + index]
    half_b[2] = drive_b[core]
    for copy in copies:
        copy.wait()


def params_of(sz, piece):
    rows = piece[piece.shape[0] - 16 :, 0 : 3 * LANES].astype(F32)[0:8]
    return rows[:, 0:LANES] + rows[:, LANES : 2 * LANES] + rows[:, 2 * LANES :]


def join_kernel(sz, meta, *refs):
    pieces, maps, params = refs[: sz.blocks], refs[-2], refs[-1]
    own = sz.states // sz.blocks
    collect_params(sz, meta, [params_of(sz, piece) for piece in pieces], params)
    for dist, piece in enumerate(pieces):
        base = (meta[4] ^ turned(sz, dist)) * own
        for to_rows, from_rows, lanes in half_map_parts(sz):
            rows = pl.ds(pl.multiple_of(base + to_rows.start, 16), to_rows.stop - to_rows.start)
            maps[rows, :] = piece[from_rows, lanes]


def collect_params(sz, meta, smalls, params):
    own = sz.states // sz.blocks
    part = sz.width // sz.blocks
    lane = lax.broadcasted_iota(jnp.int32, (8, LANES), 1)
    row = lax.broadcasted_iota(jnp.int32, (8, LANES), 0)
    pad = jnp.zeros((8, sz.width - LANES), F32)
    total = jnp.zeros((8, sz.width), F32)
    for block in range(sz.blocks):
        piece = smalls[0]
        for dist in range(1, sz.blocks):
            piece = jnp.where((meta[4] ^ turned(sz, dist)) == block, smalls[dist], piece)
        for first, count, size in ((0, 4, part), (4, 4, own)):
            mine = jnp.where((row >= first) & (row < first + count) & (lane < size), piece, 0.0)
            wide = jnp.concatenate([mine, pad], axis=1)
            total += pltpu.roll(wide, block * size, 1) if block else wide
    params[...] = total


def place_maps(sz, meta, own_maps, mine, other, skip, out):
    own = sz.states // sz.blocks
    count = own_maps.shape[0] // 2

    def put(index, owner, value):
        out[pl.ds(pl.multiple_of(index * sz.states + owner * own, own), own), :] = value

    for index in range(2 * count):
        put(index, meta[0], own_maps[index])
    for side, pieces in ((meta[2], mine), (1 - meta[2], other)):
        for dist, piece in enumerate(pieces):
            for index in range(count):
                put(side * count + index, meta[0] ^ (dist + 1), piece[skip + index])


def open_kernel(sz, meta, perm, params, *refs):
    pieces, (hidden, normed, live, ahead, behind, stacked) = refs[: sz.blocks], refs[sz.blocks :]
    fill_masks(sz, meta, live, ahead, behind)
    place_pieces(sz, meta, pieces, stacked)
    gain = gain_of(params, 0)
    for rows in row_parts(sz):
        u = nt(perm[rows, :], stacked[...])
        hidden[rows, :] = u.astype(BF)
        normed[rows, :] = normed_rows(sz, u, gain, widen(live[rows, :], sz.width // LANES))


def enter_kernel(sz, meta, ahead, behind, params, normed, maps, other, w_in, driven, ends, send, enter):
    decay = decay_of(sz, params, 0)
    for side, half in ((meta[2], maps), (1 - meta[2], other)):
        w_in[pl.ds(pl.multiple_of(side * sz.states, sz.states), sz.states), :] = half[...]
    matmul_nt(normed, w_in, driven)
    chain_ends(sz, decay, ahead, behind, driven, 0, 0, ends)
    send_ends(sz, meta, decay, ends, enter, send)


def chain_kernel(sz, meta, ahead, behind, recv, params, ends, driven, states, enter):
    decay = decay_of(sz, params, 0)
    enter_chunk(sz, meta, recv, decay, ends, enter)
    chain_states(sz, decay, ahead, behind, driven, enter, states)


def middle_kernel(sz, meta, live, ahead, behind, states, params, normed, hidden, own_out, own_in, *refs):
    skip, gain_b, decay_b = skip_of(params, 0), gain_of(params, 1), decay_of(sz, params, 1)
    far = sz.blocks - 1
    mine, other, refs = refs[:far], refs[far : 2 * far], refs[2 * far :]
    w_out, w_in_b, slope, hidden_b, normed_b, driven_b, ends_b, send_b, enter = refs
    place_maps(sz, meta, own_out, mine, other, 0, w_out)
    place_maps(sz, meta, own_in, mine, other, 2, w_in_b)
    for rows in row_parts(sz):
        on = widen(live[rows, :], sz.width // LANES)
        u = hidden[rows, :].astype(F32) + finish_rows(sz, rows, states, w_out, skip, normed, on, slope)
        hidden_b[rows, :] = u
        v = normed_rows(sz, u, gain_b, on)
        normed_b[rows, :] = v
        driven_b[rows, :] = nt(v, w_in_b[...])
    chain_ends(sz, decay_b, ahead, behind, driven_b, 0, 0, ends_b)
    send_ends(sz, meta, decay_b, ends_b, enter, send_b)


def leave_kernel(sz, meta, live, ahead, behind, recv, params, ends, driven, normed, hidden, perm, own_out, *refs):
    decay, skip = decay_of(sz, params, 1), skip_of(params, 1)
    far = sz.blocks - 1
    mine, other, refs = refs[:far], refs[far : 2 * far], refs[2 * far :]
    w_out, states, slope, refs = *refs[:3], refs[3:]
    place_maps(sz, meta, own_out, mine, other, 3, w_out)
    pieces, (enter, last, stacked) = refs[: sz.blocks], refs[sz.blocks :]
    enter_chunk(sz, meta, recv, decay, ends, enter)
    chain_states(sz, decay, ahead, behind, driven, enter, states)
    for rows in row_parts(sz):
        on = widen(live[rows, :], sz.width // LANES)
        last[rows, :] = (hidden[rows, :] + finish_rows(sz, rows, states, w_out, skip, normed, on, slope)).astype(BF)
    cut_pieces(sz, meta, last, perm, stacked, pieces)


def turn_kernel(sz, meta, ahead, behind, slope, normed, w_out, params, perm, *refs):
    decay = decay_of(sz, params, 1)
    pieces, refs = refs[: sz.blocks], refs[sz.blocks :]
    upstream, twice, grad_states, grad_skip, ends, send, stacked, enter = refs
    place_pieces(sz, meta, pieces, stacked)
    skips = []
    for rows in row_parts(sz):
        r = nt(perm[rows, :], stacked[...])
        upstream[rows, :] = r
        skips.append(open_rows(sz, rows, r, slope, normed, w_out, twice, grad_states))
    grad_skip[...] = jnp.sum(sum(skips), axis=0, keepdims=True)
    chain_ends(sz, decay, ahead, behind, grad_states, 2 * sz.states, 0, ends)
    send_ends(sz, meta, decay, ends, enter, send)


def back_middle_kernel(sz, meta, ahead, behind, recv, params, ends, grad_states, states, upstream, slope, hidden, w_in,
                       slope_b, normed_b, w_out_b,
                       grad_driven, grad_decay, grad_gain, upstream_b, twice_b, grad_states_b, grad_skip_b, ends_b, send_b,
                       enter, half):
    decay, skip, gain, decay_b = decay_of(sz, params, 1), skip_of(params, 1), gain_of(params, 1), decay_of(sz, params, 0)
    enter_chunk(sz, meta, recv, decay, ends, enter)
    adjoint_chains(sz, decay, ahead, behind, grad_states, enter, states, half, grad_driven, grad_decay)
    gains, skips = [], []
    for rows in row_parts(sz):
        r, terms = back_rows(sz, rows, grad_driven, w_in, upstream, slope, skip, hidden, gain)
        gains.append(terms)
        upstream_b[rows, :] = r
        skips.append(open_rows(sz, rows, r, slope_b, normed_b, w_out_b, twice_b, grad_states_b))
    grad_gain[...] = jnp.sum(sum(gains), axis=0, keepdims=True)
    grad_skip_b[...] = jnp.sum(sum(skips), axis=0, keepdims=True)
    chain_ends(sz, decay_b, ahead, behind, grad_states_b, 2 * sz.states, 0, ends_b)
    send_ends(sz, meta, decay_b, ends_b, enter, send_b)


def back_chain_kernel(sz, meta, ahead, behind, recv, params, ends, grad_states, states, grad_driven, grad_decay, enter, half):
    decay = decay_of(sz, params, 0)
    enter_chunk(sz, meta, recv, decay, ends, enter)
    adjoint_chains(sz, decay, ahead, behind, grad_states, enter, states, half, grad_driven, grad_decay)


def back_leave_kernel(sz, meta, params, grad_driven, upstream, slope, hidden, w_in, perm, *refs):
    done, refs = refs[: sz.blocks], refs[sz.blocks :]
    skip, gain = skip_of(params, 0), gain_of(params, 0)
    pieces, (last, stacked) = refs[: sz.blocks], refs[sz.blocks :]
    for rows in row_parts(sz):
        r, _ = back_rows(sz, rows, grad_driven, w_in, upstream, slope, skip, hidden, gain)
        last[rows, :] = r.astype(BF)
    part = sz.width // sz.blocks
    for piece, first in zip(pieces, done):
        piece[0:part, :] = first[...]
    cut_pieces(sz, meta, last, perm, stacked, [piece.at[part : 2 * part, :] for piece in pieces])


def weight_kernel(counts, other, sz, meta, *refs):
    half = 1 - meta[2] if other else meta[2]
    pairs = 2 * len(counts)
    out, at = refs[pairs], 0
    if len(refs) > pairs + 1:
        whole, out, terms = refs[pairs:]
        value = tn(refs[0][:, pl.ds(pl.multiple_of(half * sz.states, LANES), sz.states)], refs[1][...])
        out[...] = value.astype(out.dtype)
        rows = whole[pl.ds(pl.multiple_of(half * sz.states, sz.states), sz.states), :].astype(F32)
        terms[...] = jnp.sum(column_sum(rows * value), axis=0, keepdims=True)
        return
    for index, count in enumerate(counts):
        left, right = refs[2 * index], refs[2 * index + 1]
        for group in range(count):
            cols = pl.ds(pl.multiple_of((half * count + group) * sz.states, LANES), sz.states)
            out[at : at + sz.states, :] = tn(left[:, cols], right[...]).astype(out.dtype)
            at += sz.states


def split2(x):
    hi = x.astype(BF).astype(F32)
    return hi, x - hi


class Group(NamedTuple):
    first: int
    counts: tuple
    tiny: bool

    def rows(self, sz):
        return sum(self.counts) * (sz.states // sz.blocks) + (16 if self.tiny else 0)


def bits_of(sz):
    return sz.blocks.bit_length() - 1


def step_bit(sz, step, core):
    return 1 << ((step + core) % bits_of(sz))


def far_block(sz, group, slot, core):
    return sum(step_bit(sz, group.first + j, core) for j in range(bits_of(sz)) if (slot >> j) & 1)


def own_tiny(sz, params, terms, more, gain_b, skip_a, skip_b, decay_a, decay_b, tiny):
    gain_a = (terms[...] + more[...] + skip_of(params, 0) * skip_a[...]) / gain_of(params, 0)
    tiny[...] = jnp.zeros_like(tiny)
    for index, line in enumerate((gain_a, gain_b[...], skip_a[...], skip_b[...])):
        tiny[index : index + 1, :] = line
    tiny[4:6, 0 : sz.states] = decay_a[...]
    tiny[6:8, 0 : sz.states] = decay_b[...]
    return tiny[...]


def tiny_of(sz, tiny, owner):
    own, part = sz.states // sz.blocks, sz.width // sz.blocks
    row = lax.broadcasted_iota(jnp.int32, (8, LANES), 0)
    lane = lax.broadcasted_iota(jnp.int32, (8, LANES), 1)
    value = jnp.zeros((8, LANES), F32)
    for block in range(sz.blocks):
        wide = pltpu.roll(tiny, sz.width - block * part, 1) if block else tiny
        deep = pltpu.roll(tiny, sz.width - block * own, 1) if block else tiny
        mine = jnp.where(row < 4, jnp.where(lane < part, wide[:, :LANES], 0.0), jnp.where(lane < own, deep[:, :LANES], 0.0))
        value = jnp.where(owner == block, mine, value)
    return value


def put_sums(sz, group, value, tiny, slot, kept, message, at):
    rows = value.shape[0]
    if slot % 2 == 0:
        kept[slot // 2, 0:rows, :] = value
        if group.tiny:
            kept[slot // 2, rows : rows + 8, 0:LANES] = tiny
        return at
    message[at : at + rows, :] = value.astype(BF)
    if group.tiny:
        rest = jnp.zeros((8, sz.width - 2 * LANES), F32)
        wide = jnp.concatenate([*split2(tiny), rest], axis=1)
        message[at + rows : at + rows + 16, :] = jnp.concatenate([wide, jnp.zeros_like(wide)], axis=0).astype(BF)
    return at + group.rows(sz)


def add_message(sz, group, kept, slot, message, at):
    rows = group.rows(sz) - (16 if group.tiny else 0)
    value = kept[slot, 0:rows, :] + message[at : at + rows, :].astype(F32)
    if not group.tiny:
        return value, None
    got = message[at + rows : at + rows + 16, 0 : 2 * LANES].astype(F32)[0:8]
    return value, kept[slot, rows : rows + 8, 0:LANES] + got[:, 0:LANES] + got[:, LANES:]


def step_kernel(old, new, sz, meta, *refs):
    came, refs = (refs[0], refs[1:]) if old else (None, refs)
    held, refs = refs[: len(old)], refs[len(old) :]
    if new:
        halves, refs = refs[: 2 * len(new.counts)], refs[2 * len(new.counts) :]
        if new.tiny:
            lines, refs, room = refs[:8], refs[8:-1], refs[-1]
    keeps, message = refs[:-1], refs[-1]
    at = 0
    for (group, slots, row), kept, keep in zip(old, held, keeps):
        for slot in range(slots):
            value, tiny = add_message(sz, group, kept, slot, came, row + slot * group.rows(sz))
            at = put_sums(sz, group, value, tiny, slot, keep, message, at)
    if new:
        own = sz.states // sz.blocks
        whole = own_tiny(sz, *lines, room) if new.tiny else None
        for slot in range(sz.blocks):
            owner = meta[0] ^ jnp.where(meta[2] == 0, far_block(sz, new, slot, 0), far_block(sz, new, slot, 1))
            parts = []
            for index, count in enumerate(new.counts):
                keep, got = halves[2 * index], halves[2 * index + 1]
                for one in range(count):
                    rows = pl.ds(pl.multiple_of(one * sz.states + owner * own, own), own)
                    parts.append(keep[rows, :].astype(F32) + got[rows, :].astype(F32))
            tiny = tiny_of(sz, whole, owner) if new.tiny else None
            at = put_sums(sz, new, jnp.concatenate(parts, axis=0), tiny, slot, keeps[-1], message, at)


def fold_block_kernel(planes, groups, sz, meta, *refs):
    lanes = sz.width // LANES
    held, refs = refs[: 2 * len(groups)], refs[2 * len(groups) :]
    outs, talls = refs[:planes], refs[planes:]
    at = 0
    for index, (group, row) in enumerate(groups):
        total, tiny = add_message(sz, group, held[2 * index], 0, held[2 * index + 1], row)
        rows = total.shape[0]
        tall = talls[index]
        padded = tall.shape[0] // lanes
        for block in range(lanes):
            tall[block * padded : block * padded + rows, :] = total[:, block * LANES : (block + 1) * LANES].astype(BF)
            if padded > rows:
                tall[block * padded + rows : (block + 1) * padded, :] = jnp.zeros((padded - rows, LANES), BF)
        part = tall.shape[0] // planes
        for dist, out in enumerate(outs):
            out[at : at + part, :] = tall[pl.ds(pl.multiple_of((meta[3] ^ farthest(dist, planes)) * part, part), part), :]
        at += part
    if tiny is not None:
        rows = jnp.concatenate(split2(tiny), axis=0).astype(BF)
        for out in outs:
            out[at : at + 16, :] = rows


def fold_plane_kernel(early, sz, meta, *refs):
    parts, out, tiny = refs[early:-2], refs[-2], refs[-1]
    total = refs[0][...].astype(F32)
    for piece in refs[1:early]:
        total += piece[...].astype(F32)
    top = total.shape[0]
    out[0:top, :] = total.astype(BF)
    total = parts[0][...].astype(F32)
    for piece in parts[1:]:
        total += piece[...].astype(F32)
    rows = total.shape[0] - 16
    out[top:, :] = total[0:rows].astype(BF)
    tiny[...] = total[rows : rows + 8] + total[rows + 8 :]


def finish_kernel(planes, groups, sz, meta, *refs):
    count = 2 * planes
    pieces, refs = refs[:count], refs[count:]
    tiny, lambda_log, lambda_imag, log_step, input_map = refs[0][...] + refs[1][...], *refs[2:6]
    grad_gain, grad_skip, grad_log, grad_imag, grad_step, grad_maps, grad_out = refs[6:13]
    talls, grad_in, lines = refs[13:-2], refs[-2], refs[-1]
    own = sz.states // sz.blocks
    lanes = sz.width // LANES
    start = 0
    for tall, group in zip(talls, groups):
        padded = tall.shape[0] // lanes
        part = tall.shape[0] // planes
        for side in range(2):
            half = meta[2] ^ side
            for dist in range(planes):
                rows = pl.ds(pl.multiple_of((meta[3] ^ farthest(dist, planes)) * part, part), part)
                tall[rows, :] = pieces[side * planes + dist][start : start + part, :]
            at = 0
            for which, layer, maps in group:
                out = grad_in if which == 0 else grad_out
                for one in range(maps):
                    for block in range(lanes):
                        rows = slice(block * padded + at, block * padded + at + own)
                        out[layer, half * maps + one, :, block * LANES : (block + 1) * LANES] = tall[rows, :].astype(F32)
                    at += own
        start += part
    width = sz.width // sz.blocks
    grad_gain[...] = tiny[0:2, 0:width]
    grad_skip[...] = tiny[2:4, 0:width]
    dr, di, sr, si = discretize(lambda_log[...], lambda_imag[...], log_step[...])
    lines[...] = jnp.zeros_like(lines)
    lines[0:2, 0:own] = sr
    lines[2:4, 0:own] = si
    cols = lines[...].T
    back = []
    for layer in range(2):
        qr, qi = cols[0:own, layer : layer + 1], cols[0:own, 2 + layer : 3 + layer]
        wr, wi = grad_in[layer, 0], grad_in[layer, 1]
        br, bi = input_map[layer, 0].astype(F32), input_map[layer, 1].astype(F32)
        grad_maps[layer, 0] = qr * wr + qi * wi
        grad_maps[layer, 1] = qr * wi - qi * wr
        back.append(jnp.sum(wr * br + wi * bi, axis=1, keepdims=True))
        back.append(jnp.sum(wi * br - wr * bi, axis=1, keepdims=True))
    lines[...] = jnp.zeros_like(lines)
    for index, col in enumerate(back):
        lines[0:own, index : index + 1] = col
    rows = lines[...].T
    step = jnp.exp(log_step[...])
    lr, li = -jnp.exp(lambda_log[...]), lambda_imag[...]
    norm = 1.0 / (lr * lr + li * li)
    for layer in range(2):
        at = slice(layer, layer + 1)
        a, b, h = (lr[at], li[at]), (dr[at], di[at]), step[at]
        gq = rows[2 * layer : 2 * layer + 1, 0:own], rows[2 * layer + 1 : 2 * layer + 2, 0:own]
        gd = tiny[4 + 2 * layer : 5 + 2 * layer, 0:own], tiny[5 + 2 * layer : 6 + 2 * layer, 0:own]
        inverse = a[0] * norm[at], -a[1] * norm[at]
        through = cmul(inverse[0], -inverse[1], *gq)
        gd = gd[0] + through[0], gd[1] + through[1]
        ratio = cmul(*inverse, sr[at], si[at])
        direct = cmul(ratio[0], -ratio[1], *gq)
        moved = cmul(b[0] * h, -b[1] * h, *gd)
        turn = cmul(*a, *b)
        grad_log[at, :] = (moved[0] - direct[0]) * a[0]
        grad_imag[at, :] = moved[1] - direct[1]
        grad_step[at, :] = (turn[0] * gd[0] + turn[1] * gd[1]) * h


def spread_kernel(sz, meta, *refs):
    pieces, outs, wide, sems = refs[: sz.blocks], refs[sz.blocks : -2], refs[-2], refs[-1]
    part = sz.width // sz.blocks
    copies = []
    for dist, piece in enumerate(pieces):
        owner = meta[0] ^ turned(sz, dist)
        for index, out in enumerate(outs):
            slot = dist * len(outs) + index
            wide[slot] = piece[index * part : (index + 1) * part, :].astype(F32)
            cols = pl.ds(pl.multiple_of(lax.rem(owner, sz.chunks) * sz.toks, LANES), sz.toks)
            copy = pltpu.make_async_copy(wide.at[slot], out.at[lax.div(owner, sz.chunks), :, cols], sems.at[slot])
            copy.start()
            copies.append(copy)
    for copy in copies:
        copy.wait()


VMEM = pl.BlockSpec(memory_space=pltpu.VMEM)
SMEM = pl.BlockSpec(memory_space=pltpu.SMEM)
HBM = pl.BlockSpec(memory_space=pltpu.HBM)


def call(name, sz, body, items, args, outs, scratch, limit=10, in_spec=VMEM, out_spec=VMEM, time=0.0):
    out_shape = [jax.ShapeDtypeStruct(shape, dtype) for shape, dtype in outs]

    def kernel(*refs):
        body(sz, place_of(sz, refs[0] if items else None), *refs[len(items) :])

    return pl.pallas_call(
        kernel,
        out_shape=out_shape,
        in_specs=[SMEM] * len(items) + [in_spec] * len(args),
        out_specs=[out_spec] * len(outs),
        scratch_shapes=[pltpu.VMEM(*item) if isinstance(item, tuple) else item for item in scratch],
        compiler_params=pltpu.CompilerParams(vmem_limit_bytes=limit << 20),
        cost_estimate=pl.CostEstimate(flops=int(COST * time), bytes_accessed=1000, transcendentals=0),
        name=name,
    )(*items, *args)


def on_device(tokens, cotangent, item_lengths, item_offsets, norm_gain, lambda_log, lambda_imag, log_step, input_map, output_map, skip_weight):
    micro, part, run = tokens.shape
    layers = norm_gain.shape[0]
    blocks = lax.axis_size("block")
    planes = lax.axis_size("plane")
    chunks = blocks // micro
    toks = run // chunks
    own = lambda_log.shape[1]
    width, states = part * blocks, own * blocks
    sz = Sizes(blocks, chunks, toks, run, toks // SEGS, width, states, item_lengths.shape[1])

    def swap(x, dist, axis="block"):
        return lax.ppermute(x, axis, [(i, i ^ dist) for i in range(lax.axis_size(axis))])

    def across(x, dist, back):
        pairs = []
        for c in range(2):
            for b in range(blocks):
                q = b ^ turned(sz, dist)
                pairs.append((c * blocks + b, (q % 2) * blocks + (q // 2) * 2 + c))
        return lax.ppermute(x, ("core", "block"), [pair[::-1] for pair in pairs] if back else pairs)

    def across_all(pieces, back=False):
        return [across(piece, dist, back) for dist, piece in enumerate(pieces)]

    table = jnp.stack([item_lengths, item_offsets])
    items = [jnp.stack([table, swap(table, 1, "core")])]

    def neighbour(x, dist):
        pairs = []
        for c in range(2):
            for b in range(blocks):
                q = ((b // 2) * 2 + c) ^ dist
                pairs.append((c * blocks + b, (q % 2) * blocks + (q // 2) * 2 + b % 2))
        return lax.ppermute(x, ("core", "block"), pairs)

    def swap_all(pieces, axis="block"):
        count = len(pieces)
        return [swap(piece, farthest(index, count), axis) if index else piece for index, piece in enumerate(pieces)]

    def exchange(send):
        return jnp.stack([neighbour(send[dist - 1], dist) for dist in range(1, chunks)])

    row = jnp.arange(toks, dtype=jnp.int32)[:, None]
    col = jnp.arange(toks, dtype=jnp.int32)[None, :]
    perm = ((row % SEGS) * sz.steps + row // SEGS == col).astype(BF)

    maps_own = ((2, own, width), BF)
    half_own = ((5, own, width), BF)
    given = [norm_gain, skip_weight, lambda_log, lambda_imag, log_step, input_map, output_map]
    *first_pieces, drive_b, half_b = call(
        "prepare", sz, prepare_kernel, [], [pltpu.with_memory_space_constraint(x, pltpu.HBM) for x in [tokens, *given]],
        [((first_rows(sz)[1] + 16, toks), BF)] * blocks + [maps_own, half_own],
        [(x.shape, x.dtype) for x in given] + [((8, LANES), F32), ((8, LANES), F32), maps_own, pltpu.SemaphoreType.DMA((len(given) + blocks,))],
        limit=6, in_spec=HBM)
    first_pieces = across_all(first_pieces)
    cot_cut = call("cut_cotangent", sz, cut_kernel, [], [pltpu.with_memory_space_constraint(cotangent, pltpu.HBM)],
                   [((part, toks), BF)] * blocks, [((blocks, part, toks), F32), pltpu.SemaphoreType.DMA((blocks,))], limit=4, in_spec=HBM)
    half_b, first_pieces[1], perm, cot_cut = after(half_b, first_pieces[1], perm, cot_cut)
    maps_a, params = call("join", sz, join_kernel, [], first_pieces, [((states, width), BF), ((8, width), F32)], [])
    second_mine = [swap(half_b, dist) for dist in range(1, blocks)]

    mask = ((toks, LANES), F32)
    enter = ((4, SEGS, states), F32)
    stacked = ((width, toks), BF)
    rows_f, rows_b = ((toks, width), F32), ((toks, width), BF)
    drv = ((toks, 2 * states), F32)
    sts = ((toks, 4 * states), BF)
    gst = ((toks, 4 * states), F32)
    snd = ((chunks - 1, 2, states), F32)
    w_in, w_out = ((2 * states, width), BF), ((4 * states, width), BF)
    line, gdec = ((1, width), F32), ((2, states), F32)
    piece_out = [((part, toks), BF)] * blocks

    other_a = swap(maps_a, 1, "core")
    hidden_a, normed_a, live, ahead, behind = call(
        "open", sz, open_kernel, items, [perm, params, *first_pieces], [rows_b, rows_b, mask, mask, mask], [stacked], time=3)
    w_in_a, driven_a, ends_a, send_a = call(
        "enter", sz, enter_kernel, items, [ahead, behind, params, normed_a, maps_a, other_a], [w_in, drv, enter, snd], [enter])
    recv = exchange(send_a)
    (states_a,) = call("chain", sz, chain_kernel, items, [ahead, behind, recv, params, ends_a, driven_a], [sts], [enter])
    second_mine, states_a = after(second_mine, states_a)
    second_maps = second_mine, [swap(piece, 1, "core") for piece in second_mine]
    cot_early, _ = after(cot_cut[0::2], recv)
    cot_early = [across(piece, 2 * index, False) for index, piece in enumerate(cot_early)]
    w_out_a, w_in_b, slope_a, hidden_b, normed_b, driven_b, ends_b, send_b = call(
        "middle", sz, middle_kernel, items,
        [live, ahead, behind, states_a, params, normed_a, hidden_a, output_map[0], drive_b, *second_maps[0], *second_maps[1]],
        [w_out, w_in, rows_b, rows_f, rows_b, drv, enter, snd], [enter], time=11)
    send_b, cot_early = after(send_b, cot_early)
    recv = exchange(send_b)
    cot_late, _ = after(cot_cut[1::2], send_b)
    cot_late = [across(piece, 2 * index + 1, False) for index, piece in enumerate(cot_late)]
    cot_pieces = [piece for pair in zip(cot_early, cot_late) for piece in pair]
    w_out_b, states_b, slope_b, *out_pieces = call(
        "leave", sz, leave_kernel, items,
        [live, ahead, behind, recv, params, ends_b, driven_b, normed_b, hidden_b, perm, output_map[1], *second_maps[0], *second_maps[1]],
        [w_out, sts, rows_b, *piece_out], [enter, rows_b, stacked], time=8)

    def half_grads(name, other, pairs, counts, more=(), time=0.0):
        args = [x for pair in pairs for x in pair]
        outs = [((sum(counts) * states, width), BF)] + [line] * len(more)
        return call(name, sz, partial(weight_kernel, counts, other), [], [*args, *more], outs, [], time=time)

    groups = [Group(0, (2,), False), Group(1, (3,), False), Group(2, (1,), True)]
    steps = bits_of(sz)
    kept, came, place = {}, {}, {}

    def halve(step, halves=(), tiny=()):
        old, args = [], []
        for index, group in enumerate(groups):
            if 0 < step - group.first < steps:
                slots = 1 << (steps - (step - group.first))
                old.append((group, slots, place[step - 1, index]))
                args.append(kept[index])
        if old:
            args.insert(0, came[step - 1])
        new = groups[step] if step < len(groups) else None
        outs, at = [], 0
        for index, group in enumerate(groups):
            if 0 <= step - group.first < steps:
                slots = 1 << (steps - 1 - (step - group.first))
                outs.append((index, ((slots, group.rows(sz), width), F32)))
                place[step, index] = at
                at += slots * group.rows(sz)
        results = call("halve_%d" % step, sz, partial(step_kernel, old, new), [], [*args, *halves, *tiny],
                       [shape for _, shape in outs] + [((at, width), BF)], [((8, width), F32)] if tiny else [])
        for (index, _), value in zip(outs, results):
            kept[index] = value
        return results[-1]

    def send_step(step, message):
        pairs = [(c * blocks + b, c * blocks + (b ^ step_bit(sz, step, c))) for c in range(2) for b in range(blocks)]
        came[step] = lax.ppermute(message, ("core", "block"), pairs)

    def spread(pieces):
        return call("spread", sz, spread_kernel, [], pieces, [((micro, part, run), F32)] * 2,
                    [((2 * blocks, part, toks), F32), pltpu.SemaphoreType.DMA((2 * blocks,))], limit=6, out_spec=HBM)

    lanes = width // LANES

    def tall_of(rows):
        step = max(SEGS * planes // lanes, SEGS)
        return ((lanes * (-(-rows // step) * step), LANES), BF)

    def over_planes(name, which):
        ends = [(groups[index], place[groups[index].first + steps - 1, index]) for index in which]
        talls = [tall_of(sum(group.counts) * own) for group, _ in ends]
        cut = sum(t[0][0] for t in talls) // planes + (16 if ends[-1][0].tiny else 0)
        args = [x for index in which for x in (kept[index], came[groups[index].first + steps - 1])]
        return swap_all(call(name, sz, partial(fold_block_kernel, planes, ends), [], args, [((cut, LANES), BF)] * planes, talls), "plane")

    up_b, twice_b, gstates_b, gskip_b, ends, send = call(
        "turn", sz, turn_kernel, items, [ahead, behind, slope_b, normed_b, w_out_b, params, perm, *cot_pieces],
        [rows_f, rows_b, gst, line, enter, snd], [stacked, enter], time=6)
    recv = exchange(send)
    pairs = [(states_b, twice_b)]
    (send_maps,) = half_grads("grads_a_send", True, pairs, (2,))
    got = swap(send_maps, 1, "core")
    (keep,) = half_grads("grads_a_keep", False, pairs, (2,), time=2)
    message = halve(0, (keep, got))
    recv, message = after(recv, message)
    send_step(0, message)
    gdriven_b, gdecay_b, ggain_b, up_a, twice_a, gstates_a, gskip_a, ends, send = call(
        "back_middle", sz, back_middle_kernel, items,
        [ahead, behind, recv, params, ends, gstates_b, states_b, up_b, slope_b, hidden_b, w_in_b, slope_a, normed_a, w_out_a],
        [((toks, 2 * states), BF), gdec, line, rows_f, rows_b, gst, line, enter, snd], [enter, drv], limit=12, time=11)
    recv = exchange(send)
    gdriven_b, came[0] = after(gdriven_b, came[0])
    pairs = [(gdriven_b, normed_b), (states_a, twice_a)]
    (send_maps,) = half_grads("grads_b_send", True, pairs, (1, 2))
    got = swap(send_maps, 1, "core")
    (keep,) = half_grads("grads_b_keep", False, pairs, (1, 2), time=9)
    message = halve(1, (keep, got))
    recv, message = after(recv, message)
    send_step(1, message)
    gdriven_a, gdecay_a = call(
        "back_chain", sz, back_chain_kernel, items, [ahead, behind, recv, params, ends, gstates_a, states_a],
        [((toks, 2 * states), BF), gdec], [enter, drv], limit=12, time=9)
    send_maps, terms = half_grads("grads_c_send", True, [(gdriven_a, normed_a)], (1,), [w_in_a])
    gdriven_a, send_maps = after(gdriven_a, send_maps)
    got = swap(send_maps, 1, "core")
    last_pieces = call(
        "back_leave", sz, back_leave_kernel, [], [params, gdriven_a, up_a, slope_a, hidden_a, w_in_a, perm, *out_pieces],
        [((2 * part, toks), BF)] * blocks, [rows_b, stacked], limit=12, time=3)
    last_pieces, gdriven_a, came[1] = after(last_pieces, gdriven_a, came[1])
    keep, more = half_grads("grads_c_keep", False, [(gdriven_a, normed_a)], (1,), [w_in_a], time=5)
    message = halve(2, (keep, got), (params, terms, more, ggain_b, gskip_a, gskip_b, gdecay_a, gdecay_b))
    early_sums = steps <= 2
    kept[0], message = after(kept[0], message)
    first_parts = over_planes("planes_a", [0]) if early_sums else []
    send_step(2, message)
    came[2], first_parts = after(came[2], first_parts)
    if not early_sums:
        first_parts = over_planes("planes_a", [0])
    for step in range(3, steps + 2):
        send_step(step, halve(step))
    parts = over_planes("planes", [1, 2])
    last_pieces, parts[0] = after(last_pieces, parts[0])
    early = [across(piece, 2 * dist, True) for dist, piece in enumerate(last_pieces[0::2])]
    parts[0], early = after(parts[0], early)
    sum_all, tiny = call(
        "sum", sz, partial(fold_plane_kernel, planes), [], [*first_parts, *parts],
        [((first_parts[0].shape[0] + parts[0].shape[0] - 16, LANES), BF), ((8, LANES), F32)], [])
    whole = swap_all([sum_all] * planes, "plane")
    late, _ = after(last_pieces[1::2], sum_all)
    late = [across(piece, 2 * dist + 1, True) for dist, piece in enumerate(late)]
    output, input_grad = spread([piece for pair in zip(early, late) for piece in pair])
    sum_all, tiny, output = after(sum_all, tiny, output)
    others = [swap(x, 1, "core") for x in (sum_all, tiny)]
    whole, others = after(whole, others)
    whole += [others[0], *(swap(x, 1, "core") for x in whole[1:])]
    tiny_other = others[1]
    small_out = ((layers, own), F32)
    grad_gain, grad_skip, grad_log, grad_imag, grad_step, grad_in, grad_out = call(
        "finish", sz, partial(finish_kernel, planes, ([(1, 1, 2)], [(0, 1, 1), (1, 0, 2)], [(0, 0, 1)])), [],
        [*whole, tiny, tiny_other, lambda_log, lambda_imag, log_step, input_map],
        [((layers, part), F32)] * 2 + [small_out] * 3 + [((layers, 2, own, width), F32), ((layers, 4, own, width), F32)],
        [tall_of(n * own) for n in (2, 3, 1)] + [((layers, 2, own, width), F32), ((LANES, LANES), F32)])
    return output, input_grad, grad_gain, grad_log, grad_imag, grad_step, grad_in, grad_out, grad_skip


def solution(mesh):
    rows, blocks = mesh.devices.shape
    inner = Mesh(mesh.devices.reshape(rows // 2, 2, blocks), ("plane", "core", "block"))
    dp = ("plane", "core")
    half = P(None, "block")
    maps = P(None, None, "block", None)
    acts = P(None, "block", dp)
    items = P(None, dp)
    return jax.shard_map(
        on_device,
        mesh=inner,
        in_specs=(acts, acts, items, items, half, half, half, half, maps, maps, half),
        out_specs=(acts, acts, half, half, half, half, maps, maps, half),
        check_vma=False,
    )
```

```python
from functools import partial
from typing import NamedTuple

import jax
import jax.numpy as jnp
from jax import lax
from jax.experimental import pallas as pl
from jax.experimental.pallas import tpu as pltpu
from jax.sharding import Mesh, PartitionSpec as P

EPSILON = 1e-05
SEGS = 16
LANES = 128
BF = jnp.bfloat16
F32 = jnp.float32
GELU_C = 0.7978845608028654
GELU_A = 0.044715
COST = 400_000_000


class Sizes(NamedTuple):
    blocks: int
    chunks: int
    toks: int
    run: int
    steps: int
    width: int
    states: int
    items: int


def turned(sz, index):
    return sz.blocks - 1 - index


def farthest(index, count):
    return count - index if index else 0


def place_of(sz, table):
    me, core = lax.axis_index("block"), lax.axis_index("core")
    q = lax.div(me, 2) * 2 + core
    mine, chunk = lax.div(q, sz.chunks), lax.rem(q, sz.chunks)
    out = [me, chunk, core, lax.axis_index("plane"), q]
    if table is not None:
        side = lax.rem(me, 2) ^ core
        for which in range(2):
            out += [table[side, which, mine, index] for index in range(sz.items)]
    return out


def nt(a, b):
    return lax.dot_general(a, b, (((1,), (1,)), ((), ())), preferred_element_type=F32)


def nn(a, b):
    return lax.dot_general(a, b, (((1,), (0,)), ((), ())), preferred_element_type=F32)


def tn(a, b):
    return lax.dot_general(a, b, (((0,), (0,)), ((), ())), preferred_element_type=F32)


def after(*values):
    return lax.optimization_barrier(values)


def cmul(ar, ai, br, bi):
    return ar * br - ai * bi, ar * bi + ai * br


def rows_of(step):
    return pl.ds(pl.multiple_of(step * SEGS, SEGS), SEGS)


def widen(mask, count):
    return jnp.concatenate([mask] * count, axis=1)


def item_of(sz, meta, index):
    begin = meta[5 + sz.items + index]
    return begin, begin + meta[5 + index]


def fill_masks(sz, meta, live, ahead, behind):
    base = meta[1] * sz.toks
    seg = lax.broadcasted_iota(jnp.int32, (SEGS, LANES), 0)

    def body(step, carry):
        pos = base + seg * sz.steps + step
        inside = jnp.zeros((SEGS, LANES), F32)
        onward = jnp.zeros((SEGS, LANES), F32)
        onward_next = jnp.zeros((SEGS, LANES), F32)
        for index in range(sz.items):
            begin, end = item_of(sz, meta, index)
            inside = jnp.where((pos >= begin) & (pos < end), 1.0, inside)
            onward = jnp.where((pos > begin) & (pos < end), 1.0, onward)
            onward_next = jnp.where((pos >= begin) & (pos + 1 < end), 1.0, onward_next)
        onward_next = jnp.where(pos + 1 < sz.run, onward_next, 0.0)
        live[rows_of(step), :] = inside
        ahead[rows_of(step), :] = onward
        behind[rows_of(step), :] = onward_next
        return carry

    lax.fori_loop(0, sz.steps, body, 0, unroll=4)


def through(sz, meta, first, length):
    ahead = behind = False
    for index in range(sz.items):
        begin, end = item_of(sz, meta, index)
        ahead = ahead | ((begin < first) & (end >= first + length))
        behind = behind | ((begin <= first) & (end > first + length))
    behind = behind & (first + length < sz.run)
    return ahead, behind


def power(pair, count):
    while count > 1:
        pair = cmul(*pair, *pair)
        count //= 2
    return pair


def column_blocks(sz, decay):
    out = []
    for q in range(sz.states // LANES):
        cols = slice(q * LANES, (q + 1) * LANES)
        out.append((decay[0:1, cols], decay[1:2, cols]))
    return out


def spread(pairs):
    return [tuple(jnp.broadcast_to(v, (SEGS, LANES)) for v in pair) for pair in pairs]


def chain_ends(sz, decay, ahead, behind, source, ahead_col, behind_col, ends):
    nq = sz.states // LANES
    d = spread(column_blocks(sz, decay))
    zero = jnp.zeros((SEGS, LANES), F32)

    def body(step, held):
        up, down = rows_of(step), rows_of(sz.steps - 1 - step)
        on_up, on_down = ahead[up, :], behind[down, :]
        new = []
        for q in range(nq):
            for side, (rows, on, col) in enumerate(((up, on_up, ahead_col), (down, on_down, behind_col))):
                re, im = held[2 * q + side]
                re, im = cmul(*d[q], re * on, im * on)
                re += source[rows, col + q * LANES : col + (q + 1) * LANES]
                im += source[rows, col + sz.states + q * LANES : col + sz.states + (q + 1) * LANES]
                new.append((re, im))
        return tuple(new)

    held = lax.fori_loop(0, sz.steps, body, tuple((zero, zero) for _ in range(2 * nq)), unroll=4)
    for q in range(nq):
        cols = slice(q * LANES, (q + 1) * LANES)
        for side in range(2):
            ends[2 * side, :, cols] = held[2 * q + side][0]
            ends[2 * side + 1, :, cols] = held[2 * q + side][1]


def enter_states(sz, meta, decay, ends, start, enter):
    pair = (decay[0:1, :], decay[1:2, :])
    jump = power(pair, sz.steps)
    base = meta[1] * sz.toks
    state = list(start)
    for count in range(SEGS):
        for side, seg in ((0, count), (1, SEGS - 1 - count)):
            re, im = state[side]
            enter[2 * side, seg : seg + 1, :] = re
            enter[2 * side + 1, seg : seg + 1, :] = im
            passes = through(sz, meta, base + seg * sz.steps, sz.steps)[side]
            gain = jnp.where(passes, 1.0, 0.0).astype(F32)
            re, im = cmul(jump[0] * gain, jump[1] * gain, re, im)
            state[side] = (
                re + ends[2 * side, seg : seg + 1, :],
                im + ends[2 * side + 1, seg : seg + 1, :],
            )
    return state


def send_ends(sz, meta, decay, ends, enter, send):
    zero = jnp.zeros((1, sz.states), F32)
    ahead, behind = enter_states(sz, meta, decay, ends, ((zero, zero), (zero, zero)), enter)
    me = meta[1]
    for dist in range(1, sz.chunks):
        up = (me ^ dist) > me
        for part in range(2):
            send[dist - 1, part : part + 1, :] = jnp.where(up, ahead[part], behind[part])


def received(sz, meta, decay, recv):
    me = meta[1]
    zero = jnp.zeros((1, sz.states), F32)
    pair = (decay[0:1, :], decay[1:2, :])
    jump = power(pair, sz.toks) if sz.chunks > 2 else None
    sides = []
    for side in range(2):
        re, im = zero, zero
        order = range(sz.chunks) if side == 0 else range(sz.chunks - 1, -1, -1)
        for other in order:
            use = (other < me) if side == 0 else (other > me)
            slot = jnp.maximum((me ^ other) - 1, 0)
            got = recv[slot]
            new_re, new_im = got[0:1, :], got[1:2, :]
            if sz.chunks > 2:
                passes = through(sz, meta, other * sz.toks, sz.toks)[side]
                gain = jnp.where(passes, 1.0, 0.0).astype(F32)
                moved = cmul(jump[0] * gain, jump[1] * gain, re, im)
                new_re, new_im = new_re + moved[0], new_im + moved[1]
            re, im = jnp.where(use, new_re, re), jnp.where(use, new_im, im)
        sides.append((re, im))
    return sides


def load_enter(sz, enter):
    held = []
    for q in range(sz.states // LANES):
        cols = slice(q * LANES, (q + 1) * LANES)
        for side in range(2):
            held.append((enter[2 * side, :, cols], enter[2 * side + 1, :, cols]))
    return tuple(held)


def chain_states(sz, decay, ahead, behind, source, enter, states):
    nq = sz.states // LANES
    n = sz.states
    d = spread(column_blocks(sz, decay))

    def body(step, held):
        up, down = rows_of(step), rows_of(sz.steps - 1 - step)
        on_up, on_down = ahead[up, :], behind[down, :]
        new = []
        for q in range(nq):
            for side, (rows, on) in enumerate(((up, on_up), (down, on_down))):
                re, im = held[2 * q + side]
                re, im = cmul(*d[q], re * on, im * on)
                lo = q * LANES
                re += source[rows, lo : lo + LANES]
                im += source[rows, n + lo : n + lo + LANES]
                at = 2 * side * n + lo
                states[rows, at : at + LANES] = re.astype(BF)
                states[rows, at + n : at + n + LANES] = (-im).astype(BF)
                new.append((re, im))
        return tuple(new)

    lax.fori_loop(0, sz.steps, body, load_enter(sz, enter), unroll=4)


def adjoint_chains(sz, decay, ahead, behind, source, enter, states, half, grad_driven, grad_decay):
    nq = sz.states // LANES
    n = sz.states
    d = spread(column_blocks(sz, decay))
    zero = jnp.zeros((SEGS, LANES), F32)

    def make(second):
        def body(step, carry):
            held, sums = carry
            up, down = rows_of(step), rows_of(sz.steps - 1 - step)
            on_up, on_down = ahead[up, :], behind[down, :]
            new, total = [], []
            for q in range(nq):
                lo = q * LANES
                acc_re, acc_im = sums[q]
                for side, (rows, on, src, st) in enumerate(((up, on_up, 2 * n, 2 * n), (down, on_down, 0, 0))):
                    re, im = held[2 * q + side]
                    re, im = re * on, im * on
                    s_re = states[rows, st + lo : st + lo + LANES].astype(F32)
                    s_im = states[rows, st + n + lo : st + n + lo + LANES].astype(F32)
                    acc_re += re * s_re + im * s_im
                    acc_im += re * s_im - im * s_re
                    re, im = cmul(*d[q], re, im)
                    re += source[rows, src + lo : src + lo + LANES]
                    im += source[rows, src + n + lo : src + n + lo + LANES]
                    new.append((re, im))
                    if second:
                        out_re = re + half[rows, lo : lo + LANES]
                        out_im = im + half[rows, n + lo : n + lo + LANES]
                        grad_driven[rows, lo : lo + LANES] = out_re.astype(BF)
                        grad_driven[rows, n + lo : n + lo + LANES] = (-out_im).astype(BF)
                    else:
                        half[rows, lo : lo + LANES] = re
                        half[rows, n + lo : n + lo + LANES] = im
                total.append((acc_re, acc_im))
            return tuple(new), tuple(total)

        return body

    carry = (load_enter(sz, enter), tuple((zero, zero) for _ in range(nq)))
    carry = lax.fori_loop(0, sz.steps // 2, make(False), carry, unroll=2)
    carry = lax.fori_loop(sz.steps // 2, sz.steps, make(True), carry, unroll=2)
    for q in range(nq):
        cols = slice(q * LANES, (q + 1) * LANES)
        grad_decay[0:1, cols] = jnp.sum(carry[1][q][0], axis=0, keepdims=True)
        grad_decay[1:2, cols] = jnp.sum(carry[1][q][1], axis=0, keepdims=True)


ROWS = 512


def row_parts(sz):
    size = min(ROWS, sz.toks)
    return [slice(lo, lo + size) for lo in range(0, sz.toks, size)]


def matmul_nt(a, b, out, tile=256):
    for lo in range(0, b.shape[0], tile):
        out[:, lo : lo + tile] = nt(a[...], b[lo : lo + tile, :]).astype(out.dtype)


def matmul_tn(a, b, out, tile=256):
    for lo in range(0, a.shape[1], tile):
        out[lo : lo + tile, :] = tn(a[:, lo : lo + tile], b[...]).astype(out.dtype)


def column_sum(x):
    return jnp.sum(x.reshape(x.shape[0] // 8, 8, x.shape[1]), axis=0)


def scale_of(u):
    return lax.rsqrt(jnp.mean(u * u, axis=1, keepdims=True) + EPSILON)


def normed_rows(sz, u, gain, on):
    return (u * scale_of(u) * gain * on).astype(BF)


def finish_rows(sz, rows, states, w_out, skip, normed, on, slope):
    pre = 2.0 * nn(states[rows, :], w_out[...]) + skip * normed[rows, :].astype(F32)
    square = pre * pre
    th = jnp.tanh(pre * (GELU_C + (GELU_C * GELU_A) * square))
    part = 0.5 + 0.5 * th
    deriv = part + pre * (1.0 - th * th) * (0.5 * GELU_C + (1.5 * GELU_C * GELU_A) * square)
    slope[rows, :] = (on * deriv).astype(slope.dtype)
    return on * (pre * part)


def enter_chunk(sz, meta, recv, decay, ends, enter):
    enter_states(sz, meta, decay, ends, received(sz, meta, decay, recv), enter)


def back_rows(sz, rows, grad_driven, w_in, upstream, slope, skip, hidden, gain):
    u = hidden[rows, :].astype(F32)
    r = upstream[rows, :]
    gn = nn(grad_driven[rows, :], w_in[...]) + r * slope[rows, :].astype(F32) * skip
    scale = scale_of(u)
    moved = u * scale
    dn = gn * gain
    inner = jnp.sum(dn * moved, axis=1, keepdims=True) * (1.0 / sz.width)
    return r + scale * (dn - moved * inner), column_sum(gn * moved)


def open_rows(sz, rows, r, slope, normed, w_out, twice, grad_states):
    e = r * slope[rows, :].astype(F32)
    low = e.astype(BF)
    double = low + low
    twice[rows, :] = double
    grad_states[rows, :] = nt(double, w_out[...])
    return column_sum(e * normed[rows, :].astype(F32))


def gain_of(params, layer):
    return params[layer : layer + 1, :]


def skip_of(params, layer):
    return params[2 + layer : 3 + layer, :]


def decay_of(sz, params, layer):
    return params[4 + 2 * layer : 6 + 2 * layer, 0 : sz.states]


def place_pieces(sz, meta, pieces, stacked):
    part = sz.width // sz.blocks
    for dist, piece in enumerate(pieces):
        owner = meta[4] ^ turned(sz, dist)
        stacked[pl.ds(pl.multiple_of(owner * part, part), part), :] = piece[0:part, :]


def cut_pieces(sz, meta, rows, perm, stacked, pieces):
    part = sz.width // sz.blocks
    matmul_tn(rows, perm, stacked)
    for dist, piece in enumerate(pieces):
        owner = meta[4] ^ turned(sz, dist)
        piece[...] = stacked[pl.ds(pl.multiple_of(owner * part, part), part), :]


def cut_kernel(sz, meta, whole, *refs):
    outs, wide, sems = refs[: sz.blocks], refs[-2], refs[-1]
    straight = whole.dtype == BF
    copies = []
    for dist in range(sz.blocks):
        to = meta[0] ^ turned(sz, dist)
        cols = pl.ds(pl.multiple_of(lax.rem(to, sz.chunks) * sz.toks, LANES), sz.toks)
        source = whole.at[lax.div(to, sz.chunks), :, cols]
        copy = pltpu.make_async_copy(source, outs[dist] if straight else wide.at[dist], sems.at[dist])
        copy.start()
        copies.append(copy)
    for dist, copy in enumerate(copies):
        copy.wait()
        if not straight:
            outs[dist][...] = wide[dist].astype(BF)


def discretize(lambda_log, lambda_imag, log_step):
    step_size = jnp.exp(log_step)
    lambda_real = -jnp.exp(lambda_log)
    modulus = jnp.exp(lambda_real * step_size)
    decay_real = modulus * jnp.cos(lambda_imag * step_size)
    decay_imag = modulus * jnp.sin(lambda_imag * step_size)
    denominator = lambda_real * lambda_real + lambda_imag * lambda_imag
    scale_real = ((decay_real - 1.0) * lambda_real + decay_imag * lambda_imag) / denominator
    scale_imag = (decay_imag * lambda_real - (decay_real - 1.0) * lambda_imag) / denominator
    return decay_real, decay_imag, scale_real, scale_imag


def first_rows(sz):
    part, own = sz.width // sz.blocks, sz.states // sz.blocks
    return part, part + own * sz.width // sz.toks


def half_map_parts(sz):
    top, end = first_rows(sz)
    rows = end - top
    for index in range(sz.toks // sz.width):
        yield slice(index * rows, (index + 1) * rows), slice(top, end), slice(index * sz.width, (index + 1) * sz.width)


def split3(x):
    hi = x.astype(BF).astype(F32)
    mid = (x - hi).astype(BF).astype(F32)
    return hi, mid, x - hi - mid


def prepare_kernel(sz, meta, tokens, *refs):
    inputs, refs = refs[:7], refs[7:]
    outs, refs = refs[: sz.blocks], refs[sz.blocks :]
    drive_b, half_b = refs[:2]
    held, small, lines, drive_a, sems = refs[2:9], refs[9], refs[10], refs[11], refs[12]
    top, end = first_rows(sz)
    own, part = sz.states // sz.blocks, sz.width // sz.blocks
    loads, copies = [], []
    for index, (source, target) in enumerate(zip(inputs, held)):
        loads.append(pltpu.make_async_copy(source, target, sems.at[index]))
    for dist in range(sz.blocks):
        to = meta[0] ^ turned(sz, dist)
        cols = pl.ds(pl.multiple_of(lax.rem(to, sz.chunks) * sz.toks, LANES), sz.toks)
        source = tokens.at[lax.div(to, sz.chunks), :, cols]
        copies.append(pltpu.make_async_copy(source, outs[dist].at[0:top, :], sems.at[len(inputs) + dist]))
    for copy in copies + loads:
        copy.start()
    for copy in loads[:6]:
        copy.wait()
    gain, skip, lambda_log, lambda_imag, log_step, input_map, output_map = held
    dr, di, sr, si = discretize(lambda_log[...], lambda_imag[...], log_step[...])
    small[...] = jnp.zeros_like(small)
    lines[...] = jnp.zeros_like(lines)
    small[0:2, 0:part] = gain[...]
    small[2:4, 0:part] = skip[...]
    for layer in range(2):
        small[4 + 2 * layer : 5 + 2 * layer, 0:own] = dr[layer : layer + 1]
        small[5 + 2 * layer : 6 + 2 * layer, 0:own] = di[layer : layer + 1]
    lines[0:2, 0:own] = sr
    lines[2:4, 0:own] = si
    cols = lines[...].T
    for layer in range(2):
        qr, qi = cols[0:own, layer : layer + 1], cols[0:own, 2 + layer : 3 + layer]
        br, bi = input_map[layer, 0].astype(F32), input_map[layer, 1].astype(F32)
        for index, value in enumerate((qr * br - qi * bi, qr * bi + qi * br)):
            (drive_a, drive_b)[layer][index] = value.astype(BF)
    rows = jnp.concatenate([*split3(small[...]), jnp.zeros((8, sz.toks - 3 * LANES), F32)], axis=1)
    rows = jnp.concatenate([rows, jnp.zeros((8, sz.toks), F32)], axis=0).astype(BF)
    for dist, out in enumerate(outs):
        half = lax.rem(meta[0] ^ turned(sz, dist), 2)
        for from_rows, to_rows, lanes in half_map_parts(sz):
            out[to_rows, lanes] = drive_a[half, from_rows, :]
        out[end:, :] = rows
    loads[6].wait()
    core = meta[2]
    for index in range(2):
        half_b[index] = output_map[0, 2 * core + index]
        half_b[3 + index] = output_map[1, 2 * core + index]
    half_b[2] = drive_b[core]
    for copy in copies:
        copy.wait()


def params_of(sz, piece):
    rows = piece[piece.shape[0] - 16 :, 0 : 3 * LANES].astype(F32)[0:8]
    return rows[:, 0:LANES] + rows[:, LANES : 2 * LANES] + rows[:, 2 * LANES :]


def join_kernel(sz, meta, *refs):
    pieces, maps, params = refs[: sz.blocks], refs[-2], refs[-1]
    own = sz.states // sz.blocks
    collect_params(sz, meta, [params_of(sz, piece) for piece in pieces], params)
    for dist, piece in enumerate(pieces):
        base = (meta[4] ^ turned(sz, dist)) * own
        for to_rows, from_rows, lanes in half_map_parts(sz):
            rows = pl.ds(pl.multiple_of(base + to_rows.start, 16), to_rows.stop - to_rows.start)
            maps[rows, :] = piece[from_rows, lanes]


def collect_params(sz, meta, smalls, params):
    own = sz.states // sz.blocks
    part = sz.width // sz.blocks
    lane = lax.broadcasted_iota(jnp.int32, (8, LANES), 1)
    row = lax.broadcasted_iota(jnp.int32, (8, LANES), 0)
    pad = jnp.zeros((8, sz.width - LANES), F32)
    total = jnp.zeros((8, sz.width), F32)
    for block in range(sz.blocks):
        piece = smalls[0]
        for dist in range(1, sz.blocks):
            piece = jnp.where((meta[4] ^ turned(sz, dist)) == block, smalls[dist], piece)
        for first, count, size in ((0, 4, part), (4, 4, own)):
            mine = jnp.where((row >= first) & (row < first + count) & (lane < size), piece, 0.0)
            wide = jnp.concatenate([mine, pad], axis=1)
            total += pltpu.roll(wide, block * size, 1) if block else wide
    params[...] = total


def place_maps(sz, meta, own_maps, mine, other, skip, out):
    own = sz.states // sz.blocks
    count = own_maps.shape[0] // 2

    def put(index, owner, value):
        out[pl.ds(pl.multiple_of(index * sz.states + owner * own, own), own), :] = value

    for index in range(2 * count):
        put(index, meta[0], own_maps[index])
    for side, pieces in ((meta[2], mine), (1 - meta[2], other)):
        for dist, piece in enumerate(pieces):
            for index in range(count):
                put(side * count + index, meta[0] ^ (dist + 1), piece[skip + index])


def open_kernel(sz, meta, perm, params, *refs):
    pieces, (hidden, normed, live, ahead, behind, stacked) = refs[: sz.blocks], refs[sz.blocks :]
    fill_masks(sz, meta, live, ahead, behind)
    place_pieces(sz, meta, pieces, stacked)
    gain = gain_of(params, 0)
    for rows in row_parts(sz):
        u = nt(perm[rows, :], stacked[...])
        hidden[rows, :] = u.astype(BF)
        normed[rows, :] = normed_rows(sz, u, gain, widen(live[rows, :], sz.width // LANES))


def enter_kernel(sz, meta, ahead, behind, params, normed, maps, other, w_in, driven, ends, send, enter):
    decay = decay_of(sz, params, 0)
    for side, half in ((meta[2], maps), (1 - meta[2], other)):
        w_in[pl.ds(pl.multiple_of(side * sz.states, sz.states), sz.states), :] = half[...]
    matmul_nt(normed, w_in, driven)
    chain_ends(sz, decay, ahead, behind, driven, 0, 0, ends)
    send_ends(sz, meta, decay, ends, enter, send)


def chain_kernel(sz, meta, ahead, behind, recv, params, ends, driven, states, enter):
    decay = decay_of(sz, params, 0)
    enter_chunk(sz, meta, recv, decay, ends, enter)
    chain_states(sz, decay, ahead, behind, driven, enter, states)


def middle_kernel(sz, meta, live, ahead, behind, states, params, normed, hidden, own_out, own_in, *refs):
    skip, gain_b, decay_b = skip_of(params, 0), gain_of(params, 1), decay_of(sz, params, 1)
    far = sz.blocks - 1
    mine, other, refs = refs[:far], refs[far : 2 * far], refs[2 * far :]
    w_out, w_in_b, slope, hidden_b, normed_b, driven_b, ends_b, send_b, enter = refs
    place_maps(sz, meta, own_out, mine, other, 0, w_out)
    place_maps(sz, meta, own_in, mine, other, 2, w_in_b)
    for rows in row_parts(sz):
        on = widen(live[rows, :], sz.width // LANES)
        u = hidden[rows, :].astype(F32) + finish_rows(sz, rows, states, w_out, skip, normed, on, slope)
        hidden_b[rows, :] = u
        v = normed_rows(sz, u, gain_b, on)
        normed_b[rows, :] = v
        driven_b[rows, :] = nt(v, w_in_b[...])
    chain_ends(sz, decay_b, ahead, behind, driven_b, 0, 0, ends_b)
    send_ends(sz, meta, decay_b, ends_b, enter, send_b)


def leave_kernel(sz, meta, live, ahead, behind, recv, params, ends, driven, normed, hidden, own_out, *refs):
    decay, skip = decay_of(sz, params, 1), skip_of(params, 1)
    far = sz.blocks - 1
    mine, other, refs = refs[:far], refs[far : 2 * far], refs[2 * far :]
    w_out, states, slope, last, enter = refs
    place_maps(sz, meta, own_out, mine, other, 3, w_out)
    enter_chunk(sz, meta, recv, decay, ends, enter)
    chain_states(sz, decay, ahead, behind, driven, enter, states)
    for rows in row_parts(sz):
        on = widen(live[rows, :], sz.width // LANES)
        last[rows, :] = (hidden[rows, :] + finish_rows(sz, rows, states, w_out, skip, normed, on, slope)).astype(BF)


def turn_kernel(sz, meta, ahead, behind, slope, normed, w_out, params, perm, *refs):
    decay = decay_of(sz, params, 1)
    pieces, refs = refs[: sz.blocks], refs[sz.blocks :]
    upstream, twice, grad_states, grad_skip, ends, send, stacked, enter = refs
    place_pieces(sz, meta, pieces, stacked)
    skips = []
    for rows in row_parts(sz):
        r = nt(perm[rows, :], stacked[...])
        upstream[rows, :] = r
        skips.append(open_rows(sz, rows, r, slope, normed, w_out, twice, grad_states))
    grad_skip[...] = jnp.sum(sum(skips), axis=0, keepdims=True)
    chain_ends(sz, decay, ahead, behind, grad_states, 2 * sz.states, 0, ends)
    send_ends(sz, meta, decay, ends, enter, send)


def back_middle_kernel(sz, meta, ahead, behind, recv, params, ends, grad_states, states, upstream, slope, hidden, w_in,
                       slope_b, normed_b, w_out_b,
                       grad_driven, grad_decay, grad_gain, upstream_b, twice_b, grad_states_b, grad_skip_b, ends_b, send_b,
                       enter, half):
    decay, skip, gain, decay_b = decay_of(sz, params, 1), skip_of(params, 1), gain_of(params, 1), decay_of(sz, params, 0)
    enter_chunk(sz, meta, recv, decay, ends, enter)
    adjoint_chains(sz, decay, ahead, behind, grad_states, enter, states, half, grad_driven, grad_decay)
    gains, skips = [], []
    for rows in row_parts(sz):
        r, terms = back_rows(sz, rows, grad_driven, w_in, upstream, slope, skip, hidden, gain)
        gains.append(terms)
        upstream_b[rows, :] = r
        skips.append(open_rows(sz, rows, r, slope_b, normed_b, w_out_b, twice_b, grad_states_b))
    grad_gain[...] = jnp.sum(sum(gains), axis=0, keepdims=True)
    grad_skip_b[...] = jnp.sum(sum(skips), axis=0, keepdims=True)
    chain_ends(sz, decay_b, ahead, behind, grad_states_b, 2 * sz.states, 0, ends_b)
    send_ends(sz, meta, decay_b, ends_b, enter, send_b)


def back_chain_kernel(sz, meta, ahead, behind, recv, params, ends, grad_states, states, grad_driven, grad_decay, enter, half):
    decay = decay_of(sz, params, 0)
    enter_chunk(sz, meta, recv, decay, ends, enter)
    adjoint_chains(sz, decay, ahead, behind, grad_states, enter, states, half, grad_driven, grad_decay)


def back_leave_kernel(sz, meta, params, grad_driven, upstream, slope, hidden, w_in, perm, done, *refs):
    skip, gain = skip_of(params, 0), gain_of(params, 0)
    pieces, (last, stacked) = refs[: sz.blocks], refs[sz.blocks :]
    for rows in row_parts(sz):
        r, _ = back_rows(sz, rows, grad_driven, w_in, upstream, slope, skip, hidden, gain)
        last[rows, :] = r.astype(BF)
    part = sz.width // sz.blocks
    cut_pieces(sz, meta, done, perm, stacked, [piece.at[0:part, :] for piece in pieces])
    cut_pieces(sz, meta, last, perm, stacked, [piece.at[part : 2 * part, :] for piece in pieces])


def weight_kernel(counts, other, sz, meta, *refs):
    half = 1 - meta[2] if other else meta[2]
    pairs = 2 * len(counts)
    out, at = refs[pairs], 0
    if len(refs) > pairs + 1:
        whole, out, terms = refs[pairs:]
        value = tn(refs[0][:, pl.ds(pl.multiple_of(half * sz.states, LANES), sz.states)], refs[1][...])
        out[...] = value.astype(out.dtype)
        rows = whole[pl.ds(pl.multiple_of(half * sz.states, sz.states), sz.states), :].astype(F32)
        terms[...] = jnp.sum(column_sum(rows * value), axis=0, keepdims=True)
        return
    for index, count in enumerate(counts):
        left, right = refs[2 * index], refs[2 * index + 1]
        for group in range(count):
            cols = pl.ds(pl.multiple_of((half * count + group) * sz.states, LANES), sz.states)
            out[at : at + sz.states, :] = tn(left[:, cols], right[...]).astype(out.dtype)
            at += sz.states


def split2(x):
    hi = x.astype(BF).astype(F32)
    return hi, x - hi


class Group(NamedTuple):
    first: int
    counts: tuple

    def rows(self, sz):
        return sum(self.counts) * (sz.states // sz.blocks)


def bits_of(sz):
    return sz.blocks.bit_length() - 1


def step_bit(sz, step, core):
    return 1 << ((step + core) % bits_of(sz))


def far_block(sz, group, slot, core):
    return sum(step_bit(sz, group.first + j, core) for j in range(bits_of(sz)) if (slot >> j) & 1)


def own_tiny(sz, params, terms, more, gain_b, skip_a, skip_b, decay_a, decay_b, tiny):
    gain_a = (terms[...] + more[...] + skip_of(params, 0) * skip_a[...]) / gain_of(params, 0)
    tiny[...] = jnp.zeros_like(tiny)
    for index, line in enumerate((gain_a, gain_b[...], skip_a[...], skip_b[...])):
        tiny[index : index + 1, :] = line
    tiny[4:6, 0 : sz.states] = decay_a[...]
    tiny[6:8, 0 : sz.states] = decay_b[...]
    return tiny[...]


def tiny_of(sz, tiny, owner):
    own, part = sz.states // sz.blocks, sz.width // sz.blocks
    row = lax.broadcasted_iota(jnp.int32, (8, LANES), 0)
    lane = lax.broadcasted_iota(jnp.int32, (8, LANES), 1)
    value = jnp.zeros((8, LANES), F32)
    for block in range(sz.blocks):
        wide = pltpu.roll(tiny, sz.width - block * part, 1) if block else tiny
        deep = pltpu.roll(tiny, sz.width - block * own, 1) if block else tiny
        mine = jnp.where(row < 4, jnp.where(lane < part, wide[:, :LANES], 0.0), jnp.where(lane < own, deep[:, :LANES], 0.0))
        value = jnp.where(owner == block, mine, value)
    return value


def put_sums(value, slot, kept, message, at):
    if slot % 2 == 0:
        kept[slot // 2] = value
        return at
    message[at : at + value.shape[0], :] = value.astype(BF)
    return at + value.shape[0]


def add_message(sz, group, kept, slot, message, at):
    return kept[slot] + message[at : at + group.rows(sz), :].astype(F32)


def step_kernel(old, new, sz, meta, *refs):
    came, refs = (refs[0], refs[1:]) if old else (None, refs)
    held, refs = refs[: len(old)], refs[len(old) :]
    if new:
        halves, refs = refs[: 2 * len(new.counts)], refs[2 * len(new.counts) :]
    keeps, message = refs[:-1], refs[-1]
    at = 0
    for (group, slots, row), kept, keep in zip(old, held, keeps):
        for slot in range(slots):
            value = add_message(sz, group, kept, slot, came, row + slot * group.rows(sz))
            at = put_sums(value, slot, keep, message, at)
    if new:
        own = sz.states // sz.blocks
        for slot in range(sz.blocks):
            owner = meta[0] ^ jnp.where(meta[2] == 0, far_block(sz, new, slot, 0), far_block(sz, new, slot, 1))
            parts = []
            for index, count in enumerate(new.counts):
                keep, got = halves[2 * index], halves[2 * index + 1]
                for one in range(count):
                    rows = pl.ds(pl.multiple_of(one * sz.states + owner * own, own), own)
                    parts.append(keep[rows, :].astype(F32) + got[rows, :].astype(F32))
            at = put_sums(jnp.concatenate(parts, axis=0), slot, keeps[-1], message, at)


def direct_kernel(group, sz, meta, keep, got, *refs):
    own = sz.states // sz.blocks
    lines, pieces, room = refs[:8], refs[8:-1], refs[-1]
    whole = own_tiny(sz, *lines, room)
    for index, piece in enumerate(pieces):
        owner = meta[0] ^ farthest(index, sz.blocks)
        rows = pl.ds(pl.multiple_of(owner * own, own), own)
        piece[0:own, :] = (keep[rows, :].astype(F32) + got[rows, :].astype(F32)).astype(BF)
        rest = jnp.zeros((8, sz.width - 2 * LANES), F32)
        wide = jnp.concatenate([*split2(tiny_of(sz, whole, owner)), rest], axis=1)
        piece[own : own + 16, :] = jnp.concatenate([wide, jnp.zeros_like(wide)], axis=0).astype(BF)


def fold_block_kernel(planes, groups, direct, sz, meta, *refs):
    lanes = sz.width // LANES
    held, refs = refs[: 2 * len(groups)], refs[2 * len(groups) :]
    pieces, refs = (refs[: sz.blocks], refs[sz.blocks :]) if direct else ((), refs)
    outs, talls = refs[:planes], refs[planes:]
    totals = [add_message(sz, group, held[2 * index], 0, held[2 * index + 1], row) for index, (group, row) in enumerate(groups)]
    if direct:
        total = pieces[0][...].astype(F32)
        for piece in pieces[1:]:
            total += piece[...].astype(F32)
        rows = total.shape[0] - 16
        totals.append(total[0:rows])
        tiny = total[rows : rows + 8, 0:LANES] + total[rows : rows + 8, LANES : 2 * LANES]
    at = 0
    for total, tall in zip(totals, talls):
        rows = total.shape[0]
        padded = tall.shape[0] // lanes
        for block in range(lanes):
            tall[block * padded : block * padded + rows, :] = total[:, block * LANES : (block + 1) * LANES].astype(BF)
            if padded > rows:
                tall[block * padded + rows : (block + 1) * padded, :] = jnp.zeros((padded - rows, LANES), BF)
        part = tall.shape[0] // planes
        for dist, out in enumerate(outs):
            out[at : at + part, :] = tall[pl.ds(pl.multiple_of((meta[3] ^ farthest(dist, planes)) * part, part), part), :]
        at += part
    if direct:
        rows = jnp.concatenate(split2(tiny), axis=0).astype(BF)
        for out in outs:
            out[at : at + 16, :] = rows


def fold_plane_kernel(early, sz, meta, *refs):
    parts, out, tiny = refs[early:-2], refs[-2], refs[-1]
    top = 0
    if early:
        total = refs[0][...].astype(F32)
        for piece in refs[1:early]:
            total += piece[...].astype(F32)
        top = total.shape[0]
        out[0:top, :] = total.astype(BF)
    total = parts[0][...].astype(F32)
    for piece in parts[1:]:
        total += piece[...].astype(F32)
    rows = total.shape[0] - 16
    out[top:, :] = total[0:rows].astype(BF)
    tiny[...] = total[rows : rows + 8] + total[rows + 8 :]


def finish_kernel(planes, groups, sz, meta, *refs):
    count = 2 * planes
    pieces, refs = refs[:count], refs[count:]
    tiny, lambda_log, lambda_imag, log_step, input_map = refs[0][...] + refs[1][...], *refs[2:6]
    grad_gain, grad_skip, grad_log, grad_imag, grad_step, grad_maps, grad_out = refs[6:13]
    talls, grad_in, lines = refs[13:-2], refs[-2], refs[-1]
    own = sz.states // sz.blocks
    lanes = sz.width // LANES
    start = 0
    for tall, group in zip(talls, groups):
        padded = tall.shape[0] // lanes
        part = tall.shape[0] // planes
        for side in range(2):
            half = meta[2] ^ side
            for dist in range(planes):
                rows = pl.ds(pl.multiple_of((meta[3] ^ farthest(dist, planes)) * part, part), part)
                tall[rows, :] = pieces[side * planes + dist][start : start + part, :]
            at = 0
            for which, layer, maps in group:
                out = grad_in if which == 0 else grad_out
                for one in range(maps):
                    for block in range(lanes):
                        rows = slice(block * padded + at, block * padded + at + own)
                        out[layer, half * maps + one, :, block * LANES : (block + 1) * LANES] = tall[rows, :].astype(F32)
                    at += own
        start += part
    width = sz.width // sz.blocks
    grad_gain[...] = tiny[0:2, 0:width]
    grad_skip[...] = tiny[2:4, 0:width]
    dr, di, sr, si = discretize(lambda_log[...], lambda_imag[...], log_step[...])
    lines[...] = jnp.zeros_like(lines)
    lines[0:2, 0:own] = sr
    lines[2:4, 0:own] = si
    cols = lines[...].T
    back = []
    for layer in range(2):
        qr, qi = cols[0:own, layer : layer + 1], cols[0:own, 2 + layer : 3 + layer]
        wr, wi = grad_in[layer, 0], grad_in[layer, 1]
        br, bi = input_map[layer, 0].astype(F32), input_map[layer, 1].astype(F32)
        grad_maps[layer, 0] = qr * wr + qi * wi
        grad_maps[layer, 1] = qr * wi - qi * wr
        back.append(jnp.sum(wr * br + wi * bi, axis=1, keepdims=True))
        back.append(jnp.sum(wi * br - wr * bi, axis=1, keepdims=True))
    lines[...] = jnp.zeros_like(lines)
    for index, col in enumerate(back):
        lines[0:own, index : index + 1] = col
    rows = lines[...].T
    step = jnp.exp(log_step[...])
    lr, li = -jnp.exp(lambda_log[...]), lambda_imag[...]
    norm = 1.0 / (lr * lr + li * li)
    for layer in range(2):
        at = slice(layer, layer + 1)
        a, b, h = (lr[at], li[at]), (dr[at], di[at]), step[at]
        gq = rows[2 * layer : 2 * layer + 1, 0:own], rows[2 * layer + 1 : 2 * layer + 2, 0:own]
        gd = tiny[4 + 2 * layer : 5 + 2 * layer, 0:own], tiny[5 + 2 * layer : 6 + 2 * layer, 0:own]
        inverse = a[0] * norm[at], -a[1] * norm[at]
        through = cmul(inverse[0], -inverse[1], *gq)
        gd = gd[0] + through[0], gd[1] + through[1]
        ratio = cmul(*inverse, sr[at], si[at])
        direct = cmul(ratio[0], -ratio[1], *gq)
        moved = cmul(b[0] * h, -b[1] * h, *gd)
        turn = cmul(*a, *b)
        grad_log[at, :] = (moved[0] - direct[0]) * a[0]
        grad_imag[at, :] = moved[1] - direct[1]
        grad_step[at, :] = (turn[0] * gd[0] + turn[1] * gd[1]) * h


def spread_kernel(sz, meta, *refs):
    pieces, outs, wide, sems = refs[: sz.blocks], refs[sz.blocks : -2], refs[-2], refs[-1]
    part = sz.width // sz.blocks
    copies = []
    for dist, piece in enumerate(pieces):
        owner = meta[0] ^ turned(sz, dist)
        for index, out in enumerate(outs):
            slot = dist * len(outs) + index
            wide[slot] = piece[index * part : (index + 1) * part, :].astype(F32)
            cols = pl.ds(pl.multiple_of(lax.rem(owner, sz.chunks) * sz.toks, LANES), sz.toks)
            copy = pltpu.make_async_copy(wide.at[slot], out.at[lax.div(owner, sz.chunks), :, cols], sems.at[slot])
            copy.start()
            copies.append(copy)
    for copy in copies:
        copy.wait()


VMEM = pl.BlockSpec(memory_space=pltpu.VMEM)
SMEM = pl.BlockSpec(memory_space=pltpu.SMEM)
HBM = pl.BlockSpec(memory_space=pltpu.HBM)


def call(name, sz, body, items, args, outs, scratch, limit=10, in_spec=VMEM, out_spec=VMEM, time=0.0):
    out_shape = [jax.ShapeDtypeStruct(shape, dtype) for shape, dtype in outs]

    def kernel(*refs):
        body(sz, place_of(sz, refs[0] if items else None), *refs[len(items) :])

    return pl.pallas_call(
        kernel,
        out_shape=out_shape,
        in_specs=[SMEM] * len(items) + [in_spec] * len(args),
        out_specs=[out_spec] * len(outs),
        scratch_shapes=[pltpu.VMEM(*item) if isinstance(item, tuple) else item for item in scratch],
        compiler_params=pltpu.CompilerParams(vmem_limit_bytes=limit << 20),
        cost_estimate=pl.CostEstimate(flops=int(COST * time), bytes_accessed=1000, transcendentals=0),
        name=name,
    )(*items, *args)


def on_device(tokens, cotangent, item_lengths, item_offsets, norm_gain, lambda_log, lambda_imag, log_step, input_map, output_map, skip_weight):
    micro, part, run = tokens.shape
    layers = norm_gain.shape[0]
    blocks = lax.axis_size("block")
    planes = lax.axis_size("plane")
    chunks = blocks // micro
    toks = run // chunks
    own = lambda_log.shape[1]
    width, states = part * blocks, own * blocks
    sz = Sizes(blocks, chunks, toks, run, toks // SEGS, width, states, item_lengths.shape[1])

    def swap(x, dist, axis="block"):
        return lax.ppermute(x, axis, [(i, i ^ dist) for i in range(lax.axis_size(axis))])

    def across(x, dist, back):
        pairs = []
        for c in range(2):
            for b in range(blocks):
                q = b ^ turned(sz, dist)
                pairs.append((c * blocks + b, (q % 2) * blocks + (q // 2) * 2 + c))
        return lax.ppermute(x, ("core", "block"), [pair[::-1] for pair in pairs] if back else pairs)

    def across_all(pieces, back=False):
        return [across(piece, dist, back) for dist, piece in enumerate(pieces)]

    table = jnp.stack([item_lengths, item_offsets])
    items = [jnp.stack([table, swap(table, 1, "core")])]

    def neighbour(x, dist):
        pairs = []
        for c in range(2):
            for b in range(blocks):
                q = ((b // 2) * 2 + c) ^ dist
                pairs.append((c * blocks + b, (q % 2) * blocks + (q // 2) * 2 + b % 2))
        return lax.ppermute(x, ("core", "block"), pairs)

    def swap_all(pieces, axis="block"):
        count = len(pieces)
        return [swap(piece, farthest(index, count), axis) if index else piece for index, piece in enumerate(pieces)]

    def exchange(send):
        return jnp.stack([neighbour(send[dist - 1], dist) for dist in range(1, chunks)])

    row = jnp.arange(toks, dtype=jnp.int32)[:, None]
    col = jnp.arange(toks, dtype=jnp.int32)[None, :]
    perm = ((row % SEGS) * sz.steps + row // SEGS == col).astype(BF)

    maps_own = ((2, own, width), BF)
    half_own = ((5, own, width), BF)
    given = [norm_gain, skip_weight, lambda_log, lambda_imag, log_step, input_map, output_map]
    *first_pieces, drive_b, half_b = call(
        "prepare", sz, prepare_kernel, [], [pltpu.with_memory_space_constraint(x, pltpu.HBM) for x in [tokens, *given]],
        [((first_rows(sz)[1] + 16, toks), BF)] * blocks + [maps_own, half_own],
        [(x.shape, x.dtype) for x in given] + [((8, LANES), F32), ((8, LANES), F32), maps_own, pltpu.SemaphoreType.DMA((len(given) + blocks,))],
        limit=6, in_spec=HBM)
    first_pieces = across_all(first_pieces)
    cot_cut = call("cut_cotangent", sz, cut_kernel, [], [pltpu.with_memory_space_constraint(cotangent, pltpu.HBM)],
                   [((part, toks), BF)] * blocks, [((blocks, part, toks), F32), pltpu.SemaphoreType.DMA((blocks,))], limit=4, in_spec=HBM)
    half_b, first_pieces[1], perm, cot_cut = after(half_b, first_pieces[1], perm, cot_cut)
    maps_a, params = call("join", sz, join_kernel, [], first_pieces, [((states, width), BF), ((8, width), F32)], [])
    second_mine = [swap(half_b, dist) for dist in range(1, blocks)]

    mask = ((toks, LANES), F32)
    enter = ((4, SEGS, states), F32)
    stacked = ((width, toks), BF)
    rows_f, rows_b = ((toks, width), F32), ((toks, width), BF)
    drv = ((toks, 2 * states), F32)
    sts = ((toks, 4 * states), BF)
    gst = ((toks, 4 * states), F32)
    snd = ((chunks - 1, 2, states), F32)
    w_in, w_out = ((2 * states, width), BF), ((4 * states, width), BF)
    line, gdec = ((1, width), F32), ((2, states), F32)
    piece_out = [((part, toks), BF)] * blocks

    other_a = swap(maps_a, 1, "core")
    hidden_a, normed_a, live, ahead, behind = call(
        "open", sz, open_kernel, items, [perm, params, *first_pieces], [rows_b, rows_b, mask, mask, mask], [stacked], time=3)
    w_in_a, driven_a, ends_a, send_a = call(
        "enter", sz, enter_kernel, items, [ahead, behind, params, normed_a, maps_a, other_a], [w_in, drv, enter, snd], [enter])
    recv = exchange(send_a)
    (states_a,) = call("chain", sz, chain_kernel, items, [ahead, behind, recv, params, ends_a, driven_a], [sts], [enter])
    second_mine, states_a = after(second_mine, states_a)
    second_maps = second_mine, [swap(piece, 1, "core") for piece in second_mine]
    cot_cut, _ = after(cot_cut, recv)
    cot_pieces = across_all(cot_cut)
    w_out_a, w_in_b, slope_a, hidden_b, normed_b, driven_b, ends_b, send_b = call(
        "middle", sz, middle_kernel, items,
        [live, ahead, behind, states_a, params, normed_a, hidden_a, output_map[0], drive_b, *second_maps[0], *second_maps[1]],
        [w_out, w_in, rows_b, rows_f, rows_b, drv, enter, snd], [enter], time=11)
    recv = exchange(send_b)
    w_out_b, states_b, slope_b, last_b = call(
        "leave", sz, leave_kernel, items,
        [live, ahead, behind, recv, params, ends_b, driven_b, normed_b, hidden_b, output_map[1], *second_maps[0], *second_maps[1]],
        [w_out, sts, rows_b, rows_b], [enter])

    def half_grads(name, other, pairs, counts, more=(), time=0.0):
        args = [x for pair in pairs for x in pair]
        outs = [((sum(counts) * states, width), BF)] + [line] * len(more)
        return call(name, sz, partial(weight_kernel, counts, other), [], [*args, *more], outs, [], time=time)

    groups = [Group(0, (2,)), Group(1, (3,))]
    steps = bits_of(sz)
    kept, came, place = {}, {}, {}

    def halve(step, halves=()):
        old, args = [], []
        for index, group in enumerate(groups):
            if 0 < step - group.first < steps:
                slots = 1 << (steps - (step - group.first))
                old.append((group, slots, place[step - 1, index]))
                args.append(kept[index])
        if old:
            args.insert(0, came[step - 1])
        new = groups[step] if step < len(groups) else None
        outs, at = [], 0
        for index, group in enumerate(groups):
            if 0 <= step - group.first < steps:
                slots = 1 << (steps - 1 - (step - group.first))
                outs.append((index, ((slots, group.rows(sz), width), F32)))
                place[step, index] = at
                at += slots * group.rows(sz)
        results = call("halve_%d" % step, sz, partial(step_kernel, old, new), [], [*args, *halves],
                       [shape for _, shape in outs] + [((at, width), BF)], [])
        for (index, _), value in zip(outs, results):
            kept[index] = value
        return results[-1]

    def send_step(step, message):
        pairs = [(c * blocks + b, c * blocks + (b ^ step_bit(sz, step, c))) for c in range(2) for b in range(blocks)]
        came[step] = lax.ppermute(message, ("core", "block"), pairs)

    def spread(pieces):
        return call("spread", sz, spread_kernel, [], pieces, [((micro, part, run), F32)] * 2,
                    [((2 * blocks, part, toks), F32), pltpu.SemaphoreType.DMA((2 * blocks,))], limit=6, out_spec=HBM, time=9)

    lanes = width // LANES

    def tall_of(rows):
        step = max(SEGS * planes // lanes, SEGS)
        return ((lanes * (-(-rows // step) * step), LANES), BF)

    def over_planes(name, which, direct=()):
        ends = [(groups[index], place[groups[index].first + steps - 1, index]) for index in which]
        talls = [tall_of(group.rows(sz)) for group, _ in ends] + [tall_of(own)] * bool(direct)
        cut = sum(t[0][0] for t in talls) // planes + (16 if direct else 0)
        args = [x for index in which for x in (kept[index], came[groups[index].first + steps - 1])]
        return swap_all(call(name, sz, partial(fold_block_kernel, planes, ends, bool(direct)), [], [*args, *direct],
                             [((cut, LANES), BF)] * planes, talls), "plane")

    up_b, twice_b, gstates_b, gskip_b, ends, send = call(
        "turn", sz, turn_kernel, items, [ahead, behind, slope_b, normed_b, w_out_b, params, perm, *cot_pieces],
        [rows_f, rows_b, gst, line, enter, snd], [stacked, enter], time=6)
    recv = exchange(send)
    pairs = [(states_b, twice_b)]
    (send_maps,) = half_grads("grads_a_send", True, pairs, (2,))
    got = swap(send_maps, 1, "core")
    (keep,) = half_grads("grads_a_keep", False, pairs, (2,), time=2)
    message = halve(0, (keep, got))
    recv, message = after(recv, message)
    send_step(0, message)
    gdriven_b, gdecay_b, ggain_b, up_a, twice_a, gstates_a, gskip_a, ends, send = call(
        "back_middle", sz, back_middle_kernel, items,
        [ahead, behind, recv, params, ends, gstates_b, states_b, up_b, slope_b, hidden_b, w_in_b, slope_a, normed_a, w_out_a],
        [((toks, 2 * states), BF), gdec, line, rows_f, rows_b, gst, line, enter, snd], [enter, drv], limit=12, time=11)
    recv = exchange(send)
    gdriven_b, came[0] = after(gdriven_b, came[0])
    pairs = [(gdriven_b, normed_b), (states_a, twice_a)]
    (send_maps,) = half_grads("grads_b_send", True, pairs, (1, 2))
    got = swap(send_maps, 1, "core")
    (keep,) = half_grads("grads_b_keep", False, pairs, (1, 2), time=9)
    message = halve(1, (keep, got))
    recv, message = after(recv, message)
    send_step(1, message)
    gdriven_a, gdecay_a = call(
        "back_chain", sz, back_chain_kernel, items, [ahead, behind, recv, params, ends, gstates_a, states_a],
        [((toks, 2 * states), BF), gdec], [enter, drv], limit=12, time=9)
    send_maps, terms = half_grads("grads_c_send", True, [(gdriven_a, normed_a)], (1,), [w_in_a])
    gdriven_a, send_maps = after(gdriven_a, send_maps)
    got = swap(send_maps, 1, "core")
    keep, more = half_grads("grads_c_keep", False, [(gdriven_a, normed_a)], (1,), [w_in_a], time=0)
    sums_c = list(call(
        "direct", sz, partial(direct_kernel, None), [],
        [keep, got, params, terms, more, ggain_b, gskip_a, gskip_b, gdecay_a, gdecay_b], [((own + 16, width), BF)] * blocks, [((8, width), F32)]))
    gdriven_a, sums_c[0] = after(gdriven_a, sums_c[0])
    sums_c = swap_all(sums_c)
    last_pieces = call(
        "back_leave", sz, back_leave_kernel, [], [params, gdriven_a, up_a, slope_a, hidden_a, w_in_a, perm, last_b],
        [((2 * part, toks), BF)] * blocks, [rows_b, stacked], limit=12, time=6)
    last_pieces, came[1], sums_c = after(last_pieces, came[1], sums_c)
    message = halve(2)
    kept[0], message = after(kept[0], message)
    first_parts = over_planes("planes_a", [0]) if steps <= 2 else []
    send_step(2, message)
    if first_parts:
        came[2], first_parts = after(came[2], first_parts)
    for step in range(3, steps + 1):
        send_step(step, halve(step))
    parts = over_planes("planes", [1] if first_parts else [0, 1], sums_c)
    last_pieces, parts[0] = after(last_pieces, parts[0])
    early = [across(piece, 2 * dist, True) for dist, piece in enumerate(last_pieces[0::2])]
    parts[0], early = after(parts[0], early)
    sum_all, tiny = call(
        "sum", sz, partial(fold_plane_kernel, len(first_parts)), [], [*first_parts, *parts],
        [((sum(x[0].shape[0] for x in (first_parts, parts) if x) - 16, LANES), BF), ((8, LANES), F32)], [])
    whole = swap_all([sum_all] * planes, "plane")
    late, _ = after(last_pieces[1::2], sum_all)
    late = [across(piece, 2 * dist + 1, True) for dist, piece in enumerate(late)]
    whole = swap_all([sum_all] * planes, "plane")
    late, others = after(late, [sum_all, tiny, *whole[planes - 0 :]])
    others = [swap(x, 1, "core") for x in others]
    output, input_grad = spread([piece for pair in zip(early, late) for piece in pair])
    far = whole[1 : planes - 0]
    far, others, output = after(far, others, output)
    far = [swap(x, 1, "core") for x in far]
    whole += [others[0], *far, *others[2:]]
    tiny_other = others[1]
    small_out = ((layers, own), F32)
    grad_gain, grad_skip, grad_log, grad_imag, grad_step, grad_in, grad_out = call(
        "finish", sz, partial(finish_kernel, planes, ([(1, 1, 2)], [(0, 1, 1), (1, 0, 2)], [(0, 0, 1)])), [],
        [*whole, tiny, tiny_other, lambda_log, lambda_imag, log_step, input_map],
        [((layers, part), F32)] * 2 + [small_out] * 3 + [((layers, 2, own, width), F32), ((layers, 4, own, width), F32)],
        [tall_of(n * own) for n in (2, 3, 1)] + [((layers, 2, own, width), F32), ((LANES, LANES), F32)])
    return output, input_grad, grad_gain, grad_log, grad_imag, grad_step, grad_in, grad_out, grad_skip


def solution(mesh):
    rows, blocks = mesh.devices.shape
    inner = Mesh(mesh.devices.reshape(rows // 2, 2, blocks), ("plane", "core", "block"))
    dp = ("plane", "core")
    half = P(None, "block")
    maps = P(None, None, "block", None)
    acts = P(None, "block", dp)
    items = P(None, dp)
    return jax.shard_map(
        on_device,
        mesh=inner,
        in_specs=(acts, acts, items, items, half, half, half, half, maps, maps, half),
        out_specs=(acts, acts, half, half, half, half, maps, maps, half),
        check_vma=False,
    )
```

```python
from functools import partial
from typing import NamedTuple

import jax
import jax.numpy as jnp
from jax import lax
from jax.experimental import pallas as pl
from jax.experimental.pallas import tpu as pltpu
from jax.sharding import Mesh, PartitionSpec as P

EPSILON = 1e-05
SEGS = 16
LANES = 128
BF = jnp.bfloat16
F32 = jnp.float32
GELU_C = 0.7978845608028654
GELU_A = 0.044715
COST = 400_000_000


class Sizes(NamedTuple):
    blocks: int
    chunks: int
    toks: int
    run: int
    steps: int
    width: int
    states: int
    items: int


def turned(sz, index):
    return sz.blocks - 1 - index


def farthest(index, count):
    return count - index if index else 0


def place_of(sz, table):
    me, core = lax.axis_index("block"), lax.axis_index("core")
    q = lax.div(me, 2) * 2 + core
    mine, chunk = lax.div(q, sz.chunks), lax.rem(q, sz.chunks)
    out = [me, chunk, core, lax.axis_index("plane"), q]
    if table is not None:
        side = lax.rem(me, 2) ^ core
        for which in range(2):
            out += [table[side, which, mine, index] for index in range(sz.items)]
    return out


def nt(a, b):
    return lax.dot_general(a, b, (((1,), (1,)), ((), ())), preferred_element_type=F32)


def nn(a, b):
    return lax.dot_general(a, b, (((1,), (0,)), ((), ())), preferred_element_type=F32)


def tn(a, b):
    return lax.dot_general(a, b, (((0,), (0,)), ((), ())), preferred_element_type=F32)


def after(*values):
    return lax.optimization_barrier(values)


def cmul(ar, ai, br, bi):
    return ar * br - ai * bi, ar * bi + ai * br


def rows_of(step):
    return pl.ds(pl.multiple_of(step * SEGS, SEGS), SEGS)


def widen(mask, count):
    return jnp.concatenate([mask] * count, axis=1)


def item_of(sz, meta, index):
    begin = meta[5 + sz.items + index]
    return begin, begin + meta[5 + index]


def fill_masks(sz, meta, live, ahead, behind):
    base = meta[1] * sz.toks
    seg = lax.broadcasted_iota(jnp.int32, (SEGS, LANES), 0)

    def body(step, carry):
        pos = base + seg * sz.steps + step
        inside = jnp.zeros((SEGS, LANES), F32)
        onward = jnp.zeros((SEGS, LANES), F32)
        onward_next = jnp.zeros((SEGS, LANES), F32)
        for index in range(sz.items):
            begin, end = item_of(sz, meta, index)
            inside = jnp.where((pos >= begin) & (pos < end), 1.0, inside)
            onward = jnp.where((pos > begin) & (pos < end), 1.0, onward)
            onward_next = jnp.where((pos >= begin) & (pos + 1 < end), 1.0, onward_next)
        onward_next = jnp.where(pos + 1 < sz.run, onward_next, 0.0)
        live[rows_of(step), :] = inside
        ahead[rows_of(step), :] = onward
        behind[rows_of(step), :] = onward_next
        return carry

    lax.fori_loop(0, sz.steps, body, 0, unroll=4)


def through(sz, meta, first, length):
    ahead = behind = False
    for index in range(sz.items):
        begin, end = item_of(sz, meta, index)
        ahead = ahead | ((begin < first) & (end >= first + length))
        behind = behind | ((begin <= first) & (end > first + length))
    behind = behind & (first + length < sz.run)
    return ahead, behind


def power(pair, count):
    while count > 1:
        pair = cmul(*pair, *pair)
        count //= 2
    return pair


def column_blocks(sz, decay):
    out = []
    for q in range(sz.states // LANES):
        cols = slice(q * LANES, (q + 1) * LANES)
        out.append((decay[0:1, cols], decay[1:2, cols]))
    return out


def spread(pairs):
    return [tuple(jnp.broadcast_to(v, (SEGS, LANES)) for v in pair) for pair in pairs]


def chain_ends(sz, decay, ahead, behind, source, ahead_col, behind_col, ends):
    nq = sz.states // LANES
    d = spread(column_blocks(sz, decay))
    zero = jnp.zeros((SEGS, LANES), F32)

    def body(step, held):
        up, down = rows_of(step), rows_of(sz.steps - 1 - step)
        on_up, on_down = ahead[up, :], behind[down, :]
        new = []
        for q in range(nq):
            for side, (rows, on, col) in enumerate(((up, on_up, ahead_col), (down, on_down, behind_col))):
                re, im = held[2 * q + side]
                re, im = cmul(*d[q], re * on, im * on)
                re += source[rows, col + q * LANES : col + (q + 1) * LANES]
                im += source[rows, col + sz.states + q * LANES : col + sz.states + (q + 1) * LANES]
                new.append((re, im))
        return tuple(new)

    held = lax.fori_loop(0, sz.steps, body, tuple((zero, zero) for _ in range(2 * nq)), unroll=4)
    for q in range(nq):
        cols = slice(q * LANES, (q + 1) * LANES)
        for side in range(2):
            ends[2 * side, :, cols] = held[2 * q + side][0]
            ends[2 * side + 1, :, cols] = held[2 * q + side][1]


def enter_states(sz, meta, decay, ends, start, enter):
    pair = (decay[0:1, :], decay[1:2, :])
    jump = power(pair, sz.steps)
    base = meta[1] * sz.toks
    state = list(start)
    for count in range(SEGS):
        for side, seg in ((0, count), (1, SEGS - 1 - count)):
            re, im = state[side]
            enter[2 * side, seg : seg + 1, :] = re
            enter[2 * side + 1, seg : seg + 1, :] = im
            passes = through(sz, meta, base + seg * sz.steps, sz.steps)[side]
            gain = jnp.where(passes, 1.0, 0.0).astype(F32)
            re, im = cmul(jump[0] * gain, jump[1] * gain, re, im)
            state[side] = (
                re + ends[2 * side, seg : seg + 1, :],
                im + ends[2 * side + 1, seg : seg + 1, :],
            )
    return state


def send_ends(sz, meta, decay, ends, enter, send):
    zero = jnp.zeros((1, sz.states), F32)
    ahead, behind = enter_states(sz, meta, decay, ends, ((zero, zero), (zero, zero)), enter)
    me = meta[1]
    for dist in range(1, sz.chunks):
        up = (me ^ dist) > me
        for part in range(2):
            send[dist - 1, part : part + 1, :] = jnp.where(up, ahead[part], behind[part])


def received(sz, meta, decay, recv):
    me = meta[1]
    zero = jnp.zeros((1, sz.states), F32)
    pair = (decay[0:1, :], decay[1:2, :])
    jump = power(pair, sz.toks) if sz.chunks > 2 else None
    sides = []
    for side in range(2):
        re, im = zero, zero
        order = range(sz.chunks) if side == 0 else range(sz.chunks - 1, -1, -1)
        for other in order:
            use = (other < me) if side == 0 else (other > me)
            slot = jnp.maximum((me ^ other) - 1, 0)
            got = recv[slot]
            new_re, new_im = got[0:1, :], got[1:2, :]
            if sz.chunks > 2:
                passes = through(sz, meta, other * sz.toks, sz.toks)[side]
                gain = jnp.where(passes, 1.0, 0.0).astype(F32)
                moved = cmul(jump[0] * gain, jump[1] * gain, re, im)
                new_re, new_im = new_re + moved[0], new_im + moved[1]
            re, im = jnp.where(use, new_re, re), jnp.where(use, new_im, im)
        sides.append((re, im))
    return sides


def load_enter(sz, enter):
    held = []
    for q in range(sz.states // LANES):
        cols = slice(q * LANES, (q + 1) * LANES)
        for side in range(2):
            held.append((enter[2 * side, :, cols], enter[2 * side + 1, :, cols]))
    return tuple(held)


def chain_states(sz, decay, ahead, behind, source, enter, states):
    nq = sz.states // LANES
    n = sz.states
    d = spread(column_blocks(sz, decay))

    def body(step, held):
        up, down = rows_of(step), rows_of(sz.steps - 1 - step)
        on_up, on_down = ahead[up, :], behind[down, :]
        new = []
        for q in range(nq):
            for side, (rows, on) in enumerate(((up, on_up), (down, on_down))):
                re, im = held[2 * q + side]
                re, im = cmul(*d[q], re * on, im * on)
                lo = q * LANES
                re += source[rows, lo : lo + LANES]
                im += source[rows, n + lo : n + lo + LANES]
                at = 2 * side * n + lo
                states[rows, at : at + LANES] = re.astype(BF)
                states[rows, at + n : at + n + LANES] = (-im).astype(BF)
                new.append((re, im))
        return tuple(new)

    lax.fori_loop(0, sz.steps, body, load_enter(sz, enter), unroll=4)


def adjoint_chains(sz, decay, ahead, behind, source, enter, states, half, grad_driven, grad_decay):
    nq = sz.states // LANES
    n = sz.states
    d = spread(column_blocks(sz, decay))
    zero = jnp.zeros((SEGS, LANES), F32)

    def make(second):
        def body(step, carry):
            held, sums = carry
            up, down = rows_of(step), rows_of(sz.steps - 1 - step)
            on_up, on_down = ahead[up, :], behind[down, :]
            new, total = [], []
            for q in range(nq):
                lo = q * LANES
                acc_re, acc_im = sums[q]
                for side, (rows, on, src, st) in enumerate(((up, on_up, 2 * n, 2 * n), (down, on_down, 0, 0))):
                    re, im = held[2 * q + side]
                    re, im = re * on, im * on
                    s_re = states[rows, st + lo : st + lo + LANES].astype(F32)
                    s_im = states[rows, st + n + lo : st + n + lo + LANES].astype(F32)
                    acc_re += re * s_re + im * s_im
                    acc_im += re * s_im - im * s_re
                    re, im = cmul(*d[q], re, im)
                    re += source[rows, src + lo : src + lo + LANES]
                    im += source[rows, src + n + lo : src + n + lo + LANES]
                    new.append((re, im))
                    if second:
                        out_re = re + half[rows, lo : lo + LANES]
                        out_im = im + half[rows, n + lo : n + lo + LANES]
                        grad_driven[rows, lo : lo + LANES] = out_re.astype(BF)
                        grad_driven[rows, n + lo : n + lo + LANES] = (-out_im).astype(BF)
                    else:
                        half[rows, lo : lo + LANES] = re
                        half[rows, n + lo : n + lo + LANES] = im
                total.append((acc_re, acc_im))
            return tuple(new), tuple(total)

        return body

    carry = (load_enter(sz, enter), tuple((zero, zero) for _ in range(nq)))
    carry = lax.fori_loop(0, sz.steps // 2, make(False), carry, unroll=2)
    carry = lax.fori_loop(sz.steps // 2, sz.steps, make(True), carry, unroll=2)
    for q in range(nq):
        cols = slice(q * LANES, (q + 1) * LANES)
        grad_decay[0:1, cols] = jnp.sum(carry[1][q][0], axis=0, keepdims=True)
        grad_decay[1:2, cols] = jnp.sum(carry[1][q][1], axis=0, keepdims=True)


ROWS = 512


def row_parts(sz):
    size = min(ROWS, sz.toks)
    return [slice(lo, lo + size) for lo in range(0, sz.toks, size)]


def matmul_nt(a, b, out, tile=256):
    for lo in range(0, b.shape[0], tile):
        out[:, lo : lo + tile] = nt(a[...], b[lo : lo + tile, :]).astype(out.dtype)


def matmul_tn(a, b, out, tile=256):
    for lo in range(0, a.shape[1], tile):
        out[lo : lo + tile, :] = tn(a[:, lo : lo + tile], b[...]).astype(out.dtype)


def column_sum(x):
    return jnp.sum(x.reshape(x.shape[0] // 8, 8, x.shape[1]), axis=0)


def scale_of(u):
    return lax.rsqrt(jnp.mean(u * u, axis=1, keepdims=True) + EPSILON)


def normed_rows(sz, u, gain, on):
    return (u * scale_of(u) * gain * on).astype(BF)


def finish_rows(sz, rows, states, w_out, skip, normed, on, slope):
    pre = 2.0 * nn(states[rows, :], w_out[...]) + skip * normed[rows, :].astype(F32)
    square = pre * pre
    th = jnp.tanh(pre * (GELU_C + (GELU_C * GELU_A) * square))
    part = 0.5 + 0.5 * th
    deriv = part + pre * (1.0 - th * th) * (0.5 * GELU_C + (1.5 * GELU_C * GELU_A) * square)
    slope[rows, :] = (on * deriv).astype(slope.dtype)
    return on * (pre * part)


def enter_chunk(sz, meta, recv, decay, ends, enter):
    enter_states(sz, meta, decay, ends, received(sz, meta, decay, recv), enter)


def back_rows(sz, rows, grad_driven, w_in, upstream, slope, skip, hidden, gain):
    u = hidden[rows, :].astype(F32)
    r = upstream[rows, :]
    gn = nn(grad_driven[rows, :], w_in[...]) + r * slope[rows, :].astype(F32) * skip
    scale = scale_of(u)
    moved = u * scale
    dn = gn * gain
    inner = jnp.sum(dn * moved, axis=1, keepdims=True) * (1.0 / sz.width)
    return r + scale * (dn - moved * inner), column_sum(gn * moved)


def open_rows(sz, rows, r, slope, normed, w_out, twice, grad_states):
    e = r * slope[rows, :].astype(F32)
    low = e.astype(BF)
    double = low + low
    twice[rows, :] = double
    grad_states[rows, :] = nt(double, w_out[...])
    return column_sum(e * normed[rows, :].astype(F32))


def gain_of(params, layer):
    return params[layer : layer + 1, :]


def skip_of(params, layer):
    return params[2 + layer : 3 + layer, :]


def decay_of(sz, params, layer):
    return params[4 + 2 * layer : 6 + 2 * layer, 0 : sz.states]


def place_pieces(sz, meta, pieces, stacked):
    part = sz.width // sz.blocks
    for dist, piece in enumerate(pieces):
        owner = meta[4] ^ turned(sz, dist)
        stacked[pl.ds(pl.multiple_of(owner * part, part), part), :] = piece[0:part, :]


def cut_pieces(sz, meta, rows, perm, stacked, pieces):
    part = sz.width // sz.blocks
    matmul_tn(rows, perm, stacked)
    for dist, piece in enumerate(pieces):
        owner = meta[4] ^ turned(sz, dist)
        piece[...] = stacked[pl.ds(pl.multiple_of(owner * part, part), part), :]


def cut_kernel(sz, meta, whole, *refs):
    outs, wide, sems = refs[: sz.blocks], refs[-2], refs[-1]
    straight = whole.dtype == BF
    copies = []
    for dist in range(sz.blocks):
        to = meta[0] ^ turned(sz, dist)
        cols = pl.ds(pl.multiple_of(lax.rem(to, sz.chunks) * sz.toks, LANES), sz.toks)
        source = whole.at[lax.div(to, sz.chunks), :, cols]
        copy = pltpu.make_async_copy(source, outs[dist] if straight else wide.at[dist], sems.at[dist])
        copy.start()
        copies.append(copy)
    for dist, copy in enumerate(copies):
        copy.wait()
        if not straight:
            outs[dist][...] = wide[dist].astype(BF)


def discretize(lambda_log, lambda_imag, log_step):
    step_size = jnp.exp(log_step)
    lambda_real = -jnp.exp(lambda_log)
    modulus = jnp.exp(lambda_real * step_size)
    decay_real = modulus * jnp.cos(lambda_imag * step_size)
    decay_imag = modulus * jnp.sin(lambda_imag * step_size)
    denominator = lambda_real * lambda_real + lambda_imag * lambda_imag
    scale_real = ((decay_real - 1.0) * lambda_real + decay_imag * lambda_imag) / denominator
    scale_imag = (decay_imag * lambda_real - (decay_real - 1.0) * lambda_imag) / denominator
    return decay_real, decay_imag, scale_real, scale_imag


def first_rows(sz):
    part, own = sz.width // sz.blocks, sz.states // sz.blocks
    return part, part + own * sz.width // sz.toks


def half_map_parts(sz):
    top, end = first_rows(sz)
    rows = end - top
    for index in range(sz.toks // sz.width):
        yield slice(index * rows, (index + 1) * rows), slice(top, end), slice(index * sz.width, (index + 1) * sz.width)


def split3(x):
    hi = x.astype(BF).astype(F32)
    mid = (x - hi).astype(BF).astype(F32)
    return hi, mid, x - hi - mid


def prepare_kernel(sz, meta, tokens, *refs):
    inputs, refs = refs[:7], refs[7:]
    outs, refs = refs[: sz.blocks], refs[sz.blocks :]
    drive_b, half_b = refs[:2]
    held, small, lines, drive_a, sems = refs[2:9], refs[9], refs[10], refs[11], refs[12]
    top, end = first_rows(sz)
    own, part = sz.states // sz.blocks, sz.width // sz.blocks
    loads, copies = [], []
    for index, (source, target) in enumerate(zip(inputs, held)):
        loads.append(pltpu.make_async_copy(source, target, sems.at[index]))
    for dist in range(sz.blocks):
        to = meta[0] ^ turned(sz, dist)
        cols = pl.ds(pl.multiple_of(lax.rem(to, sz.chunks) * sz.toks, LANES), sz.toks)
        source = tokens.at[lax.div(to, sz.chunks), :, cols]
        copies.append(pltpu.make_async_copy(source, outs[dist].at[0:top, :], sems.at[len(inputs) + dist]))
    for copy in copies + loads:
        copy.start()
    for copy in loads[:6]:
        copy.wait()
    gain, skip, lambda_log, lambda_imag, log_step, input_map, output_map = held
    dr, di, sr, si = discretize(lambda_log[...], lambda_imag[...], log_step[...])
    small[...] = jnp.zeros_like(small)
    lines[...] = jnp.zeros_like(lines)
    small[0:2, 0:part] = gain[...]
    small[2:4, 0:part] = skip[...]
    for layer in range(2):
        small[4 + 2 * layer : 5 + 2 * layer, 0:own] = dr[layer : layer + 1]
        small[5 + 2 * layer : 6 + 2 * layer, 0:own] = di[layer : layer + 1]
    lines[0:2, 0:own] = sr
    lines[2:4, 0:own] = si
    cols = lines[...].T
    for layer in range(2):
        qr, qi = cols[0:own, layer : layer + 1], cols[0:own, 2 + layer : 3 + layer]
        br, bi = input_map[layer, 0].astype(F32), input_map[layer, 1].astype(F32)
        for index, value in enumerate((qr * br - qi * bi, qr * bi + qi * br)):
            (drive_a, drive_b)[layer][index] = value.astype(BF)
    rows = jnp.concatenate([*split3(small[...]), jnp.zeros((8, sz.toks - 3 * LANES), F32)], axis=1)
    rows = jnp.concatenate([rows, jnp.zeros((8, sz.toks), F32)], axis=0).astype(BF)
    for dist, out in enumerate(outs):
        half = lax.rem(meta[0] ^ turned(sz, dist), 2)
        for from_rows, to_rows, lanes in half_map_parts(sz):
            out[to_rows, lanes] = drive_a[half, from_rows, :]
        out[end:, :] = rows
    loads[6].wait()
    core = meta[2]
    for index in range(2):
        half_b[index] = output_map[0, 2 * core + index]
        half_b[3 + index] = output_map[1, 2 * core + index]
    half_b[2] = drive_b[core]
    for copy in copies:
        copy.wait()


def params_of(sz, piece):
    rows = piece[piece.shape[0] - 16 :, 0 : 3 * LANES].astype(F32)[0:8]
    return rows[:, 0:LANES] + rows[:, LANES : 2 * LANES] + rows[:, 2 * LANES :]


def join_kernel(sz, meta, *refs):
    pieces, maps, params = refs[: sz.blocks], refs[-2], refs[-1]
    own = sz.states // sz.blocks
    collect_params(sz, meta, [params_of(sz, piece) for piece in pieces], params)
    for dist, piece in enumerate(pieces):
        base = (meta[4] ^ turned(sz, dist)) * own
        for to_rows, from_rows, lanes in half_map_parts(sz):
            rows = pl.ds(pl.multiple_of(base + to_rows.start, 16), to_rows.stop - to_rows.start)
            maps[rows, :] = piece[from_rows, lanes]


def collect_params(sz, meta, smalls, params):
    own = sz.states // sz.blocks
    part = sz.width // sz.blocks
    lane = lax.broadcasted_iota(jnp.int32, (8, LANES), 1)
    row = lax.broadcasted_iota(jnp.int32, (8, LANES), 0)
    pad = jnp.zeros((8, sz.width - LANES), F32)
    total = jnp.zeros((8, sz.width), F32)
    for block in range(sz.blocks):
        piece = smalls[0]
        for dist in range(1, sz.blocks):
            piece = jnp.where((meta[4] ^ turned(sz, dist)) == block, smalls[dist], piece)
        for first, count, size in ((0, 4, part), (4, 4, own)):
            mine = jnp.where((row >= first) & (row < first + count) & (lane < size), piece, 0.0)
            wide = jnp.concatenate([mine, pad], axis=1)
            total += pltpu.roll(wide, block * size, 1) if block else wide
    params[...] = total


def block_order(sz, core):
    held = [0]
    for step in range(bits_of(sz)):
        held += [dist ^ step_bit(sz, step, core) for dist in held]
    return held[1:]


def pile_kernel(sz, meta, *refs):
    at = 0
    for piece in refs[:-1]:
        refs[-1][at : at + piece.shape[0]] = piece[...]
        at += piece.shape[0]


def place_maps(sz, meta, own_maps, mine, other, skip, out):
    own = sz.states // sz.blocks
    count = own_maps.shape[0] // 2

    def put(index, owner, value):
        out[pl.ds(pl.multiple_of(index * sz.states + owner * own, own), own), :] = value

    for index in range(2 * count):
        put(index, meta[0], own_maps[index])
    for side, pieces in ((meta[2], mine), (1 - meta[2], other)):
        for place, (even, odd) in enumerate(zip(block_order(sz, 0), block_order(sz, 1)), 1):
            message = place.bit_length() - 1
            each = pieces[message].shape[0] >> message
            owner = meta[0] ^ jnp.where(side == 0, even, odd)
            for index in range(count):
                put(side * count + index, owner, pieces[message][(place - (1 << message)) * each + skip + index])


def open_kernel(sz, meta, perm, params, *refs):
    pieces, (hidden, normed, live, ahead, behind, stacked) = refs[: sz.blocks], refs[sz.blocks :]
    fill_masks(sz, meta, live, ahead, behind)
    place_pieces(sz, meta, pieces, stacked)
    gain = gain_of(params, 0)
    for rows in row_parts(sz):
        u = nt(perm[rows, :], stacked[...])
        hidden[rows, :] = u.astype(BF)
        normed[rows, :] = normed_rows(sz, u, gain, widen(live[rows, :], sz.width // LANES))


def enter_kernel(sz, meta, ahead, behind, params, normed, maps, other, w_in, driven, ends, send, enter):
    decay = decay_of(sz, params, 0)
    for side, half in ((meta[2], maps), (1 - meta[2], other)):
        w_in[pl.ds(pl.multiple_of(side * sz.states, sz.states), sz.states), :] = half[...]
    matmul_nt(normed, w_in, driven)
    chain_ends(sz, decay, ahead, behind, driven, 0, 0, ends)
    send_ends(sz, meta, decay, ends, enter, send)


def chain_kernel(sz, meta, ahead, behind, recv, params, ends, driven, states, enter):
    decay = decay_of(sz, params, 0)
    enter_chunk(sz, meta, recv, decay, ends, enter)
    chain_states(sz, decay, ahead, behind, driven, enter, states)


def middle_kernel(sz, meta, live, ahead, behind, states, params, normed, hidden, own_out, own_in, *refs):
    skip, gain_b, decay_b = skip_of(params, 0), gain_of(params, 1), decay_of(sz, params, 1)
    far = bits_of(sz)
    mine, other, refs = refs[:far], refs[far : 2 * far], refs[2 * far :]
    w_out, w_in_b, slope, hidden_b, normed_b, driven_b, ends_b, send_b, enter = refs
    place_maps(sz, meta, own_out, mine, other, 0, w_out)
    place_maps(sz, meta, own_in, mine, other, 2, w_in_b)
    for rows in row_parts(sz):
        on = widen(live[rows, :], sz.width // LANES)
        u = hidden[rows, :].astype(F32) + finish_rows(sz, rows, states, w_out, skip, normed, on, slope)
        hidden_b[rows, :] = u
        v = normed_rows(sz, u, gain_b, on)
        normed_b[rows, :] = v
        driven_b[rows, :] = nt(v, w_in_b[...])
    chain_ends(sz, decay_b, ahead, behind, driven_b, 0, 0, ends_b)
    send_ends(sz, meta, decay_b, ends_b, enter, send_b)


def leave_kernel(sz, meta, live, ahead, behind, recv, params, ends, driven, normed, hidden, own_out, *refs):
    decay, skip = decay_of(sz, params, 1), skip_of(params, 1)
    far = bits_of(sz)
    mine, other, refs = refs[:far], refs[far : 2 * far], refs[2 * far :]
    w_out, states, slope, last, enter = refs
    place_maps(sz, meta, own_out, mine, other, 3, w_out)
    enter_chunk(sz, meta, recv, decay, ends, enter)
    chain_states(sz, decay, ahead, behind, driven, enter, states)
    for rows in row_parts(sz):
        on = widen(live[rows, :], sz.width // LANES)
        last[rows, :] = (hidden[rows, :] + finish_rows(sz, rows, states, w_out, skip, normed, on, slope)).astype(BF)


def turn_kernel(sz, meta, ahead, behind, slope, normed, w_out, params, perm, *refs):
    decay = decay_of(sz, params, 1)
    pieces, refs = refs[: sz.blocks], refs[sz.blocks :]
    upstream, twice, grad_states, grad_skip, ends, send, stacked, enter = refs
    place_pieces(sz, meta, pieces, stacked)
    skips = []
    for rows in row_parts(sz):
        r = nt(perm[rows, :], stacked[...])
        upstream[rows, :] = r
        skips.append(open_rows(sz, rows, r, slope, normed, w_out, twice, grad_states))
    grad_skip[...] = jnp.sum(sum(skips), axis=0, keepdims=True)
    chain_ends(sz, decay, ahead, behind, grad_states, 2 * sz.states, 0, ends)
    send_ends(sz, meta, decay, ends, enter, send)


def back_middle_kernel(sz, meta, ahead, behind, recv, params, ends, grad_states, states, upstream, slope, hidden, w_in,
                       slope_b, normed_b, w_out_b,
                       grad_driven, grad_decay, grad_gain, upstream_b, twice_b, grad_states_b, grad_skip_b, ends_b, send_b,
                       enter, half):
    decay, skip, gain, decay_b = decay_of(sz, params, 1), skip_of(params, 1), gain_of(params, 1), decay_of(sz, params, 0)
    enter_chunk(sz, meta, recv, decay, ends, enter)
    adjoint_chains(sz, decay, ahead, behind, grad_states, enter, states, half, grad_driven, grad_decay)
    gains, skips = [], []
    for rows in row_parts(sz):
        r, terms = back_rows(sz, rows, grad_driven, w_in, upstream, slope, skip, hidden, gain)
        gains.append(terms)
        upstream_b[rows, :] = r
        skips.append(open_rows(sz, rows, r, slope_b, normed_b, w_out_b, twice_b, grad_states_b))
    grad_gain[...] = jnp.sum(sum(gains), axis=0, keepdims=True)
    grad_skip_b[...] = jnp.sum(sum(skips), axis=0, keepdims=True)
    chain_ends(sz, decay_b, ahead, behind, grad_states_b, 2 * sz.states, 0, ends_b)
    send_ends(sz, meta, decay_b, ends_b, enter, send_b)


def back_chain_kernel(sz, meta, ahead, behind, recv, params, ends, grad_states, states, grad_driven, grad_decay, enter, half):
    decay = decay_of(sz, params, 0)
    enter_chunk(sz, meta, recv, decay, ends, enter)
    adjoint_chains(sz, decay, ahead, behind, grad_states, enter, states, half, grad_driven, grad_decay)


def back_leave_kernel(sz, meta, params, grad_driven, upstream, slope, hidden, w_in, perm, done, *refs):
    skip, gain = skip_of(params, 0), gain_of(params, 0)
    pieces, (last, stacked) = refs[: sz.blocks], refs[sz.blocks :]
    for rows in row_parts(sz):
        r, _ = back_rows(sz, rows, grad_driven, w_in, upstream, slope, skip, hidden, gain)
        last[rows, :] = r.astype(BF)
    part = sz.width // sz.blocks
    cut_pieces(sz, meta, done, perm, stacked, [piece.at[0:part, :] for piece in pieces])
    cut_pieces(sz, meta, last, perm, stacked, [piece.at[part : 2 * part, :] for piece in pieces])


def weight_kernel(counts, other, sz, meta, *refs):
    half = 1 - meta[2] if other else meta[2]
    pairs = 2 * len(counts)
    out, at = refs[pairs], 0
    if len(refs) > pairs + 1:
        whole, out, terms = refs[pairs:]
        value = tn(refs[0][:, pl.ds(pl.multiple_of(half * sz.states, LANES), sz.states)], refs[1][...])
        out[...] = value.astype(out.dtype)
        rows = whole[pl.ds(pl.multiple_of(half * sz.states, sz.states), sz.states), :].astype(F32)
        terms[...] = jnp.sum(column_sum(rows * value), axis=0, keepdims=True)
        return
    for index, count in enumerate(counts):
        left, right = refs[2 * index], refs[2 * index + 1]
        for group in range(count):
            cols = pl.ds(pl.multiple_of((half * count + group) * sz.states, LANES), sz.states)
            out[at : at + sz.states, :] = tn(left[:, cols], right[...]).astype(out.dtype)
            at += sz.states


def split2(x):
    hi = x.astype(BF).astype(F32)
    return hi, x - hi


class Group(NamedTuple):
    first: int
    counts: tuple

    def rows(self, sz):
        return sum(self.counts) * (sz.states // sz.blocks)


def bits_of(sz):
    return sz.blocks.bit_length() - 1


def step_bit(sz, step, core):
    return 1 << ((step + core) % bits_of(sz))


def far_block(sz, group, slot, core):
    return sum(step_bit(sz, group.first + j, core) for j in range(bits_of(sz)) if (slot >> j) & 1)


def own_tiny(sz, params, terms, more, gain_b, skip_a, skip_b, decay_a, decay_b, tiny):
    gain_a = (terms[...] + more[...] + skip_of(params, 0) * skip_a[...]) / gain_of(params, 0)
    tiny[...] = jnp.zeros_like(tiny)
    for index, line in enumerate((gain_a, gain_b[...], skip_a[...], skip_b[...])):
        tiny[index : index + 1, :] = line
    tiny[4:6, 0 : sz.states] = decay_a[...]
    tiny[6:8, 0 : sz.states] = decay_b[...]
    return tiny[...]


def tiny_of(sz, tiny, owner):
    own, part = sz.states // sz.blocks, sz.width // sz.blocks
    row = lax.broadcasted_iota(jnp.int32, (8, LANES), 0)
    lane = lax.broadcasted_iota(jnp.int32, (8, LANES), 1)
    value = jnp.zeros((8, LANES), F32)
    for block in range(sz.blocks):
        wide = pltpu.roll(tiny, sz.width - block * part, 1) if block else tiny
        deep = pltpu.roll(tiny, sz.width - block * own, 1) if block else tiny
        mine = jnp.where(row < 4, jnp.where(lane < part, wide[:, :LANES], 0.0), jnp.where(lane < own, deep[:, :LANES], 0.0))
        value = jnp.where(owner == block, mine, value)
    return value


def put_sums(value, slot, kept, message, at):
    if slot % 2 == 0:
        kept[slot // 2] = value
        return at
    message[at : at + value.shape[0], :] = value.astype(BF)
    return at + value.shape[0]


def add_message(sz, group, kept, slot, message, at):
    return kept[slot] + message[at : at + group.rows(sz), :].astype(F32)


def step_kernel(old, new, sz, meta, *refs):
    came, refs = (refs[0], refs[1:]) if old else (None, refs)
    held, refs = refs[: len(old)], refs[len(old) :]
    if new:
        halves, refs = refs[: 2 * len(new.counts)], refs[2 * len(new.counts) :]
    keeps, message = refs[:-1], refs[-1]
    at = 0
    for (group, slots, row), kept, keep in zip(old, held, keeps):
        for slot in range(slots):
            value = add_message(sz, group, kept, slot, came, row + slot * group.rows(sz))
            at = put_sums(value, slot, keep, message, at)
    if new:
        own = sz.states // sz.blocks
        for slot in range(sz.blocks):
            owner = meta[0] ^ jnp.where(meta[2] == 0, far_block(sz, new, slot, 0), far_block(sz, new, slot, 1))
            parts = []
            for index, count in enumerate(new.counts):
                keep, got = halves[2 * index], halves[2 * index + 1]
                for one in range(count):
                    rows = pl.ds(pl.multiple_of(one * sz.states + owner * own, own), own)
                    parts.append(keep[rows, :].astype(F32) + got[rows, :].astype(F32))
            at = put_sums(jnp.concatenate(parts, axis=0), slot, keeps[-1], message, at)


def direct_kernel(group, sz, meta, keep, got, *refs):
    own = sz.states // sz.blocks
    lines, pieces, room = refs[:8], refs[8:-1], refs[-1]
    whole = own_tiny(sz, *lines, room)
    for index, piece in enumerate(pieces):
        owner = meta[0] ^ farthest(index, sz.blocks)
        rows = pl.ds(pl.multiple_of(owner * own, own), own)
        piece[0:own, :] = (keep[rows, :].astype(F32) + got[rows, :].astype(F32)).astype(BF)
        rest = jnp.zeros((8, sz.width - 2 * LANES), F32)
        wide = jnp.concatenate([*split2(tiny_of(sz, whole, owner)), rest], axis=1)
        piece[own : own + 16, :] = jnp.concatenate([wide, jnp.zeros_like(wide)], axis=0).astype(BF)


def fold_block_kernel(planes, groups, direct, sz, meta, *refs):
    lanes = sz.width // LANES
    held, refs = refs[: 2 * len(groups)], refs[2 * len(groups) :]
    pieces, refs = (refs[: sz.blocks], refs[sz.blocks :]) if direct else ((), refs)
    outs, talls = refs[:planes], refs[planes:]
    totals = [add_message(sz, group, held[2 * index], 0, held[2 * index + 1], row) for index, (group, row) in enumerate(groups)]
    if direct:
        total = pieces[0][...].astype(F32)
        for piece in pieces[1:]:
            total += piece[...].astype(F32)
        rows = total.shape[0] - 16
        totals.append(total[0:rows])
        tiny = total[rows : rows + 8, 0:LANES] + total[rows : rows + 8, LANES : 2 * LANES]
    at = 0
    for total, tall in zip(totals, talls):
        rows = total.shape[0]
        padded = tall.shape[0] // lanes
        for block in range(lanes):
            tall[block * padded : block * padded + rows, :] = total[:, block * LANES : (block + 1) * LANES].astype(BF)
            if padded > rows:
                tall[block * padded + rows : (block + 1) * padded, :] = jnp.zeros((padded - rows, LANES), BF)
        part = tall.shape[0] // planes
        for dist, out in enumerate(outs):
            out[at : at + part, :] = tall[pl.ds(pl.multiple_of((meta[3] ^ farthest(dist, planes)) * part, part), part), :]
        at += part
    if direct:
        rows = jnp.concatenate(split2(tiny), axis=0).astype(BF)
        for out in outs:
            out[at : at + 16, :] = rows


def fold_plane_kernel(early, sz, meta, *refs):
    parts, out, tiny = refs[early:-2], refs[-2], refs[-1]
    top = 0
    if early:
        total = refs[0][...].astype(F32)
        for piece in refs[1:early]:
            total += piece[...].astype(F32)
        top = total.shape[0]
        out[0:top, :] = total.astype(BF)
    total = parts[0][...].astype(F32)
    for piece in parts[1:]:
        total += piece[...].astype(F32)
    rows = total.shape[0] - 16
    out[top:, :] = total[0:rows].astype(BF)
    tiny[...] = total[rows : rows + 8] + total[rows + 8 :]


def finish_kernel(planes, groups, sz, meta, *refs):
    count = 2 * planes
    pieces, refs = refs[:count], refs[count:]
    tiny, lambda_log, lambda_imag, log_step, input_map = refs[0][...] + refs[1][...], *refs[2:6]
    grad_gain, grad_skip, grad_log, grad_imag, grad_step, grad_maps, grad_out = refs[6:13]
    talls, grad_in, lines = refs[13:-2], refs[-2], refs[-1]
    own = sz.states // sz.blocks
    lanes = sz.width // LANES
    start = 0
    for tall, group in zip(talls, groups):
        padded = tall.shape[0] // lanes
        part = tall.shape[0] // planes
        for side in range(2):
            half = meta[2] ^ side
            for dist in range(planes):
                rows = pl.ds(pl.multiple_of((meta[3] ^ farthest(dist, planes)) * part, part), part)
                tall[rows, :] = pieces[side * planes + dist][start : start + part, :]
            at = 0
            for which, layer, maps in group:
                out = grad_in if which == 0 else grad_out
                for one in range(maps):
                    for block in range(lanes):
                        rows = slice(block * padded + at, block * padded + at + own)
                        out[layer, half * maps + one, :, block * LANES : (block + 1) * LANES] = tall[rows, :].astype(F32)
                    at += own
        start += part
    width = sz.width // sz.blocks
    grad_gain[...] = tiny[0:2, 0:width]
    grad_skip[...] = tiny[2:4, 0:width]
    dr, di, sr, si = discretize(lambda_log[...], lambda_imag[...], log_step[...])
    lines[...] = jnp.zeros_like(lines)
    lines[0:2, 0:own] = sr
    lines[2:4, 0:own] = si
    cols = lines[...].T
    back = []
    for layer in range(2):
        qr, qi = cols[0:own, layer : layer + 1], cols[0:own, 2 + layer : 3 + layer]
        wr, wi = grad_in[layer, 0], grad_in[layer, 1]
        br, bi = input_map[layer, 0].astype(F32), input_map[layer, 1].astype(F32)
        grad_maps[layer, 0] = qr * wr + qi * wi
        grad_maps[layer, 1] = qr * wi - qi * wr
        back.append(jnp.sum(wr * br + wi * bi, axis=1, keepdims=True))
        back.append(jnp.sum(wi * br - wr * bi, axis=1, keepdims=True))
    lines[...] = jnp.zeros_like(lines)
    for index, col in enumerate(back):
        lines[0:own, index : index + 1] = col
    rows = lines[...].T
    step = jnp.exp(log_step[...])
    lr, li = -jnp.exp(lambda_log[...]), lambda_imag[...]
    norm = 1.0 / (lr * lr + li * li)
    for layer in range(2):
        at = slice(layer, layer + 1)
        a, b, h = (lr[at], li[at]), (dr[at], di[at]), step[at]
        gq = rows[2 * layer : 2 * layer + 1, 0:own], rows[2 * layer + 1 : 2 * layer + 2, 0:own]
        gd = tiny[4 + 2 * layer : 5 + 2 * layer, 0:own], tiny[5 + 2 * layer : 6 + 2 * layer, 0:own]
        inverse = a[0] * norm[at], -a[1] * norm[at]
        through = cmul(inverse[0], -inverse[1], *gq)
        gd = gd[0] + through[0], gd[1] + through[1]
        ratio = cmul(*inverse, sr[at], si[at])
        direct = cmul(ratio[0], -ratio[1], *gq)
        moved = cmul(b[0] * h, -b[1] * h, *gd)
        turn = cmul(*a, *b)
        grad_log[at, :] = (moved[0] - direct[0]) * a[0]
        grad_imag[at, :] = moved[1] - direct[1]
        grad_step[at, :] = (turn[0] * gd[0] + turn[1] * gd[1]) * h


def spread_kernel(sz, meta, *refs):
    pieces, outs, wide, sems = refs[: sz.blocks], refs[sz.blocks : -2], refs[-2], refs[-1]
    part = sz.width // sz.blocks
    copies = []
    for dist, piece in enumerate(pieces):
        owner = meta[0] ^ turned(sz, dist)
        for index, out in enumerate(outs):
            slot = dist * len(outs) + index
            wide[slot] = piece[index * part : (index + 1) * part, :].astype(F32)
            cols = pl.ds(pl.multiple_of(lax.rem(owner, sz.chunks) * sz.toks, LANES), sz.toks)
            copy = pltpu.make_async_copy(wide.at[slot], out.at[lax.div(owner, sz.chunks), :, cols], sems.at[slot])
            copy.start()
            copies.append(copy)
    for copy in copies:
        copy.wait()


VMEM = pl.BlockSpec(memory_space=pltpu.VMEM)
SMEM = pl.BlockSpec(memory_space=pltpu.SMEM)
HBM = pl.BlockSpec(memory_space=pltpu.HBM)


def call(name, sz, body, items, args, outs, scratch, limit=10, in_spec=VMEM, out_spec=VMEM, time=0.0):
    out_shape = [jax.ShapeDtypeStruct(shape, dtype) for shape, dtype in outs]

    def kernel(*refs):
        body(sz, place_of(sz, refs[0] if items else None), *refs[len(items) :])

    return pl.pallas_call(
        kernel,
        out_shape=out_shape,
        in_specs=[SMEM] * len(items) + [in_spec] * len(args),
        out_specs=[out_spec] * len(outs),
        scratch_shapes=[pltpu.VMEM(*item) if isinstance(item, tuple) else item for item in scratch],
        compiler_params=pltpu.CompilerParams(vmem_limit_bytes=limit << 20),
        cost_estimate=pl.CostEstimate(flops=int(COST * time), bytes_accessed=1000, transcendentals=0),
        name=name,
    )(*items, *args)


def on_device(tokens, cotangent, item_lengths, item_offsets, norm_gain, lambda_log, lambda_imag, log_step, input_map, output_map, skip_weight):
    micro, part, run = tokens.shape
    layers = norm_gain.shape[0]
    blocks = lax.axis_size("block")
    planes = lax.axis_size("plane")
    chunks = blocks // micro
    toks = run // chunks
    own = lambda_log.shape[1]
    width, states = part * blocks, own * blocks
    sz = Sizes(blocks, chunks, toks, run, toks // SEGS, width, states, item_lengths.shape[1])

    def swap(x, dist, axis="block"):
        return lax.ppermute(x, axis, [(i, i ^ dist) for i in range(lax.axis_size(axis))])

    def across(x, dist, back):
        pairs = []
        for c in range(2):
            for b in range(blocks):
                q = b ^ turned(sz, dist)
                pairs.append((c * blocks + b, (q % 2) * blocks + (q // 2) * 2 + c))
        return lax.ppermute(x, ("core", "block"), [pair[::-1] for pair in pairs] if back else pairs)

    def across_all(pieces, back=False):
        return [across(piece, dist, back) for dist, piece in enumerate(pieces)]

    table = jnp.stack([item_lengths, item_offsets])
    items = [jnp.stack([table, swap(table, 1, "core")])]

    def neighbour(x, dist):
        pairs = []
        for c in range(2):
            for b in range(blocks):
                q = ((b // 2) * 2 + c) ^ dist
                pairs.append((c * blocks + b, (q % 2) * blocks + (q // 2) * 2 + b % 2))
        return lax.ppermute(x, ("core", "block"), pairs)

    def swap_all(pieces, axis="block"):
        count = len(pieces)
        return [swap(piece, farthest(index, count), axis) if index else piece for index, piece in enumerate(pieces)]

    def exchange(send):
        return jnp.stack([neighbour(send[dist - 1], dist) for dist in range(1, chunks)])

    row = jnp.arange(toks, dtype=jnp.int32)[:, None]
    col = jnp.arange(toks, dtype=jnp.int32)[None, :]
    perm = ((row % SEGS) * sz.steps + row // SEGS == col).astype(BF)

    maps_own = ((2, own, width), BF)
    half_own = ((5, own, width), BF)
    given = [norm_gain, skip_weight, lambda_log, lambda_imag, log_step, input_map, output_map]
    *first_pieces, drive_b, half_b = call(
        "prepare", sz, prepare_kernel, [], [pltpu.with_memory_space_constraint(x, pltpu.HBM) for x in [tokens, *given]],
        [((first_rows(sz)[1] + 16, toks), BF)] * blocks + [maps_own, half_own],
        [(x.shape, x.dtype) for x in given] + [((8, LANES), F32), ((8, LANES), F32), maps_own, pltpu.SemaphoreType.DMA((len(given) + blocks,))],
        limit=6, in_spec=HBM)
    first_pieces = across_all(first_pieces)
    cot_cut = call("cut_cotangent", sz, cut_kernel, [], [pltpu.with_memory_space_constraint(cotangent, pltpu.HBM)],
                   [((part, toks), BF)] * blocks, [((blocks, part, toks), F32), pltpu.SemaphoreType.DMA((blocks,))], limit=4, in_spec=HBM)
    first_pieces[1], perm, cot_cut = after(first_pieces[1], perm, cot_cut)
    second_mine, held = [], half_b
    for step in range(bits_of(sz)):
        pairs = [(c * blocks + b, c * blocks + (b ^ step_bit(sz, step, c))) for c in range(2) for b in range(blocks)]
        second_mine.append(lax.ppermute(held, ("core", "block"), pairs))
        if step == 0:
            second_mine[0], first_pieces = after(second_mine[0], first_pieces)
        if step + 1 < bits_of(sz):
            (held,) = call("pile_%d" % step, sz, pile_kernel, [], [held, second_mine[-1]], [((2 * held.shape[0], own, width), BF)], [])
    maps_a, params = call("join", sz, join_kernel, [], first_pieces, [((states, width), BF), ((8, width), F32)], [])


    mask = ((toks, LANES), F32)
    enter = ((4, SEGS, states), F32)
    stacked = ((width, toks), BF)
    rows_f, rows_b = ((toks, width), F32), ((toks, width), BF)
    drv = ((toks, 2 * states), F32)
    sts = ((toks, 4 * states), BF)
    gst = ((toks, 4 * states), F32)
    snd = ((chunks - 1, 2, states), F32)
    w_in, w_out = ((2 * states, width), BF), ((4 * states, width), BF)
    line, gdec = ((1, width), F32), ((2, states), F32)
    piece_out = [((part, toks), BF)] * blocks

    other_a = swap(maps_a, 1, "core")
    hidden_a, normed_a, live, ahead, behind = call(
        "open", sz, open_kernel, items, [perm, params, *first_pieces], [rows_b, rows_b, mask, mask, mask], [stacked], time=3)
    w_in_a, driven_a, ends_a, send_a = call(
        "enter", sz, enter_kernel, items, [ahead, behind, params, normed_a, maps_a, other_a], [w_in, drv, enter, snd], [enter])
    recv = exchange(send_a)
    (states_a,) = call("chain", sz, chain_kernel, items, [ahead, behind, recv, params, ends_a, driven_a], [sts], [enter])
    second_mine, states_a = after(second_mine, states_a)
    second_maps = second_mine, [swap(piece, 1, "core") for piece in second_mine]
    cot_cut, _ = after(cot_cut, recv)
    cot_pieces = across_all(cot_cut)
    w_out_a, w_in_b, slope_a, hidden_b, normed_b, driven_b, ends_b, send_b = call(
        "middle", sz, middle_kernel, items,
        [live, ahead, behind, states_a, params, normed_a, hidden_a, output_map[0], drive_b, *second_maps[0], *second_maps[1]],
        [w_out, w_in, rows_b, rows_f, rows_b, drv, enter, snd], [enter], time=11)
    recv = exchange(send_b)
    w_out_b, states_b, slope_b, last_b = call(
        "leave", sz, leave_kernel, items,
        [live, ahead, behind, recv, params, ends_b, driven_b, normed_b, hidden_b, output_map[1], *second_maps[0], *second_maps[1]],
        [w_out, sts, rows_b, rows_b], [enter])

    def half_grads(name, other, pairs, counts, more=(), time=0.0):
        args = [x for pair in pairs for x in pair]
        outs = [((sum(counts) * states, width), BF)] + [line] * len(more)
        return call(name, sz, partial(weight_kernel, counts, other), [], [*args, *more], outs, [], time=time)

    groups = [Group(0, (2,)), Group(1, (3,))]
    steps = bits_of(sz)
    kept, came, place = {}, {}, {}

    def halve(step, halves=()):
        old, args = [], []
        for index, group in enumerate(groups):
            if 0 < step - group.first < steps:
                slots = 1 << (steps - (step - group.first))
                old.append((group, slots, place[step - 1, index]))
                args.append(kept[index])
        if old:
            args.insert(0, came[step - 1])
        new = groups[step] if step < len(groups) else None
        outs, at = [], 0
        for index, group in enumerate(groups):
            if 0 <= step - group.first < steps:
                slots = 1 << (steps - 1 - (step - group.first))
                outs.append((index, ((slots, group.rows(sz), width), F32)))
                place[step, index] = at
                at += slots * group.rows(sz)
        results = call("halve_%d" % step, sz, partial(step_kernel, old, new), [], [*args, *halves],
                       [shape for _, shape in outs] + [((at, width), BF)], [])
        for (index, _), value in zip(outs, results):
            kept[index] = value
        return results[-1]

    def send_step(step, message):
        pairs = [(c * blocks + b, c * blocks + (b ^ step_bit(sz, step, c))) for c in range(2) for b in range(blocks)]
        came[step] = lax.ppermute(message, ("core", "block"), pairs)

    def spread(pieces):
        return call("spread", sz, spread_kernel, [], pieces, [((micro, part, run), F32)] * 2,
                    [((2 * blocks, part, toks), F32), pltpu.SemaphoreType.DMA((2 * blocks,))], limit=6, out_spec=HBM, time=9)

    lanes = width // LANES

    def tall_of(rows):
        step = max(SEGS * planes // lanes, SEGS)
        return ((lanes * (-(-rows // step) * step), LANES), BF)

    def over_planes(name, which, direct=()):
        ends = [(groups[index], place[groups[index].first + steps - 1, index]) for index in which]
        talls = [tall_of(group.rows(sz)) for group, _ in ends] + [tall_of(own)] * bool(direct)
        cut = sum(t[0][0] for t in talls) // planes + (16 if direct else 0)
        args = [x for index in which for x in (kept[index], came[groups[index].first + steps - 1])]
        return swap_all(call(name, sz, partial(fold_block_kernel, planes, ends, bool(direct)), [], [*args, *direct],
                             [((cut, LANES), BF)] * planes, talls), "plane")

    up_b, twice_b, gstates_b, gskip_b, ends, send = call(
        "turn", sz, turn_kernel, items, [ahead, behind, slope_b, normed_b, w_out_b, params, perm, *cot_pieces],
        [rows_f, rows_b, gst, line, enter, snd], [stacked, enter], time=6)
    recv = exchange(send)
    pairs = [(states_b, twice_b)]
    (send_maps,) = half_grads("grads_a_send", True, pairs, (2,))
    got = swap(send_maps, 1, "core")
    (keep,) = half_grads("grads_a_keep", False, pairs, (2,), time=2)
    message = halve(0, (keep, got))
    recv, message = after(recv, message)
    send_step(0, message)
    gdriven_b, gdecay_b, ggain_b, up_a, twice_a, gstates_a, gskip_a, ends, send = call(
        "back_middle", sz, back_middle_kernel, items,
        [ahead, behind, recv, params, ends, gstates_b, states_b, up_b, slope_b, hidden_b, w_in_b, slope_a, normed_a, w_out_a],
        [((toks, 2 * states), BF), gdec, line, rows_f, rows_b, gst, line, enter, snd], [enter, drv], limit=12, time=11)
    recv = exchange(send)
    gdriven_b, came[0] = after(gdriven_b, came[0])
    pairs = [(gdriven_b, normed_b), (states_a, twice_a)]
    (send_maps,) = half_grads("grads_b_send", True, pairs, (1, 2))
    got = swap(send_maps, 1, "core")
    (keep,) = half_grads("grads_b_keep", False, pairs, (1, 2), time=9)
    message = halve(1, (keep, got))
    recv, message = after(recv, message)
    send_step(1, message)
    gdriven_a, gdecay_a = call(
        "back_chain", sz, back_chain_kernel, items, [ahead, behind, recv, params, ends, gstates_a, states_a],
        [((toks, 2 * states), BF), gdec], [enter, drv], limit=12, time=9)
    send_maps, terms = half_grads("grads_c_send", True, [(gdriven_a, normed_a)], (1,), [w_in_a])
    gdriven_a, send_maps = after(gdriven_a, send_maps)
    got = swap(send_maps, 1, "core")
    keep, more = half_grads("grads_c_keep", False, [(gdriven_a, normed_a)], (1,), [w_in_a], time=0)
    sums_c = list(call(
        "direct", sz, partial(direct_kernel, None), [],
        [keep, got, params, terms, more, ggain_b, gskip_a, gskip_b, gdecay_a, gdecay_b], [((own + 16, width), BF)] * blocks, [((8, width), F32)]))
    gdriven_a, sums_c[0] = after(gdriven_a, sums_c[0])
    sums_c = swap_all(sums_c)
    last_pieces = call(
        "back_leave", sz, back_leave_kernel, [], [params, gdriven_a, up_a, slope_a, hidden_a, w_in_a, perm, last_b],
        [((2 * part, toks), BF)] * blocks, [rows_b, stacked], limit=12, time=6)
    last_pieces, came[1], sums_c = after(last_pieces, came[1], sums_c)
    message = halve(2)
    kept[0], message = after(kept[0], message)
    first_parts = over_planes("planes_a", [0]) if steps <= 2 else []
    send_step(2, message)
    if first_parts:
        came[2], first_parts = after(came[2], first_parts)
    for step in range(3, steps + 1):
        send_step(step, halve(step))
    parts = over_planes("planes", [1] if first_parts else [0, 1], sums_c)
    last_pieces, parts[0] = after(last_pieces, parts[0])
    early = [across(piece, 2 * dist, True) for dist, piece in enumerate(last_pieces[0::2])]
    parts[0], early = after(parts[0], early)
    sum_all, tiny = call(
        "sum", sz, partial(fold_plane_kernel, len(first_parts)), [], [*first_parts, *parts],
        [((sum(x[0].shape[0] for x in (first_parts, parts) if x) - 16, LANES), BF), ((8, LANES), F32)], [])
    whole = swap_all([sum_all] * planes, "plane")
    late, _ = after(last_pieces[1::2], sum_all)
    late = [across(piece, 2 * dist + 1, True) for dist, piece in enumerate(late)]
    whole = swap_all([sum_all] * planes, "plane")
    late, others = after(late, [sum_all, tiny, *whole[planes - 0 :]])
    others = [swap(x, 1, "core") for x in others]
    output, input_grad = spread([piece for pair in zip(early, late) for piece in pair])
    far = whole[1 : planes - 0]
    far, others, output = after(far, others, output)
    far = [swap(x, 1, "core") for x in far]
    whole += [others[0], *far, *others[2:]]
    tiny_other = others[1]
    small_out = ((layers, own), F32)
    grad_gain, grad_skip, grad_log, grad_imag, grad_step, grad_in, grad_out = call(
        "finish", sz, partial(finish_kernel, planes, ([(1, 1, 2)], [(0, 1, 1), (1, 0, 2)], [(0, 0, 1)])), [],
        [*whole, tiny, tiny_other, lambda_log, lambda_imag, log_step, input_map],
        [((layers, part), F32)] * 2 + [small_out] * 3 + [((layers, 2, own, width), F32), ((layers, 4, own, width), F32)],
        [tall_of(n * own) for n in (2, 3, 1)] + [((layers, 2, own, width), F32), ((LANES, LANES), F32)])
    return output, input_grad, grad_gain, grad_log, grad_imag, grad_step, grad_in, grad_out, grad_skip


def solution(mesh):
    rows, blocks = mesh.devices.shape
    inner = Mesh(mesh.devices.reshape(rows // 2, 2, blocks), ("plane", "core", "block"))
    dp = ("plane", "core")
    half = P(None, "block")
    maps = P(None, None, "block", None)
    acts = P(None, "block", dp)
    items = P(None, dp)
    return jax.shard_map(
        on_device,
        mesh=inner,
        in_specs=(acts, acts, items, items, half, half, half, half, maps, maps, half),
        out_specs=(acts, acts, half, half, half, half, maps, maps, half),
        check_vma=False,
    )
```

```python
from functools import partial
from typing import NamedTuple

import jax
import jax.numpy as jnp
from jax import lax
from jax.experimental import pallas as pl
from jax.experimental.pallas import tpu as pltpu
from jax.sharding import Mesh, PartitionSpec as P

EPSILON = 1e-05
SEGS = 16
LANES = 128
BF = jnp.bfloat16
F32 = jnp.float32
GELU_C = 0.7978845608028654
GELU_A = 0.044715
COST = 400_000_000


class Sizes(NamedTuple):
    blocks: int
    chunks: int
    toks: int
    run: int
    steps: int
    width: int
    states: int
    items: int


def turned(sz, index):
    return sz.blocks - 1 - index


def farthest(index, count):
    return count - index if index else 0


def place_of(sz, table):
    me, core = lax.axis_index("block"), lax.axis_index("core")
    q = lax.div(me, 2) * 2 + core
    mine, chunk = lax.div(q, sz.chunks), lax.rem(q, sz.chunks)
    out = [me, chunk, core, lax.axis_index("plane"), q]
    if table is not None:
        side = lax.rem(me, 2) ^ core
        for which in range(2):
            out += [table[side, which, mine, index] for index in range(sz.items)]
    return out


def nt(a, b):
    return lax.dot_general(a, b, (((1,), (1,)), ((), ())), preferred_element_type=F32)


def nn(a, b):
    return lax.dot_general(a, b, (((1,), (0,)), ((), ())), preferred_element_type=F32)


def tn(a, b):
    return lax.dot_general(a, b, (((0,), (0,)), ((), ())), preferred_element_type=F32)


def after(*values):
    return lax.optimization_barrier(values)


def cmul(ar, ai, br, bi):
    return ar * br - ai * bi, ar * bi + ai * br


def rows_of(step):
    return pl.ds(pl.multiple_of(step * SEGS, SEGS), SEGS)


def widen(mask, count):
    return jnp.concatenate([mask] * count, axis=1)


def item_of(sz, meta, index):
    begin = meta[5 + sz.items + index]
    return begin, begin + meta[5 + index]


def fill_masks(sz, meta, live, ahead, behind):
    base = meta[1] * sz.toks
    seg = lax.broadcasted_iota(jnp.int32, (SEGS, LANES), 0)

    def body(step, carry):
        pos = base + seg * sz.steps + step
        inside = jnp.zeros((SEGS, LANES), F32)
        onward = jnp.zeros((SEGS, LANES), F32)
        onward_next = jnp.zeros((SEGS, LANES), F32)
        for index in range(sz.items):
            begin, end = item_of(sz, meta, index)
            inside = jnp.where((pos >= begin) & (pos < end), 1.0, inside)
            onward = jnp.where((pos > begin) & (pos < end), 1.0, onward)
            onward_next = jnp.where((pos >= begin) & (pos + 1 < end), 1.0, onward_next)
        onward_next = jnp.where(pos + 1 < sz.run, onward_next, 0.0)
        live[rows_of(step), :] = inside
        ahead[rows_of(step), :] = onward
        behind[rows_of(step), :] = onward_next
        return carry

    lax.fori_loop(0, sz.steps, body, 0, unroll=8)


def through(sz, meta, first, length):
    ahead = behind = False
    for index in range(sz.items):
        begin, end = item_of(sz, meta, index)
        ahead = ahead | ((begin < first) & (end >= first + length))
        behind = behind | ((begin <= first) & (end > first + length))
    behind = behind & (first + length < sz.run)
    return ahead, behind


def power(pair, count):
    while count > 1:
        pair = cmul(*pair, *pair)
        count //= 2
    return pair


def column_blocks(sz, decay):
    out = []
    for q in range(sz.states // LANES):
        cols = slice(q * LANES, (q + 1) * LANES)
        out.append((decay[0:1, cols], decay[1:2, cols]))
    return out


def spread(pairs):
    return [tuple(jnp.broadcast_to(v, (SEGS, LANES)) for v in pair) for pair in pairs]


def chain_ends(sz, decay, ahead, behind, source, ahead_col, behind_col, ends):
    nq = sz.states // LANES
    d = spread(column_blocks(sz, decay))
    zero = jnp.zeros((SEGS, LANES), F32)

    def body(step, held):
        up, down = rows_of(step), rows_of(sz.steps - 1 - step)
        on_up, on_down = ahead[up, :], behind[down, :]
        new = []
        for q in range(nq):
            for side, (rows, on, col) in enumerate(((up, on_up, ahead_col), (down, on_down, behind_col))):
                re, im = held[2 * q + side]
                re, im = cmul(*d[q], re * on, im * on)
                re += source[rows, col + q * LANES : col + (q + 1) * LANES]
                im += source[rows, col + sz.states + q * LANES : col + sz.states + (q + 1) * LANES]
                new.append((re, im))
        return tuple(new)

    held = lax.fori_loop(0, sz.steps, body, tuple((zero, zero) for _ in range(2 * nq)), unroll=8)
    for q in range(nq):
        cols = slice(q * LANES, (q + 1) * LANES)
        for side in range(2):
            ends[2 * side, :, cols] = held[2 * q + side][0]
            ends[2 * side + 1, :, cols] = held[2 * q + side][1]


def enter_states(sz, meta, decay, ends, start, enter):
    pair = (decay[0:1, :], decay[1:2, :])
    jump = power(pair, sz.steps)
    base = meta[1] * sz.toks
    state = list(start)
    for count in range(SEGS):
        for side, seg in ((0, count), (1, SEGS - 1 - count)):
            re, im = state[side]
            enter[2 * side, seg : seg + 1, :] = re
            enter[2 * side + 1, seg : seg + 1, :] = im
            passes = through(sz, meta, base + seg * sz.steps, sz.steps)[side]
            gain = jnp.where(passes, 1.0, 0.0).astype(F32)
            re, im = cmul(jump[0] * gain, jump[1] * gain, re, im)
            state[side] = (
                re + ends[2 * side, seg : seg + 1, :],
                im + ends[2 * side + 1, seg : seg + 1, :],
            )
    return state


def send_ends(sz, meta, decay, ends, enter, send):
    zero = jnp.zeros((1, sz.states), F32)
    ahead, behind = enter_states(sz, meta, decay, ends, ((zero, zero), (zero, zero)), enter)
    me = meta[1]
    for dist in range(1, sz.chunks):
        up = (me ^ dist) > me
        for part in range(2):
            send[dist - 1, part : part + 1, :] = jnp.where(up, ahead[part], behind[part])


def received(sz, meta, decay, recv):
    me = meta[1]
    zero = jnp.zeros((1, sz.states), F32)
    pair = (decay[0:1, :], decay[1:2, :])
    jump = power(pair, sz.toks) if sz.chunks > 2 else None
    sides = []
    for side in range(2):
        re, im = zero, zero
        order = range(sz.chunks) if side == 0 else range(sz.chunks - 1, -1, -1)
        for other in order:
            use = (other < me) if side == 0 else (other > me)
            slot = jnp.maximum((me ^ other) - 1, 0)
            got = recv[slot]
            new_re, new_im = got[0:1, :], got[1:2, :]
            if sz.chunks > 2:
                passes = through(sz, meta, other * sz.toks, sz.toks)[side]
                gain = jnp.where(passes, 1.0, 0.0).astype(F32)
                moved = cmul(jump[0] * gain, jump[1] * gain, re, im)
                new_re, new_im = new_re + moved[0], new_im + moved[1]
            re, im = jnp.where(use, new_re, re), jnp.where(use, new_im, im)
        sides.append((re, im))
    return sides


def load_enter(sz, enter):
    held = []
    for q in range(sz.states // LANES):
        cols = slice(q * LANES, (q + 1) * LANES)
        for side in range(2):
            held.append((enter[2 * side, :, cols], enter[2 * side + 1, :, cols]))
    return tuple(held)


def chain_states(sz, decay, ahead, behind, source, enter, states):
    nq = sz.states // LANES
    n = sz.states
    d = spread(column_blocks(sz, decay))

    def body(step, held):
        up, down = rows_of(step), rows_of(sz.steps - 1 - step)
        on_up, on_down = ahead[up, :], behind[down, :]
        new = []
        for q in range(nq):
            for side, (rows, on) in enumerate(((up, on_up), (down, on_down))):
                re, im = held[2 * q + side]
                re, im = cmul(*d[q], re * on, im * on)
                lo = q * LANES
                re += source[rows, lo : lo + LANES]
                im += source[rows, n + lo : n + lo + LANES]
                at = 2 * side * n + lo
                states[rows, at : at + LANES] = re.astype(BF)
                states[rows, at + n : at + n + LANES] = (-im).astype(BF)
                new.append((re, im))
        return tuple(new)

    lax.fori_loop(0, sz.steps, body, load_enter(sz, enter), unroll=8)


def adjoint_chains(sz, decay, ahead, behind, source, enter, states, half, grad_driven, grad_decay):
    nq = sz.states // LANES
    n = sz.states
    d = spread(column_blocks(sz, decay))
    zero = jnp.zeros((SEGS, LANES), F32)

    def make(second):
        def body(step, carry):
            held, sums = carry
            up, down = rows_of(step), rows_of(sz.steps - 1 - step)
            on_up, on_down = ahead[up, :], behind[down, :]
            new, total = [], []
            for q in range(nq):
                lo = q * LANES
                acc_re, acc_im = sums[q]
                for side, (rows, on, src, st) in enumerate(((up, on_up, 2 * n, 2 * n), (down, on_down, 0, 0))):
                    re, im = held[2 * q + side]
                    re, im = re * on, im * on
                    s_re = states[rows, st + lo : st + lo + LANES].astype(F32)
                    s_im = states[rows, st + n + lo : st + n + lo + LANES].astype(F32)
                    acc_re += re * s_re + im * s_im
                    acc_im += re * s_im - im * s_re
                    re, im = cmul(*d[q], re, im)
                    re += source[rows, src + lo : src + lo + LANES]
                    im += source[rows, src + n + lo : src + n + lo + LANES]
                    new.append((re, im))
                    if second:
                        out_re = re + half[rows, lo : lo + LANES]
                        out_im = im + half[rows, n + lo : n + lo + LANES]
                        grad_driven[rows, lo : lo + LANES] = out_re.astype(BF)
                        grad_driven[rows, n + lo : n + lo + LANES] = (-out_im).astype(BF)
                    else:
                        half[rows, lo : lo + LANES] = re
                        half[rows, n + lo : n + lo + LANES] = im
                total.append((acc_re, acc_im))
            return tuple(new), tuple(total)

        return body

    carry = (load_enter(sz, enter), tuple((zero, zero) for _ in range(nq)))
    carry = lax.fori_loop(0, sz.steps // 2, make(False), carry, unroll=4)
    carry = lax.fori_loop(sz.steps // 2, sz.steps, make(True), carry, unroll=4)
    for q in range(nq):
        cols = slice(q * LANES, (q + 1) * LANES)
        grad_decay[0:1, cols] = jnp.sum(carry[1][q][0], axis=0, keepdims=True)
        grad_decay[1:2, cols] = jnp.sum(carry[1][q][1], axis=0, keepdims=True)


ROWS = 512


def row_parts(sz):
    size = min(ROWS, sz.toks)
    return [slice(lo, lo + size) for lo in range(0, sz.toks, size)]


def matmul_nt(a, b, out, tile=256):
    for lo in range(0, b.shape[0], tile):
        out[:, lo : lo + tile] = nt(a[...], b[lo : lo + tile, :]).astype(out.dtype)


def matmul_tn(a, b, out, tile=256):
    for lo in range(0, a.shape[1], tile):
        out[lo : lo + tile, :] = tn(a[:, lo : lo + tile], b[...]).astype(out.dtype)


def column_sum(x):
    return jnp.sum(x.reshape(x.shape[0] // 8, 8, x.shape[1]), axis=0)


def scale_of(u):
    return lax.rsqrt(jnp.mean(u * u, axis=1, keepdims=True) + EPSILON)


def normed_rows(sz, u, gain, on):
    return (u * scale_of(u) * gain * on).astype(BF)


def finish_rows(sz, rows, states, w_out, skip, normed, on, slope):
    pre = 2.0 * nn(states[rows, :], w_out[...]) + skip * normed[rows, :].astype(F32)
    square = pre * pre
    th = jnp.tanh(pre * (GELU_C + (GELU_C * GELU_A) * square))
    part = 0.5 + 0.5 * th
    deriv = part + pre * (1.0 - th * th) * (0.5 * GELU_C + (1.5 * GELU_C * GELU_A) * square)
    slope[rows, :] = (on * deriv).astype(slope.dtype)
    return on * (pre * part)


def enter_chunk(sz, meta, recv, decay, ends, enter):
    enter_states(sz, meta, decay, ends, received(sz, meta, decay, recv), enter)


def back_rows(sz, rows, grad_driven, w_in, upstream, slope, skip, hidden, gain):
    u = hidden[rows, :].astype(F32)
    r = upstream[rows, :]
    gn = nn(grad_driven[rows, :], w_in[...]) + r * slope[rows, :].astype(F32) * skip
    scale = scale_of(u)
    moved = u * scale
    dn = gn * gain
    inner = jnp.sum(dn * moved, axis=1, keepdims=True) * (1.0 / sz.width)
    return r + scale * (dn - moved * inner), column_sum(gn * moved)


def open_rows(sz, rows, r, slope, normed, w_out, twice, grad_states):
    e = r * slope[rows, :].astype(F32)
    low = e.astype(BF)
    double = low + low
    twice[rows, :] = double
    grad_states[rows, :] = nt(double, w_out[...])
    return column_sum(e * normed[rows, :].astype(F32))


def gain_of(params, layer):
    return params[layer : layer + 1, :]


def skip_of(params, layer):
    return params[2 + layer : 3 + layer, :]


def decay_of(sz, params, layer):
    return params[4 + 2 * layer : 6 + 2 * layer, 0 : sz.states]


def place_pieces(sz, meta, pieces, stacked):
    part = sz.width // sz.blocks
    for dist, piece in enumerate(pieces):
        owner = meta[4] ^ turned(sz, dist)
        stacked[pl.ds(pl.multiple_of(owner * part, part), part), :] = piece[0:part, :]


def cut_pieces(sz, meta, rows, perm, stacked, pieces):
    part = sz.width // sz.blocks
    matmul_tn(rows, perm, stacked)
    for dist, piece in enumerate(pieces):
        owner = meta[4] ^ turned(sz, dist)
        piece[...] = stacked[pl.ds(pl.multiple_of(owner * part, part), part), :]


def cut_kernel(sz, meta, whole, *refs):
    outs, wide, sems = refs[: sz.blocks], refs[-2], refs[-1]
    straight = whole.dtype == BF
    copies = []
    for dist in range(sz.blocks):
        to = meta[0] ^ turned(sz, dist)
        cols = pl.ds(pl.multiple_of(lax.rem(to, sz.chunks) * sz.toks, LANES), sz.toks)
        source = whole.at[lax.div(to, sz.chunks), :, cols]
        copy = pltpu.make_async_copy(source, outs[dist] if straight else wide.at[dist], sems.at[dist])
        copy.start()
        copies.append(copy)
    for dist, copy in enumerate(copies):
        copy.wait()
        if not straight:
            outs[dist][...] = wide[dist].astype(BF)


def discretize(lambda_log, lambda_imag, log_step):
    step_size = jnp.exp(log_step)
    lambda_real = -jnp.exp(lambda_log)
    modulus = jnp.exp(lambda_real * step_size)
    decay_real = modulus * jnp.cos(lambda_imag * step_size)
    decay_imag = modulus * jnp.sin(lambda_imag * step_size)
    denominator = lambda_real * lambda_real + lambda_imag * lambda_imag
    scale_real = ((decay_real - 1.0) * lambda_real + decay_imag * lambda_imag) / denominator
    scale_imag = (decay_imag * lambda_real - (decay_real - 1.0) * lambda_imag) / denominator
    return decay_real, decay_imag, scale_real, scale_imag


def first_rows(sz):
    part, own = sz.width // sz.blocks, sz.states // sz.blocks
    return part, part + own * sz.width // sz.toks


def half_map_parts(sz):
    top, end = first_rows(sz)
    rows = end - top
    for index in range(sz.toks // sz.width):
        yield slice(index * rows, (index + 1) * rows), slice(top, end), slice(index * sz.width, (index + 1) * sz.width)


def split3(x):
    hi = x.astype(BF).astype(F32)
    mid = (x - hi).astype(BF).astype(F32)
    return hi, mid, x - hi - mid


def prepare_kernel(sz, meta, tokens, *refs):
    inputs, refs = refs[:7], refs[7:]
    outs, refs = refs[: sz.blocks], refs[sz.blocks :]
    drive_b, half_b = refs[:2]
    held, small, lines, drive_a, sems = refs[2:9], refs[9], refs[10], refs[11], refs[12]
    top, end = first_rows(sz)
    own, part = sz.states // sz.blocks, sz.width // sz.blocks
    loads, copies = [], []
    for index, (source, target) in enumerate(zip(inputs, held)):
        loads.append(pltpu.make_async_copy(source, target, sems.at[index]))
    for dist in range(sz.blocks):
        to = meta[0] ^ turned(sz, dist)
        cols = pl.ds(pl.multiple_of(lax.rem(to, sz.chunks) * sz.toks, LANES), sz.toks)
        source = tokens.at[lax.div(to, sz.chunks), :, cols]
        copies.append(pltpu.make_async_copy(source, outs[dist].at[0:top, :], sems.at[len(inputs) + dist]))
    for copy in copies + loads:
        copy.start()
    for copy in loads[:6]:
        copy.wait()
    gain, skip, lambda_log, lambda_imag, log_step, input_map, output_map = held
    dr, di, sr, si = discretize(lambda_log[...], lambda_imag[...], log_step[...])
    small[...] = jnp.zeros_like(small)
    lines[...] = jnp.zeros_like(lines)
    small[0:2, 0:part] = gain[...]
    small[2:4, 0:part] = skip[...]
    for layer in range(2):
        small[4 + 2 * layer : 5 + 2 * layer, 0:own] = dr[layer : layer + 1]
        small[5 + 2 * layer : 6 + 2 * layer, 0:own] = di[layer : layer + 1]
    lines[0:2, 0:own] = sr
    lines[2:4, 0:own] = si
    cols = lines[...].T
    for layer in range(2):
        qr, qi = cols[0:own, layer : layer + 1], cols[0:own, 2 + layer : 3 + layer]
        br, bi = input_map[layer, 0].astype(F32), input_map[layer, 1].astype(F32)
        for index, value in enumerate((qr * br - qi * bi, qr * bi + qi * br)):
            (drive_a, drive_b)[layer][index] = value.astype(BF)
    rows = jnp.concatenate([*split3(small[...]), jnp.zeros((8, sz.toks - 3 * LANES), F32)], axis=1)
    rows = jnp.concatenate([rows, jnp.zeros((8, sz.toks), F32)], axis=0).astype(BF)
    for dist, out in enumerate(outs):
        half = lax.rem(meta[0] ^ turned(sz, dist), 2)
        for from_rows, to_rows, lanes in half_map_parts(sz):
            out[to_rows, lanes] = drive_a[half, from_rows, :]
        out[end:, :] = rows
    loads[6].wait()
    core = meta[2]
    for index in range(2):
        half_b[index] = output_map[0, 2 * core + index]
        half_b[3 + index] = output_map[1, 2 * core + index]
    half_b[2] = drive_b[core]
    for copy in copies:
        copy.wait()


def params_of(sz, piece):
    rows = piece[piece.shape[0] - 16 :, 0 : 3 * LANES].astype(F32)[0:8]
    return rows[:, 0:LANES] + rows[:, LANES : 2 * LANES] + rows[:, 2 * LANES :]


def join_kernel(sz, meta, *refs):
    pieces, maps, params = refs[: sz.blocks], refs[-2], refs[-1]
    own = sz.states // sz.blocks
    collect_params(sz, meta, [params_of(sz, piece) for piece in pieces], params)
    for dist, piece in enumerate(pieces):
        base = (meta[4] ^ turned(sz, dist)) * own
        for to_rows, from_rows, lanes in half_map_parts(sz):
            rows = pl.ds(pl.multiple_of(base + to_rows.start, 16), to_rows.stop - to_rows.start)
            maps[rows, :] = piece[from_rows, lanes]


def collect_params(sz, meta, smalls, params):
    own = sz.states // sz.blocks
    part = sz.width // sz.blocks
    lane = lax.broadcasted_iota(jnp.int32, (8, LANES), 1)
    row = lax.broadcasted_iota(jnp.int32, (8, LANES), 0)
    pad = jnp.zeros((8, sz.width - LANES), F32)
    total = jnp.zeros((8, sz.width), F32)
    for block in range(sz.blocks):
        piece = smalls[0]
        for dist in range(1, sz.blocks):
            piece = jnp.where((meta[4] ^ turned(sz, dist)) == block, smalls[dist], piece)
        for first, count, size in ((0, 4, part), (4, 4, own)):
            mine = jnp.where((row >= first) & (row < first + count) & (lane < size), piece, 0.0)
            wide = jnp.concatenate([mine, pad], axis=1)
            total += pltpu.roll(wide, block * size, 1) if block else wide
    params[...] = total


def block_order(sz, core):
    held = [0]
    for step in range(bits_of(sz)):
        held += [dist ^ step_bit(sz, step, core) for dist in held]
    return held[1:]


def pile_kernel(sz, meta, *refs):
    at = 0
    for piece in refs[:-1]:
        refs[-1][at : at + piece.shape[0]] = piece[...]
        at += piece.shape[0]


def place_maps(sz, meta, own_maps, mine, other, skip, out):
    own = sz.states // sz.blocks
    count = own_maps.shape[0] // 2

    def put(index, owner, value):
        out[pl.ds(pl.multiple_of(index * sz.states + owner * own, own), own), :] = value

    for index in range(2 * count):
        put(index, meta[0], own_maps[index])
    for side, pieces in ((meta[2], mine), (1 - meta[2], other)):
        for place, (even, odd) in enumerate(zip(block_order(sz, 0), block_order(sz, 1)), 1):
            message = place.bit_length() - 1
            each = pieces[message].shape[0] >> message
            owner = meta[0] ^ jnp.where(side == 0, even, odd)
            for index in range(count):
                put(side * count + index, owner, pieces[message][(place - (1 << message)) * each + skip + index])


def open_kernel(sz, meta, perm, params, *refs):
    pieces, (hidden, normed, live, ahead, behind, stacked) = refs[: sz.blocks], refs[sz.blocks :]
    fill_masks(sz, meta, live, ahead, behind)
    place_pieces(sz, meta, pieces, stacked)
    gain = gain_of(params, 0)
    for rows in row_parts(sz):
        u = nt(perm[rows, :], stacked[...])
        hidden[rows, :] = u.astype(BF)
        normed[rows, :] = normed_rows(sz, u, gain, widen(live[rows, :], sz.width // LANES))


def enter_kernel(sz, meta, ahead, behind, params, normed, maps, other, w_in, driven, ends, send, enter):
    decay = decay_of(sz, params, 0)
    for side, half in ((meta[2], maps), (1 - meta[2], other)):
        w_in[pl.ds(pl.multiple_of(side * sz.states, sz.states), sz.states), :] = half[...]
    matmul_nt(normed, w_in, driven)
    chain_ends(sz, decay, ahead, behind, driven, 0, 0, ends)
    send_ends(sz, meta, decay, ends, enter, send)


def chain_kernel(sz, meta, ahead, behind, recv, params, ends, driven, states, enter):
    decay = decay_of(sz, params, 0)
    enter_chunk(sz, meta, recv, decay, ends, enter)
    chain_states(sz, decay, ahead, behind, driven, enter, states)


def middle_kernel(sz, meta, live, ahead, behind, states, params, normed, hidden, own_out, own_in, *refs):
    skip, gain_b, decay_b = skip_of(params, 0), gain_of(params, 1), decay_of(sz, params, 1)
    far = bits_of(sz)
    mine, other, refs = refs[:far], refs[far : 2 * far], refs[2 * far :]
    w_out, w_in_b, slope, hidden_b, normed_b, driven_b, ends_b, send_b, enter = refs
    place_maps(sz, meta, own_out, mine, other, 0, w_out)
    place_maps(sz, meta, own_in, mine, other, 2, w_in_b)
    for rows in row_parts(sz):
        on = widen(live[rows, :], sz.width // LANES)
        u = hidden[rows, :].astype(F32) + finish_rows(sz, rows, states, w_out, skip, normed, on, slope)
        hidden_b[rows, :] = u
        v = normed_rows(sz, u, gain_b, on)
        normed_b[rows, :] = v
        driven_b[rows, :] = nt(v, w_in_b[...])
    chain_ends(sz, decay_b, ahead, behind, driven_b, 0, 0, ends_b)
    send_ends(sz, meta, decay_b, ends_b, enter, send_b)


def leave_kernel(sz, meta, live, ahead, behind, recv, params, ends, driven, normed, hidden, own_out, *refs):
    decay, skip = decay_of(sz, params, 1), skip_of(params, 1)
    far = bits_of(sz)
    mine, other, refs = refs[:far], refs[far : 2 * far], refs[2 * far :]
    w_out, states, slope, last, enter = refs
    place_maps(sz, meta, own_out, mine, other, 3, w_out)
    enter_chunk(sz, meta, recv, decay, ends, enter)
    chain_states(sz, decay, ahead, behind, driven, enter, states)
    for rows in row_parts(sz):
        on = widen(live[rows, :], sz.width // LANES)
        last[rows, :] = (hidden[rows, :] + finish_rows(sz, rows, states, w_out, skip, normed, on, slope)).astype(BF)


def turn_kernel(sz, meta, ahead, behind, slope, normed, w_out, params, perm, *refs):
    decay = decay_of(sz, params, 1)
    pieces, refs = refs[: sz.blocks], refs[sz.blocks :]
    upstream, twice, grad_states, grad_skip, ends, send, stacked, enter = refs
    place_pieces(sz, meta, pieces, stacked)
    skips = []
    for rows in row_parts(sz):
        r = nt(perm[rows, :], stacked[...])
        upstream[rows, :] = r
        skips.append(open_rows(sz, rows, r, slope, normed, w_out, twice, grad_states))
    grad_skip[...] = jnp.sum(sum(skips), axis=0, keepdims=True)
    chain_ends(sz, decay, ahead, behind, grad_states, 2 * sz.states, 0, ends)
    send_ends(sz, meta, decay, ends, enter, send)


def back_middle_kernel(sz, meta, ahead, behind, recv, params, ends, grad_states, states, upstream, slope, hidden, w_in,
                       slope_b, normed_b, w_out_b,
                       grad_driven, grad_decay, grad_gain, upstream_b, twice_b, grad_states_b, grad_skip_b, ends_b, send_b,
                       enter, half):
    decay, skip, gain, decay_b = decay_of(sz, params, 1), skip_of(params, 1), gain_of(params, 1), decay_of(sz, params, 0)
    enter_chunk(sz, meta, recv, decay, ends, enter)
    adjoint_chains(sz, decay, ahead, behind, grad_states, enter, states, half, grad_driven, grad_decay)
    gains, skips = [], []
    for rows in row_parts(sz):
        r, terms = back_rows(sz, rows, grad_driven, w_in, upstream, slope, skip, hidden, gain)
        gains.append(terms)
        upstream_b[rows, :] = r
        skips.append(open_rows(sz, rows, r, slope_b, normed_b, w_out_b, twice_b, grad_states_b))
    grad_gain[...] = jnp.sum(sum(gains), axis=0, keepdims=True)
    grad_skip_b[...] = jnp.sum(sum(skips), axis=0, keepdims=True)
    chain_ends(sz, decay_b, ahead, behind, grad_states_b, 2 * sz.states, 0, ends_b)
    send_ends(sz, meta, decay_b, ends_b, enter, send_b)


def back_chain_kernel(sz, meta, ahead, behind, recv, params, ends, grad_states, states, grad_driven, grad_decay, enter, half):
    decay = decay_of(sz, params, 0)
    enter_chunk(sz, meta, recv, decay, ends, enter)
    adjoint_chains(sz, decay, ahead, behind, grad_states, enter, states, half, grad_driven, grad_decay)


def back_leave_kernel(sz, meta, params, grad_driven, upstream, slope, hidden, w_in, perm, done, *refs):
    skip, gain = skip_of(params, 0), gain_of(params, 0)
    pieces, (last, stacked) = refs[: sz.blocks], refs[sz.blocks :]
    for rows in row_parts(sz):
        r, _ = back_rows(sz, rows, grad_driven, w_in, upstream, slope, skip, hidden, gain)
        last[rows, :] = r.astype(BF)
    part = sz.width // sz.blocks
    cut_pieces(sz, meta, done, perm, stacked, [piece.at[0:part, :] for piece in pieces])
    cut_pieces(sz, meta, last, perm, stacked, [piece.at[part : 2 * part, :] for piece in pieces])


def weight_kernel(counts, other, sz, meta, *refs):
    half = 1 - meta[2] if other else meta[2]
    pairs = 2 * len(counts)
    out, at = refs[pairs], 0
    if len(refs) > pairs + 1:
        whole, out, terms = refs[pairs:]
        value = tn(refs[0][:, pl.ds(pl.multiple_of(half * sz.states, LANES), sz.states)], refs[1][...])
        out[...] = value.astype(out.dtype)
        rows = whole[pl.ds(pl.multiple_of(half * sz.states, sz.states), sz.states), :].astype(F32)
        terms[...] = jnp.sum(column_sum(rows * value), axis=0, keepdims=True)
        return
    for index, count in enumerate(counts):
        left, right = refs[2 * index], refs[2 * index + 1]
        for group in range(count):
            cols = pl.ds(pl.multiple_of((half * count + group) * sz.states, LANES), sz.states)
            out[at : at + sz.states, :] = tn(left[:, cols], right[...]).astype(out.dtype)
            at += sz.states


def split2(x):
    hi = x.astype(BF).astype(F32)
    return hi, x - hi


class Group(NamedTuple):
    first: int
    counts: tuple

    def rows(self, sz):
        return sum(self.counts) * (sz.states // sz.blocks)


def bits_of(sz):
    return sz.blocks.bit_length() - 1


def step_bit(sz, step, core):
    return 1 << ((step + core) % bits_of(sz))


def far_block(sz, group, slot, core):
    return sum(step_bit(sz, group.first + j, core) for j in range(bits_of(sz)) if (slot >> j) & 1)


def own_tiny(sz, params, terms, more, gain_b, skip_a, skip_b, decay_a, decay_b, tiny):
    gain_a = (terms[...] + more[...] + skip_of(params, 0) * skip_a[...]) / gain_of(params, 0)
    tiny[...] = jnp.zeros_like(tiny)
    for index, line in enumerate((gain_a, gain_b[...], skip_a[...], skip_b[...])):
        tiny[index : index + 1, :] = line
    tiny[4:6, 0 : sz.states] = decay_a[...]
    tiny[6:8, 0 : sz.states] = decay_b[...]
    return tiny[...]


def tiny_of(sz, tiny, owner):
    own, part = sz.states // sz.blocks, sz.width // sz.blocks
    row = lax.broadcasted_iota(jnp.int32, (8, LANES), 0)
    lane = lax.broadcasted_iota(jnp.int32, (8, LANES), 1)
    value = jnp.zeros((8, LANES), F32)
    for block in range(sz.blocks):
        wide = pltpu.roll(tiny, sz.width - block * part, 1) if block else tiny
        deep = pltpu.roll(tiny, sz.width - block * own, 1) if block else tiny
        mine = jnp.where(row < 4, jnp.where(lane < part, wide[:, :LANES], 0.0), jnp.where(lane < own, deep[:, :LANES], 0.0))
        value = jnp.where(owner == block, mine, value)
    return value


def put_sums(value, slot, kept, message, at):
    if slot % 2 == 0:
        kept[slot // 2] = value
        return at
    message[at : at + value.shape[0], :] = value.astype(BF)
    return at + value.shape[0]


def add_message(sz, group, kept, slot, message, at):
    return kept[slot] + message[at : at + group.rows(sz), :].astype(F32)


def step_kernel(old, new, sz, meta, *refs):
    came, refs = (refs[0], refs[1:]) if old else (None, refs)
    held, refs = refs[: len(old)], refs[len(old) :]
    if new:
        halves, refs = refs[: 2 * len(new.counts)], refs[2 * len(new.counts) :]
    keeps, message = refs[:-1], refs[-1]
    at = 0
    for (group, slots, row), kept, keep in zip(old, held, keeps):
        for slot in range(slots):
            value = add_message(sz, group, kept, slot, came, row + slot * group.rows(sz))
            at = put_sums(value, slot, keep, message, at)
    if new:
        own = sz.states // sz.blocks
        for slot in range(sz.blocks):
            owner = meta[0] ^ jnp.where(meta[2] == 0, far_block(sz, new, slot, 0), far_block(sz, new, slot, 1))
            parts = []
            for index, count in enumerate(new.counts):
                keep, got = halves[2 * index], halves[2 * index + 1]
                for one in range(count):
                    rows = pl.ds(pl.multiple_of(one * sz.states + owner * own, own), own)
                    parts.append(keep[rows, :].astype(F32) + got[rows, :].astype(F32))
            at = put_sums(jnp.concatenate(parts, axis=0), slot, keeps[-1], message, at)


def direct_kernel(group, sz, meta, keep, got, *refs):
    own = sz.states // sz.blocks
    lines, pieces, room = refs[:8], refs[8:-1], refs[-1]
    whole = own_tiny(sz, *lines, room)
    for index, piece in enumerate(pieces):
        owner = meta[0] ^ farthest(index, sz.blocks)
        rows = pl.ds(pl.multiple_of(owner * own, own), own)
        piece[0:own, :] = (keep[rows, :].astype(F32) + got[rows, :].astype(F32)).astype(BF)
        rest = jnp.zeros((8, sz.width - 2 * LANES), F32)
        wide = jnp.concatenate([*split2(tiny_of(sz, whole, owner)), rest], axis=1)
        piece[own : own + 16, :] = jnp.concatenate([wide, jnp.zeros_like(wide)], axis=0).astype(BF)


def fold_block_kernel(planes, groups, direct, sz, meta, *refs):
    lanes = sz.width // LANES
    held, refs = refs[: 2 * len(groups)], refs[2 * len(groups) :]
    pieces, refs = (refs[: sz.blocks], refs[sz.blocks :]) if direct else ((), refs)
    outs, talls = refs[:planes], refs[planes:]
    totals = [add_message(sz, group, held[2 * index], 0, held[2 * index + 1], row) for index, (group, row) in enumerate(groups)]
    if direct:
        total = pieces[0][...].astype(F32)
        for piece in pieces[1:]:
            total += piece[...].astype(F32)
        rows = total.shape[0] - 16
        totals.append(total[0:rows])
        tiny = total[rows : rows + 8, 0:LANES] + total[rows : rows + 8, LANES : 2 * LANES]
    at = 0
    for total, tall in zip(totals, talls):
        rows = total.shape[0]
        padded = tall.shape[0] // lanes
        for block in range(lanes):
            tall[block * padded : block * padded + rows, :] = total[:, block * LANES : (block + 1) * LANES].astype(BF)
            if padded > rows:
                tall[block * padded + rows : (block + 1) * padded, :] = jnp.zeros((padded - rows, LANES), BF)
        part = tall.shape[0] // planes
        for dist, out in enumerate(outs):
            out[at : at + part, :] = tall[pl.ds(pl.multiple_of((meta[3] ^ farthest(dist, planes)) * part, part), part), :]
        at += part
    if direct:
        rows = jnp.concatenate(split2(tiny), axis=0).astype(BF)
        for out in outs:
            out[at : at + 16, :] = rows


def fold_plane_kernel(early, sz, meta, *refs):
    parts, out, tiny = refs[early:-2], refs[-2], refs[-1]
    top = 0
    if early:
        total = refs[0][...].astype(F32)
        for piece in refs[1:early]:
            total += piece[...].astype(F32)
        top = total.shape[0]
        out[0:top, :] = total.astype(BF)
    total = parts[0][...].astype(F32)
    for piece in parts[1:]:
        total += piece[...].astype(F32)
    rows = total.shape[0] - 16
    out[top:, :] = total[0:rows].astype(BF)
    tiny[...] = total[rows : rows + 8] + total[rows + 8 :]


def finish_kernel(planes, groups, sz, meta, *refs):
    count = 2 * planes
    pieces, refs = refs[:count], refs[count:]
    tiny, lambda_log, lambda_imag, log_step, input_map = refs[0][...] + refs[1][...], *refs[2:6]
    grad_gain, grad_skip, grad_log, grad_imag, grad_step, grad_maps, grad_out = refs[6:13]
    talls, grad_in, lines = refs[13:-2], refs[-2], refs[-1]
    own = sz.states // sz.blocks
    lanes = sz.width // LANES
    start = 0
    for tall, group in zip(talls, groups):
        padded = tall.shape[0] // lanes
        part = tall.shape[0] // planes
        for side in range(2):
            half = meta[2] ^ side
            for dist in range(planes):
                rows = pl.ds(pl.multiple_of((meta[3] ^ farthest(dist, planes)) * part, part), part)
                tall[rows, :] = pieces[side * planes + dist][start : start + part, :]
            at = 0
            for which, layer, maps in group:
                out = grad_in if which == 0 else grad_out
                for one in range(maps):
                    for block in range(lanes):
                        rows = slice(block * padded + at, block * padded + at + own)
                        out[layer, half * maps + one, :, block * LANES : (block + 1) * LANES] = tall[rows, :].astype(F32)
                    at += own
        start += part
    width = sz.width // sz.blocks
    grad_gain[...] = tiny[0:2, 0:width]
    grad_skip[...] = tiny[2:4, 0:width]
    dr, di, sr, si = discretize(lambda_log[...], lambda_imag[...], log_step[...])
    lines[...] = jnp.zeros_like(lines)
    lines[0:2, 0:own] = sr
    lines[2:4, 0:own] = si
    cols = lines[...].T
    back = []
    for layer in range(2):
        qr, qi = cols[0:own, layer : layer + 1], cols[0:own, 2 + layer : 3 + layer]
        wr, wi = grad_in[layer, 0], grad_in[layer, 1]
        br, bi = input_map[layer, 0].astype(F32), input_map[layer, 1].astype(F32)
        grad_maps[layer, 0] = qr * wr + qi * wi
        grad_maps[layer, 1] = qr * wi - qi * wr
        back.append(jnp.sum(wr * br + wi * bi, axis=1, keepdims=True))
        back.append(jnp.sum(wi * br - wr * bi, axis=1, keepdims=True))
    lines[...] = jnp.zeros_like(lines)
    for index, col in enumerate(back):
        lines[0:own, index : index + 1] = col
    rows = lines[...].T
    step = jnp.exp(log_step[...])
    lr, li = -jnp.exp(lambda_log[...]), lambda_imag[...]
    norm = 1.0 / (lr * lr + li * li)
    for layer in range(2):
        at = slice(layer, layer + 1)
        a, b, h = (lr[at], li[at]), (dr[at], di[at]), step[at]
        gq = rows[2 * layer : 2 * layer + 1, 0:own], rows[2 * layer + 1 : 2 * layer + 2, 0:own]
        gd = tiny[4 + 2 * layer : 5 + 2 * layer, 0:own], tiny[5 + 2 * layer : 6 + 2 * layer, 0:own]
        inverse = a[0] * norm[at], -a[1] * norm[at]
        through = cmul(inverse[0], -inverse[1], *gq)
        gd = gd[0] + through[0], gd[1] + through[1]
        ratio = cmul(*inverse, sr[at], si[at])
        direct = cmul(ratio[0], -ratio[1], *gq)
        moved = cmul(b[0] * h, -b[1] * h, *gd)
        turn = cmul(*a, *b)
        grad_log[at, :] = (moved[0] - direct[0]) * a[0]
        grad_imag[at, :] = moved[1] - direct[1]
        grad_step[at, :] = (turn[0] * gd[0] + turn[1] * gd[1]) * h


def spread_kernel(sz, meta, *refs):
    pieces, outs, wide, sems = refs[: sz.blocks], refs[sz.blocks : -2], refs[-2], refs[-1]
    part = sz.width // sz.blocks
    copies = []
    for dist, piece in enumerate(pieces):
        owner = meta[0] ^ turned(sz, dist)
        for index, out in enumerate(outs):
            slot = dist * len(outs) + index
            wide[slot] = piece[index * part : (index + 1) * part, :].astype(F32)
            cols = pl.ds(pl.multiple_of(lax.rem(owner, sz.chunks) * sz.toks, LANES), sz.toks)
            copy = pltpu.make_async_copy(wide.at[slot], out.at[lax.div(owner, sz.chunks), :, cols], sems.at[slot])
            copy.start()
            copies.append(copy)
    for copy in copies:
        copy.wait()


VMEM = pl.BlockSpec(memory_space=pltpu.VMEM)
SMEM = pl.BlockSpec(memory_space=pltpu.SMEM)
HBM = pl.BlockSpec(memory_space=pltpu.HBM)


def call(name, sz, body, items, args, outs, scratch, limit=10, in_spec=VMEM, out_spec=VMEM, time=0.0):
    out_shape = [jax.ShapeDtypeStruct(shape, dtype) for shape, dtype in outs]

    def kernel(*refs):
        body(sz, place_of(sz, refs[0] if items else None), *refs[len(items) :])

    return pl.pallas_call(
        kernel,
        out_shape=out_shape,
        in_specs=[SMEM] * len(items) + [in_spec] * len(args),
        out_specs=[out_spec] * len(outs),
        scratch_shapes=[pltpu.VMEM(*item) if isinstance(item, tuple) else item for item in scratch],
        compiler_params=pltpu.CompilerParams(vmem_limit_bytes=limit << 20),
        cost_estimate=pl.CostEstimate(flops=int(COST * time), bytes_accessed=1000, transcendentals=0),
        name=name,
    )(*items, *args)


def on_device(tokens, cotangent, item_lengths, item_offsets, norm_gain, lambda_log, lambda_imag, log_step, input_map, output_map, skip_weight):
    micro, part, run = tokens.shape
    layers = norm_gain.shape[0]
    blocks = lax.axis_size("block")
    planes = lax.axis_size("plane")
    chunks = blocks // micro
    toks = run // chunks
    own = lambda_log.shape[1]
    width, states = part * blocks, own * blocks
    sz = Sizes(blocks, chunks, toks, run, toks // SEGS, width, states, item_lengths.shape[1])

    def swap(x, dist, axis="block"):
        return lax.ppermute(x, axis, [(i, i ^ dist) for i in range(lax.axis_size(axis))])

    def across(x, dist, back):
        pairs = []
        for c in range(2):
            for b in range(blocks):
                q = b ^ turned(sz, dist)
                pairs.append((c * blocks + b, (q % 2) * blocks + (q // 2) * 2 + c))
        return lax.ppermute(x, ("core", "block"), [pair[::-1] for pair in pairs] if back else pairs)

    def across_all(pieces, back=False):
        return [across(piece, dist, back) for dist, piece in enumerate(pieces)]

    table = jnp.stack([item_lengths, item_offsets])
    other_table = swap(table, 1, "core")

    def neighbour(x, dist):
        pairs = []
        for c in range(2):
            for b in range(blocks):
                q = ((b // 2) * 2 + c) ^ dist
                pairs.append((c * blocks + b, (q % 2) * blocks + (q // 2) * 2 + b % 2))
        return lax.ppermute(x, ("core", "block"), pairs)

    def swap_all(pieces, axis="block"):
        count = len(pieces)
        return [swap(piece, farthest(index, count), axis) if index else piece for index, piece in enumerate(pieces)]

    def exchange(send):
        return jnp.stack([neighbour(send[dist - 1], dist) for dist in range(1, chunks)])

    row = jnp.arange(toks, dtype=jnp.int32)[:, None]
    col = jnp.arange(toks, dtype=jnp.int32)[None, :]
    perm = ((row % SEGS) * sz.steps + row // SEGS == col).astype(BF)

    maps_own = ((2, own, width), BF)
    half_own = ((5, own, width), BF)
    given = [norm_gain, skip_weight, lambda_log, lambda_imag, log_step, input_map, output_map]
    *first_pieces, drive_b, half_b = call(
        "prepare", sz, prepare_kernel, [], [pltpu.with_memory_space_constraint(x, pltpu.HBM) for x in [tokens, *given]],
        [((first_rows(sz)[1] + 16, toks), BF)] * blocks + [maps_own, half_own],
        [(x.shape, x.dtype) for x in given] + [((8, LANES), F32), ((8, LANES), F32), maps_own, pltpu.SemaphoreType.DMA((len(given) + blocks,))],
        limit=6, in_spec=HBM)
    first_pieces = across_all(first_pieces)
    cot_cut = call("cut_cotangent", sz, cut_kernel, [], [pltpu.with_memory_space_constraint(cotangent, pltpu.HBM)],
                   [((part, toks), BF)] * blocks, [((blocks, part, toks), F32), pltpu.SemaphoreType.DMA((blocks,))], limit=4, in_spec=HBM)
    first_pieces[1], perm, cot_cut = after(first_pieces[1], perm, cot_cut)
    second_mine, held = [], half_b
    for step in range(bits_of(sz)):
        pairs = [(c * blocks + b, c * blocks + (b ^ step_bit(sz, step, c))) for c in range(2) for b in range(blocks)]
        second_mine.append(lax.ppermute(held, ("core", "block"), pairs))
        if step == 0:
            second_mine[0], first_pieces = after(second_mine[0], first_pieces)
        if step + 1 < bits_of(sz):
            (held,) = call("pile_%d" % step, sz, pile_kernel, [], [held, second_mine[-1]], [((2 * held.shape[0], own, width), BF)], [])
    maps_a, params = call("join", sz, join_kernel, [], first_pieces, [((states, width), BF), ((8, width), F32)], [])
    maps_a, other_table = after(maps_a, other_table)
    items = [jnp.stack([table, other_table])]


    mask = ((toks, LANES), F32)
    enter = ((4, SEGS, states), F32)
    stacked = ((width, toks), BF)
    rows_f, rows_b = ((toks, width), F32), ((toks, width), BF)
    drv = ((toks, 2 * states), F32)
    sts = ((toks, 4 * states), BF)
    gst = ((toks, 4 * states), F32)
    snd = ((chunks - 1, 2, states), F32)
    w_in, w_out = ((2 * states, width), BF), ((4 * states, width), BF)
    line, gdec = ((1, width), F32), ((2, states), F32)
    piece_out = [((part, toks), BF)] * blocks

    other_a = swap(maps_a, 1, "core")
    hidden_a, normed_a, live, ahead, behind = call(
        "open", sz, open_kernel, items, [perm, params, *first_pieces], [rows_b, rows_b, mask, mask, mask], [stacked], time=3)
    w_in_a, driven_a, ends_a, send_a = call(
        "enter", sz, enter_kernel, items, [ahead, behind, params, normed_a, maps_a, other_a], [w_in, drv, enter, snd], [enter])
    recv = exchange(send_a)
    early_maps = [swap(piece, 1, "core") for piece in second_mine[:-1]]
    recv, early_maps = after(recv, early_maps)
    (states_a,) = call("chain", sz, chain_kernel, items, [ahead, behind, recv, params, ends_a, driven_a], [sts], [enter])
    last_mine, states_a = after(second_mine[-1], states_a)
    second_maps = [*second_mine[:-1], last_mine], [*early_maps, swap(last_mine, 1, "core")]
    cot_cut, _ = after(cot_cut, recv)
    cot_pieces = across_all(cot_cut)
    w_out_a, w_in_b, slope_a, hidden_b, normed_b, driven_b, ends_b, send_b = call(
        "middle", sz, middle_kernel, items,
        [live, ahead, behind, states_a, params, normed_a, hidden_a, output_map[0], drive_b, *second_maps[0], *second_maps[1]],
        [w_out, w_in, rows_b, rows_f, rows_b, drv, enter, snd], [enter], time=11)
    recv = exchange(send_b)
    w_out_b, states_b, slope_b, last_b = call(
        "leave", sz, leave_kernel, items,
        [live, ahead, behind, recv, params, ends_b, driven_b, normed_b, hidden_b, output_map[1], *second_maps[0], *second_maps[1]],
        [w_out, sts, rows_b, rows_b], [enter])

    def half_grads(name, other, pairs, counts, more=(), time=0.0):
        args = [x for pair in pairs for x in pair]
        outs = [((sum(counts) * states, width), BF)] + [line] * len(more)
        return call(name, sz, partial(weight_kernel, counts, other), [], [*args, *more], outs, [], time=time)

    groups = [Group(0, (2,)), Group(1, (3,))]
    steps = bits_of(sz)
    kept, came, place = {}, {}, {}

    def halve(step, halves=()):
        old, args = [], []
        for index, group in enumerate(groups):
            if 0 < step - group.first < steps:
                slots = 1 << (steps - (step - group.first))
                old.append((group, slots, place[step - 1, index]))
                args.append(kept[index])
        if old:
            args.insert(0, came[step - 1])
        new = groups[step] if step < len(groups) else None
        outs, at = [], 0
        for index, group in enumerate(groups):
            if 0 <= step - group.first < steps:
                slots = 1 << (steps - 1 - (step - group.first))
                outs.append((index, ((slots, group.rows(sz), width), F32)))
                place[step, index] = at
                at += slots * group.rows(sz)
        results = call("halve_%d" % step, sz, partial(step_kernel, old, new), [], [*args, *halves],
                       [shape for _, shape in outs] + [((at, width), BF)], [])
        for (index, _), value in zip(outs, results):
            kept[index] = value
        return results[-1]

    def send_step(step, message):
        pairs = [(c * blocks + b, c * blocks + (b ^ step_bit(sz, step, c))) for c in range(2) for b in range(blocks)]
        came[step] = lax.ppermute(message, ("core", "block"), pairs)

    def spread(pieces):
        return call("spread", sz, spread_kernel, [], pieces, [((micro, part, run), F32)] * 2,
                    [((2 * blocks, part, toks), F32), pltpu.SemaphoreType.DMA((2 * blocks,))], limit=6, out_spec=HBM, time=9)

    lanes = width // LANES

    def tall_of(rows):
        step = max(SEGS * planes // lanes, SEGS)
        return ((lanes * (-(-rows // step) * step), LANES), BF)

    def over_planes(name, which, direct=()):
        ends = [(groups[index], place[groups[index].first + steps - 1, index]) for index in which]
        talls = [tall_of(group.rows(sz)) for group, _ in ends] + [tall_of(own)] * bool(direct)
        cut = sum(t[0][0] for t in talls) // planes + (16 if direct else 0)
        args = [x for index in which for x in (kept[index], came[groups[index].first + steps - 1])]
        return swap_all(call(name, sz, partial(fold_block_kernel, planes, ends, bool(direct)), [], [*args, *direct],
                             [((cut, LANES), BF)] * planes, talls), "plane")

    up_b, twice_b, gstates_b, gskip_b, ends, send = call(
        "turn", sz, turn_kernel, items, [ahead, behind, slope_b, normed_b, w_out_b, params, perm, *cot_pieces],
        [rows_f, rows_b, gst, line, enter, snd], [stacked, enter], time=6)
    recv = exchange(send)
    pairs = [(states_b, twice_b)]
    (send_maps,) = half_grads("grads_a_send", True, pairs, (2,))
    got = swap(send_maps, 1, "core")
    (keep,) = half_grads("grads_a_keep", False, pairs, (2,), time=2)
    message = halve(0, (keep, got))
    recv, message = after(recv, message)
    send_step(0, message)
    gdriven_b, gdecay_b, ggain_b, up_a, twice_a, gstates_a, gskip_a, ends, send = call(
        "back_middle", sz, back_middle_kernel, items,
        [ahead, behind, recv, params, ends, gstates_b, states_b, up_b, slope_b, hidden_b, w_in_b, slope_a, normed_a, w_out_a],
        [((toks, 2 * states), BF), gdec, line, rows_f, rows_b, gst, line, enter, snd], [enter, drv], limit=12, time=11)
    recv = exchange(send)
    gdriven_b, came[0] = after(gdriven_b, came[0])
    pairs = [(gdriven_b, normed_b), (states_a, twice_a)]
    (send_maps,) = half_grads("grads_b_send", True, pairs, (1, 2))
    got = swap(send_maps, 1, "core")
    (keep,) = half_grads("grads_b_keep", False, pairs, (1, 2), time=9)
    message = halve(1, (keep, got))
    recv, message = after(recv, message)
    send_step(1, message)
    gdriven_a, gdecay_a = call(
        "back_chain", sz, back_chain_kernel, items, [ahead, behind, recv, params, ends, gstates_a, states_a],
        [((toks, 2 * states), BF), gdec], [enter, drv], limit=12, time=9)
    send_maps, terms = half_grads("grads_c_send", True, [(gdriven_a, normed_a)], (1,), [w_in_a])
    gdriven_a, send_maps = after(gdriven_a, send_maps)
    got = swap(send_maps, 1, "core")
    keep, more = half_grads("grads_c_keep", False, [(gdriven_a, normed_a)], (1,), [w_in_a], time=0)
    sums_c = list(call(
        "direct", sz, partial(direct_kernel, None), [],
        [keep, got, params, terms, more, ggain_b, gskip_a, gskip_b, gdecay_a, gdecay_b], [((own + 16, width), BF)] * blocks, [((8, width), F32)]))
    gdriven_a, sums_c[0] = after(gdriven_a, sums_c[0])
    sums_c = swap_all(sums_c)
    last_pieces = call(
        "back_leave", sz, back_leave_kernel, [], [params, gdriven_a, up_a, slope_a, hidden_a, w_in_a, perm, last_b],
        [((2 * part, toks), BF)] * blocks, [rows_b, stacked], limit=12, time=6)
    last_pieces, came[1], sums_c = after(last_pieces, came[1], sums_c)
    message = halve(2)
    kept[0], message = after(kept[0], message)
    first_parts = over_planes("planes_a", [0]) if steps <= 2 else []
    send_step(2, message)
    if first_parts:
        came[2], first_parts = after(came[2], first_parts)
    for step in range(3, steps + 1):
        send_step(step, halve(step))
    parts = over_planes("planes", [1] if first_parts else [0, 1], sums_c)
    last_pieces, parts[0] = after(last_pieces, parts[0])
    early = [across(piece, 2 * dist, True) for dist, piece in enumerate(last_pieces[0::2])]
    parts[0], early = after(parts[0], early)
    sum_all, tiny = call(
        "sum", sz, partial(fold_plane_kernel, len(first_parts)), [], [*first_parts, *parts],
        [((sum(x[0].shape[0] for x in (first_parts, parts) if x) - 16, LANES), BF), ((8, LANES), F32)], [])
    whole = swap_all([sum_all] * planes, "plane")
    late, _ = after(last_pieces[1::2], sum_all)
    late = [across(piece, 2 * dist + 1, True) for dist, piece in enumerate(late)]
    whole = swap_all([sum_all] * planes, "plane")
    late, others = after(late, [sum_all, tiny, *whole[planes - 0 :]])
    others = [swap(x, 1, "core") for x in others]
    output, input_grad = spread([piece for pair in zip(early, late) for piece in pair])
    far = whole[1 : planes - 0]
    far, others, output = after(far, others, output)
    far = [swap(x, 1, "core") for x in far]
    whole += [others[0], *far, *others[2:]]
    tiny_other = others[1]
    small_out = ((layers, own), F32)
    grad_gain, grad_skip, grad_log, grad_imag, grad_step, grad_in, grad_out = call(
        "finish", sz, partial(finish_kernel, planes, ([(1, 1, 2)], [(0, 1, 1), (1, 0, 2)], [(0, 0, 1)])), [],
        [*whole, tiny, tiny_other, lambda_log, lambda_imag, log_step, input_map],
        [((layers, part), F32)] * 2 + [small_out] * 3 + [((layers, 2, own, width), F32), ((layers, 4, own, width), F32)],
        [tall_of(n * own) for n in (2, 3, 1)] + [((layers, 2, own, width), F32), ((LANES, LANES), F32)])
    return output, input_grad, grad_gain, grad_log, grad_imag, grad_step, grad_in, grad_out, grad_skip


def solution(mesh):
    rows, blocks = mesh.devices.shape
    inner = Mesh(mesh.devices.reshape(rows // 2, 2, blocks), ("plane", "core", "block"))
    dp = ("plane", "core")
    half = P(None, "block")
    maps = P(None, None, "block", None)
    acts = P(None, "block", dp)
    items = P(None, dp)
    return jax.shard_map(
        on_device,
        mesh=inner,
        in_specs=(acts, acts, items, items, half, half, half, half, maps, maps, half),
        out_specs=(acts, acts, half, half, half, half, maps, maps, half),
        check_vma=False,
    )
```

```python
from functools import partial
from typing import NamedTuple

import jax
import jax.numpy as jnp
from jax import lax
from jax.experimental import pallas as pl
from jax.experimental.pallas import tpu as pltpu
from jax.sharding import Mesh, PartitionSpec as P

EPSILON = 1e-05
SEGS = 16
LANES = 128
BF = jnp.bfloat16
F32 = jnp.float32
GELU_C = 0.7978845608028654
GELU_A = 0.044715
COST = 400_000_000


class Sizes(NamedTuple):
    blocks: int
    chunks: int
    toks: int
    run: int
    steps: int
    width: int
    states: int
    items: int


def turned(sz, index):
    return sz.blocks - 1 - index


def farthest(index, count):
    return count - index if index else 0


def place_of(sz, table):
    me, core = lax.axis_index("block"), lax.axis_index("core")
    q = lax.div(me, 2) * 2 + core
    mine, chunk = lax.div(q, sz.chunks), lax.rem(q, sz.chunks)
    out = [me, chunk, core, lax.axis_index("plane"), q]
    if table is not None:
        side = lax.rem(me, 2) ^ core
        for which in range(2):
            out += [table[side, which, mine, index] for index in range(sz.items)]
    return out


def nt(a, b):
    return lax.dot_general(a, b, (((1,), (1,)), ((), ())), preferred_element_type=F32)


def nn(a, b):
    return lax.dot_general(a, b, (((1,), (0,)), ((), ())), preferred_element_type=F32)


def tn(a, b):
    return lax.dot_general(a, b, (((0,), (0,)), ((), ())), preferred_element_type=F32)


def after(*values):
    return lax.optimization_barrier(values)


def cmul(ar, ai, br, bi):
    return ar * br - ai * bi, ar * bi + ai * br


def rows_of(step):
    return pl.ds(pl.multiple_of(step * SEGS, SEGS), SEGS)


def widen(mask, count):
    return jnp.concatenate([mask] * count, axis=1)


def item_of(sz, meta, index):
    begin = meta[5 + sz.items + index]
    return begin, begin + meta[5 + index]


def fill_masks(sz, meta, live, ahead, behind):
    base = meta[1] * sz.toks
    seg = lax.broadcasted_iota(jnp.int32, (SEGS, LANES), 0)

    def body(step, carry):
        pos = base + seg * sz.steps + step
        inside = jnp.zeros((SEGS, LANES), F32)
        onward = jnp.zeros((SEGS, LANES), F32)
        onward_next = jnp.zeros((SEGS, LANES), F32)
        for index in range(sz.items):
            begin, end = item_of(sz, meta, index)
            inside = jnp.where((pos >= begin) & (pos < end), 1.0, inside)
            onward = jnp.where((pos > begin) & (pos < end), 1.0, onward)
            onward_next = jnp.where((pos >= begin) & (pos + 1 < end), 1.0, onward_next)
        onward_next = jnp.where(pos + 1 < sz.run, onward_next, 0.0)
        live[rows_of(step), :] = inside
        ahead[rows_of(step), :] = onward
        behind[rows_of(step), :] = onward_next
        return carry

    lax.fori_loop(0, sz.steps, body, 0, unroll=8)


def through(sz, meta, first, length):
    ahead = behind = False
    for index in range(sz.items):
        begin, end = item_of(sz, meta, index)
        ahead = ahead | ((begin < first) & (end >= first + length))
        behind = behind | ((begin <= first) & (end > first + length))
    behind = behind & (first + length < sz.run)
    return ahead, behind


def power(pair, count):
    while count > 1:
        pair = cmul(*pair, *pair)
        count //= 2
    return pair


def column_blocks(sz, decay):
    out = []
    for q in range(sz.states // LANES):
        cols = slice(q * LANES, (q + 1) * LANES)
        out.append((decay[0:1, cols], decay[1:2, cols]))
    return out


def spread(pairs):
    return [tuple(jnp.broadcast_to(v, (SEGS, LANES)) for v in pair) for pair in pairs]


def chain_ends(sz, decay, ahead, behind, source, ahead_col, behind_col, ends):
    nq = sz.states // LANES
    d = spread(column_blocks(sz, decay))
    zero = jnp.zeros((SEGS, LANES), F32)

    def body(step, held):
        up, down = rows_of(step), rows_of(sz.steps - 1 - step)
        on_up, on_down = ahead[up, :], behind[down, :]
        new = []
        for q in range(nq):
            for side, (rows, on, col) in enumerate(((up, on_up, ahead_col), (down, on_down, behind_col))):
                re, im = held[2 * q + side]
                re, im = cmul(*d[q], re * on, im * on)
                re += source[rows, col + q * LANES : col + (q + 1) * LANES]
                im += source[rows, col + sz.states + q * LANES : col + sz.states + (q + 1) * LANES]
                new.append((re, im))
        return tuple(new)

    held = lax.fori_loop(0, sz.steps, body, tuple((zero, zero) for _ in range(2 * nq)), unroll=8)
    for q in range(nq):
        cols = slice(q * LANES, (q + 1) * LANES)
        for side in range(2):
            ends[2 * side, :, cols] = held[2 * q + side][0]
            ends[2 * side + 1, :, cols] = held[2 * q + side][1]


def enter_states(sz, meta, decay, ends, start, enter):
    pair = (decay[0:1, :], decay[1:2, :])
    jump = power(pair, sz.steps)
    base = meta[1] * sz.toks
    state = list(start)
    for count in range(SEGS):
        for side, seg in ((0, count), (1, SEGS - 1 - count)):
            re, im = state[side]
            enter[2 * side, seg : seg + 1, :] = re
            enter[2 * side + 1, seg : seg + 1, :] = im
            passes = through(sz, meta, base + seg * sz.steps, sz.steps)[side]
            gain = jnp.where(passes, 1.0, 0.0).astype(F32)
            re, im = cmul(jump[0] * gain, jump[1] * gain, re, im)
            state[side] = (
                re + ends[2 * side, seg : seg + 1, :],
                im + ends[2 * side + 1, seg : seg + 1, :],
            )
    return state


def send_ends(sz, meta, decay, ends, enter, send):
    zero = jnp.zeros((1, sz.states), F32)
    ahead, behind = enter_states(sz, meta, decay, ends, ((zero, zero), (zero, zero)), enter)
    me = meta[1]
    for dist in range(1, sz.chunks):
        up = (me ^ dist) > me
        for part in range(2):
            send[dist - 1, part : part + 1, :] = jnp.where(up, ahead[part], behind[part])


def received(sz, meta, decay, recv):
    me = meta[1]
    zero = jnp.zeros((1, sz.states), F32)
    pair = (decay[0:1, :], decay[1:2, :])
    jump = power(pair, sz.toks) if sz.chunks > 2 else None
    sides = []
    for side in range(2):
        re, im = zero, zero
        order = range(sz.chunks) if side == 0 else range(sz.chunks - 1, -1, -1)
        for other in order:
            use = (other < me) if side == 0 else (other > me)
            slot = jnp.maximum((me ^ other) - 1, 0)
            got = recv[slot]
            new_re, new_im = got[0:1, :], got[1:2, :]
            if sz.chunks > 2:
                passes = through(sz, meta, other * sz.toks, sz.toks)[side]
                gain = jnp.where(passes, 1.0, 0.0).astype(F32)
                moved = cmul(jump[0] * gain, jump[1] * gain, re, im)
                new_re, new_im = new_re + moved[0], new_im + moved[1]
            re, im = jnp.where(use, new_re, re), jnp.where(use, new_im, im)
        sides.append((re, im))
    return sides


def load_enter(sz, enter):
    held = []
    for q in range(sz.states // LANES):
        cols = slice(q * LANES, (q + 1) * LANES)
        for side in range(2):
            held.append((enter[2 * side, :, cols], enter[2 * side + 1, :, cols]))
    return tuple(held)


def chain_states(sz, decay, ahead, behind, source, enter, states):
    nq = sz.states // LANES
    n = sz.states
    d = spread(column_blocks(sz, decay))

    def body(step, held):
        up, down = rows_of(step), rows_of(sz.steps - 1 - step)
        on_up, on_down = ahead[up, :], behind[down, :]
        new = []
        for q in range(nq):
            for side, (rows, on) in enumerate(((up, on_up), (down, on_down))):
                re, im = held[2 * q + side]
                re, im = cmul(*d[q], re * on, im * on)
                lo = q * LANES
                re += source[rows, lo : lo + LANES]
                im += source[rows, n + lo : n + lo + LANES]
                at = 2 * side * n + lo
                states[rows, at : at + LANES] = re.astype(BF)
                states[rows, at + n : at + n + LANES] = (-im).astype(BF)
                new.append((re, im))
        return tuple(new)

    lax.fori_loop(0, sz.steps, body, load_enter(sz, enter), unroll=8)


def adjoint_chains(sz, decay, ahead, behind, source, enter, states, half, grad_driven, grad_decay):
    nq = sz.states // LANES
    n = sz.states
    d = spread(column_blocks(sz, decay))
    zero = jnp.zeros((SEGS, LANES), F32)

    def make(second):
        def body(step, carry):
            held, sums = carry
            up, down = rows_of(step), rows_of(sz.steps - 1 - step)
            on_up, on_down = ahead[up, :], behind[down, :]
            new, total = [], []
            for q in range(nq):
                lo = q * LANES
                acc_re, acc_im = sums[q]
                for side, (rows, on, src, st) in enumerate(((up, on_up, 2 * n, 2 * n), (down, on_down, 0, 0))):
                    re, im = held[2 * q + side]
                    re, im = re * on, im * on
                    s_re = states[rows, st + lo : st + lo + LANES].astype(F32)
                    s_im = states[rows, st + n + lo : st + n + lo + LANES].astype(F32)
                    acc_re += re * s_re + im * s_im
                    acc_im += re * s_im - im * s_re
                    re, im = cmul(*d[q], re, im)
                    re += source[rows, src + lo : src + lo + LANES]
                    im += source[rows, src + n + lo : src + n + lo + LANES]
                    new.append((re, im))
                    if second:
                        out_re = re + half[rows, lo : lo + LANES]
                        out_im = im + half[rows, n + lo : n + lo + LANES]
                        grad_driven[rows, lo : lo + LANES] = out_re.astype(BF)
                        grad_driven[rows, n + lo : n + lo + LANES] = (-out_im).astype(BF)
                    else:
                        half[rows, lo : lo + LANES] = re
                        half[rows, n + lo : n + lo + LANES] = im
                total.append((acc_re, acc_im))
            return tuple(new), tuple(total)

        return body

    carry = (load_enter(sz, enter), tuple((zero, zero) for _ in range(nq)))
    carry = lax.fori_loop(0, sz.steps // 2, make(False), carry, unroll=4)
    carry = lax.fori_loop(sz.steps // 2, sz.steps, make(True), carry, unroll=4)
    for q in range(nq):
        cols = slice(q * LANES, (q + 1) * LANES)
        grad_decay[0:1, cols] = jnp.sum(carry[1][q][0], axis=0, keepdims=True)
        grad_decay[1:2, cols] = jnp.sum(carry[1][q][1], axis=0, keepdims=True)


ROWS = 512


def row_parts(sz):
    size = min(ROWS, sz.toks)
    return [slice(lo, lo + size) for lo in range(0, sz.toks, size)]


def matmul_nt(a, b, out, tile=256):
    for lo in range(0, b.shape[0], tile):
        out[:, lo : lo + tile] = nt(a[...], b[lo : lo + tile, :]).astype(out.dtype)


def matmul_tn(a, b, out, tile=256):
    for lo in range(0, a.shape[1], tile):
        out[lo : lo + tile, :] = tn(a[:, lo : lo + tile], b[...]).astype(out.dtype)


def column_sum(x):
    return jnp.sum(x.reshape(x.shape[0] // 8, 8, x.shape[1]), axis=0)


def scale_of(u):
    return lax.rsqrt(jnp.mean(u * u, axis=1, keepdims=True) + EPSILON)


def normed_rows(sz, u, gain, on):
    return (u * scale_of(u) * gain * on).astype(BF)


def finish_rows(sz, rows, states, w_out, skip, normed, on, slope):
    pre = 2.0 * nn(states[rows, :], w_out[...]) + skip * normed[rows, :].astype(F32)
    square = pre * pre
    th = jnp.tanh(pre * (GELU_C + (GELU_C * GELU_A) * square))
    part = 0.5 + 0.5 * th
    deriv = part + pre * (1.0 - th * th) * (0.5 * GELU_C + (1.5 * GELU_C * GELU_A) * square)
    slope[rows, :] = (on * deriv).astype(slope.dtype)
    return on * (pre * part)


def enter_chunk(sz, meta, recv, decay, ends, enter):
    enter_states(sz, meta, decay, ends, received(sz, meta, decay, recv), enter)


def back_rows(sz, rows, grad_driven, w_in, upstream, slope, skip, hidden, gain):
    u = hidden[rows, :].astype(F32)
    r = upstream[rows, :]
    gn = nn(grad_driven[rows, :], w_in[...]) + r * slope[rows, :].astype(F32) * skip
    scale = scale_of(u)
    moved = u * scale
    dn = gn * gain
    inner = jnp.sum(dn * moved, axis=1, keepdims=True) * (1.0 / sz.width)
    return r + scale * (dn - moved * inner), column_sum(gn * moved)


def open_rows(sz, rows, r, slope, normed, w_out, twice, grad_states):
    e = r * slope[rows, :].astype(F32)
    low = e.astype(BF)
    double = low + low
    twice[rows, :] = double
    grad_states[rows, :] = nt(double, w_out[...])
    return column_sum(e * normed[rows, :].astype(F32))


def gain_of(params, layer):
    return params[layer : layer + 1, :]


def skip_of(params, layer):
    return params[2 + layer : 3 + layer, :]


def decay_of(sz, params, layer):
    return params[4 + 2 * layer : 6 + 2 * layer, 0 : sz.states]


def place_pieces(sz, meta, pieces, stacked):
    part = sz.width // sz.blocks
    for dist, piece in enumerate(pieces):
        owner = meta[4] ^ turned(sz, dist)
        stacked[pl.ds(pl.multiple_of(owner * part, part), part), :] = piece[0:part, :]


def cut_pieces(sz, meta, rows, perm, stacked, pieces):
    part = sz.width // sz.blocks
    matmul_tn(rows, perm, stacked)
    for dist, piece in enumerate(pieces):
        owner = meta[4] ^ turned(sz, dist)
        piece[...] = stacked[pl.ds(pl.multiple_of(owner * part, part), part), :]


def cut_kernel(sz, meta, whole, *refs):
    outs, wide, sems = refs[: sz.blocks], refs[-2], refs[-1]
    straight = whole.dtype == BF
    copies = []
    for dist in range(sz.blocks):
        to = meta[0] ^ turned(sz, dist)
        cols = pl.ds(pl.multiple_of(lax.rem(to, sz.chunks) * sz.toks, LANES), sz.toks)
        source = whole.at[lax.div(to, sz.chunks), :, cols]
        copy = pltpu.make_async_copy(source, outs[dist] if straight else wide.at[dist], sems.at[dist])
        copy.start()
        copies.append(copy)
    for dist, copy in enumerate(copies):
        copy.wait()
        if not straight:
            outs[dist][...] = wide[dist].astype(BF)


def discretize(lambda_log, lambda_imag, log_step):
    step_size = jnp.exp(log_step)
    lambda_real = -jnp.exp(lambda_log)
    modulus = jnp.exp(lambda_real * step_size)
    decay_real = modulus * jnp.cos(lambda_imag * step_size)
    decay_imag = modulus * jnp.sin(lambda_imag * step_size)
    denominator = lambda_real * lambda_real + lambda_imag * lambda_imag
    scale_real = ((decay_real - 1.0) * lambda_real + decay_imag * lambda_imag) / denominator
    scale_imag = (decay_imag * lambda_real - (decay_real - 1.0) * lambda_imag) / denominator
    return decay_real, decay_imag, scale_real, scale_imag


def first_rows(sz):
    part, own = sz.width // sz.blocks, sz.states // sz.blocks
    return part, part + own * sz.width // sz.toks


def half_map_parts(sz):
    top, end = first_rows(sz)
    rows = end - top
    for index in range(sz.toks // sz.width):
        yield slice(index * rows, (index + 1) * rows), slice(top, end), slice(index * sz.width, (index + 1) * sz.width)


def split3(x):
    hi = x.astype(BF).astype(F32)
    mid = (x - hi).astype(BF).astype(F32)
    return hi, mid, x - hi - mid


def prepare_kernel(sz, meta, tokens, *refs):
    inputs, refs = refs[:7], refs[7:]
    outs, refs = refs[: sz.blocks], refs[sz.blocks :]
    drive_b, half_b = refs[:2]
    held, small, lines, drive_a, sems = refs[2:9], refs[9], refs[10], refs[11], refs[12]
    top, end = first_rows(sz)
    own, part = sz.states // sz.blocks, sz.width // sz.blocks
    loads, copies = [], []
    for index, (source, target) in enumerate(zip(inputs, held)):
        loads.append(pltpu.make_async_copy(source, target, sems.at[index]))
    for dist in range(sz.blocks):
        to = meta[0] ^ turned(sz, dist)
        cols = pl.ds(pl.multiple_of(lax.rem(to, sz.chunks) * sz.toks, LANES), sz.toks)
        source = tokens.at[lax.div(to, sz.chunks), :, cols]
        copies.append(pltpu.make_async_copy(source, outs[dist].at[0:top, :], sems.at[len(inputs) + dist]))
    for copy in copies + loads:
        copy.start()
    for copy in loads[:6]:
        copy.wait()
    gain, skip, lambda_log, lambda_imag, log_step, input_map, output_map = held
    dr, di, sr, si = discretize(lambda_log[...], lambda_imag[...], log_step[...])
    small[...] = jnp.zeros_like(small)
    lines[...] = jnp.zeros_like(lines)
    small[0:2, 0:part] = gain[...]
    small[2:4, 0:part] = skip[...]
    for layer in range(2):
        small[4 + 2 * layer : 5 + 2 * layer, 0:own] = dr[layer : layer + 1]
        small[5 + 2 * layer : 6 + 2 * layer, 0:own] = di[layer : layer + 1]
    lines[0:2, 0:own] = sr
    lines[2:4, 0:own] = si
    cols = lines[...].T
    for layer in range(2):
        qr, qi = cols[0:own, layer : layer + 1], cols[0:own, 2 + layer : 3 + layer]
        br, bi = input_map[layer, 0].astype(F32), input_map[layer, 1].astype(F32)
        for index, value in enumerate((qr * br - qi * bi, qr * bi + qi * br)):
            (drive_a, drive_b)[layer][index] = value.astype(BF)
    rows = jnp.concatenate([*split3(small[...]), jnp.zeros((8, sz.toks - 3 * LANES), F32)], axis=1)
    rows = jnp.concatenate([rows, jnp.zeros((8, sz.toks), F32)], axis=0).astype(BF)
    for dist, out in enumerate(outs):
        half = lax.rem(meta[0] ^ turned(sz, dist), 2)
        for from_rows, to_rows, lanes in half_map_parts(sz):
            out[to_rows, lanes] = drive_a[half, from_rows, :]
        out[end:, :] = rows
    loads[6].wait()
    core = meta[2]
    for index in range(2):
        half_b[index] = output_map[0, 2 * core + index]
        half_b[3 + index] = output_map[1, 2 * core + index]
    half_b[2] = drive_b[core]
    for copy in copies:
        copy.wait()


def params_of(sz, piece):
    rows = piece[piece.shape[0] - 16 :, 0 : 3 * LANES].astype(F32)[0:8]
    return rows[:, 0:LANES] + rows[:, LANES : 2 * LANES] + rows[:, 2 * LANES :]


def join_kernel(sz, meta, *refs):
    pieces, maps, params = refs[: sz.blocks], refs[-2], refs[-1]
    own = sz.states // sz.blocks
    collect_params(sz, meta, [params_of(sz, piece) for piece in pieces], params)
    for dist, piece in enumerate(pieces):
        base = (meta[4] ^ turned(sz, dist)) * own
        for to_rows, from_rows, lanes in half_map_parts(sz):
            rows = pl.ds(pl.multiple_of(base + to_rows.start, 16), to_rows.stop - to_rows.start)
            maps[rows, :] = piece[from_rows, lanes]


def collect_params(sz, meta, smalls, params):
    own = sz.states // sz.blocks
    part = sz.width // sz.blocks
    lane = lax.broadcasted_iota(jnp.int32, (8, LANES), 1)
    row = lax.broadcasted_iota(jnp.int32, (8, LANES), 0)
    pad = jnp.zeros((8, sz.width - LANES), F32)
    total = jnp.zeros((8, sz.width), F32)
    for block in range(sz.blocks):
        piece = smalls[0]
        for dist in range(1, sz.blocks):
            piece = jnp.where((meta[4] ^ turned(sz, dist)) == block, smalls[dist], piece)
        for first, count, size in ((0, 4, part), (4, 4, own)):
            mine = jnp.where((row >= first) & (row < first + count) & (lane < size), piece, 0.0)
            wide = jnp.concatenate([mine, pad], axis=1)
            total += pltpu.roll(wide, block * size, 1) if block else wide
    params[...] = total


def block_order(sz, core):
    held = [0]
    for step in range(bits_of(sz)):
        held += [dist ^ step_bit(sz, step, core) for dist in held]
    return held[1:]


def pile_kernel(sz, meta, *refs):
    at = 0
    for piece in refs[:-1]:
        refs[-1][at : at + piece.shape[0]] = piece[...]
        at += piece.shape[0]


def place_maps(sz, meta, own_maps, mine, other, skip, out):
    own = sz.states // sz.blocks
    count = own_maps.shape[0] // 2

    def put(index, owner, value):
        out[pl.ds(pl.multiple_of(index * sz.states + owner * own, own), own), :] = value

    for index in range(2 * count):
        put(index, meta[0], own_maps[index])
    for side, pieces in ((meta[2], mine), (1 - meta[2], other)):
        for place, (even, odd) in enumerate(zip(block_order(sz, 0), block_order(sz, 1)), 1):
            message = place.bit_length() - 1
            each = pieces[message].shape[0] >> message
            owner = meta[0] ^ jnp.where(side == 0, even, odd)
            for index in range(count):
                put(side * count + index, owner, pieces[message][(place - (1 << message)) * each + skip + index])


def open_kernel(sz, meta, perm, params, *refs):
    pieces, (hidden, normed, live, ahead, behind, stacked) = refs[: sz.blocks], refs[sz.blocks :]
    fill_masks(sz, meta, live, ahead, behind)
    place_pieces(sz, meta, pieces, stacked)
    gain = gain_of(params, 0)
    for rows in row_parts(sz):
        u = nt(perm[rows, :], stacked[...])
        hidden[rows, :] = u.astype(BF)
        normed[rows, :] = normed_rows(sz, u, gain, widen(live[rows, :], sz.width // LANES))


def enter_kernel(sz, meta, ahead, behind, params, normed, maps, other, w_in, driven, ends, send, enter):
    decay = decay_of(sz, params, 0)
    for side, half in ((meta[2], maps), (1 - meta[2], other)):
        w_in[pl.ds(pl.multiple_of(side * sz.states, sz.states), sz.states), :] = half[...]
    matmul_nt(normed, w_in, driven)
    chain_ends(sz, decay, ahead, behind, driven, 0, 0, ends)
    send_ends(sz, meta, decay, ends, enter, send)


def chain_kernel(sz, meta, ahead, behind, recv, params, ends, driven, states, enter):
    decay = decay_of(sz, params, 0)
    enter_chunk(sz, meta, recv, decay, ends, enter)
    chain_states(sz, decay, ahead, behind, driven, enter, states)


def middle_kernel(sz, meta, live, ahead, behind, states, params, normed, hidden, own_out, own_in, *refs):
    skip, gain_b, decay_b = skip_of(params, 0), gain_of(params, 1), decay_of(sz, params, 1)
    far = bits_of(sz)
    mine, other, refs = refs[:far], refs[far : 2 * far], refs[2 * far :]
    w_out, w_in_b, slope, hidden_b, normed_b, driven_b, ends_b, send_b, enter = refs
    place_maps(sz, meta, own_out, mine, other, 0, w_out)
    place_maps(sz, meta, own_in, mine, other, 2, w_in_b)
    for rows in row_parts(sz):
        on = widen(live[rows, :], sz.width // LANES)
        u = hidden[rows, :].astype(F32) + finish_rows(sz, rows, states, w_out, skip, normed, on, slope)
        hidden_b[rows, :] = u
        v = normed_rows(sz, u, gain_b, on)
        normed_b[rows, :] = v
        driven_b[rows, :] = nt(v, w_in_b[...])
    chain_ends(sz, decay_b, ahead, behind, driven_b, 0, 0, ends_b)
    send_ends(sz, meta, decay_b, ends_b, enter, send_b)


def leave_kernel(sz, meta, live, ahead, behind, recv, params, ends, driven, normed, hidden, own_out, *refs):
    decay, skip = decay_of(sz, params, 1), skip_of(params, 1)
    far = bits_of(sz)
    mine, other, refs = refs[:far], refs[far : 2 * far], refs[2 * far :]
    w_out, states, slope, last, enter = refs
    place_maps(sz, meta, own_out, mine, other, 3, w_out)
    enter_chunk(sz, meta, recv, decay, ends, enter)
    chain_states(sz, decay, ahead, behind, driven, enter, states)
    for rows in row_parts(sz):
        on = widen(live[rows, :], sz.width // LANES)
        last[rows, :] = (hidden[rows, :] + finish_rows(sz, rows, states, w_out, skip, normed, on, slope)).astype(BF)


def turn_kernel(sz, meta, ahead, behind, slope, normed, w_out, params, perm, *refs):
    decay = decay_of(sz, params, 1)
    pieces, refs = refs[: sz.blocks], refs[sz.blocks :]
    upstream, twice, grad_states, grad_skip, ends, send, stacked, enter = refs
    place_pieces(sz, meta, pieces, stacked)
    skips = []
    for rows in row_parts(sz):
        r = nt(perm[rows, :], stacked[...])
        upstream[rows, :] = r
        skips.append(open_rows(sz, rows, r, slope, normed, w_out, twice, grad_states))
    grad_skip[...] = jnp.sum(sum(skips), axis=0, keepdims=True)
    chain_ends(sz, decay, ahead, behind, grad_states, 2 * sz.states, 0, ends)
    send_ends(sz, meta, decay, ends, enter, send)


def back_middle_kernel(sz, meta, ahead, behind, recv, params, ends, grad_states, states, upstream, slope, hidden, w_in,
                       slope_b, normed_b, w_out_b,
                       grad_driven, grad_decay, grad_gain, upstream_b, twice_b, grad_states_b, grad_skip_b, ends_b, send_b,
                       enter, half):
    decay, skip, gain, decay_b = decay_of(sz, params, 1), skip_of(params, 1), gain_of(params, 1), decay_of(sz, params, 0)
    enter_chunk(sz, meta, recv, decay, ends, enter)
    adjoint_chains(sz, decay, ahead, behind, grad_states, enter, states, half, grad_driven, grad_decay)
    gains, skips = [], []
    for rows in row_parts(sz):
        r, terms = back_rows(sz, rows, grad_driven, w_in, upstream, slope, skip, hidden, gain)
        gains.append(terms)
        upstream_b[rows, :] = r
        skips.append(open_rows(sz, rows, r, slope_b, normed_b, w_out_b, twice_b, grad_states_b))
    grad_gain[...] = jnp.sum(sum(gains), axis=0, keepdims=True)
    grad_skip_b[...] = jnp.sum(sum(skips), axis=0, keepdims=True)
    chain_ends(sz, decay_b, ahead, behind, grad_states_b, 2 * sz.states, 0, ends_b)
    send_ends(sz, meta, decay_b, ends_b, enter, send_b)


def back_chain_kernel(sz, meta, ahead, behind, recv, params, ends, grad_states, states, grad_driven, grad_decay, enter, half):
    decay = decay_of(sz, params, 0)
    enter_chunk(sz, meta, recv, decay, ends, enter)
    adjoint_chains(sz, decay, ahead, behind, grad_states, enter, states, half, grad_driven, grad_decay)


def back_leave_kernel(sz, meta, params, grad_driven, upstream, slope, hidden, w_in, perm, done, *refs):
    skip, gain = skip_of(params, 0), gain_of(params, 0)
    pieces, (last, stacked) = refs[: sz.blocks], refs[sz.blocks :]
    for rows in row_parts(sz):
        r, _ = back_rows(sz, rows, grad_driven, w_in, upstream, slope, skip, hidden, gain)
        last[rows, :] = r.astype(BF)
    part = sz.width // sz.blocks
    cut_pieces(sz, meta, done, perm, stacked, [piece.at[0:part, :] for piece in pieces])
    cut_pieces(sz, meta, last, perm, stacked, [piece.at[part : 2 * part, :] for piece in pieces])


def weight_kernel(counts, other, sz, meta, *refs):
    half = 1 - meta[2] if other else meta[2]
    pairs = 2 * len(counts)
    out, at = refs[pairs], 0
    if len(refs) > pairs + 1:
        whole, out, terms = refs[pairs:]
        value = tn(refs[0][:, pl.ds(pl.multiple_of(half * sz.states, LANES), sz.states)], refs[1][...])
        out[...] = value.astype(out.dtype)
        rows = whole[pl.ds(pl.multiple_of(half * sz.states, sz.states), sz.states), :].astype(F32)
        terms[...] = jnp.sum(column_sum(rows * value), axis=0, keepdims=True)
        return
    for index, count in enumerate(counts):
        left, right = refs[2 * index], refs[2 * index + 1]
        for group in range(count):
            cols = pl.ds(pl.multiple_of((half * count + group) * sz.states, LANES), sz.states)
            out[at : at + sz.states, :] = tn(left[:, cols], right[...]).astype(out.dtype)
            at += sz.states


def split2(x):
    hi = x.astype(BF).astype(F32)
    return hi, x - hi


class Group(NamedTuple):
    first: int
    counts: tuple

    def rows(self, sz):
        return sum(self.counts) * (sz.states // sz.blocks)


def bits_of(sz):
    return sz.blocks.bit_length() - 1


def step_bit(sz, step, core):
    return 1 << ((step + core) % bits_of(sz))


def far_block(sz, group, slot, core):
    return sum(step_bit(sz, group.first + j, core) for j in range(bits_of(sz)) if (slot >> j) & 1)


def own_tiny(sz, params, terms, more, gain_b, skip_a, skip_b, decay_a, decay_b, tiny):
    gain_a = (terms[...] + more[...] + skip_of(params, 0) * skip_a[...]) / gain_of(params, 0)
    tiny[...] = jnp.zeros_like(tiny)
    for index, line in enumerate((gain_a, gain_b[...], skip_a[...], skip_b[...])):
        tiny[index : index + 1, :] = line
    tiny[4:6, 0 : sz.states] = decay_a[...]
    tiny[6:8, 0 : sz.states] = decay_b[...]
    return tiny[...]


def tiny_of(sz, tiny, owner):
    own, part = sz.states // sz.blocks, sz.width // sz.blocks
    row = lax.broadcasted_iota(jnp.int32, (8, LANES), 0)
    lane = lax.broadcasted_iota(jnp.int32, (8, LANES), 1)
    value = jnp.zeros((8, LANES), F32)
    for block in range(sz.blocks):
        wide = pltpu.roll(tiny, sz.width - block * part, 1) if block else tiny
        deep = pltpu.roll(tiny, sz.width - block * own, 1) if block else tiny
        mine = jnp.where(row < 4, jnp.where(lane < part, wide[:, :LANES], 0.0), jnp.where(lane < own, deep[:, :LANES], 0.0))
        value = jnp.where(owner == block, mine, value)
    return value


def put_sums(value, slot, kept, message, at):
    if slot % 2 == 0:
        kept[slot // 2] = value
        return at
    message[at : at + value.shape[0], :] = value.astype(BF)
    return at + value.shape[0]


def add_message(sz, group, kept, slot, message, at):
    return kept[slot] + message[at : at + group.rows(sz), :].astype(F32)


def step_kernel(old, new, sz, meta, *refs):
    came, refs = (refs[0], refs[1:]) if old else (None, refs)
    held, refs = refs[: len(old)], refs[len(old) :]
    if new:
        halves, refs = refs[: 2 * len(new.counts)], refs[2 * len(new.counts) :]
    keeps, message = refs[:-1], refs[-1]
    at = 0
    for (group, slots, row), kept, keep in zip(old, held, keeps):
        for slot in range(slots):
            value = add_message(sz, group, kept, slot, came, row + slot * group.rows(sz))
            at = put_sums(value, slot, keep, message, at)
    if new:
        own = sz.states // sz.blocks
        for slot in range(sz.blocks):
            owner = meta[0] ^ jnp.where(meta[2] == 0, far_block(sz, new, slot, 0), far_block(sz, new, slot, 1))
            parts = []
            for index, count in enumerate(new.counts):
                keep, got = halves[2 * index], halves[2 * index + 1]
                for one in range(count):
                    rows = pl.ds(pl.multiple_of(one * sz.states + owner * own, own), own)
                    parts.append(keep[rows, :].astype(F32) + got[rows, :].astype(F32))
            at = put_sums(jnp.concatenate(parts, axis=0), slot, keeps[-1], message, at)


def direct_kernel(group, sz, meta, keep, got, *refs):
    own = sz.states // sz.blocks
    lines, pieces, room = refs[:8], refs[8:-1], refs[-1]
    whole = own_tiny(sz, *lines, room)
    for index, piece in enumerate(pieces):
        owner = meta[0] ^ farthest(index, sz.blocks)
        rows = pl.ds(pl.multiple_of(owner * own, own), own)
        piece[0:own, :] = (keep[rows, :].astype(F32) + got[rows, :].astype(F32)).astype(BF)
        rest = jnp.zeros((8, sz.width - 2 * LANES), F32)
        wide = jnp.concatenate([*split2(tiny_of(sz, whole, owner)), rest], axis=1)
        piece[own : own + 16, :] = jnp.concatenate([wide, jnp.zeros_like(wide)], axis=0).astype(BF)


def fold_block_kernel(planes, groups, direct, sz, meta, *refs):
    lanes = sz.width // LANES
    held, refs = refs[: 2 * len(groups)], refs[2 * len(groups) :]
    pieces, refs = (refs[: sz.blocks], refs[sz.blocks :]) if direct else ((), refs)
    outs, talls = refs[:planes], refs[planes:]
    totals = [add_message(sz, group, held[2 * index], 0, held[2 * index + 1], row) for index, (group, row) in enumerate(groups)]
    if direct:
        total = pieces[0][...].astype(F32)
        for piece in pieces[1:]:
            total += piece[...].astype(F32)
        rows = total.shape[0] - 16
        totals.append(total[0:rows])
        tiny = total[rows : rows + 8, 0:LANES] + total[rows : rows + 8, LANES : 2 * LANES]
    at = 0
    for total, tall in zip(totals, talls):
        rows = total.shape[0]
        padded = tall.shape[0] // lanes
        for block in range(lanes):
            tall[block * padded : block * padded + rows, :] = total[:, block * LANES : (block + 1) * LANES].astype(BF)
            if padded > rows:
                tall[block * padded + rows : (block + 1) * padded, :] = jnp.zeros((padded - rows, LANES), BF)
        part = tall.shape[0] // planes
        for dist, out in enumerate(outs):
            out[at : at + part, :] = tall[pl.ds(pl.multiple_of((meta[3] ^ farthest(dist, planes)) * part, part), part), :]
        at += part
    if direct:
        rows = jnp.concatenate(split2(tiny), axis=0).astype(BF)
        for out in outs:
            out[at : at + 16, :] = rows


def fold_plane_kernel(early, sz, meta, *refs):
    parts, out, tiny = refs[early:-2], refs[-2], refs[-1]
    top = 0
    if early:
        total = refs[0][...].astype(F32)
        for piece in refs[1:early]:
            total += piece[...].astype(F32)
        top = total.shape[0]
        out[0:top, :] = total.astype(BF)
    total = parts[0][...].astype(F32)
    for piece in parts[1:]:
        total += piece[...].astype(F32)
    rows = total.shape[0] - 16
    out[top:, :] = total[0:rows].astype(BF)
    tiny[...] = total[rows : rows + 8] + total[rows + 8 :]


def finish_kernel(planes, groups, sz, meta, *refs):
    count = 2 * planes
    pieces, refs = refs[:count], refs[count:]
    tiny, lambda_log, lambda_imag, log_step, input_map = refs[0][...] + refs[1][...], *refs[2:6]
    grad_gain, grad_skip, grad_log, grad_imag, grad_step, grad_maps, grad_out = refs[6:13]
    talls, grad_in, lines = refs[13:-2], refs[-2], refs[-1]
    own = sz.states // sz.blocks
    lanes = sz.width // LANES
    start = 0
    for tall, group in zip(talls, groups):
        padded = tall.shape[0] // lanes
        part = tall.shape[0] // planes
        for side in range(2):
            half = meta[2] ^ side
            for dist in range(planes):
                rows = pl.ds(pl.multiple_of((meta[3] ^ farthest(dist, planes)) * part, part), part)
                tall[rows, :] = pieces[side * planes + dist][start : start + part, :]
            at = 0
            for which, layer, maps in group:
                out = grad_in if which == 0 else grad_out
                for one in range(maps):
                    for block in range(lanes):
                        rows = slice(block * padded + at, block * padded + at + own)
                        out[layer, half * maps + one, :, block * LANES : (block + 1) * LANES] = tall[rows, :].astype(F32)
                    at += own
        start += part
    width = sz.width // sz.blocks
    grad_gain[...] = tiny[0:2, 0:width]
    grad_skip[...] = tiny[2:4, 0:width]
    dr, di, sr, si = discretize(lambda_log[...], lambda_imag[...], log_step[...])
    lines[...] = jnp.zeros_like(lines)
    lines[0:2, 0:own] = sr
    lines[2:4, 0:own] = si
    cols = lines[...].T
    back = []
    for layer in range(2):
        qr, qi = cols[0:own, layer : layer + 1], cols[0:own, 2 + layer : 3 + layer]
        wr, wi = grad_in[layer, 0], grad_in[layer, 1]
        br, bi = input_map[layer, 0].astype(F32), input_map[layer, 1].astype(F32)
        grad_maps[layer, 0] = qr * wr + qi * wi
        grad_maps[layer, 1] = qr * wi - qi * wr
        back.append(jnp.sum(wr * br + wi * bi, axis=1, keepdims=True))
        back.append(jnp.sum(wi * br - wr * bi, axis=1, keepdims=True))
    lines[...] = jnp.zeros_like(lines)
    for index, col in enumerate(back):
        lines[0:own, index : index + 1] = col
    rows = lines[...].T
    step = jnp.exp(log_step[...])
    lr, li = -jnp.exp(lambda_log[...]), lambda_imag[...]
    norm = 1.0 / (lr * lr + li * li)
    for layer in range(2):
        at = slice(layer, layer + 1)
        a, b, h = (lr[at], li[at]), (dr[at], di[at]), step[at]
        gq = rows[2 * layer : 2 * layer + 1, 0:own], rows[2 * layer + 1 : 2 * layer + 2, 0:own]
        gd = tiny[4 + 2 * layer : 5 + 2 * layer, 0:own], tiny[5 + 2 * layer : 6 + 2 * layer, 0:own]
        inverse = a[0] * norm[at], -a[1] * norm[at]
        through = cmul(inverse[0], -inverse[1], *gq)
        gd = gd[0] + through[0], gd[1] + through[1]
        ratio = cmul(*inverse, sr[at], si[at])
        direct = cmul(ratio[0], -ratio[1], *gq)
        moved = cmul(b[0] * h, -b[1] * h, *gd)
        turn = cmul(*a, *b)
        grad_log[at, :] = (moved[0] - direct[0]) * a[0]
        grad_imag[at, :] = moved[1] - direct[1]
        grad_step[at, :] = (turn[0] * gd[0] + turn[1] * gd[1]) * h


def spread_kernel(indices, count, sz, meta, *refs):
    pieces, outs, wide, sems = refs[: len(indices)], refs[-2 - count : -2], refs[-2], refs[-1]
    part = sz.width // sz.blocks
    copies = []
    for piece, dist in zip(pieces, indices):
        owner = meta[0] ^ turned(sz, dist)
        for index, out in enumerate(outs):
            slot = len(copies)
            wide[slot] = piece[index * part : (index + 1) * part, :].astype(F32)
            cols = pl.ds(pl.multiple_of(lax.rem(owner, sz.chunks) * sz.toks, LANES), sz.toks)
            copy = pltpu.make_async_copy(wide.at[slot], out.at[lax.div(owner, sz.chunks), :, cols], sems.at[slot])
            copy.start()
            copies.append(copy)
    for copy in copies:
        copy.wait()


VMEM = pl.BlockSpec(memory_space=pltpu.VMEM)
SMEM = pl.BlockSpec(memory_space=pltpu.SMEM)
HBM = pl.BlockSpec(memory_space=pltpu.HBM)


def call(name, sz, body, items, args, outs, scratch, limit=10, in_spec=VMEM, out_spec=VMEM, time=0.0, onto=()):
    out_shape = [jax.ShapeDtypeStruct(shape, dtype) for shape, dtype in outs]

    def kernel(*refs):
        body(sz, place_of(sz, refs[0] if items else None), *refs[len(items) :])

    return pl.pallas_call(
        kernel,
        out_shape=out_shape,
        in_specs=[SMEM] * len(items) + [in_spec] * len(args) + [HBM] * len(onto),
        out_specs=[out_spec] * len(outs),
        scratch_shapes=[pltpu.VMEM(*item) if isinstance(item, tuple) else item for item in scratch],
        compiler_params=pltpu.CompilerParams(vmem_limit_bytes=limit << 20),
        input_output_aliases={len(items) + len(args) + index: index for index in range(len(onto))},
        cost_estimate=pl.CostEstimate(flops=int(COST * time), bytes_accessed=1000, transcendentals=0),
        name=name,
    )(*items, *args, *onto)


def on_device(tokens, cotangent, item_lengths, item_offsets, norm_gain, lambda_log, lambda_imag, log_step, input_map, output_map, skip_weight):
    micro, part, run = tokens.shape
    layers = norm_gain.shape[0]
    blocks = lax.axis_size("block")
    planes = lax.axis_size("plane")
    chunks = blocks // micro
    toks = run // chunks
    own = lambda_log.shape[1]
    width, states = part * blocks, own * blocks
    sz = Sizes(blocks, chunks, toks, run, toks // SEGS, width, states, item_lengths.shape[1])

    def swap(x, dist, axis="block"):
        return lax.ppermute(x, axis, [(i, i ^ dist) for i in range(lax.axis_size(axis))])

    def across(x, dist, back):
        pairs = []
        for c in range(2):
            for b in range(blocks):
                q = b ^ turned(sz, dist)
                pairs.append((c * blocks + b, (q % 2) * blocks + (q // 2) * 2 + c))
        return lax.ppermute(x, ("core", "block"), [pair[::-1] for pair in pairs] if back else pairs)

    def across_all(pieces, back=False):
        return [across(piece, dist, back) for dist, piece in enumerate(pieces)]

    table = jnp.stack([item_lengths, item_offsets])
    other_table = swap(table, 1, "core")

    def neighbour(x, dist):
        pairs = []
        for c in range(2):
            for b in range(blocks):
                q = ((b // 2) * 2 + c) ^ dist
                pairs.append((c * blocks + b, (q % 2) * blocks + (q // 2) * 2 + b % 2))
        return lax.ppermute(x, ("core", "block"), pairs)

    def swap_all(pieces, axis="block"):
        count = len(pieces)
        return [swap(piece, farthest(index, count), axis) if index else piece for index, piece in enumerate(pieces)]

    def exchange(send):
        return jnp.stack([neighbour(send[dist - 1], dist) for dist in range(1, chunks)])

    row = jnp.arange(toks, dtype=jnp.int32)[:, None]
    col = jnp.arange(toks, dtype=jnp.int32)[None, :]
    perm = ((row % SEGS) * sz.steps + row // SEGS == col).astype(BF)

    maps_own = ((2, own, width), BF)
    half_own = ((5, own, width), BF)
    given = [norm_gain, skip_weight, lambda_log, lambda_imag, log_step, input_map, output_map]
    *first_pieces, drive_b, half_b = call(
        "prepare", sz, prepare_kernel, [], [pltpu.with_memory_space_constraint(x, pltpu.HBM) for x in [tokens, *given]],
        [((first_rows(sz)[1] + 16, toks), BF)] * blocks + [maps_own, half_own],
        [(x.shape, x.dtype) for x in given] + [((8, LANES), F32), ((8, LANES), F32), maps_own, pltpu.SemaphoreType.DMA((len(given) + blocks,))],
        limit=6, in_spec=HBM)
    first_pieces = across_all(first_pieces)
    cot_cut = call("cut_cotangent", sz, cut_kernel, [], [pltpu.with_memory_space_constraint(cotangent, pltpu.HBM)],
                   [((part, toks), BF)] * blocks, [((blocks, part, toks), F32), pltpu.SemaphoreType.DMA((blocks,))], limit=4, in_spec=HBM)
    first_pieces[1], perm, cot_cut = after(first_pieces[1], perm, cot_cut)
    second_mine, held = [], half_b
    for step in range(bits_of(sz)):
        pairs = [(c * blocks + b, c * blocks + (b ^ step_bit(sz, step, c))) for c in range(2) for b in range(blocks)]
        second_mine.append(lax.ppermute(held, ("core", "block"), pairs))
        if step == 0:
            second_mine[0], first_pieces = after(second_mine[0], first_pieces)
        if step + 1 < bits_of(sz):
            (held,) = call("pile_%d" % step, sz, pile_kernel, [], [held, second_mine[-1]], [((2 * held.shape[0], own, width), BF)], [])
    maps_a, params = call("join", sz, join_kernel, [], first_pieces, [((states, width), BF), ((8, width), F32)], [])
    maps_a, other_table = after(maps_a, other_table)
    items = [jnp.stack([table, other_table])]


    mask = ((toks, LANES), F32)
    enter = ((4, SEGS, states), F32)
    stacked = ((width, toks), BF)
    rows_f, rows_b = ((toks, width), F32), ((toks, width), BF)
    drv = ((toks, 2 * states), F32)
    sts = ((toks, 4 * states), BF)
    gst = ((toks, 4 * states), F32)
    snd = ((chunks - 1, 2, states), F32)
    w_in, w_out = ((2 * states, width), BF), ((4 * states, width), BF)
    line, gdec = ((1, width), F32), ((2, states), F32)
    piece_out = [((part, toks), BF)] * blocks

    other_a = swap(maps_a, 1, "core")
    hidden_a, normed_a, live, ahead, behind = call(
        "open", sz, open_kernel, items, [perm, params, *first_pieces], [rows_b, rows_b, mask, mask, mask], [stacked], time=3)
    w_in_a, driven_a, ends_a, send_a = call(
        "enter", sz, enter_kernel, items, [ahead, behind, params, normed_a, maps_a, other_a], [w_in, drv, enter, snd], [enter])
    recv = exchange(send_a)
    early_maps = [swap(piece, 1, "core") for piece in second_mine[:-1]]
    recv, early_maps = after(recv, early_maps)
    (states_a,) = call("chain", sz, chain_kernel, items, [ahead, behind, recv, params, ends_a, driven_a], [sts], [enter])
    last_mine, states_a = after(second_mine[-1], states_a)
    second_maps = [*second_mine[:-1], last_mine], [*early_maps, swap(last_mine, 1, "core")]
    cot_cut, _ = after(cot_cut, recv)
    cot_pieces = across_all(cot_cut)
    w_out_a, w_in_b, slope_a, hidden_b, normed_b, driven_b, ends_b, send_b = call(
        "middle", sz, middle_kernel, items,
        [live, ahead, behind, states_a, params, normed_a, hidden_a, output_map[0], drive_b, *second_maps[0], *second_maps[1]],
        [w_out, w_in, rows_b, rows_f, rows_b, drv, enter, snd], [enter], time=11)
    recv = exchange(send_b)
    w_out_b, states_b, slope_b, last_b = call(
        "leave", sz, leave_kernel, items,
        [live, ahead, behind, recv, params, ends_b, driven_b, normed_b, hidden_b, output_map[1], *second_maps[0], *second_maps[1]],
        [w_out, sts, rows_b, rows_b], [enter])

    def half_grads(name, other, pairs, counts, more=(), time=0.0):
        args = [x for pair in pairs for x in pair]
        outs = [((sum(counts) * states, width), BF)] + [line] * len(more)
        return call(name, sz, partial(weight_kernel, counts, other), [], [*args, *more], outs, [], time=time)

    groups = [Group(0, (2,)), Group(1, (3,))]
    steps = bits_of(sz)
    kept, came, place = {}, {}, {}

    def halve(step, halves=()):
        old, args = [], []
        for index, group in enumerate(groups):
            if 0 < step - group.first < steps:
                slots = 1 << (steps - (step - group.first))
                old.append((group, slots, place[step - 1, index]))
                args.append(kept[index])
        if old:
            args.insert(0, came[step - 1])
        new = groups[step] if step < len(groups) else None
        outs, at = [], 0
        for index, group in enumerate(groups):
            if 0 <= step - group.first < steps:
                slots = 1 << (steps - 1 - (step - group.first))
                outs.append((index, ((slots, group.rows(sz), width), F32)))
                place[step, index] = at
                at += slots * group.rows(sz)
        results = call("halve_%d" % step, sz, partial(step_kernel, old, new), [], [*args, *halves],
                       [shape for _, shape in outs] + [((at, width), BF)], [])
        for (index, _), value in zip(outs, results):
            kept[index] = value
        return results[-1]

    def send_step(step, message):
        pairs = [(c * blocks + b, c * blocks + (b ^ step_bit(sz, step, c))) for c in range(2) for b in range(blocks)]
        came[step] = lax.ppermute(message, ("core", "block"), pairs)

    def spread(name, pieces, first, onto=(), time=0.0):
        indices = tuple(range(first, blocks, 2))
        return call(name, sz, partial(spread_kernel, indices, 2), [], pieces, [((micro, part, run), F32)] * 2,
                    [((blocks, part, toks), F32), pltpu.SemaphoreType.DMA((blocks,))], limit=6, out_spec=HBM, time=time, onto=onto)

    lanes = width // LANES

    def tall_of(rows):
        step = max(SEGS * planes // lanes, SEGS)
        return ((lanes * (-(-rows // step) * step), LANES), BF)

    def over_planes(name, which, direct=(), send=True):
        ends = [(groups[index], place[groups[index].first + steps - 1, index]) for index in which]
        talls = [tall_of(group.rows(sz)) for group, _ in ends] + [tall_of(own)] * bool(direct)
        cut = sum(t[0][0] for t in talls) // planes + (16 if direct else 0)
        args = [x for index in which for x in (kept[index], came[groups[index].first + steps - 1])]
        parts = call(name, sz, partial(fold_block_kernel, planes, ends, bool(direct)), [], [*args, *direct],
                     [((cut, LANES), BF)] * planes, talls)
        return swap_all(parts, "plane") if send else parts

    up_b, twice_b, gstates_b, gskip_b, ends, send = call(
        "turn", sz, turn_kernel, items, [ahead, behind, slope_b, normed_b, w_out_b, params, perm, *cot_pieces],
        [rows_f, rows_b, gst, line, enter, snd], [stacked, enter], time=6)
    recv = exchange(send)
    pairs = [(states_b, twice_b)]
    (send_maps,) = half_grads("grads_a_send", True, pairs, (2,))
    got = swap(send_maps, 1, "core")
    (keep,) = half_grads("grads_a_keep", False, pairs, (2,), time=2)
    message = halve(0, (keep, got))
    recv, message = after(recv, message)
    send_step(0, message)
    gdriven_b, gdecay_b, ggain_b, up_a, twice_a, gstates_a, gskip_a, ends, send = call(
        "back_middle", sz, back_middle_kernel, items,
        [ahead, behind, recv, params, ends, gstates_b, states_b, up_b, slope_b, hidden_b, w_in_b, slope_a, normed_a, w_out_a],
        [((toks, 2 * states), BF), gdec, line, rows_f, rows_b, gst, line, enter, snd], [enter, drv], limit=12, time=11)
    recv = exchange(send)
    gdriven_b, came[0] = after(gdriven_b, came[0])
    pairs = [(gdriven_b, normed_b), (states_a, twice_a)]
    (send_maps,) = half_grads("grads_b_send", True, pairs, (1, 2))
    got = swap(send_maps, 1, "core")
    (keep,) = half_grads("grads_b_keep", False, pairs, (1, 2), time=9)
    message = halve(1, (keep, got))
    recv, message = after(recv, message)
    send_step(1, message)
    gdriven_a, gdecay_a = call(
        "back_chain", sz, back_chain_kernel, items, [ahead, behind, recv, params, ends, gstates_a, states_a],
        [((toks, 2 * states), BF), gdec], [enter, drv], limit=12, time=9)
    send_maps, terms = half_grads("grads_c_send", True, [(gdriven_a, normed_a)], (1,), [w_in_a])
    gdriven_a, send_maps = after(gdriven_a, send_maps)
    got = swap(send_maps, 1, "core")
    keep, more = half_grads("grads_c_keep", False, [(gdriven_a, normed_a)], (1,), [w_in_a], time=0)
    sums_c = list(call(
        "direct", sz, partial(direct_kernel, None), [],
        [keep, got, params, terms, more, ggain_b, gskip_a, gskip_b, gdecay_a, gdecay_b], [((own + 16, width), BF)] * blocks, [((8, width), F32)]))
    gdriven_a, sums_c[0] = after(gdriven_a, sums_c[0])
    sums_c = swap_all(sums_c)
    message = halve(2)
    kept[0], message = after(kept[0], message)
    first_parts = over_planes("planes_a", [0], send=False) if steps <= 2 else []
    first_parts, sums_c = after(first_parts, sums_c)
    first_parts = swap_all(first_parts, "plane")
    send_step(2, message)
    gdriven_a, message = after(gdriven_a, message)
    last_pieces = call(
        "back_leave", sz, back_leave_kernel, [], [params, gdriven_a, up_a, slope_a, hidden_a, w_in_a, perm, last_b],
        [((2 * part, toks), BF)] * blocks, [rows_b, stacked], limit=12, time=6)
    last_pieces, came[2], first_parts = after(last_pieces, came[2], first_parts)
    for step in range(3, steps + 1):
        send_step(step, halve(step))
    parts = over_planes("planes", [1] if first_parts else [0, 1], sums_c)
    last_pieces, parts[0] = after(last_pieces, parts[0])
    early = [across(piece, 2 * dist, True) for dist, piece in enumerate(last_pieces[0::2])]
    parts[0], early = after(parts[0], early)
    sum_all, tiny = call(
        "sum", sz, partial(fold_plane_kernel, len(first_parts)), [], [*first_parts, *parts],
        [((sum(x[0].shape[0] for x in (first_parts, parts) if x) - 16, LANES), BF), ((8, LANES), F32)], [])
    whole = swap_all([sum_all] * planes, "plane")
    late, _ = after(last_pieces[1::2], sum_all)
    late = [across(piece, 2 * dist + 1, True) for dist, piece in enumerate(late)]
    whole = swap_all([sum_all] * planes, "plane")
    late, others = after(late, [sum_all, tiny, *whole[planes - 0 :]])
    others = [swap(x, 1, "core") for x in others]
    halves = spread("spread_early", early, 0)
    late, halves = after(late, halves)
    output, input_grad = spread("spread_late", late, 1, halves, time=9)
    far = whole[1 : planes - 0]
    far, others, output = after(far, others, output)
    far = [swap(x, 1, "core") for x in far]
    whole += [others[0], *far, *others[2:]]
    tiny_other = others[1]
    small_out = ((layers, own), F32)
    grad_gain, grad_skip, grad_log, grad_imag, grad_step, grad_in, grad_out = call(
        "finish", sz, partial(finish_kernel, planes, ([(1, 1, 2)], [(0, 1, 1), (1, 0, 2)], [(0, 0, 1)])), [],
        [*whole, tiny, tiny_other, lambda_log, lambda_imag, log_step, input_map],
        [((layers, part), F32)] * 2 + [small_out] * 3 + [((layers, 2, own, width), F32), ((layers, 4, own, width), F32)],
        [tall_of(n * own) for n in (2, 3, 1)] + [((layers, 2, own, width), F32), ((LANES, LANES), F32)])
    return output, input_grad, grad_gain, grad_log, grad_imag, grad_step, grad_in, grad_out, grad_skip


def solution(mesh):
    rows, blocks = mesh.devices.shape
    inner = Mesh(mesh.devices.reshape(rows // 2, 2, blocks), ("plane", "core", "block"))
    dp = ("plane", "core")
    half = P(None, "block")
    maps = P(None, None, "block", None)
    acts = P(None, "block", dp)
    items = P(None, dp)
    return jax.shard_map(
        on_device,
        mesh=inner,
        in_specs=(acts, acts, items, items, half, half, half, half, maps, maps, half),
        out_specs=(acts, acts, half, half, half, half, maps, maps, half),
        check_vma=False,
    )
```

```python
from functools import partial
from typing import NamedTuple

import jax
import jax.numpy as jnp
from jax import lax
from jax.experimental import pallas as pl
from jax.experimental.pallas import tpu as pltpu
from jax.sharding import Mesh, PartitionSpec as P

EPSILON = 1e-05
SEGS = 16
LANES = 128
BF = jnp.bfloat16
F32 = jnp.float32
GELU_C = 0.7978845608028654
GELU_A = 0.044715
COST = 400_000_000


class Sizes(NamedTuple):
    blocks: int
    chunks: int
    toks: int
    run: int
    steps: int
    width: int
    states: int
    items: int


def turned(sz, index):
    return sz.blocks - 1 - index


def farthest(index, count):
    return count - index if index else 0


def place_of(sz, table):
    me, core = lax.axis_index("block"), lax.axis_index("core")
    q = lax.div(me, 2) * 2 + core
    mine, chunk = lax.div(q, sz.chunks), lax.rem(q, sz.chunks)
    out = [me, chunk, core, lax.axis_index("plane"), q]
    if table is not None:
        side = lax.rem(me, 2) ^ core
        for which in range(2):
            out += [table[side, which, mine, index] for index in range(sz.items)]
    return out


def nt(a, b):
    return lax.dot_general(a, b, (((1,), (1,)), ((), ())), preferred_element_type=F32)


def nn(a, b):
    return lax.dot_general(a, b, (((1,), (0,)), ((), ())), preferred_element_type=F32)


def tn(a, b):
    return lax.dot_general(a, b, (((0,), (0,)), ((), ())), preferred_element_type=F32)


def after(*values):
    return lax.optimization_barrier(values)


def cmul(ar, ai, br, bi):
    return ar * br - ai * bi, ar * bi + ai * br


def rows_of(step):
    return pl.ds(pl.multiple_of(step * SEGS, SEGS), SEGS)


def widen(mask, count):
    return jnp.concatenate([mask] * count, axis=1)


def item_of(sz, meta, index):
    begin = meta[5 + sz.items + index]
    return begin, begin + meta[5 + index]


def fill_masks(sz, meta, live, ahead, behind):
    base = meta[1] * sz.toks
    seg = lax.broadcasted_iota(jnp.int32, (SEGS, LANES), 0)

    def body(step, carry):
        pos = base + seg * sz.steps + step
        inside = jnp.zeros((SEGS, LANES), F32)
        onward = jnp.zeros((SEGS, LANES), F32)
        onward_next = jnp.zeros((SEGS, LANES), F32)
        for index in range(sz.items):
            begin, end = item_of(sz, meta, index)
            inside = jnp.where((pos >= begin) & (pos < end), 1.0, inside)
            onward = jnp.where((pos > begin) & (pos < end), 1.0, onward)
            onward_next = jnp.where((pos >= begin) & (pos + 1 < end), 1.0, onward_next)
        onward_next = jnp.where(pos + 1 < sz.run, onward_next, 0.0)
        live[rows_of(step), :] = inside
        ahead[rows_of(step), :] = onward
        behind[rows_of(step), :] = onward_next
        return carry

    lax.fori_loop(0, sz.steps, body, 0, unroll=8)


def through(sz, meta, first, length):
    ahead = behind = False
    for index in range(sz.items):
        begin, end = item_of(sz, meta, index)
        ahead = ahead | ((begin < first) & (end >= first + length))
        behind = behind | ((begin <= first) & (end > first + length))
    behind = behind & (first + length < sz.run)
    return ahead, behind


def power(pair, count):
    while count > 1:
        pair = cmul(*pair, *pair)
        count //= 2
    return pair


def column_blocks(sz, decay):
    out = []
    for q in range(sz.states // LANES):
        cols = slice(q * LANES, (q + 1) * LANES)
        out.append((decay[0:1, cols], decay[1:2, cols]))
    return out


def spread(pairs):
    return [tuple(jnp.broadcast_to(v, (SEGS, LANES)) for v in pair) for pair in pairs]


def chain_ends(sz, decay, ahead, behind, source, ahead_col, behind_col, ends):
    nq = sz.states // LANES
    d = spread(column_blocks(sz, decay))
    zero = jnp.zeros((SEGS, LANES), F32)

    def body(step, held):
        up, down = rows_of(step), rows_of(sz.steps - 1 - step)
        on_up, on_down = ahead[up, :], behind[down, :]
        new = []
        for q in range(nq):
            for side, (rows, on, col) in enumerate(((up, on_up, ahead_col), (down, on_down, behind_col))):
                re, im = held[2 * q + side]
                re, im = cmul(*d[q], re * on, im * on)
                re += source[rows, col + q * LANES : col + (q + 1) * LANES]
                im += source[rows, col + sz.states + q * LANES : col + sz.states + (q + 1) * LANES]
                new.append((re, im))
        return tuple(new)

    held = lax.fori_loop(0, sz.steps, body, tuple((zero, zero) for _ in range(2 * nq)), unroll=8)
    for q in range(nq):
        cols = slice(q * LANES, (q + 1) * LANES)
        for side in range(2):
            ends[2 * side, :, cols] = held[2 * q + side][0]
            ends[2 * side + 1, :, cols] = held[2 * q + side][1]


def enter_states(sz, meta, decay, ends, start, enter):
    pair = (decay[0:1, :], decay[1:2, :])
    jump = power(pair, sz.steps)
    base = meta[1] * sz.toks
    state = list(start)
    for count in range(SEGS):
        for side, seg in ((0, count), (1, SEGS - 1 - count)):
            re, im = state[side]
            enter[2 * side, seg : seg + 1, :] = re
            enter[2 * side + 1, seg : seg + 1, :] = im
            passes = through(sz, meta, base + seg * sz.steps, sz.steps)[side]
            gain = jnp.where(passes, 1.0, 0.0).astype(F32)
            re, im = cmul(jump[0] * gain, jump[1] * gain, re, im)
            state[side] = (
                re + ends[2 * side, seg : seg + 1, :],
                im + ends[2 * side + 1, seg : seg + 1, :],
            )
    return state


def send_ends(sz, meta, decay, ends, enter, send):
    zero = jnp.zeros((1, sz.states), F32)
    ahead, behind = enter_states(sz, meta, decay, ends, ((zero, zero), (zero, zero)), enter)
    me = meta[1]
    for dist in range(1, sz.chunks):
        up = (me ^ dist) > me
        for part in range(2):
            send[dist - 1, part : part + 1, :] = jnp.where(up, ahead[part], behind[part])


def received(sz, meta, decay, recv):
    me = meta[1]
    zero = jnp.zeros((1, sz.states), F32)
    pair = (decay[0:1, :], decay[1:2, :])
    jump = power(pair, sz.toks) if sz.chunks > 2 else None
    sides = []
    for side in range(2):
        re, im = zero, zero
        order = range(sz.chunks) if side == 0 else range(sz.chunks - 1, -1, -1)
        for other in order:
            use = (other < me) if side == 0 else (other > me)
            slot = jnp.maximum((me ^ other) - 1, 0)
            got = recv[slot]
            new_re, new_im = got[0:1, :], got[1:2, :]
            if sz.chunks > 2:
                passes = through(sz, meta, other * sz.toks, sz.toks)[side]
                gain = jnp.where(passes, 1.0, 0.0).astype(F32)
                moved = cmul(jump[0] * gain, jump[1] * gain, re, im)
                new_re, new_im = new_re + moved[0], new_im + moved[1]
            re, im = jnp.where(use, new_re, re), jnp.where(use, new_im, im)
        sides.append((re, im))
    return sides


def load_enter(sz, enter):
    held = []
    for q in range(sz.states // LANES):
        cols = slice(q * LANES, (q + 1) * LANES)
        for side in range(2):
            held.append((enter[2 * side, :, cols], enter[2 * side + 1, :, cols]))
    return tuple(held)


def chain_states(sz, decay, ahead, behind, source, enter, states):
    nq = sz.states // LANES
    n = sz.states
    d = spread(column_blocks(sz, decay))

    def body(step, held):
        up, down = rows_of(step), rows_of(sz.steps - 1 - step)
        on_up, on_down = ahead[up, :], behind[down, :]
        new = []
        for q in range(nq):
            for side, (rows, on) in enumerate(((up, on_up), (down, on_down))):
                re, im = held[2 * q + side]
                re, im = cmul(*d[q], re * on, im * on)
                lo = q * LANES
                re += source[rows, lo : lo + LANES]
                im += source[rows, n + lo : n + lo + LANES]
                at = 2 * side * n + lo
                states[rows, at : at + LANES] = re.astype(BF)
                states[rows, at + n : at + n + LANES] = (-im).astype(BF)
                new.append((re, im))
        return tuple(new)

    lax.fori_loop(0, sz.steps, body, load_enter(sz, enter), unroll=8)


def adjoint_chains(sz, decay, ahead, behind, source, enter, states, half, grad_driven, grad_decay):
    nq = sz.states // LANES
    n = sz.states
    d = spread(column_blocks(sz, decay))
    zero = jnp.zeros((SEGS, LANES), F32)

    def make(second):
        def body(step, carry):
            held, sums = carry
            up, down = rows_of(step), rows_of(sz.steps - 1 - step)
            on_up, on_down = ahead[up, :], behind[down, :]
            new, total = [], []
            for q in range(nq):
                lo = q * LANES
                acc_re, acc_im = sums[q]
                for side, (rows, on, src, st) in enumerate(((up, on_up, 2 * n, 2 * n), (down, on_down, 0, 0))):
                    re, im = held[2 * q + side]
                    re, im = re * on, im * on
                    s_re = states[rows, st + lo : st + lo + LANES].astype(F32)
                    s_im = states[rows, st + n + lo : st + n + lo + LANES].astype(F32)
                    acc_re += re * s_re + im * s_im
                    acc_im += re * s_im - im * s_re
                    re, im = cmul(*d[q], re, im)
                    re += source[rows, src + lo : src + lo + LANES]
                    im += source[rows, src + n + lo : src + n + lo + LANES]
                    new.append((re, im))
                    if second:
                        out_re = re + half[rows, lo : lo + LANES]
                        out_im = im + half[rows, n + lo : n + lo + LANES]
                        grad_driven[rows, lo : lo + LANES] = out_re.astype(BF)
                        grad_driven[rows, n + lo : n + lo + LANES] = (-out_im).astype(BF)
                    else:
                        half[rows, lo : lo + LANES] = re
                        half[rows, n + lo : n + lo + LANES] = im
                total.append((acc_re, acc_im))
            return tuple(new), tuple(total)

        return body

    carry = (load_enter(sz, enter), tuple((zero, zero) for _ in range(nq)))
    carry = lax.fori_loop(0, sz.steps // 2, make(False), carry, unroll=4)
    carry = lax.fori_loop(sz.steps // 2, sz.steps, make(True), carry, unroll=4)
    for q in range(nq):
        cols = slice(q * LANES, (q + 1) * LANES)
        grad_decay[0:1, cols] = jnp.sum(carry[1][q][0], axis=0, keepdims=True)
        grad_decay[1:2, cols] = jnp.sum(carry[1][q][1], axis=0, keepdims=True)


ROWS = 512


def row_parts(sz):
    size = min(ROWS, sz.toks)
    return [slice(lo, lo + size) for lo in range(0, sz.toks, size)]


def matmul_nt(a, b, out, tile=256):
    for lo in range(0, b.shape[0], tile):
        out[:, lo : lo + tile] = nt(a[...], b[lo : lo + tile, :]).astype(out.dtype)


def matmul_tn(a, b, out, tile=256):
    for lo in range(0, a.shape[1], tile):
        out[lo : lo + tile, :] = tn(a[:, lo : lo + tile], b[...]).astype(out.dtype)


def column_sum(x):
    return jnp.sum(x.reshape(x.shape[0] // 8, 8, x.shape[1]), axis=0)


def scale_of(u):
    return lax.rsqrt(jnp.mean(u * u, axis=1, keepdims=True) + EPSILON)


def normed_rows(sz, u, gain, on):
    return (u * scale_of(u) * gain * on).astype(BF)


def finish_rows(sz, rows, states, w_out, skip, normed, on, slope):
    pre = 2.0 * nn(states[rows, :], w_out[...]) + skip * normed[rows, :].astype(F32)
    square = pre * pre
    th = jnp.tanh(pre * (GELU_C + (GELU_C * GELU_A) * square))
    part = 0.5 + 0.5 * th
    deriv = part + pre * (1.0 - th * th) * (0.5 * GELU_C + (1.5 * GELU_C * GELU_A) * square)
    slope[rows, :] = (on * deriv).astype(slope.dtype)
    return on * (pre * part)


def enter_chunk(sz, meta, recv, decay, ends, enter):
    enter_states(sz, meta, decay, ends, received(sz, meta, decay, recv), enter)


def back_rows(sz, rows, grad_driven, w_in, upstream, slope, skip, hidden, gain):
    u = hidden[rows, :].astype(F32)
    r = upstream[rows, :]
    gn = nn(grad_driven[rows, :], w_in[...]) + r * slope[rows, :].astype(F32) * skip
    scale = scale_of(u)
    moved = u * scale
    dn = gn * gain
    inner = jnp.sum(dn * moved, axis=1, keepdims=True) * (1.0 / sz.width)
    return r + scale * (dn - moved * inner), column_sum(gn * moved)


def open_rows(sz, rows, r, slope, normed, w_out, twice, grad_states):
    e = r * slope[rows, :].astype(F32)
    low = e.astype(BF)
    double = low + low
    twice[rows, :] = double
    grad_states[rows, :] = nt(double, w_out[...])
    return column_sum(e * normed[rows, :].astype(F32))


def gain_of(params, layer):
    return params[layer : layer + 1, :]


def skip_of(params, layer):
    return params[2 + layer : 3 + layer, :]


def decay_of(sz, params, layer):
    return params[4 + 2 * layer : 6 + 2 * layer, 0 : sz.states]


def place_pieces(sz, meta, pieces, stacked):
    part = sz.width // sz.blocks
    for dist, piece in enumerate(pieces):
        owner = meta[4] ^ turned(sz, dist)
        stacked[pl.ds(pl.multiple_of(owner * part, part), part), :] = piece[0:part, :]


def cut_pieces(sz, meta, rows, perm, stacked, pieces):
    part = sz.width // sz.blocks
    matmul_tn(rows, perm, stacked)
    for dist, piece in enumerate(pieces):
        owner = meta[4] ^ turned(sz, dist)
        piece[...] = stacked[pl.ds(pl.multiple_of(owner * part, part), part), :]


def cut_kernel(sz, meta, whole, *refs):
    outs, wide, sems = refs[: sz.blocks], refs[-2], refs[-1]
    straight = whole.dtype == BF
    copies = []
    for dist in range(sz.blocks):
        to = meta[0] ^ turned(sz, dist)
        cols = pl.ds(pl.multiple_of(lax.rem(to, sz.chunks) * sz.toks, LANES), sz.toks)
        source = whole.at[lax.div(to, sz.chunks), :, cols]
        copy = pltpu.make_async_copy(source, outs[dist] if straight else wide.at[dist], sems.at[dist])
        copy.start()
        copies.append(copy)
    for dist, copy in enumerate(copies):
        copy.wait()
        if not straight:
            outs[dist][...] = wide[dist].astype(BF)


def discretize(lambda_log, lambda_imag, log_step):
    step_size = jnp.exp(log_step)
    lambda_real = -jnp.exp(lambda_log)
    modulus = jnp.exp(lambda_real * step_size)
    decay_real = modulus * jnp.cos(lambda_imag * step_size)
    decay_imag = modulus * jnp.sin(lambda_imag * step_size)
    denominator = lambda_real * lambda_real + lambda_imag * lambda_imag
    scale_real = ((decay_real - 1.0) * lambda_real + decay_imag * lambda_imag) / denominator
    scale_imag = (decay_imag * lambda_real - (decay_real - 1.0) * lambda_imag) / denominator
    return decay_real, decay_imag, scale_real, scale_imag


def first_rows(sz):
    part, own = sz.width // sz.blocks, sz.states // sz.blocks
    return part, part + own * sz.width // sz.toks


def half_map_parts(sz):
    top, end = first_rows(sz)
    rows = end - top
    for index in range(sz.toks // sz.width):
        yield slice(index * rows, (index + 1) * rows), slice(top, end), slice(index * sz.width, (index + 1) * sz.width)


def split3(x):
    hi = x.astype(BF).astype(F32)
    mid = (x - hi).astype(BF).astype(F32)
    return hi, mid, x - hi - mid


def prepare_kernel(sz, meta, tokens, *refs):
    inputs, refs = refs[:7], refs[7:]
    outs, refs = refs[: sz.blocks], refs[sz.blocks :]
    drive_b, half_b = refs[:2]
    held, small, lines, drive_a, sems = refs[2:9], refs[9], refs[10], refs[11], refs[12]
    top, end = first_rows(sz)
    own, part = sz.states // sz.blocks, sz.width // sz.blocks
    loads, copies = [], []
    for index, (source, target) in enumerate(zip(inputs, held)):
        loads.append(pltpu.make_async_copy(source, target, sems.at[index]))
    for dist in range(sz.blocks):
        to = meta[0] ^ turned(sz, dist)
        cols = pl.ds(pl.multiple_of(lax.rem(to, sz.chunks) * sz.toks, LANES), sz.toks)
        source = tokens.at[lax.div(to, sz.chunks), :, cols]
        copies.append(pltpu.make_async_copy(source, outs[dist].at[0:top, :], sems.at[len(inputs) + dist]))
    for copy in copies + loads:
        copy.start()
    for copy in loads[:6]:
        copy.wait()
    gain, skip, lambda_log, lambda_imag, log_step, input_map, output_map = held
    dr, di, sr, si = discretize(lambda_log[...], lambda_imag[...], log_step[...])
    small[...] = jnp.zeros_like(small)
    lines[...] = jnp.zeros_like(lines)
    small[0:2, 0:part] = gain[...]
    small[2:4, 0:part] = skip[...]
    for layer in range(2):
        small[4 + 2 * layer : 5 + 2 * layer, 0:own] = dr[layer : layer + 1]
        small[5 + 2 * layer : 6 + 2 * layer, 0:own] = di[layer : layer + 1]
    lines[0:2, 0:own] = sr
    lines[2:4, 0:own] = si
    cols = lines[...].T
    for layer in range(2):
        qr, qi = cols[0:own, layer : layer + 1], cols[0:own, 2 + layer : 3 + layer]
        br, bi = input_map[layer, 0].astype(F32), input_map[layer, 1].astype(F32)
        for index, value in enumerate((qr * br - qi * bi, qr * bi + qi * br)):
            (drive_a, drive_b)[layer][index] = value.astype(BF)
    rows = jnp.concatenate([*split3(small[...]), jnp.zeros((8, sz.toks - 3 * LANES), F32)], axis=1)
    rows = jnp.concatenate([rows, jnp.zeros((8, sz.toks), F32)], axis=0).astype(BF)
    for dist, out in enumerate(outs):
        half = lax.rem(meta[0] ^ turned(sz, dist), 2)
        for from_rows, to_rows, lanes in half_map_parts(sz):
            out[to_rows, lanes] = drive_a[half, from_rows, :]
        out[end:, :] = rows
    loads[6].wait()
    core = meta[2]
    for index in range(2):
        half_b[index] = output_map[0, 2 * core + index]
        half_b[3 + index] = output_map[1, 2 * core + index]
    half_b[2] = drive_b[core]
    for copy in copies:
        copy.wait()


def params_of(sz, piece):
    rows = piece[piece.shape[0] - 16 :, 0 : 3 * LANES].astype(F32)[0:8]
    return rows[:, 0:LANES] + rows[:, LANES : 2 * LANES] + rows[:, 2 * LANES :]


def join_kernel(sz, meta, *refs):
    pieces, maps, params = refs[: sz.blocks], refs[-2], refs[-1]
    own = sz.states // sz.blocks
    collect_params(sz, meta, [params_of(sz, piece) for piece in pieces], params)
    for dist, piece in enumerate(pieces):
        base = (meta[4] ^ turned(sz, dist)) * own
        for to_rows, from_rows, lanes in half_map_parts(sz):
            rows = pl.ds(pl.multiple_of(base + to_rows.start, 16), to_rows.stop - to_rows.start)
            maps[rows, :] = piece[from_rows, lanes]


def collect_params(sz, meta, smalls, params):
    own = sz.states // sz.blocks
    part = sz.width // sz.blocks
    lane = lax.broadcasted_iota(jnp.int32, (8, LANES), 1)
    row = lax.broadcasted_iota(jnp.int32, (8, LANES), 0)
    pad = jnp.zeros((8, sz.width - LANES), F32)
    total = jnp.zeros((8, sz.width), F32)
    for block in range(sz.blocks):
        piece = smalls[0]
        for dist in range(1, sz.blocks):
            piece = jnp.where((meta[4] ^ turned(sz, dist)) == block, smalls[dist], piece)
        for first, count, size in ((0, 4, part), (4, 4, own)):
            mine = jnp.where((row >= first) & (row < first + count) & (lane < size), piece, 0.0)
            wide = jnp.concatenate([mine, pad], axis=1)
            total += pltpu.roll(wide, block * size, 1) if block else wide
    params[...] = total


def block_order(sz, core):
    held = [0]
    for step in range(bits_of(sz)):
        held += [dist ^ step_bit(sz, step, core) for dist in held]
    return held[1:]


def pile_kernel(sz, meta, *refs):
    at = 0
    for piece in refs[:-1]:
        refs[-1][at : at + piece.shape[0]] = piece[...]
        at += piece.shape[0]


def place_maps(sz, meta, own_maps, mine, other, skip, out):
    own = sz.states // sz.blocks
    count = own_maps.shape[0] // 2

    def put(index, owner, value):
        out[pl.ds(pl.multiple_of(index * sz.states + owner * own, own), own), :] = value

    for index in range(2 * count):
        put(index, meta[0], own_maps[index])
    for side, pieces in ((meta[2], mine), (1 - meta[2], other)):
        for place, (even, odd) in enumerate(zip(block_order(sz, 0), block_order(sz, 1)), 1):
            message = place.bit_length() - 1
            each = pieces[message].shape[0] >> message
            owner = meta[0] ^ jnp.where(side == 0, even, odd)
            for index in range(count):
                put(side * count + index, owner, pieces[message][(place - (1 << message)) * each + skip + index])


def open_kernel(sz, meta, perm, params, *refs):
    pieces, (hidden, normed, live, ahead, behind, stacked) = refs[: sz.blocks], refs[sz.blocks :]
    fill_masks(sz, meta, live, ahead, behind)
    place_pieces(sz, meta, pieces, stacked)
    gain = gain_of(params, 0)
    for rows in row_parts(sz):
        u = nt(perm[rows, :], stacked[...])
        hidden[rows, :] = u.astype(BF)
        normed[rows, :] = normed_rows(sz, u, gain, widen(live[rows, :], sz.width // LANES))


def enter_kernel(sz, meta, ahead, behind, params, normed, maps, other, w_in, driven, ends, send, enter):
    decay = decay_of(sz, params, 0)
    for side, half in ((meta[2], maps), (1 - meta[2], other)):
        w_in[pl.ds(pl.multiple_of(side * sz.states, sz.states), sz.states), :] = half[...]
    matmul_nt(normed, w_in, driven)
    chain_ends(sz, decay, ahead, behind, driven, 0, 0, ends)
    send_ends(sz, meta, decay, ends, enter, send)


def chain_kernel(sz, meta, ahead, behind, recv, params, ends, driven, states, enter):
    decay = decay_of(sz, params, 0)
    enter_chunk(sz, meta, recv, decay, ends, enter)
    chain_states(sz, decay, ahead, behind, driven, enter, states)


def middle_kernel(sz, meta, live, ahead, behind, states, params, normed, hidden, own_out, own_in, *refs):
    skip, gain_b, decay_b = skip_of(params, 0), gain_of(params, 1), decay_of(sz, params, 1)
    far = bits_of(sz)
    mine, other, refs = refs[:far], refs[far : 2 * far], refs[2 * far :]
    w_out, w_in_b, slope, hidden_b, normed_b, driven_b, ends_b, send_b, enter = refs
    place_maps(sz, meta, own_out, mine, other, 0, w_out)
    place_maps(sz, meta, own_in, mine, other, 2, w_in_b)
    for rows in row_parts(sz):
        on = widen(live[rows, :], sz.width // LANES)
        u = hidden[rows, :].astype(F32) + finish_rows(sz, rows, states, w_out, skip, normed, on, slope)
        hidden_b[rows, :] = u
        v = normed_rows(sz, u, gain_b, on)
        normed_b[rows, :] = v
        driven_b[rows, :] = nt(v, w_in_b[...])
    chain_ends(sz, decay_b, ahead, behind, driven_b, 0, 0, ends_b)
    send_ends(sz, meta, decay_b, ends_b, enter, send_b)


def leave_kernel(sz, meta, live, ahead, behind, recv, params, ends, driven, normed, hidden, own_out, *refs):
    decay, skip = decay_of(sz, params, 1), skip_of(params, 1)
    far = bits_of(sz)
    mine, other, refs = refs[:far], refs[far : 2 * far], refs[2 * far :]
    w_out, states, slope, last, enter = refs
    place_maps(sz, meta, own_out, mine, other, 3, w_out)
    enter_chunk(sz, meta, recv, decay, ends, enter)
    chain_states(sz, decay, ahead, behind, driven, enter, states)
    for rows in row_parts(sz):
        on = widen(live[rows, :], sz.width // LANES)
        last[rows, :] = (hidden[rows, :] + finish_rows(sz, rows, states, w_out, skip, normed, on, slope)).astype(BF)


def turn_kernel(sz, meta, ahead, behind, slope, normed, w_out, params, perm, *refs):
    decay = decay_of(sz, params, 1)
    pieces, refs = refs[: sz.blocks], refs[sz.blocks :]
    upstream, twice, grad_states, grad_skip, ends, send, stacked, enter = refs
    place_pieces(sz, meta, pieces, stacked)
    skips = []
    for rows in row_parts(sz):
        r = nt(perm[rows, :], stacked[...])
        upstream[rows, :] = r
        skips.append(open_rows(sz, rows, r, slope, normed, w_out, twice, grad_states))
    grad_skip[...] = jnp.sum(sum(skips), axis=0, keepdims=True)
    chain_ends(sz, decay, ahead, behind, grad_states, 2 * sz.states, 0, ends)
    send_ends(sz, meta, decay, ends, enter, send)


def back_middle_kernel(sz, meta, ahead, behind, recv, params, ends, grad_states, states, upstream, slope, hidden, w_in,
                       slope_b, normed_b, w_out_b,
                       grad_driven, grad_decay, grad_gain, upstream_b, twice_b, grad_states_b, grad_skip_b, ends_b, send_b,
                       enter, half):
    decay, skip, gain, decay_b = decay_of(sz, params, 1), skip_of(params, 1), gain_of(params, 1), decay_of(sz, params, 0)
    enter_chunk(sz, meta, recv, decay, ends, enter)
    adjoint_chains(sz, decay, ahead, behind, grad_states, enter, states, half, grad_driven, grad_decay)
    gains, skips = [], []
    for rows in row_parts(sz):
        r, terms = back_rows(sz, rows, grad_driven, w_in, upstream, slope, skip, hidden, gain)
        gains.append(terms)
        upstream_b[rows, :] = r
        skips.append(open_rows(sz, rows, r, slope_b, normed_b, w_out_b, twice_b, grad_states_b))
    grad_gain[...] = jnp.sum(sum(gains), axis=0, keepdims=True)
    grad_skip_b[...] = jnp.sum(sum(skips), axis=0, keepdims=True)
    chain_ends(sz, decay_b, ahead, behind, grad_states_b, 2 * sz.states, 0, ends_b)
    send_ends(sz, meta, decay_b, ends_b, enter, send_b)


def back_chain_kernel(sz, meta, ahead, behind, recv, params, ends, grad_states, states, grad_driven, grad_decay, enter, half):
    decay = decay_of(sz, params, 0)
    enter_chunk(sz, meta, recv, decay, ends, enter)
    adjoint_chains(sz, decay, ahead, behind, grad_states, enter, states, half, grad_driven, grad_decay)


def back_leave_kernel(sz, meta, params, grad_driven, upstream, slope, hidden, w_in, perm, done, *refs):
    skip, gain = skip_of(params, 0), gain_of(params, 0)
    pieces, (last, stacked) = refs[: sz.blocks], refs[sz.blocks :]
    for rows in row_parts(sz):
        r, _ = back_rows(sz, rows, grad_driven, w_in, upstream, slope, skip, hidden, gain)
        last[rows, :] = r.astype(BF)
    part = sz.width // sz.blocks
    cut_pieces(sz, meta, done, perm, stacked, [piece.at[0:part, :] for piece in pieces])
    cut_pieces(sz, meta, last, perm, stacked, [piece.at[part : 2 * part, :] for piece in pieces])


def weight_kernel(counts, other, sz, meta, *refs):
    half = 1 - meta[2] if other else meta[2]
    pairs = 2 * len(counts)
    out, at = refs[pairs], 0
    if len(refs) > pairs + 1:
        whole, out, terms = refs[pairs:]
        value = tn(refs[0][:, pl.ds(pl.multiple_of(half * sz.states, LANES), sz.states)], refs[1][...])
        out[...] = value.astype(out.dtype)
        rows = whole[pl.ds(pl.multiple_of(half * sz.states, sz.states), sz.states), :].astype(F32)
        terms[...] = jnp.sum(column_sum(rows * value), axis=0, keepdims=True)
        return
    for index, count in enumerate(counts):
        left, right = refs[2 * index], refs[2 * index + 1]
        for group in range(count):
            cols = pl.ds(pl.multiple_of((half * count + group) * sz.states, LANES), sz.states)
            out[at : at + sz.states, :] = tn(left[:, cols], right[...]).astype(out.dtype)
            at += sz.states


def split2(x):
    hi = x.astype(BF).astype(F32)
    return hi, x - hi


class Group(NamedTuple):
    first: int
    counts: tuple

    def rows(self, sz):
        return sum(self.counts) * (sz.states // sz.blocks)


def bits_of(sz):
    return sz.blocks.bit_length() - 1


def step_bit(sz, step, core):
    return 1 << ((step + core) % bits_of(sz))


def far_block(sz, group, slot, core):
    return sum(step_bit(sz, group.first + j, core) for j in range(bits_of(sz)) if (slot >> j) & 1)


def own_tiny(sz, params, terms, more, gain_b, skip_a, skip_b, decay_a, decay_b, tiny):
    gain_a = (terms[...] + more[...] + skip_of(params, 0) * skip_a[...]) / gain_of(params, 0)
    tiny[...] = jnp.zeros_like(tiny)
    for index, line in enumerate((gain_a, gain_b[...], skip_a[...], skip_b[...])):
        tiny[index : index + 1, :] = line
    tiny[4:6, 0 : sz.states] = decay_a[...]
    tiny[6:8, 0 : sz.states] = decay_b[...]
    return tiny[...]


def tiny_of(sz, tiny, owner):
    own, part = sz.states // sz.blocks, sz.width // sz.blocks
    row = lax.broadcasted_iota(jnp.int32, (8, LANES), 0)
    lane = lax.broadcasted_iota(jnp.int32, (8, LANES), 1)
    value = jnp.zeros((8, LANES), F32)
    for block in range(sz.blocks):
        wide = pltpu.roll(tiny, sz.width - block * part, 1) if block else tiny
        deep = pltpu.roll(tiny, sz.width - block * own, 1) if block else tiny
        mine = jnp.where(row < 4, jnp.where(lane < part, wide[:, :LANES], 0.0), jnp.where(lane < own, deep[:, :LANES], 0.0))
        value = jnp.where(owner == block, mine, value)
    return value


def put_sums(value, slot, kept, message, at):
    if slot % 2 == 0:
        kept[slot // 2] = value
        return at
    message[at : at + value.shape[0], :] = value.astype(BF)
    return at + value.shape[0]


def add_message(sz, group, kept, slot, message, at):
    return kept[slot] + message[at : at + group.rows(sz), :].astype(F32)


def step_kernel(old, new, sz, meta, *refs):
    came, refs = (refs[0], refs[1:]) if old else (None, refs)
    held, refs = refs[: len(old)], refs[len(old) :]
    if new:
        halves, refs = refs[: 2 * len(new.counts)], refs[2 * len(new.counts) :]
    keeps, message = refs[:-1], refs[-1]
    at = 0
    for (group, slots, row), kept, keep in zip(old, held, keeps):
        for slot in range(slots):
            value = add_message(sz, group, kept, slot, came, row + slot * group.rows(sz))
            at = put_sums(value, slot, keep, message, at)
    if new:
        own = sz.states // sz.blocks
        for slot in range(sz.blocks):
            owner = meta[0] ^ jnp.where(meta[2] == 0, far_block(sz, new, slot, 0), far_block(sz, new, slot, 1))
            parts = []
            for index, count in enumerate(new.counts):
                keep, got = halves[2 * index], halves[2 * index + 1]
                for one in range(count):
                    rows = pl.ds(pl.multiple_of(one * sz.states + owner * own, own), own)
                    parts.append(keep[rows, :].astype(F32) + got[rows, :].astype(F32))
            at = put_sums(jnp.concatenate(parts, axis=0), slot, keeps[-1], message, at)


def direct_kernel(group, sz, meta, keep, got, *refs):
    own = sz.states // sz.blocks
    lines, pieces, room = refs[:8], refs[8:-1], refs[-1]
    whole = own_tiny(sz, *lines, room)
    for index, piece in enumerate(pieces):
        owner = meta[0] ^ farthest(index, sz.blocks)
        rows = pl.ds(pl.multiple_of(owner * own, own), own)
        piece[0:own, :] = (keep[rows, :].astype(F32) + got[rows, :].astype(F32)).astype(BF)
        rest = jnp.zeros((8, sz.width - 2 * LANES), F32)
        wide = jnp.concatenate([*split2(tiny_of(sz, whole, owner)), rest], axis=1)
        piece[own : own + 16, :] = jnp.concatenate([wide, jnp.zeros_like(wide)], axis=0).astype(BF)


def fold_block_kernel(planes, groups, direct, sz, meta, *refs):
    lanes = sz.width // LANES
    held, refs = refs[: 2 * len(groups)], refs[2 * len(groups) :]
    pieces, refs = (refs[: sz.blocks], refs[sz.blocks :]) if direct else ((), refs)
    outs, talls = refs[:planes], refs[planes:]
    totals = [add_message(sz, group, held[2 * index], 0, held[2 * index + 1], row) for index, (group, row) in enumerate(groups)]
    if direct:
        total = pieces[0][...].astype(F32)
        for piece in pieces[1:]:
            total += piece[...].astype(F32)
        rows = total.shape[0] - 16
        totals.append(total[0:rows])
        tiny = total[rows : rows + 8, 0:LANES] + total[rows : rows + 8, LANES : 2 * LANES]
    at = 0
    for total, tall in zip(totals, talls):
        rows = total.shape[0]
        padded = tall.shape[0] // lanes
        for block in range(lanes):
            tall[block * padded : block * padded + rows, :] = total[:, block * LANES : (block + 1) * LANES].astype(BF)
            if padded > rows:
                tall[block * padded + rows : (block + 1) * padded, :] = jnp.zeros((padded - rows, LANES), BF)
        part = tall.shape[0] // planes
        for dist, out in enumerate(outs):
            out[at : at + part, :] = tall[pl.ds(pl.multiple_of((meta[3] ^ farthest(dist, planes)) * part, part), part), :]
        at += part
    if direct:
        rows = jnp.concatenate(split2(tiny), axis=0).astype(BF)
        for out in outs:
            out[at : at + 16, :] = rows


def fold_plane_kernel(early, sz, meta, *refs):
    parts, out, tiny = refs[early:-2], refs[-2], refs[-1]
    top = 0
    if early:
        total = refs[0][...].astype(F32)
        for piece in refs[1:early]:
            total += piece[...].astype(F32)
        top = total.shape[0]
        out[0:top, :] = total.astype(BF)
    total = parts[0][...].astype(F32)
    for piece in parts[1:]:
        total += piece[...].astype(F32)
    rows = total.shape[0] - 16
    out[top:, :] = total[0:rows].astype(BF)
    tiny[...] = total[rows : rows + 8] + total[rows + 8 :]


def finish_kernel(planes, groups, sz, meta, *refs):
    count = 2 * planes
    pieces, refs = refs[:count], refs[count:]
    tiny, lambda_log, lambda_imag, log_step, input_map = refs[0][...] + refs[1][...], *refs[2:6]
    grad_gain, grad_skip, grad_log, grad_imag, grad_step, grad_maps, grad_out = refs[6:13]
    talls, grad_in, lines = refs[13:-2], refs[-2], refs[-1]
    own = sz.states // sz.blocks
    lanes = sz.width // LANES
    start = 0
    for tall, group in zip(talls, groups):
        padded = tall.shape[0] // lanes
        part = tall.shape[0] // planes
        for side in range(2):
            half = meta[2] ^ side
            for dist in range(planes):
                rows = pl.ds(pl.multiple_of((meta[3] ^ farthest(dist, planes)) * part, part), part)
                tall[rows, :] = pieces[side * planes + dist][start : start + part, :]
            at = 0
            for which, layer, maps in group:
                out = grad_in if which == 0 else grad_out
                for one in range(maps):
                    for block in range(lanes):
                        rows = slice(block * padded + at, block * padded + at + own)
                        out[layer, half * maps + one, :, block * LANES : (block + 1) * LANES] = tall[rows, :].astype(F32)
                    at += own
        start += part
    width = sz.width // sz.blocks
    grad_gain[...] = tiny[0:2, 0:width]
    grad_skip[...] = tiny[2:4, 0:width]
    dr, di, sr, si = discretize(lambda_log[...], lambda_imag[...], log_step[...])
    lines[...] = jnp.zeros_like(lines)
    lines[0:2, 0:own] = sr
    lines[2:4, 0:own] = si
    cols = lines[...].T
    back = []
    for layer in range(2):
        qr, qi = cols[0:own, layer : layer + 1], cols[0:own, 2 + layer : 3 + layer]
        wr, wi = grad_in[layer, 0], grad_in[layer, 1]
        br, bi = input_map[layer, 0].astype(F32), input_map[layer, 1].astype(F32)
        grad_maps[layer, 0] = qr * wr + qi * wi
        grad_maps[layer, 1] = qr * wi - qi * wr
        back.append(jnp.sum(wr * br + wi * bi, axis=1, keepdims=True))
        back.append(jnp.sum(wi * br - wr * bi, axis=1, keepdims=True))
    lines[...] = jnp.zeros_like(lines)
    for index, col in enumerate(back):
        lines[0:own, index : index + 1] = col
    rows = lines[...].T
    step = jnp.exp(log_step[...])
    lr, li = -jnp.exp(lambda_log[...]), lambda_imag[...]
    norm = 1.0 / (lr * lr + li * li)
    for layer in range(2):
        at = slice(layer, layer + 1)
        a, b, h = (lr[at], li[at]), (dr[at], di[at]), step[at]
        gq = rows[2 * layer : 2 * layer + 1, 0:own], rows[2 * layer + 1 : 2 * layer + 2, 0:own]
        gd = tiny[4 + 2 * layer : 5 + 2 * layer, 0:own], tiny[5 + 2 * layer : 6 + 2 * layer, 0:own]
        inverse = a[0] * norm[at], -a[1] * norm[at]
        through = cmul(inverse[0], -inverse[1], *gq)
        gd = gd[0] + through[0], gd[1] + through[1]
        ratio = cmul(*inverse, sr[at], si[at])
        direct = cmul(ratio[0], -ratio[1], *gq)
        moved = cmul(b[0] * h, -b[1] * h, *gd)
        turn = cmul(*a, *b)
        grad_log[at, :] = (moved[0] - direct[0]) * a[0]
        grad_imag[at, :] = moved[1] - direct[1]
        grad_step[at, :] = (turn[0] * gd[0] + turn[1] * gd[1]) * h


def spread_kernel(indices, count, sz, meta, *refs):
    pieces, outs, wide, sems = refs[: len(indices)], refs[-2 - count : -2], refs[-2], refs[-1]
    part = sz.width // sz.blocks
    copies = []
    for piece, dist in zip(pieces, indices):
        owner = meta[0] ^ turned(sz, dist)
        for index, out in enumerate(outs):
            slot = len(copies)
            wide[slot] = piece[index * part : (index + 1) * part, :].astype(F32)
            cols = pl.ds(pl.multiple_of(lax.rem(owner, sz.chunks) * sz.toks, LANES), sz.toks)
            copy = pltpu.make_async_copy(wide.at[slot], out.at[lax.div(owner, sz.chunks), :, cols], sems.at[slot])
            copy.start()
            copies.append(copy)
    for copy in copies:
        copy.wait()


VMEM = pl.BlockSpec(memory_space=pltpu.VMEM)
SMEM = pl.BlockSpec(memory_space=pltpu.SMEM)
HBM = pl.BlockSpec(memory_space=pltpu.HBM)


def call(name, sz, body, items, args, outs, scratch, limit=10, in_spec=VMEM, out_spec=VMEM, time=0.0, onto=()):
    out_shape = [jax.ShapeDtypeStruct(shape, dtype) for shape, dtype in outs]

    def kernel(*refs):
        body(sz, place_of(sz, refs[0] if items else None), *refs[len(items) :])

    return pl.pallas_call(
        kernel,
        out_shape=out_shape,
        in_specs=[SMEM] * len(items) + [in_spec] * len(args) + [HBM] * len(onto),
        out_specs=[out_spec] * len(outs),
        scratch_shapes=[pltpu.VMEM(*item) if isinstance(item, tuple) else item for item in scratch],
        compiler_params=pltpu.CompilerParams(vmem_limit_bytes=limit << 20),
        input_output_aliases={len(items) + len(args) + index: index for index in range(len(onto))},
        cost_estimate=pl.CostEstimate(flops=int(COST * time), bytes_accessed=1000, transcendentals=0),
        name=name,
    )(*items, *args, *onto)


def on_device(tokens, cotangent, item_lengths, item_offsets, norm_gain, lambda_log, lambda_imag, log_step, input_map, output_map, skip_weight):
    micro, part, run = tokens.shape
    layers = norm_gain.shape[0]
    blocks = lax.axis_size("block")
    planes = lax.axis_size("plane")
    chunks = blocks // micro
    toks = run // chunks
    own = lambda_log.shape[1]
    width, states = part * blocks, own * blocks
    sz = Sizes(blocks, chunks, toks, run, toks // SEGS, width, states, item_lengths.shape[1])

    def swap(x, dist, axis="block"):
        return lax.ppermute(x, axis, [(i, i ^ dist) for i in range(lax.axis_size(axis))])

    def across(x, dist, back):
        pairs = []
        for c in range(2):
            for b in range(blocks):
                q = b ^ turned(sz, dist)
                pairs.append((c * blocks + b, (q % 2) * blocks + (q // 2) * 2 + c))
        return lax.ppermute(x, ("core", "block"), [pair[::-1] for pair in pairs] if back else pairs)

    def across_all(pieces, back=False):
        return [across(piece, dist, back) for dist, piece in enumerate(pieces)]

    table = jnp.stack([item_lengths, item_offsets])
    other_table = swap(table, 1, "core")

    def neighbour(x, dist):
        pairs = []
        for c in range(2):
            for b in range(blocks):
                q = ((b // 2) * 2 + c) ^ dist
                pairs.append((c * blocks + b, (q % 2) * blocks + (q // 2) * 2 + b % 2))
        return lax.ppermute(x, ("core", "block"), pairs)

    def swap_all(pieces, axis="block"):
        count = len(pieces)
        return [swap(piece, farthest(index, count), axis) if index else piece for index, piece in enumerate(pieces)]

    def exchange(send):
        return jnp.stack([neighbour(send[dist - 1], dist) for dist in range(1, chunks)])

    row = jnp.arange(toks, dtype=jnp.int32)[:, None]
    col = jnp.arange(toks, dtype=jnp.int32)[None, :]
    perm = ((row % SEGS) * sz.steps + row // SEGS == col).astype(BF)

    maps_own = ((2, own, width), BF)
    half_own = ((5, own, width), BF)
    given = [norm_gain, skip_weight, lambda_log, lambda_imag, log_step, input_map, output_map]
    *first_pieces, drive_b, half_b = call(
        "prepare", sz, prepare_kernel, [], [pltpu.with_memory_space_constraint(x, pltpu.HBM) for x in [tokens, *given]],
        [((first_rows(sz)[1] + 16, toks), BF)] * blocks + [maps_own, half_own],
        [(x.shape, x.dtype) for x in given] + [((8, LANES), F32), ((8, LANES), F32), maps_own, pltpu.SemaphoreType.DMA((len(given) + blocks,))],
        limit=6, in_spec=HBM)
    first_pieces = across_all(first_pieces)
    cot_cut = call("cut_cotangent", sz, cut_kernel, [], [pltpu.with_memory_space_constraint(cotangent, pltpu.HBM)],
                   [((part, toks), BF)] * blocks, [((blocks, part, toks), F32), pltpu.SemaphoreType.DMA((blocks,))], limit=4, in_spec=HBM)
    first_pieces[1], perm, cot_cut = after(first_pieces[1], perm, cot_cut)
    second_mine, held = [], half_b
    for step in range(bits_of(sz)):
        pairs = [(c * blocks + b, c * blocks + (b ^ step_bit(sz, step, c))) for c in range(2) for b in range(blocks)]
        second_mine.append(lax.ppermute(held, ("core", "block"), pairs))
        if step == 0:
            second_mine[0], first_pieces = after(second_mine[0], first_pieces)
        if step + 1 < bits_of(sz):
            (held,) = call("pile_%d" % step, sz, pile_kernel, [], [held, second_mine[-1]], [((2 * held.shape[0], own, width), BF)], [])
    maps_a, params = call("join", sz, join_kernel, [], first_pieces, [((states, width), BF), ((8, width), F32)], [])
    maps_a, other_table = after(maps_a, other_table)
    items = [jnp.stack([table, other_table])]


    mask = ((toks, LANES), F32)
    enter = ((4, SEGS, states), F32)
    stacked = ((width, toks), BF)
    rows_f, rows_b = ((toks, width), F32), ((toks, width), BF)
    drv = ((toks, 2 * states), F32)
    sts = ((toks, 4 * states), BF)
    gst = ((toks, 4 * states), F32)
    snd = ((chunks - 1, 2, states), F32)
    w_in, w_out = ((2 * states, width), BF), ((4 * states, width), BF)
    line, gdec = ((1, width), F32), ((2, states), F32)
    piece_out = [((part, toks), BF)] * blocks

    other_a = swap(maps_a, 1, "core")
    hidden_a, normed_a, live, ahead, behind = call(
        "open", sz, open_kernel, items, [perm, params, *first_pieces], [rows_b, rows_b, mask, mask, mask], [stacked], time=3)
    w_in_a, driven_a, ends_a, send_a = call(
        "enter", sz, enter_kernel, items, [ahead, behind, params, normed_a, maps_a, other_a], [w_in, drv, enter, snd], [enter])
    recv = exchange(send_a)
    early_maps = [swap(piece, 1, "core") for piece in second_mine[:-1]]
    recv, early_maps = after(recv, early_maps)
    (states_a,) = call("chain", sz, chain_kernel, items, [ahead, behind, recv, params, ends_a, driven_a], [sts], [enter])
    last_mine, states_a = after(second_mine[-1], states_a)
    second_maps = [*second_mine[:-1], last_mine], [*early_maps, swap(last_mine, 1, "core")]
    cot_cut, _ = after(cot_cut, recv)
    cot_pieces = across_all(cot_cut)
    w_out_a, w_in_b, slope_a, hidden_b, normed_b, driven_b, ends_b, send_b = call(
        "middle", sz, middle_kernel, items,
        [live, ahead, behind, states_a, params, normed_a, hidden_a, output_map[0], drive_b, *second_maps[0], *second_maps[1]],
        [w_out, w_in, rows_b, rows_f, rows_b, drv, enter, snd], [enter], time=11)
    recv = exchange(send_b)
    w_out_b, states_b, slope_b, last_b = call(
        "leave", sz, leave_kernel, items,
        [live, ahead, behind, recv, params, ends_b, driven_b, normed_b, hidden_b, output_map[1], *second_maps[0], *second_maps[1]],
        [w_out, sts, rows_b, rows_b], [enter])

    def half_grads(name, other, pairs, counts, more=(), time=0.0):
        args = [x for pair in pairs for x in pair]
        outs = [((sum(counts) * states, width), BF)] + [line] * len(more)
        return call(name, sz, partial(weight_kernel, counts, other), [], [*args, *more], outs, [], time=time)

    groups = [Group(0, (2,)), Group(1, (3,))]
    steps = bits_of(sz)
    kept, came, place = {}, {}, {}

    def halve(step, halves=()):
        old, args = [], []
        for index, group in enumerate(groups):
            if 0 < step - group.first < steps:
                slots = 1 << (steps - (step - group.first))
                old.append((group, slots, place[step - 1, index]))
                args.append(kept[index])
        if old:
            args.insert(0, came[step - 1])
        new = groups[step] if step < len(groups) else None
        outs, at = [], 0
        for index, group in enumerate(groups):
            if 0 <= step - group.first < steps:
                slots = 1 << (steps - 1 - (step - group.first))
                outs.append((index, ((slots, group.rows(sz), width), F32)))
                place[step, index] = at
                at += slots * group.rows(sz)
        results = call("halve_%d" % step, sz, partial(step_kernel, old, new), [], [*args, *halves],
                       [shape for _, shape in outs] + [((at, width), BF)], [])
        for (index, _), value in zip(outs, results):
            kept[index] = value
        return results[-1]

    def send_step(step, message):
        pairs = [(c * blocks + b, c * blocks + (b ^ step_bit(sz, step, c))) for c in range(2) for b in range(blocks)]
        came[step] = lax.ppermute(message, ("core", "block"), pairs)

    def spread(name, pieces, first, onto=(), time=0.0):
        indices = tuple(range(first, blocks, 2))
        return call(name, sz, partial(spread_kernel, indices, 2), [], pieces, [((micro, part, run), F32)] * 2,
                    [((blocks, part, toks), F32), pltpu.SemaphoreType.DMA((blocks,))], limit=6, out_spec=HBM, time=time, onto=onto)

    lanes = width // LANES

    def tall_of(rows):
        step = max(SEGS * planes // lanes, SEGS)
        return ((lanes * (-(-rows // step) * step), LANES), BF)

    def over_planes(name, which, direct=()):
        ends = [(groups[index], place[groups[index].first + steps - 1, index]) for index in which]
        talls = [tall_of(group.rows(sz)) for group, _ in ends] + [tall_of(own)] * bool(direct)
        cut = sum(t[0][0] for t in talls) // planes + (16 if direct else 0)
        args = [x for index in which for x in (kept[index], came[groups[index].first + steps - 1])]
        return swap_all(call(name, sz, partial(fold_block_kernel, planes, ends, bool(direct)), [], [*args, *direct],
                             [((cut, LANES), BF)] * planes, talls), "plane")

    up_b, twice_b, gstates_b, gskip_b, ends, send = call(
        "turn", sz, turn_kernel, items, [ahead, behind, slope_b, normed_b, w_out_b, params, perm, *cot_pieces],
        [rows_f, rows_b, gst, line, enter, snd], [stacked, enter], time=6)
    recv = exchange(send)
    pairs = [(states_b, twice_b)]
    (send_maps,) = half_grads("grads_a_send", True, pairs, (2,))
    got = swap(send_maps, 1, "core")
    (keep,) = half_grads("grads_a_keep", False, pairs, (2,), time=2)
    message = halve(0, (keep, got))
    recv, message = after(recv, message)
    send_step(0, message)
    gdriven_b, gdecay_b, ggain_b, up_a, twice_a, gstates_a, gskip_a, ends, send = call(
        "back_middle", sz, back_middle_kernel, items,
        [ahead, behind, recv, params, ends, gstates_b, states_b, up_b, slope_b, hidden_b, w_in_b, slope_a, normed_a, w_out_a],
        [((toks, 2 * states), BF), gdec, line, rows_f, rows_b, gst, line, enter, snd], [enter, drv], limit=12, time=11)
    recv = exchange(send)
    gdriven_b, came[0] = after(gdriven_b, came[0])
    pairs = [(gdriven_b, normed_b), (states_a, twice_a)]
    (send_maps,) = half_grads("grads_b_send", True, pairs, (1, 2))
    got = swap(send_maps, 1, "core")
    (keep,) = half_grads("grads_b_keep", False, pairs, (1, 2), time=9)
    message = halve(1, (keep, got))
    recv, message = after(recv, message)
    send_step(1, message)
    gdriven_a, gdecay_a = call(
        "back_chain", sz, back_chain_kernel, items, [ahead, behind, recv, params, ends, gstates_a, states_a],
        [((toks, 2 * states), BF), gdec], [enter, drv], limit=12, time=9)
    send_maps, terms = half_grads("grads_c_send", True, [(gdriven_a, normed_a)], (1,), [w_in_a])
    gdriven_a, send_maps = after(gdriven_a, send_maps)
    got = swap(send_maps, 1, "core")
    keep, more = half_grads("grads_c_keep", False, [(gdriven_a, normed_a)], (1,), [w_in_a], time=0)
    sums_c = list(call(
        "direct", sz, partial(direct_kernel, None), [],
        [keep, got, params, terms, more, ggain_b, gskip_a, gskip_b, gdecay_a, gdecay_b], [((own + 16, width), BF)] * blocks, [((8, width), F32)]))
    gdriven_a, sums_c[0] = after(gdriven_a, sums_c[0])
    sums_c = swap_all(sums_c)
    last_pieces = call(
        "back_leave", sz, back_leave_kernel, [], [params, gdriven_a, up_a, slope_a, hidden_a, w_in_a, perm, last_b],
        [((2 * part, toks), BF)] * blocks, [rows_b, stacked], limit=12, time=6)
    last_pieces, came[1], sums_c = after(last_pieces, came[1], sums_c)
    message = halve(2)
    kept[0], message = after(kept[0], message)
    first_parts = over_planes("planes_a", [0]) if steps <= 2 else []
    send_step(2, message)
    if first_parts:
        came[2], first_parts = after(came[2], first_parts)
    for step in range(3, steps + 1):
        send_step(step, halve(step))
    parts = over_planes("planes", [1] if first_parts else [0, 1], sums_c)
    last_pieces, parts[0] = after(last_pieces, parts[0])
    early = [across(piece, 2 * dist, True) for dist, piece in enumerate(last_pieces[0::2])]
    parts[0], early = after(parts[0], early)
    sum_all, tiny = call(
        "sum", sz, partial(fold_plane_kernel, len(first_parts)), [], [*first_parts, *parts],
        [((sum(x[0].shape[0] for x in (first_parts, parts) if x) - 16, LANES), BF), ((8, LANES), F32)], [])
    whole = swap_all([sum_all] * planes, "plane")
    late, _ = after(last_pieces[1::2], sum_all)
    late = [across(piece, 2 * dist + 1, True) for dist, piece in enumerate(late)]
    whole = swap_all([sum_all] * planes, "plane")
    late, others = after(late, [sum_all, tiny, *whole[planes - 0 :]])
    others = [swap(x, 1, "core") for x in others]
    halves = spread("spread_early", early, 0)
    late, halves = after(late, halves)
    output, input_grad = spread("spread_late", late, 1, halves, time=9)
    far = whole[1 : planes - 0]
    far, others, output = after(far, others, output)
    far = [swap(x, 1, "core") for x in far]
    whole += [others[0], *far, *others[2:]]
    tiny_other = others[1]
    small_out = ((layers, own), F32)
    grad_gain, grad_skip, grad_log, grad_imag, grad_step, grad_in, grad_out = call(
        "finish", sz, partial(finish_kernel, planes, ([(1, 1, 2)], [(0, 1, 1), (1, 0, 2)], [(0, 0, 1)])), [],
        [*whole, tiny, tiny_other, lambda_log, lambda_imag, log_step, input_map],
        [((layers, part), F32)] * 2 + [small_out] * 3 + [((layers, 2, own, width), F32), ((layers, 4, own, width), F32)],
        [tall_of(n * own) for n in (2, 3, 1)] + [((layers, 2, own, width), F32), ((LANES, LANES), F32)])
    return output, input_grad, grad_gain, grad_log, grad_imag, grad_step, grad_in, grad_out, grad_skip


def solution(mesh):
    rows, blocks = mesh.devices.shape
    inner = Mesh(mesh.devices.reshape(rows // 2, 2, blocks), ("plane", "core", "block"))
    dp = ("plane", "core")
    half = P(None, "block")
    maps = P(None, None, "block", None)
    acts = P(None, "block", dp)
    items = P(None, dp)
    return jax.shard_map(
        on_device,
        mesh=inner,
        in_specs=(acts, acts, items, items, half, half, half, half, maps, maps, half),
        out_specs=(acts, acts, half, half, half, half, maps, maps, half),
        check_vma=False,
    )
```
